32 devices in a mesh: depth: 4 (over y, x), rows: 8 (over z, core).
Axes of the slice: x: 2, y: 2, z: 4, core: 2. Of those that a mesh axis runs over, the one named last changes fastest.
Arguments:
- hologram: bfloat16 [4096, 4096], P('rows'), may hold values from 0.25 to 1.75
- background: bfloat16 [4096, 4096], P('rows'), may hold values from 0.5 to 2
Outputs:
- focus: float32 [4096, 4096], P('rows')
The draws below stay inside these ranges and needn't reach their ends.
All inputs are finite; a program needn't handle non-finite values.
Results may differ from the reference program's by a relative error of at most 0.025.
Values may be sent and summed in bfloat16 or wider, within the bound.
No kernel may reach another device: no remote copies, remote signals or barrier semaphores. Data moves between devices by JAX's collectives and lax.ppermute only.
A program may use at most 128 MiB of HBM per device.

```python
import math
import jax
import jax.numpy as jnp
from jax import lax

N = 4096
RADIX = 64
PLANES = 4


def block_scale(stream_key, shape, split, low, largest):
    def one(position, blocks):
        steps = jax.random.uniform(jax.random.fold_in(jax.random.fold_in(stream_key, 6), position), (blocks,), jnp.float32, low / len(split), largest / len(split))
        return jnp.repeat(jnp.exp(steps), shape[position] // blocks).reshape((-1,) + (1,) * (len(shape) - position - 1))

    gain = one(*split[0])
    for cut in split[1:]:
        gain = gain * one(*cut)
    return gain


def setup_inputs(seed: int = 0) -> dict:
    seeds = jax.random.split(jax.random.key(seed), 3)
    hologram = jnp.clip(0.25 + 1.5 * jax.random.uniform(seeds[0], (N, N), jnp.float32) ** block_scale(seeds[0], (N, N), ((0, 8),), -0.2, 0.2), 0.25, 1.75).astype(jnp.bfloat16)
    background = jnp.clip(jnp.exp(math.log(2.0) - 1.3862944 * jax.random.uniform(seeds[1], (N, N), jnp.float32) ** block_scale(seeds[1], (N, N), ((0, 8),), -0.2, 0.2)), 0.5, 2.0).astype(jnp.bfloat16)
    return dict(hologram=hologram, background=background)


wave_number = 0.6
depth_start = 8.0
depth_step = 2.0

def fourier_tables(radix_size, sign_value):
    indices = jnp.arange(radix_size, dtype=jnp.int32)
    products = indices[:, None] * indices[None, :] % radix_size
    angles = products.astype(jnp.float32) * (sign_value * 2.0 * math.pi / radix_size)
    scaling = 1.0 / math.sqrt(radix_size)
    cosine_part = jnp.cos(angles) * scaling
    sine_part = jnp.sin(angles) * scaling
    matrix = jnp.stack([jnp.stack([cosine_part, -sine_part]), jnp.stack([sine_part, cosine_part])])
    return matrix.astype(jnp.bfloat16)

def twiddle_table(radix_size, sign_value):
    indices = jnp.arange(radix_size, dtype=jnp.int32)
    total = radix_size * radix_size
    products = indices[:, None] * indices[None, :] % total
    angles = products.astype(jnp.float32) * (sign_value * 2.0 * math.pi / total)
    return (jnp.cos(angles), jnp.sin(angles))

def rotate(data, cosine_part, sine_part):
    return jnp.stack([data[0] * cosine_part - data[1] * sine_part, data[0] * sine_part + data[1] * cosine_part])

def contract(form, matrix, data):
    return jnp.einsum(form, matrix.astype(jnp.float32), data.astype(jnp.float32))

def forward_last(data):
    batch_size = data.shape[1]
    shaped = data.reshape(2, batch_size, RADIX, RADIX)
    matrix = fourier_tables(RADIX, -1.0)
    cosine_part, sine_part = twiddle_table(RADIX, -1.0)
    opening = contract('ocka,cmab->omkb', matrix, shaped)
    sectioned = rotate(opening, cosine_part, sine_part).astype(jnp.bfloat16)
    closing = contract('ocjb,cmkb->omkj', matrix, sectioned)
    return closing.reshape(2, batch_size, N).astype(jnp.bfloat16)

def forward_first(data):
    batch_size = data.shape[2]
    shaped = data.reshape(2, RADIX, RADIX, batch_size)
    matrix = fourier_tables(RADIX, -1.0)
    cosine_part, sine_part = twiddle_table(RADIX, -1.0)
    opening = contract('ocka,cabm->okbm', matrix, shaped)
    sectioned = rotate(opening, cosine_part[:, :, None], sine_part[:, :, None]).astype(jnp.bfloat16)
    closing = contract('ocjb,ckbm->okjm', matrix, sectioned)
    return closing.reshape(2, N, batch_size).astype(jnp.bfloat16)

def inverse_last(data):
    batch_size = data.shape[1]
    shaped = data.reshape(2, batch_size, RADIX, RADIX)
    matrix = fourier_tables(RADIX, 1.0)
    cosine_part, sine_part = twiddle_table(RADIX, 1.0)
    opening = contract('ocbj,cmkj->omkb', matrix, shaped)
    sectioned = rotate(opening, cosine_part, sine_part).astype(jnp.bfloat16)
    closing = contract('ocak,cmkb->omab', matrix, sectioned)
    return closing.reshape(2, batch_size, N)

def inverse_first(data):
    batch_size = data.shape[2]
    shaped = data.reshape(2, RADIX, RADIX, batch_size)
    matrix = fourier_tables(RADIX, 1.0)
    cosine_part, sine_part = twiddle_table(RADIX, 1.0)
    opening = contract('ocbj,ckjm->okbm', matrix, shaped)
    sectioned = rotate(opening, cosine_part[:, :, None], sine_part[:, :, None]).astype(jnp.bfloat16)
    closing = contract('ocak,ckbm->oabm', matrix, sectioned)
    return closing.reshape(2, N, batch_size)

def frequencies(positions):
    natural = positions // RADIX + RADIX * (positions % RADIX)
    signed_freq = jnp.where(natural >= N // 2, natural - N, natural)
    return signed_freq.astype(jnp.float32) / N

def propagator(freq_rows, freq_cols, distance):
    radial = freq_rows[:, None] ** 2 + freq_cols[None, :] ** 2
    limit = wave_number * wave_number
    amplitude = jnp.exp(-2.0 * math.pi * distance * jnp.sqrt(jnp.maximum(radial - limit, 0.0)))
    phase_angle = 2.0 * math.pi * distance * (jnp.sqrt(jnp.maximum(limit - radial, 0.0)) - wave_number)
    return (amplitude * jnp.cos(phase_angle), amplitude * jnp.sin(phase_angle))

def propagate(spectrum, cosine_part, sine_part):
    return rotate(spectrum.astype(jnp.float32), cosine_part, sine_part).astype(jnp.bfloat16)

def sharpness(lower_plane, centre_block, upper_plane, north_row, south_row):
    centre = centre_block.astype(jnp.float32)
    east_col = jnp.concatenate([centre[..., 1:], centre[..., -1:]], axis=-1)
    west_col = jnp.concatenate([centre[..., :1], centre[..., :-1]], axis=-1)
    depth_diff = upper_plane.astype(jnp.float32) - lower_plane.astype(jnp.float32)
    row_diff = south_row.astype(jnp.float32) - north_row.astype(jnp.float32)
    col_diff = east_col - west_col
    return (depth_diff * depth_diff + row_diff * row_diff + col_diff * col_diff) / 8.0

def reference(hologram, background):
    contrast = (hologram.astype(jnp.float32) / background.astype(jnp.float32) - 1.0).astype(jnp.bfloat16)
    hologram_field = jnp.stack([contrast, jnp.zeros_like(contrast)])
    spectrum = forward_first(forward_last(hologram_field))
    positions = jnp.arange(N, dtype=jnp.int32)
    freq_all = frequencies(positions)

    def intensity_of(plane_slot):
        distance = depth_start + depth_step * plane_slot.astype(jnp.float32)
        cosine_part, sine_part = propagator(freq_all, freq_all, distance)
        propagated = propagate(spectrum, cosine_part, sine_part)
        halfway = inverse_first(propagated).astype(jnp.bfloat16)
        result_field = inverse_last(halfway)
        return (result_field[0] * result_field[0] + result_field[1] * result_field[1]).astype(jnp.bfloat16)
    opening_plane = intensity_of(jnp.int32(0))

    def advance(carry, plane_slot):
        previous, current, sharpest = carry
        following = intensity_of(jnp.minimum(plane_slot + 1, PLANES - 1).astype(jnp.int32))
        north_row = jnp.concatenate([current[:1], current[:-1]], axis=0)
        south_row = jnp.concatenate([current[1:], current[-1:]], axis=0)
        scores = sharpness(previous, current, following, north_row, south_row)
        return ((current, following, jnp.maximum(sharpest, scores)), None)
    start = (opening_plane, opening_plane, jnp.zeros((N, N), jnp.float32))
    final, unused = lax.scan(advance, start, jnp.arange(PLANES, dtype=jnp.int32))
    return final[2]
```

```python
import functools
import math

import jax
import jax.numpy as jnp
import numpy as np
from jax import lax
from jax.experimental import pallas as pl
from jax.experimental.pallas import tpu as pltpu
from jax.sharding import Mesh
from jax.sharding import PartitionSpec as P

N = 4096
RADIX = 64
PL_DEV = 1


wave_number = 0.6
depth_start = 8.0
depth_step = 2.0


def padded_2(block, sides, width):
    for axis, dim in sides:
        count = lax.axis_size(axis)
        forward = [(i, i + 1) for i in range(count - 1)]
        backward = [(target, source) for source, target in forward]
        low = lax.ppermute(
            lax.slice_in_dim(block, block.shape[dim] - width, None, axis=dim), axis, forward
        )
        high = lax.ppermute(lax.slice_in_dim(block, 0, width, axis=dim), axis, backward)
        block = jnp.concatenate([low, block, high], axis=dim)
    return block


def fourier_tables(radix_size, sign_value):
    indices = jnp.arange(radix_size, dtype=jnp.int32)
    products = indices[:, None] * indices[None, :] % radix_size
    angles = products.astype(jnp.float32) * (sign_value * 2.0 * math.pi / radix_size)
    scaling = 1.0 / math.sqrt(radix_size)
    cosine_part = jnp.cos(angles) * scaling
    sine_part = jnp.sin(angles) * scaling
    matrix = jnp.stack([jnp.stack([cosine_part, -sine_part]), jnp.stack([sine_part, cosine_part])])
    return matrix.astype(jnp.bfloat16)


def twiddle_table(radix_size, sign_value):
    indices = jnp.arange(radix_size, dtype=jnp.int32)
    total = radix_size * radix_size
    products = indices[:, None] * indices[None, :] % total
    angles = products.astype(jnp.float32) * (sign_value * 2.0 * math.pi / total)
    return (jnp.cos(angles), jnp.sin(angles))


def rotate(data, cosine_part, sine_part):
    return jnp.stack(
        [data[0] * cosine_part - data[1] * sine_part, data[0] * sine_part + data[1] * cosine_part]
    )


def contract(form, matrix, data):
    return jnp.einsum(form, matrix, data, preferred_element_type=jnp.float32)


def forward_real(data):
    batch_size = data.shape[1]
    shaped = data.reshape(RADIX, RADIX, batch_size)
    matrix = fourier_tables(RADIX, -1.0)
    cosine_part, sine_part = twiddle_table(RADIX, -1.0)
    opening = contract("oka,abm->okbm", matrix[:, 0], shaped)
    sectioned = rotate(opening, cosine_part[:, :, None], sine_part[:, :, None]).astype(jnp.bfloat16)
    closing = contract("ocjb,ckbm->okjm", matrix, sectioned)
    return closing.reshape(2, N, batch_size).astype(jnp.bfloat16)


def forward_first(data):
    batch_size = data.shape[2]
    shaped = data.reshape(2, RADIX, RADIX, batch_size)
    matrix = fourier_tables(RADIX, -1.0)
    cosine_part, sine_part = twiddle_table(RADIX, -1.0)
    opening = contract("ocka,cabm->okbm", matrix, shaped)
    sectioned = rotate(opening, cosine_part[:, :, None], sine_part[:, :, None]).astype(jnp.bfloat16)
    closing = contract("ocjb,ckbm->okjm", matrix, sectioned)
    return closing.reshape(2, N, batch_size).astype(jnp.bfloat16)


def inverse_first(data):
    batch_size = data.shape[2]
    shaped = data.reshape(2, RADIX, RADIX, batch_size)
    matrix = fourier_tables(RADIX, 1.0)
    cosine_part, sine_part = twiddle_table(RADIX, 1.0)
    opening = contract("ocbj,ckjm->okbm", matrix, shaped)
    sectioned = rotate(opening, cosine_part[:, :, None], sine_part[:, :, None]).astype(jnp.bfloat16)
    closing = contract("ocak,ckbm->oabm", matrix, sectioned)
    return closing.reshape(2, N, batch_size)


def frequencies(positions):
    natural = positions // RADIX + RADIX * (positions % RADIX)
    signed_freq = jnp.where(natural >= N // 2, natural - N, natural)
    return signed_freq.astype(jnp.float32) / N


def propagator(freq_whole, freq_own, distance):
    radial = freq_whole[:, None] ** 2 + freq_own[None, :] ** 2
    limit = wave_number * wave_number
    amplitude = jnp.exp(-2.0 * math.pi * distance * jnp.sqrt(jnp.maximum(radial - limit, 0.0)))
    phase_angle = (
        2.0 * math.pi * distance * (jnp.sqrt(jnp.maximum(limit - radial, 0.0)) - wave_number)
    )
    return (amplitude * jnp.cos(phase_angle), amplitude * jnp.sin(phase_angle))


def propagate(spectrum, cosine_part, sine_part):
    return rotate(spectrum.astype(jnp.float32), cosine_part, sine_part).astype(jnp.bfloat16)


def shards(hologram, background):
    row_count = hologram.shape[0]
    contrast = (hologram.astype(jnp.float32) / background.astype(jnp.float32) - 1.0).astype(
        jnp.bfloat16
    )
    along_rows = forward_real(contrast.T)
    columns = lax.all_to_all(
        jnp.swapaxes(along_rows, 1, 2), "rows", split_axis=2, concat_axis=1, tiled=True
    )
    spectrum = forward_first(columns)
    row_index = lax.axis_index("rows")
    own_positions = row_index * row_count + jnp.arange(row_count, dtype=jnp.int32)
    freq_own = frequencies(own_positions)
    freq_whole = frequencies(jnp.arange(N, dtype=jnp.int32))
    depth_index = lax.axis_index("depth")
    distance = depth_start + depth_step * (depth_index * PL_DEV + 0).astype(jnp.float32)
    cosine_part, sine_part = propagator(freq_whole, freq_own, distance)
    propagated = propagate(spectrum, cosine_part, sine_part)
    halfway = inverse_first(propagated).astype(jnp.bfloat16)
    restored = lax.all_to_all(
        jnp.swapaxes(halfway, 1, 2), "rows", split_axis=2, concat_axis=1, tiled=True
    )
    result_field = inverse_first(restored)
    intensities = [
        (result_field[0] * result_field[0] + result_field[1] * result_field[1]).astype(jnp.bfloat16)
    ]
    stacked = jnp.stack(intensities)
    padded = padded_2(stacked, (("depth", 0), ("rows", 2)), 1)
    centre_block = padded[1:-1, :, 1:-1]
    plane_ids = jnp.arange(PL_DEV, dtype=jnp.int32)[:, None, None]
    row_ids = jnp.arange(row_count, dtype=jnp.int32)[None, None, :]
    depth_count = lax.axis_size("depth")
    row_groups = lax.axis_size("rows")
    lower_plane = jnp.where(
        (depth_index == 0) & (plane_ids == 0), centre_block, padded[:-2, :, 1:-1]
    )
    upper_plane = jnp.where(
        (depth_index == depth_count - 1) & (plane_ids == PL_DEV - 1),
        centre_block,
        padded[2:, :, 1:-1],
    )
    north_row = jnp.where((row_index == 0) & (row_ids == 0), centre_block, padded[1:-1, :, :-2])
    south_row = jnp.where(
        (row_index == row_groups - 1) & (row_ids == row_count - 1),
        centre_block,
        padded[1:-1, :, 2:],
    )
    centre = centre_block.astype(jnp.float32)
    east_col = jnp.concatenate([centre[:, 1:], centre[:, -1:]], axis=1)
    west_col = jnp.concatenate([centre[:, :1], centre[:, :-1]], axis=1)
    depth_diff = upper_plane.astype(jnp.float32) - lower_plane.astype(jnp.float32)
    row_diff = south_row.astype(jnp.float32) - north_row.astype(jnp.float32)
    col_diff = east_col - west_col
    scores = (depth_diff * depth_diff + row_diff * row_diff + col_diff * col_diff) / 8.0
    sharpest = jnp.max(scores, axis=0)
    merged = lax.pmax(sharpest.astype(jnp.bfloat16), "depth").astype(sharpest.dtype)
    return merged.T


OUT = 16
INN = 256
CLS = 8
LANE = 128


def slot_frequencies():
    table = np.arange(CLS)[:, None] + OUT * np.arange(INN)[None, :]
    half = np.arange(INN // 2)
    table[0] = np.concatenate([OUT * half, CLS + OUT * half])
    return table


def angles(products):
    return 2.0 * np.pi * (products % N) / N


def row_forward_tables():
    freq = slot_frequencies()
    theta = angles(np.arange(INN)[None, :, None] * freq[:, None, :])
    cos, sin = np.cos(theta) / 64.0, np.sin(theta) / 64.0
    top = np.stack([cos, -sin], axis=2)
    low = np.stack([sin, cos], axis=2)
    first = np.arange(INN) < INN // 2
    low[0] = np.where(first, 0.0, top[0])
    top[0] = np.where(first, top[0], 0.0)
    full = np.concatenate([top, low], axis=1)
    full = full.reshape(CLS, 2 * INN, 2, 2, LANE).transpose(0, 1, 3, 2, 4)
    return full.reshape(CLS, 2 * INN, 2 * INN).astype(jnp.bfloat16)


def row_forward_weights():
    turn = 2.0 * np.pi * np.arange(CLS)[:, None] * np.arange(OUT)[None, :] / OUT
    re, im = np.cos(turn), -np.sin(turn)
    im[0] = (-1.0) ** np.arange(OUT)
    return np.stack([re, im], axis=1).reshape(-1).astype(np.float32)


def row_inverse_tables():
    freq = slot_frequencies()
    theta = angles(freq[:, :, None] * np.arange(INN)[None, None, :])
    cos, sin = np.cos(theta) / 32.0, np.sin(theta) / 32.0
    full = np.zeros((CLS, 2, INN, 2, INN))
    full[:, 0, :, 0], full[:, 0, :, 1] = cos, sin
    full[:, 1, :, 0], full[:, 1, :, 1] = -sin, cos
    half = INN // 2
    full[0] = 0.0
    full[0, 0, :half, 0], full[0, 1, :half, 0] = cos[0, :half], -sin[0, :half]
    full[0, 0, half:, 1], full[0, 1, half:, 1] = cos[0, half:], -sin[0, half:]
    full[0, 0, 0, 0] = 1.0 / 64.0
    full[0, 1, 0, 0] = (-1.0) ** np.arange(INN) / 64.0
    full = full.reshape(CLS, 2, 2, LANE, 2 * INN).transpose(0, 2, 1, 3, 4)
    return full.reshape(CLS, 2 * INN, 2 * INN).astype(jnp.bfloat16)


def column_tables():
    turn = 2.0 * np.pi * np.arange(OUT)[:, None] * np.arange(OUT)[None, :] / OUT
    eye = np.eye(16)
    outer_cos, outer_sin = np.kron(np.cos(turn), eye) / 4.0, np.kron(np.sin(turn), eye) / 4.0
    outer = np.concatenate([outer_cos, -outer_sin])
    half_rows = outer_cos.shape[0] // 2
    back = np.stack(
        [
            np.concatenate([outer_cos[i * half_rows :][:half_rows], outer_sin[i * half_rows :][:half_rows]])
            for i in range(2)
        ]
    )
    freq = np.arange(OUT)[:, None] + OUT * np.arange(INN)[None, :]
    theta = angles(freq[:, :, None] * np.arange(INN)[None, None, :])
    inner = np.concatenate([np.cos(theta), -np.sin(theta)], axis=1) / 16.0
    theta = theta.transpose(0, 2, 1)
    inner_back = np.concatenate([np.cos(theta), np.sin(theta)], axis=1) / 16.0
    cast = lambda table: table.astype(jnp.bfloat16)
    return cast(outer), cast(inner), cast(inner_back), cast(back)


def dot(left, right):
    return jnp.dot(left, right, preferred_element_type=jnp.float32)


def split_complex(both, width):
    rows = both.shape[0] // 2
    top, low = both[:rows], both[rows:]
    return top[:, :width] - low[:, width:], top[:, width:] + low[:, :width]


def quarter_kernel(radial):
    gap = wave_number * wave_number - radial
    root = jnp.sqrt(jnp.abs(gap))
    inside = gap > 0.0
    half_pi = 0.5 * math.pi
    angle = half_pi * (jnp.where(inside, root, 0.0) - wave_number)
    decay = jnp.exp(jnp.where(inside, 0.0, -half_pi * root))
    square = angle * angle
    sine = 1.0 / 362880.0
    for c in (-1.0 / 5040.0, 1.0 / 120.0, -1.0 / 6.0, 1.0):
        sine = sine * square + c
    cosine = -1.0 / 3628800.0
    for c in (1.0 / 40320.0, -1.0 / 720.0, 1.0 / 24.0, -0.5, 1.0):
        cosine = cosine * square + c
    return decay * cosine, decay * (sine * angle)


def squared(re, im):
    return (re - im) * (re + im), 2.0 * re * im


def start_and_step(radial):
    value = quarter_kernel(radial)
    distance = 0.25
    step = None
    while distance < depth_start:
        value = squared(*value)
        distance *= 2.0
        if distance == depth_step:
            step = value
    return value, step


def signed_fraction(natural):
    return jnp.where(natural >= N // 2, natural - N, natural).astype(jnp.float32) * (1.0 / N)


def row_forward_kernel(own, weights, holo, back, table, out, nyquist, acc):
    rows = holo.shape[0]
    group = own[0]
    lane = lax.broadcasted_iota(jnp.int32, (16, INN), 1)
    sign = jnp.where(lane % 2 == 0, 1.0, -1.0)

    def strip(i, carry):
        here = pl.ds(pl.multiple_of(i * 16, 16), 16)
        sums = [jnp.zeros((16, INN), jnp.float32) for _ in range(5)]
        for a in range(OUT):
            there = pl.ds(a * INN, INN)
            value = holo[here, there].astype(jnp.float32) / back[here, there].astype(jnp.float32)
            value = (value - 1.0).astype(jnp.bfloat16).astype(jnp.float32)
            for q in range(4):
                w = weights[(group * 2 + q // 2) * (2 * OUT) + (q % 2) * OUT + a]
                sums[q] = sums[q] + value * w
            sums[4] = sums[4] + value
        for q in range(4):
            acc[q // 2, here, pl.ds((q % 2) * INN, INN)] = sums[q].astype(jnp.bfloat16)
        turned = sums[4] * sign
        nyquist[here, :] = turned[:, :LANE] + turned[:, LANE:]
        return carry

    lax.fori_loop(0, rows // 16, strip, 0)
    for q in range(2):
        result = dot(acc[q], table[q]).astype(jnp.bfloat16)
        for low in range(2):
            part = result[:, low * 2 * LANE : (low + 1) * 2 * LANE]
            for high in range(2):
                out[high, low, q] = part


def row_forward(own, hologram, background):
    rows = hologram.shape[0]
    block = 128
    table = jnp.asarray(row_forward_tables())
    weights = jnp.asarray(row_forward_weights())
    return pl.pallas_call(
        row_forward_kernel,
        grid_spec=pltpu.PrefetchScalarGridSpec(
            num_scalar_prefetch=2,
            grid=(rows // block,),
            in_specs=[
                pl.BlockSpec((block, N), lambda i, o, w: (i, 0)),
                pl.BlockSpec((block, N), lambda i, o, w: (i, 0)),
                pl.BlockSpec((2, 2 * INN, 2 * INN), lambda i, o, w: (o[0], 0, 0)),
            ],
            out_specs=[
                pl.BlockSpec((2, 2, 2, block, 2 * LANE), lambda i, o, w: (0, 0, 0, i, 0)),
                pl.BlockSpec((block, LANE), lambda i, o, w: (i, 0)),
            ],
            scratch_shapes=[pltpu.VMEM((2, block, 2 * INN), jnp.bfloat16)],
        ),
        out_shape=[
            jax.ShapeDtypeStruct((2, 2, 2, rows, 2 * LANE), jnp.bfloat16),
            jax.ShapeDtypeStruct((rows, LANE), jnp.float32),
        ],
        compiler_params=pltpu.CompilerParams(vmem_limit_bytes=40 * 1024 * 1024),
        cost_estimate=pl.CostEstimate(flops=10**10, bytes_accessed=12 * 2**20, transcendentals=0),
        name="row_forward",
    )(own, weights, hologram, background, table)


def column_kernel(planes, data, fx2, outer, inner, inner_back, back, out, first, mixed, second):
    step = pl.program_id(0)
    width = LANE

    @pl.when(step == 0)
    def _():
        def chunk(i, carry):
            here = pl.ds(pl.multiple_of(i * 16, 16), 16)
            block = data[:, here, :].reshape(OUT * 16, 2 * width)
            re, im = split_complex(dot(outer[...], block), width)
            value = jnp.concatenate([re, im], axis=1).astype(jnp.bfloat16)
            first[:, here, :] = value.reshape(OUT, 16, 2 * width)
            return carry

        lax.fori_loop(0, INN // 16, chunk, 0)

    @pl.when(step < OUT)
    def _():
        both = dot(inner[0], first[step])
        strip = 32
        for i in range(INN // strip):
            rows = slice(i * strip, (i + 1) * strip)
            low_rows = slice(INN + i * strip, INN + (i + 1) * strip)
            yr = both[rows, :width] - both[low_rows, width:]
            yi = both[rows, width:] + both[low_rows, :width]
            position = lax.broadcasted_iota(jnp.int32, (strip, width), 0) + i * strip
            fy = signed_fraction(step + OUT * position)
            (kr, ki), (sr, si) = start_and_step(fy * fy + fx2[...])
            for g in range(planes):
                for part, factor in enumerate((kr, ki)):
                    at = (g * 2 + part) * 2 * width
                    mixed[rows, at : at + width] = (yr * factor).astype(jnp.bfloat16)
                    mixed[rows, at + width : at + 2 * width] = (yi * factor).astype(jnp.bfloat16)
                if g + 1 < planes:
                    kr, ki = kr * sr - ki * si, kr * si + ki * sr
        for g in range(2 * planes):
            lanes = slice(g * 2 * width, (g + 1) * 2 * width)
            re, im = split_complex(dot(inner_back[0], mixed[:, lanes]), width)
            second[step, :, lanes] = jnp.concatenate([re, im], axis=1).astype(jnp.bfloat16)

    @pl.when(step >= OUT)
    def _():
        here = pl.ds(pl.multiple_of((step - OUT) * 16, 16), 16)
        for g in range(2 * planes):
            lanes = slice(g * 2 * width, (g + 1) * 2 * width)
            block = second[:, here, lanes].reshape(OUT * 16, 2 * width)
            re, im = split_complex(dot(back[0], block), width)
            value = jnp.concatenate([re, im], axis=1).astype(jnp.bfloat16)
            value = value.reshape(2, 2, 2, 16, 2 * width)
            for low in range(2):
                for core in range(2):
                    for high in range(2):
                        out[high, 0, low, core, :, lanes] = value[low, core, high]


def columns(half, planes, data, fx2):
    outer, inner, inner_back, back = (jnp.asarray(t) for t in column_tables())
    lanes = planes * 4 * LANE
    mib = 2**20
    inner_at = lambda i, o: (jnp.minimum(i, OUT - 1), 0, 0)
    chunk = lambda i: jnp.maximum(i - OUT, 0)
    return pl.pallas_call(
        lambda o, *refs: column_kernel(planes, *refs),
        grid_spec=pltpu.PrefetchScalarGridSpec(
            num_scalar_prefetch=1,
            grid=(2 * OUT,),
            in_specs=[
                pl.BlockSpec((OUT, INN, 2 * LANE), lambda i, o: (0, 0, 0)),
                pl.BlockSpec((1, LANE), lambda i, o: (0, 0)),
                pl.BlockSpec((2 * INN, INN), lambda i, o: (0, 0)),
                pl.BlockSpec((1, 2 * INN, INN), inner_at),
                pl.BlockSpec((1, 2 * INN, INN), inner_at),
                pl.BlockSpec((1, INN, INN), lambda i, o: (o[0], 0, 0)),
            ],
            out_specs=pl.BlockSpec(
                (2, 1, 2, 2, 16, lanes), lambda i, o: (0, chunk(i) // 8, 0, 0, chunk(i) % 8, 0)
            ),
            scratch_shapes=[
                pltpu.VMEM((OUT, INN, 2 * LANE), jnp.bfloat16),
                pltpu.VMEM((INN, lanes), jnp.bfloat16),
                pltpu.VMEM((OUT, INN, lanes), jnp.bfloat16),
            ],
        ),
        out_shape=jax.ShapeDtypeStruct((2, 2, 2, 2, LANE, lanes), jnp.bfloat16),
        compiler_params=pltpu.CompilerParams(vmem_limit_bytes=48 * mib),
        cost_estimate=pl.CostEstimate(flops=2 * 10**10, bytes_accessed=20 * mib, transcendentals=0),
        name="columns",
    )(half, data, fx2, outer, inner, inner_back, back)


def sixteen_points(re, im):
    c = math.sqrt(0.5)
    c1, c3 = math.cos(math.pi / 8), math.cos(3 * math.pi / 8)
    r0, r1, r2, r3, r4, r5, r6, r7 = re
    r8, i1, i2, i3, i4, i5, i6, i7 = im
    sum08, dif08, sum26, dif26 = r0 + r8, r0 - r8, r2 + r6, c * (r2 - r6)
    base = sum08 + r4
    even = [base + sum26, dif08 + dif26, sum08 - r4, dif08 - dif26, base - sum26]
    sum17, dif17, sum35, dif35 = r1 + r7, r1 - r7, r3 + r5, r3 - r5
    odd = [sum17 + sum35, c1 * dif17 + c3 * dif35, c * (sum17 - sum35), c3 * dif17 - c1 * dif35]
    cosines = [even[a] + odd[a] for a in range(4)] + [even[4]]
    cosines += [even[8 - a] - odd[8 - a] for a in range(5, 9)]
    s17, d17, s35, d35 = i1 + i7, i1 - i7, i3 + i5, i3 - i5
    sines_odd = [None, c3 * s17 + c1 * s35, c * (d17 + d35), c1 * s17 - c3 * s35, d17 - d35]
    s26 = c * (i2 + i6)
    sines_even = [None, s26 + i4, i2 - i6, s26 - i4]
    sines = [None] + [sines_odd[a] + sines_even[a] for a in (1, 2, 3)] + [sines_odd[4]]
    sines += [sines_odd[8 - a] - sines_even[8 - a] for a in (5, 6, 7)]
    result = [cosines[0]] + [cosines[a] - sines[a] for a in range(1, 8)] + [cosines[8]]
    return result + [cosines[16 - a] + sines[16 - a] for a in range(9, 16)]


def row_inverse_kernel(parts, nyquist, table, out, opened):
    plane = pl.program_id(0)
    rows = out.shape[1]
    lane = lax.broadcasted_iota(jnp.int32, (rows, LANE), 1)
    for part in range(2):
        at = part * 2 * LANE
        column = jnp.sum(jnp.where(lane == plane * 2 + part, nyquist[...], 0.0), axis=1, keepdims=True)
        for group in range(CLS):
            pieces = [parts[group // 2, low, group % 2, :, pl.ds(at, 2 * LANE)] for low in range(2)]
            block = jnp.concatenate(pieces, axis=1)
            if group == 0:
                first = jnp.where(lane == 0, column.astype(jnp.bfloat16), block[:, LANE : 2 * LANE])
                block = jnp.concatenate([block[:, :LANE], first, block[:, 2 * LANE :]], axis=1)
            opened[part, group] = dot(block, table[group])

    def strip(i, carry):
        here = pl.ds(pl.multiple_of(i * 16, 16), 16)
        for tile in range(INN // LANE):
            total = None
            for part in range(2):
                re = [opened[part, g, here, pl.ds(tile * LANE, LANE)] for g in range(CLS)]
                im = [opened[part, g, here, pl.ds(INN + tile * LANE, LANE)] for g in range(CLS)]
                values = sixteen_points(re, im)
                if total is None:
                    total = [v * v for v in values]
                else:
                    total = [t + v * v for t, v in zip(total, values)]
            for a in range(OUT):
                out[0, here, pl.ds(a * INN + tile * LANE, LANE)] = total[a].astype(jnp.bfloat16)
        return carry

    lax.fori_loop(0, rows // 16, strip, 0)


def row_inverse(planes, parts, nyquist):
    rows = parts.shape[3]
    table = jnp.asarray(row_inverse_tables())
    mib = 2**20
    return pl.pallas_call(
        row_inverse_kernel,
        grid=(planes,),
        in_specs=[
            pl.BlockSpec((4, 2, 2, rows, 4 * LANE), lambda g: (0, 0, 0, 0, g)),
            pl.BlockSpec((rows, LANE), lambda g: (0, 0)),
            pl.BlockSpec((CLS, 2 * INN, 2 * INN), lambda g: (0, 0, 0)),
        ],
        out_specs=pl.BlockSpec((1, rows, N), lambda g: (g, 0, 0)),
        out_shape=jax.ShapeDtypeStruct((planes, rows, N), jnp.bfloat16),
        scratch_shapes=[pltpu.VMEM((2, CLS, rows, 2 * INN), jnp.float32)],
        compiler_params=pltpu.CompilerParams(vmem_limit_bytes=40 * mib),
        cost_estimate=pl.CostEstimate(flops=10**10, bytes_accessed=20 * mib, transcendentals=0),
        name="row_inverse",
    )(parts, nyquist, table)


def nyquist_kernel(planes, data, out):
    size = RADIX
    row = lax.broadcasted_iota(jnp.int32, (size, size), 0)
    col = lax.broadcasted_iota(jnp.int32, (size, size), 1)
    turn = (row * col % size).astype(jnp.float32) * (2.0 * math.pi / size)
    wr, wi = jnp.cos(turn) * (1.0 / 8.0), jnp.sin(turn) * (1.0 / 8.0)
    twist = (row * col).astype(jnp.float32) * (2.0 * math.pi / (size * size))
    vr, vi = jnp.cos(twist), jnp.sin(twist)

    def exact(left, right):
        return jnp.dot(left, right, preferred_element_type=jnp.float32, precision=lax.Precision.HIGHEST)

    def product(xr, xi, yr, yi):
        return exact(xr, yr) - exact(xi, yi), exact(xr, yi) + exact(xi, yr)

    def rotated(xr, xi, yr, yi):
        return xr * yr - xi * yi, xr * yi + xi * yr

    ar, ai = rotated(exact(wr, data[...]), exact(-wi, data[...]), vr, -vi)
    yr, yi = product(ar, ai, wr, -wi)
    fy = signed_fraction(row + size * col)
    (kr, ki), (sr, si) = start_and_step(fy * fy + 0.25)
    for g in range(planes):
        pr, pi = rotated(yr, yi, kr, ki)
        br, bi = rotated(*product(pr, pi, wr, wi), vr, vi)
        ur, ui = product(wr, wi, br, bi)
        out[2 * g] = ur
        out[2 * g + 1] = ui
        kr, ki = rotated(kr, ki, sr, si)


def nyquist_column(planes, data):
    return pl.pallas_call(
        functools.partial(nyquist_kernel, planes),
        out_shape=jax.ShapeDtypeStruct((2 * planes, RADIX, RADIX), jnp.float32),
        cost_estimate=pl.CostEstimate(flops=10**7, bytes_accessed=2**18, transcendentals=0),
        name="nyquist",
    )(data)


def focus_kernel(intensity, north, south, out, held):
    planes, rows = intensity.shape[0], intensity.shape[1]
    for g in range(planes):
        held[g, 8 : 8 + rows, :] = intensity[g].astype(jnp.float32)
        held[g, 0:8, :] = jnp.broadcast_to(north[g : g + 1].astype(jnp.float32), (8, N))
        held[g, 8 + rows : 16 + rows, :] = jnp.broadcast_to(south[g : g + 1].astype(jnp.float32), (8, N))
    tile = 512
    lane = lax.broadcasted_iota(jnp.int32, (16, tile), 1)
    for i in range(rows // 16):
        r = 8 + i * 16
        for t in range(N // tile):
            lanes = slice(t * tile, (t + 1) * tile)
            centre = [held[g, r : r + 16, lanes] for g in range(planes)]
            best = None
            for g in range(planes):
                depth = centre[min(g + 1, planes - 1)] - centre[max(g - 1, 0)]
                down = held[g, r + 1 : r + 17, lanes] - held[g, r - 1 : r + 15, lanes]
                first, last = max(t * tile - 1, 0), min((t + 1) * tile, N - 1)
                right = pltpu.roll(centre[g], tile - 1, 1)
                right = jnp.where(lane == tile - 1, held[g, r : r + 16, last : last + 1], right)
                left = pltpu.roll(centre[g], 1, 1)
                left = jnp.where(lane == 0, held[g, r : r + 16, first : first + 1], left)
                across = right - left
                score = depth * depth + down * down + across * across
                best = score if best is None else jnp.maximum(best, score)
            out[i * 16 : (i + 1) * 16, lanes] = (best * 0.125).astype(jnp.bfloat16)


def focus_measure(intensity, north, south):
    planes, rows, _ = intensity.shape
    mib = 2**20
    return pl.pallas_call(
        focus_kernel,
        out_shape=jax.ShapeDtypeStruct((rows, N), jnp.bfloat16),
        scratch_shapes=[pltpu.VMEM((planes, rows + 16, N), jnp.float32)],
        compiler_params=pltpu.CompilerParams(vmem_limit_bytes=40 * mib),
        cost_estimate=pl.CostEstimate(flops=10**8, bytes_accessed=6 * mib, transcendentals=0),
        name="focus",
    )(intensity, north, south)


def assemble_kernel(own, mine, ax, ay, axy, bx, by, byx, out):
    slot = pl.program_id(0)
    half = ax.shape[0]
    for s, (a, b) in enumerate(((None, None), (ax, bx), (ay, by), (axy, byx))):

        @pl.when(slot == s)
        def _():
            if a is None:
                out[...] = mine[...].astype(jnp.float32)
            else:
                out[:half] = a[...].astype(jnp.float32)
                out[half:] = b[...].astype(jnp.float32)


def assemble(depth_index, mine, halves):
    rows = mine.shape[0]
    whole = lambda shape: pl.BlockSpec(shape, lambda s, o: (0, 0))
    return pl.pallas_call(
        assemble_kernel,
        grid_spec=pltpu.PrefetchScalarGridSpec(
            num_scalar_prefetch=1,
            grid=(4,),
            in_specs=[whole((rows, N))] + [whole((rows // 2, N))] * 6,
            out_specs=pl.BlockSpec((rows, N), lambda s, o: (jnp.bitwise_xor(s, o[0]), 0)),
        ),
        out_shape=jax.ShapeDtypeStruct((4 * rows, N), jnp.float32),
        compiler_params=pltpu.CompilerParams(vmem_limit_bytes=40 * 2**20),
        cost_estimate=pl.CostEstimate(flops=10**6, bytes_accessed=12 * 2**20, transcendentals=0),
        name="assemble",
    )(depth_index, mine, *halves)


def exchange_depth(mine):
    half = mine.shape[0] // 2
    a, b = mine[:half], mine[half:]
    over_x = [(i, i ^ 1) for i in range(4)]
    over_y = [(i, i ^ 2) for i in range(4)]
    ax, by = lax.ppermute(a, "depth", over_x), lax.ppermute(b, "depth", over_y)
    ay, axy = lax.ppermute(a, "depth", over_y), lax.ppermute(ax, "depth", over_y)
    bx, byx = lax.ppermute(b, "depth", over_x), lax.ppermute(by, "depth", over_x)
    return ax, ay, axy, bx, by, byx


def half_spectrum_shards(hologram, background):
    rows = hologram.shape[0]
    planes = lax.axis_size("depth") * PL_DEV
    depth, high = lax.axis_index("depth"), lax.axis_index("high")
    low, core = lax.axis_index("low"), lax.axis_index("core")
    as_scalar = lambda value: jnp.reshape(value, (1,)).astype(jnp.int32)
    everyone = ("depth", "high", "low", "core")
    slab = ("high", "low", "core")

    sections, alternating = row_forward(as_scalar(depth), hologram, background)
    column_sum = lax.all_gather(jnp.sum(alternating, axis=1) * (1.0 / 64.0), slab, tiled=True)
    data = lax.all_to_all(
        sections.reshape(8, rows, 2 * LANE), slab, split_axis=0, concat_axis=0, tiled=True
    )

    group = depth * 2 + core
    slot = low * LANE + jnp.arange(LANE, dtype=jnp.int32)
    special = jnp.where(low == 0, 0, CLS) + OUT * jnp.arange(LANE, dtype=jnp.int32)
    fx = signed_fraction(jnp.where(group == 0, special, group + OUT * slot))
    halfway = columns(as_scalar(high), planes, data.reshape(OUT, INN, 2 * LANE), (fx * fx)[None])
    own = rows // 4
    parts = lax.all_to_all(
        halfway.reshape(16, own, -1), ("depth", "low", "core"), split_axis=0, concat_axis=0, tiled=True
    )
    first_row = ((high * 2 + low) * 2 + core) * rows + depth * own
    middle = nyquist_column(planes, column_sum.reshape(RADIX, RADIX)).reshape(2 * planes, N)
    middle = lax.dynamic_slice_in_dim(middle, first_row, own, axis=1).T
    middle = jnp.pad(middle, ((0, 0), (0, LANE - 2 * planes)))
    intensity = row_inverse(planes, parts.reshape(4, 2, 2, own, -1), middle)

    order = [
        ((d * 2 + h) * 2 + l) * 2 + c
        for h in range(2)
        for l in range(2)
        for c in range(2)
        for d in range(4)
    ]
    down = list(zip(order[:-1], order[1:]))
    up = [(target, source) for source, target in down]
    north = lax.ppermute(intensity[:, -1], everyone, down)
    south = lax.ppermute(intensity[:, 0], everyone, up)
    north = jnp.where(first_row == 0, intensity[:, 0], north)
    south = jnp.where(first_row == N - own, intensity[:, -1], south)
    mine = focus_measure(intensity, north, south)
    return assemble(as_scalar(depth), mine, exchange_depth(mine))


def solution(mesh):
    spec = P("rows", None)
    if mesh.shape["depth"] == 4 and mesh.shape["rows"] == 8:
        split = Mesh(mesh.devices.reshape(4, 2, 2, 2), ("depth", "high", "low", "core"))
        spec = P(("high", "low", "core"), None)
        body = half_spectrum_shards
    else:
        split, body = mesh, shards
    return jax.shard_map(body, mesh=split, in_specs=(spec, spec), out_specs=spec, check_vma=False)
```

```python
import functools
import math

import jax
import jax.numpy as jnp
import numpy as np
from jax import lax
from jax.experimental import pallas as pl
from jax.experimental.pallas import tpu as pltpu
from jax.sharding import Mesh
from jax.sharding import PartitionSpec as P

N = 4096
RADIX = 64
PL_DEV = 1


wave_number = 0.6
depth_start = 8.0
depth_step = 2.0


def padded_2(block, sides, width):
    for axis, dim in sides:
        count = lax.axis_size(axis)
        forward = [(i, i + 1) for i in range(count - 1)]
        backward = [(target, source) for source, target in forward]
        low = lax.ppermute(
            lax.slice_in_dim(block, block.shape[dim] - width, None, axis=dim), axis, forward
        )
        high = lax.ppermute(lax.slice_in_dim(block, 0, width, axis=dim), axis, backward)
        block = jnp.concatenate([low, block, high], axis=dim)
    return block


def fourier_tables(radix_size, sign_value):
    indices = jnp.arange(radix_size, dtype=jnp.int32)
    products = indices[:, None] * indices[None, :] % radix_size
    angles = products.astype(jnp.float32) * (sign_value * 2.0 * math.pi / radix_size)
    scaling = 1.0 / math.sqrt(radix_size)
    cosine_part = jnp.cos(angles) * scaling
    sine_part = jnp.sin(angles) * scaling
    matrix = jnp.stack([jnp.stack([cosine_part, -sine_part]), jnp.stack([sine_part, cosine_part])])
    return matrix.astype(jnp.bfloat16)


def twiddle_table(radix_size, sign_value):
    indices = jnp.arange(radix_size, dtype=jnp.int32)
    total = radix_size * radix_size
    products = indices[:, None] * indices[None, :] % total
    angles = products.astype(jnp.float32) * (sign_value * 2.0 * math.pi / total)
    return (jnp.cos(angles), jnp.sin(angles))


def rotate(data, cosine_part, sine_part):
    return jnp.stack(
        [data[0] * cosine_part - data[1] * sine_part, data[0] * sine_part + data[1] * cosine_part]
    )


def contract(form, matrix, data):
    return jnp.einsum(form, matrix, data, preferred_element_type=jnp.float32)


def forward_real(data):
    batch_size = data.shape[1]
    shaped = data.reshape(RADIX, RADIX, batch_size)
    matrix = fourier_tables(RADIX, -1.0)
    cosine_part, sine_part = twiddle_table(RADIX, -1.0)
    opening = contract("oka,abm->okbm", matrix[:, 0], shaped)
    sectioned = rotate(opening, cosine_part[:, :, None], sine_part[:, :, None]).astype(jnp.bfloat16)
    closing = contract("ocjb,ckbm->okjm", matrix, sectioned)
    return closing.reshape(2, N, batch_size).astype(jnp.bfloat16)


def forward_first(data):
    batch_size = data.shape[2]
    shaped = data.reshape(2, RADIX, RADIX, batch_size)
    matrix = fourier_tables(RADIX, -1.0)
    cosine_part, sine_part = twiddle_table(RADIX, -1.0)
    opening = contract("ocka,cabm->okbm", matrix, shaped)
    sectioned = rotate(opening, cosine_part[:, :, None], sine_part[:, :, None]).astype(jnp.bfloat16)
    closing = contract("ocjb,ckbm->okjm", matrix, sectioned)
    return closing.reshape(2, N, batch_size).astype(jnp.bfloat16)


def inverse_first(data):
    batch_size = data.shape[2]
    shaped = data.reshape(2, RADIX, RADIX, batch_size)
    matrix = fourier_tables(RADIX, 1.0)
    cosine_part, sine_part = twiddle_table(RADIX, 1.0)
    opening = contract("ocbj,ckjm->okbm", matrix, shaped)
    sectioned = rotate(opening, cosine_part[:, :, None], sine_part[:, :, None]).astype(jnp.bfloat16)
    closing = contract("ocak,ckbm->oabm", matrix, sectioned)
    return closing.reshape(2, N, batch_size)


def frequencies(positions):
    natural = positions // RADIX + RADIX * (positions % RADIX)
    signed_freq = jnp.where(natural >= N // 2, natural - N, natural)
    return signed_freq.astype(jnp.float32) / N


def propagator(freq_whole, freq_own, distance):
    radial = freq_whole[:, None] ** 2 + freq_own[None, :] ** 2
    limit = wave_number * wave_number
    amplitude = jnp.exp(-2.0 * math.pi * distance * jnp.sqrt(jnp.maximum(radial - limit, 0.0)))
    phase_angle = (
        2.0 * math.pi * distance * (jnp.sqrt(jnp.maximum(limit - radial, 0.0)) - wave_number)
    )
    return (amplitude * jnp.cos(phase_angle), amplitude * jnp.sin(phase_angle))


def propagate(spectrum, cosine_part, sine_part):
    return rotate(spectrum.astype(jnp.float32), cosine_part, sine_part).astype(jnp.bfloat16)


def shards(hologram, background):
    row_count = hologram.shape[0]
    contrast = (hologram.astype(jnp.float32) / background.astype(jnp.float32) - 1.0).astype(
        jnp.bfloat16
    )
    along_rows = forward_real(contrast.T)
    columns = lax.all_to_all(
        jnp.swapaxes(along_rows, 1, 2), "rows", split_axis=2, concat_axis=1, tiled=True
    )
    spectrum = forward_first(columns)
    row_index = lax.axis_index("rows")
    own_positions = row_index * row_count + jnp.arange(row_count, dtype=jnp.int32)
    freq_own = frequencies(own_positions)
    freq_whole = frequencies(jnp.arange(N, dtype=jnp.int32))
    depth_index = lax.axis_index("depth")
    distance = depth_start + depth_step * (depth_index * PL_DEV + 0).astype(jnp.float32)
    cosine_part, sine_part = propagator(freq_whole, freq_own, distance)
    propagated = propagate(spectrum, cosine_part, sine_part)
    halfway = inverse_first(propagated).astype(jnp.bfloat16)
    restored = lax.all_to_all(
        jnp.swapaxes(halfway, 1, 2), "rows", split_axis=2, concat_axis=1, tiled=True
    )
    result_field = inverse_first(restored)
    intensities = [
        (result_field[0] * result_field[0] + result_field[1] * result_field[1]).astype(jnp.bfloat16)
    ]
    stacked = jnp.stack(intensities)
    padded = padded_2(stacked, (("depth", 0), ("rows", 2)), 1)
    centre_block = padded[1:-1, :, 1:-1]
    plane_ids = jnp.arange(PL_DEV, dtype=jnp.int32)[:, None, None]
    row_ids = jnp.arange(row_count, dtype=jnp.int32)[None, None, :]
    depth_count = lax.axis_size("depth")
    row_groups = lax.axis_size("rows")
    lower_plane = jnp.where(
        (depth_index == 0) & (plane_ids == 0), centre_block, padded[:-2, :, 1:-1]
    )
    upper_plane = jnp.where(
        (depth_index == depth_count - 1) & (plane_ids == PL_DEV - 1),
        centre_block,
        padded[2:, :, 1:-1],
    )
    north_row = jnp.where((row_index == 0) & (row_ids == 0), centre_block, padded[1:-1, :, :-2])
    south_row = jnp.where(
        (row_index == row_groups - 1) & (row_ids == row_count - 1),
        centre_block,
        padded[1:-1, :, 2:],
    )
    centre = centre_block.astype(jnp.float32)
    east_col = jnp.concatenate([centre[:, 1:], centre[:, -1:]], axis=1)
    west_col = jnp.concatenate([centre[:, :1], centre[:, :-1]], axis=1)
    depth_diff = upper_plane.astype(jnp.float32) - lower_plane.astype(jnp.float32)
    row_diff = south_row.astype(jnp.float32) - north_row.astype(jnp.float32)
    col_diff = east_col - west_col
    scores = (depth_diff * depth_diff + row_diff * row_diff + col_diff * col_diff) / 8.0
    sharpest = jnp.max(scores, axis=0)
    merged = lax.pmax(sharpest.astype(jnp.bfloat16), "depth").astype(sharpest.dtype)
    return merged.T


OUT = 16
INN = 256
CLS = 8
LANE = 128
MIB = 2**20
VMEM = 60 * MIB


def slot_frequencies():
    table = np.arange(CLS)[:, None] + OUT * np.arange(INN)[None, :]
    half = np.arange(INN // 2)
    table[0] = np.concatenate([OUT * half, CLS + OUT * half])
    return table


def angles(products):
    return 2.0 * np.pi * (products % N) / N


def row_forward_tables():
    freq = slot_frequencies()
    theta = angles(np.arange(INN)[None, :, None] * freq[:, None, :])
    cos, sin = np.cos(theta) / 64.0, np.sin(theta) / 64.0
    top = np.stack([cos, -sin], axis=2)
    low = np.stack([sin, cos], axis=2)
    first = np.arange(INN) < INN // 2
    low[0] = np.where(first, 0.0, top[0])
    top[0] = np.where(first, top[0], 0.0)
    full = np.concatenate([top, low], axis=1)
    full = full.reshape(CLS, 2 * INN, 2, 2, LANE).transpose(0, 1, 3, 2, 4)
    return full.reshape(CLS, 2 * INN, 2 * INN).astype(jnp.bfloat16)


def row_forward_weights():
    turn = 2.0 * np.pi * np.arange(CLS)[:, None] * np.arange(OUT)[None, :] / OUT
    re, im = np.cos(turn), -np.sin(turn)
    im[0] = (-1.0) ** np.arange(OUT)
    return np.stack([re, im], axis=1).reshape(-1).astype(np.float32)


def row_inverse_tables():
    freq = slot_frequencies()
    theta = angles(freq[:, :, None] * np.arange(INN)[None, None, :])
    cos, sin = np.cos(theta) / 32.0, np.sin(theta) / 32.0
    full = np.zeros((CLS, 2, INN, 2, INN))
    full[:, 0, :, 0], full[:, 0, :, 1] = cos, sin
    full[:, 1, :, 0], full[:, 1, :, 1] = -sin, cos
    half = INN // 2
    full[0] = 0.0
    full[0, 0, :half, 0], full[0, 1, :half, 0] = cos[0, :half], -sin[0, :half]
    full[0, 0, half:, 1], full[0, 1, half:, 1] = cos[0, half:], -sin[0, half:]
    full[0, 0, 0, 0] = 1.0 / 64.0
    full[0, 1, 0, 0] = (-1.0) ** np.arange(INN) / 64.0
    full = full.reshape(CLS, 2, 2, LANE, 2 * INN).transpose(0, 2, 1, 3, 4)
    return full.reshape(CLS, 2 * INN, 2 * INN).astype(jnp.bfloat16)


def column_tables():
    turn = 2.0 * np.pi * np.arange(OUT)[:, None] * np.arange(OUT)[None, :] / OUT
    eye = np.eye(16)
    outer_cos, outer_sin = np.kron(np.cos(turn), eye) / 4.0, np.kron(np.sin(turn), eye) / 4.0
    outer = np.concatenate([outer_cos, -outer_sin])
    outer = outer.reshape(-1, 8, 2, 16).swapaxes(1, 2).reshape(outer.shape)
    half_rows = outer_cos.shape[0] // 2
    back = np.stack(
        [
            np.concatenate([outer_cos[i * half_rows :][:half_rows], outer_sin[i * half_rows :][:half_rows]])
            for i in range(2)
        ]
    )
    freq = np.arange(OUT)[:, None] + OUT * np.arange(INN)[None, :]
    theta = angles(freq[:, :, None] * np.arange(INN)[None, None, :])
    inner = np.concatenate([np.cos(theta), -np.sin(theta)], axis=1) / 16.0
    theta = theta.transpose(0, 2, 1)
    inner_back = np.concatenate([np.cos(theta), np.sin(theta)], axis=1) / 16.0
    cast = lambda table: table.astype(jnp.bfloat16)
    return cast(outer), cast(inner), cast(inner_back), cast(back)


def dot(left, right):
    return jnp.dot(left, right, preferred_element_type=jnp.float32)


def split_complex(both, width):
    rows = both.shape[0] // 2
    top, low = both[:rows], both[rows:]
    return top[:, :width] - low[:, width:], top[:, width:] + low[:, :width]


def quarter_kernel(radial):
    gap = wave_number * wave_number - radial
    root = jnp.sqrt(jnp.abs(gap))
    inside = gap > 0.0
    half_pi = 0.5 * math.pi
    angle = half_pi * (jnp.where(inside, root, 0.0) - wave_number)
    decay = jnp.exp(jnp.where(inside, 0.0, -half_pi * root))
    square = angle * angle
    sine = 1.0 / 362880.0
    for c in (-1.0 / 5040.0, 1.0 / 120.0, -1.0 / 6.0, 1.0):
        sine = sine * square + c
    cosine = -1.0 / 3628800.0
    for c in (1.0 / 40320.0, -1.0 / 720.0, 1.0 / 24.0, -0.5, 1.0):
        cosine = cosine * square + c
    return decay * cosine, decay * (sine * angle)


def squared(re, im):
    return (re - im) * (re + im), 2.0 * re * im


def start_and_step(radial):
    value = quarter_kernel(radial)
    distance = 0.25
    step = None
    while distance < depth_start:
        value = squared(*value)
        distance *= 2.0
        if distance == depth_step:
            step = value
    return value, step


def signed_fraction(natural):
    return jnp.where(natural >= N // 2, natural - N, natural).astype(jnp.float32) * (1.0 / N)


def row_forward_kernel(own, weights, holo, back, table, out, acc, held):
    step = pl.program_id(0)
    rows = holo.shape[0]
    group = own[0]
    lane = lax.broadcasted_iota(jnp.int32, (16, INN), 1)
    sign = jnp.where(lane % 2 == 0, 1.0, -1.0).astype(jnp.bfloat16)

    def strip(i, carry):
        here = pl.ds(pl.multiple_of(i * 16, 16), 16)
        sums = [jnp.zeros((16, INN), jnp.float32) for _ in range(5)]
        for a in range(OUT):
            there = pl.ds(a * INN, INN)
            value = holo[here, there].astype(jnp.float32) / back[here, there].astype(jnp.float32)
            value = (value - 1.0).astype(jnp.bfloat16).astype(jnp.float32)
            for q in range(4):
                w = weights[(group * 2 + q // 2) * (2 * OUT) + (q % 2) * OUT + a]
                sums[q] = sums[q] + value * w
            sums[4] = sums[4] + value
        for q in range(4):
            acc[q // 2, here, pl.ds((q % 2) * INN, INN)] = sums[q].astype(jnp.bfloat16)
        acc[2, here, pl.ds(0, INN)] = sums[4].astype(jnp.bfloat16)
        return carry

    lax.fori_loop(0, rows // 16, strip, 0)
    here = pl.ds(pl.multiple_of(step * rows, rows), rows)
    for q in range(2):
        result = dot(acc[q], table[q]).astype(jnp.bfloat16)
        for low in range(2):
            part = result[:, low * 2 * LANE : (low + 1) * 2 * LANE]
            for high in range(2):
                out[high, low, q, here, :] = part
    alternating = lax.dot_general(
        sign, acc[2, :, :INN], (((1,), (1,)), ((), ())), preferred_element_type=jnp.float32
    )
    held[step] = alternating * (1.0 / 64.0)

    @pl.when(step == pl.num_programs(0) - 1)
    def _():
        rows_of = [jnp.concatenate([held[2 * r], held[2 * r + 1]], axis=1) for r in range(2)]
        extra = jnp.where(lax.broadcasted_iota(jnp.int32, (16, INN), 0) == 0, rows_of[0], rows_of[1])
        extra = extra.astype(jnp.bfloat16)
        for high in range(2):
            for low in range(2):
                for q in range(2):
                    out[high, low, q, pl.ds(4 * rows, 16), :] = extra


def row_forward(own, hologram, background):
    rows = hologram.shape[0]
    block = LANE
    table = jnp.asarray(row_forward_tables())
    weights = jnp.asarray(row_forward_weights())
    shape = (2, 2, 2, rows + 16, 2 * LANE)
    return pl.pallas_call(
        row_forward_kernel,
        grid_spec=pltpu.PrefetchScalarGridSpec(
            num_scalar_prefetch=2,
            grid=(rows // block,),
            in_specs=[
                pl.BlockSpec((block, N), lambda i, o, w: (i, 0)),
                pl.BlockSpec((block, N), lambda i, o, w: (i, 0)),
                pl.BlockSpec((2, 2 * INN, 2 * INN), lambda i, o, w: (o[0], 0, 0)),
            ],
            out_specs=pl.BlockSpec(shape, lambda i, o, w: (0, 0, 0, 0, 0)),
            scratch_shapes=[
                pltpu.VMEM((3, block, 2 * INN), jnp.bfloat16),
                pltpu.VMEM((rows // block, 16, LANE), jnp.float32),
            ],
        ),
        out_shape=jax.ShapeDtypeStruct(shape, jnp.bfloat16),
        compiler_params=pltpu.CompilerParams(vmem_limit_bytes=VMEM),
        cost_estimate=pl.CostEstimate(flops=10**10, bytes_accessed=12 * MIB, transcendentals=0),
        name="row_forward",
    )(own, weights, hologram, background, table)


def propagator_kernel(planes, fx2, out):
    step = pl.program_id(0)
    strip = 32
    for i in range(INN // strip):
        rows = slice(i * strip, (i + 1) * strip)
        position = lax.broadcasted_iota(jnp.int32, (strip, LANE), 0) + i * strip
        fy = signed_fraction(step + OUT * position)
        (kr, ki), (sr, si) = start_and_step(fy * fy + fx2[...])
        for g in range(planes):
            out[g, 0, rows, :LANE] = kr
            out[g, 0, rows, LANE:] = ki
            if g + 1 < planes:
                kr, ki = kr * sr - ki * si, kr * si + ki * sr


def propagators(planes, fx2):
    return pl.pallas_call(
        functools.partial(propagator_kernel, planes),
        grid=(OUT,),
        in_specs=[pl.BlockSpec((1, LANE), lambda i: (0, 0))],
        out_specs=pl.BlockSpec((planes, 1, INN, 2 * LANE), lambda i: (0, i, 0, 0)),
        out_shape=jax.ShapeDtypeStruct((planes, OUT, INN, 2 * LANE), jnp.float32),
        compiler_params=pltpu.CompilerParams(vmem_limit_bytes=VMEM),
        cost_estimate=pl.CostEstimate(flops=10**9, bytes_accessed=16 * MIB, transcendentals=10**6),
        name="propagators",
    )(fx2)


PER = 4


def mix_and_open(k, slot, yr, yi, kernels, inner_back, mixed, second):
    width = LANE
    for part in range(2):
        factor = kernels[:, part * width : (part + 1) * width]
        at = part * 2 * width
        mixed[slot, :, at : at + width] = (yr * factor).astype(jnp.bfloat16)
        mixed[slot, :, at + width : at + 2 * width] = (yi * factor).astype(jnp.bfloat16)
    both = dot(inner_back, mixed[slot])
    for part in range(2):
        lanes = slice(part * 2 * width, (part + 1) * 2 * width)
        re, im = split_complex(both[:, lanes], width)
        second[k, :, lanes] = jnp.concatenate([re, im], axis=1).astype(jnp.bfloat16)


def close_columns(start, back, second, out):
    width = LANE
    for c in range(PER):
        here = pl.ds(pl.multiple_of((start + c) * 16, 16), 16)
        both = dot(back[0], second[:, here, :].reshape(OUT * 16, 4 * width))
        rows = slice(c * 16, (c + 1) * 16)
        for part in range(2):
            lanes = slice(part * 2 * width, (part + 1) * 2 * width)
            re, im = split_complex(both[:, lanes], width)
            value = jnp.concatenate([re, im], axis=1).astype(jnp.bfloat16)
            value = value.reshape(2, 2, 2, 16, 2 * width)
            for low in range(2):
                for core in range(2):
                    for high in range(2):
                        out[high, 0, low, core, rows, lanes] = value[low, core, high]


def first_columns_kernel(
    half, data, kernels, outer, inner, inner_back, back, out, spectrum, first, mixed, second
):
    step = pl.program_id(0)
    width = LANE

    @pl.when(step == 0)
    def _():
        for i in range(INN // 16):
            here = slice(i * 16, (i + 1) * 16)
            there = slice(INN + i * 16, INN + (i + 1) * 16)
            block = jnp.concatenate([data[:, here, :], data[:, there, :]], axis=0)
            re, im = split_complex(dot(outer[...], block.reshape(OUT * 16, 2 * width)), width)
            value = jnp.concatenate([re, im], axis=1).astype(jnp.bfloat16)
            first[:, here, :] = value.reshape(OUT, 16, 2 * width)

    @pl.when(step < OUT // PER)
    def _():
        for c in range(PER):
            k = step * PER + c
            yr, yi = split_complex(dot(inner[c], first[k]), width)
            spectrum[c] = jnp.concatenate([yr, yi], axis=1).astype(jnp.bfloat16)
            mix_and_open(k, c, yr, yi, kernels[0, c], inner_back[c], mixed, second)

    @pl.when(step >= OUT // PER)
    def _():
        close_columns((step - OUT // PER) * PER, back, second, out)


def next_columns_kernel(half, spectrum, kernels, inner_back, back, out, mixed, second):
    step = pl.program_id(1)
    width = LANE

    @pl.when(step < OUT // PER)
    def _():
        for c in range(PER):
            values = spectrum[c].astype(jnp.float32)
            yr, yi = values[:, :width], values[:, width:]
            mix_and_open(step * PER + c, c, yr, yi, kernels[0, c], inner_back[c], mixed, second)

    @pl.when(step >= OUT // PER)
    def _():
        close_columns((step - OUT // PER) * PER, back, second, out)


STEPS = OUT // PER


def opening_step(s):
    return jnp.minimum(s, STEPS - 1)


def closing_step(s):
    return jnp.maximum(s - STEPS, 0)


def first_columns(half, data, kernels):
    outer, inner, inner_back, back = (jnp.asarray(t) for t in column_tables())
    rows = data.shape[1] - 16
    opening = lambda i, o: (opening_step(i), 0, 0)
    return pl.pallas_call(
        first_columns_kernel,
        grid_spec=pltpu.PrefetchScalarGridSpec(
            num_scalar_prefetch=1,
            grid=(2 * STEPS,),
            in_specs=[
                pl.BlockSpec((8, rows, 2 * LANE), lambda i, o: (0, 0, 0)),
                pl.BlockSpec((1, PER, INN, 2 * LANE), lambda i, o: (0, opening_step(i), 0, 0)),
                pl.BlockSpec((2 * INN, INN), lambda i, o: (0, 0)),
                pl.BlockSpec((PER, 2 * INN, INN), opening),
                pl.BlockSpec((PER, 2 * INN, INN), opening),
                pl.BlockSpec((1, INN, INN), lambda i, o: (o[0], 0, 0)),
            ],
            out_specs=[
                pl.BlockSpec(
                    (2, 1, 2, 2, PER * 16, 4 * LANE),
                    lambda i, o: (0, closing_step(i) // 2, 0, 0, closing_step(i) % 2, 0),
                ),
                pl.BlockSpec((PER, INN, 2 * LANE), opening),
            ],
            scratch_shapes=[
                pltpu.VMEM((OUT, INN, 2 * LANE), jnp.bfloat16),
                pltpu.VMEM((PER, INN, 4 * LANE), jnp.bfloat16),
                pltpu.VMEM((OUT, INN, 4 * LANE), jnp.bfloat16),
            ],
        ),
        out_shape=[
            jax.ShapeDtypeStruct((2, 2, 2, 2, LANE, 4 * LANE), jnp.bfloat16),
            jax.ShapeDtypeStruct((OUT, INN, 2 * LANE), jnp.bfloat16),
        ],
        compiler_params=pltpu.CompilerParams(vmem_limit_bytes=VMEM),
        cost_estimate=pl.CostEstimate(flops=10**10, bytes_accessed=20 * MIB, transcendentals=0),
        name="first_columns",
    )(half, data, kernels, outer, inner, inner_back, back)


def next_columns(half, plane, count, spectrum, kernels):
    _, _, inner_back, back = (jnp.asarray(t) for t in column_tables())
    opening = lambda g, i, o: (opening_step(i), 0, 0)
    return pl.pallas_call(
        next_columns_kernel,
        grid_spec=pltpu.PrefetchScalarGridSpec(
            num_scalar_prefetch=1,
            grid=(count, 2 * STEPS),
            in_specs=[
                pl.BlockSpec((PER, INN, 2 * LANE), opening),
                pl.BlockSpec(
                    (1, PER, INN, 2 * LANE), lambda g, i, o: (plane + g, opening_step(i), 0, 0)
                ),
                pl.BlockSpec((PER, 2 * INN, INN), opening),
                pl.BlockSpec((1, INN, INN), lambda g, i, o: (o[0], 0, 0)),
            ],
            out_specs=pl.BlockSpec(
                (2, 1, 2, 2, PER * 16, 4 * LANE),
                lambda g, i, o: (0, closing_step(i) // 2, 0, 0, closing_step(i) % 2, g),
            ),
            scratch_shapes=[
                pltpu.VMEM((PER, INN, 4 * LANE), jnp.bfloat16),
                pltpu.VMEM((OUT, INN, 4 * LANE), jnp.bfloat16),
            ],
        ),
        out_shape=jax.ShapeDtypeStruct((2, 2, 2, 2, LANE, count * 4 * LANE), jnp.bfloat16),
        compiler_params=pltpu.CompilerParams(vmem_limit_bytes=VMEM),
        cost_estimate=pl.CostEstimate(
            flops=count * 7 * 10**9, bytes_accessed=count * 16 * MIB, transcendentals=0
        ),
        name="next_columns",
    )(half, spectrum, kernels, inner_back, back)


def sixteen_points(re, im):
    c = math.sqrt(0.5)
    c1, c3 = math.cos(math.pi / 8), math.cos(3 * math.pi / 8)
    r0, r1, r2, r3, r4, r5, r6, r7 = re
    r8, i1, i2, i3, i4, i5, i6, i7 = im
    sum08, dif08, sum26, dif26 = r0 + r8, r0 - r8, r2 + r6, c * (r2 - r6)
    base = sum08 + r4
    even = [base + sum26, dif08 + dif26, sum08 - r4, dif08 - dif26, base - sum26]
    sum17, dif17, sum35, dif35 = r1 + r7, r1 - r7, r3 + r5, r3 - r5
    odd = [sum17 + sum35, c1 * dif17 + c3 * dif35, c * (sum17 - sum35), c3 * dif17 - c1 * dif35]
    cosines = [even[a] + odd[a] for a in range(4)] + [even[4]]
    cosines += [even[8 - a] - odd[8 - a] for a in range(5, 9)]
    s17, d17, s35, d35 = i1 + i7, i1 - i7, i3 + i5, i3 - i5
    sines_odd = [None, c3 * s17 + c1 * s35, c * (d17 + d35), c1 * s17 - c3 * s35, d17 - d35]
    s26 = c * (i2 + i6)
    sines_even = [None, s26 + i4, i2 - i6, s26 - i4]
    sines = [None] + [sines_odd[a] + sines_even[a] for a in (1, 2, 3)] + [sines_odd[4]]
    sines += [sines_odd[8 - a] - sines_even[8 - a] for a in (5, 6, 7)]
    result = [cosines[0]] + [cosines[a] - sines[a] for a in range(1, 8)] + [cosines[8]]
    return result + [cosines[16 - a] + sines[16 - a] for a in range(9, 16)]


def row_inverse_kernel(plane, parts, nyquist, table, out, edges, opened):
    current = plane + pl.program_id(0)
    rows = parts.shape[3]
    lane = lax.broadcasted_iota(jnp.int32, (rows, LANE), 1)
    for part in range(2):
        at = part * 2 * LANE
        mine = jnp.where(lane == current * 2 + part, nyquist[...], 0.0)
        column = jnp.sum(mine, axis=1, keepdims=True).astype(jnp.bfloat16)
        for group in range(CLS):
            low, high = (parts[group // 2, i, group % 2, :, at : at + 2 * LANE] for i in range(2))
            if group == 0:
                first = jnp.where(lane == 0, column, low[:, LANE:])
                low = jnp.concatenate([low[:, :LANE], first], axis=1)
            opened[part, group] = dot(jnp.concatenate([low, high], axis=1), table[group])

    def strip(i, carry):
        here = pl.ds(pl.multiple_of(i * 16, 16), 16)
        for tile in range(INN // LANE):
            total = None
            for part in range(2):
                re = [opened[part, g, here, tile * LANE : (tile + 1) * LANE] for g in range(CLS)]
                im = [
                    opened[part, g, here, INN + tile * LANE : INN + (tile + 1) * LANE]
                    for g in range(CLS)
                ]
                values = sixteen_points(re, im)
                if total is None:
                    total = [v * v for v in values]
                else:
                    total = [t + v * v for t, v in zip(total, values)]
            for a in range(OUT):
                lanes = slice(a * INN + tile * LANE, a * INN + (tile + 1) * LANE)
                out[0, here, lanes] = total[a].astype(jnp.bfloat16)
        return carry

    lax.fori_loop(0, rows // 16, strip, 0)
    edges[0, 0:8, :] = out[0, 0:16, :].astype(jnp.float32)[0:8]
    edges[0, 8:16, :] = out[0, rows - 16 :, :].astype(jnp.float32)[8:16]


def row_inverse(plane, count, parts, nyquist):
    rows = parts.shape[3]
    table = jnp.asarray(row_inverse_tables())
    return pl.pallas_call(
        functools.partial(row_inverse_kernel, plane),
        grid=(count,),
        in_specs=[
            pl.BlockSpec((4, 2, 2, rows, 4 * LANE), lambda g: (0, 0, 0, 0, g)),
            pl.BlockSpec((rows, LANE), lambda g: (0, 0)),
            pl.BlockSpec((CLS, 2 * INN, 2 * INN), lambda g: (0, 0, 0)),
        ],
        out_specs=[
            pl.BlockSpec((1, rows, N), lambda g: (g, 0, 0)),
            pl.BlockSpec((1, 16, N), lambda g: (g, 0, 0)),
        ],
        out_shape=[
            jax.ShapeDtypeStruct((count, rows, N), jnp.bfloat16),
            jax.ShapeDtypeStruct((count, 16, N), jnp.float32),
        ],
        scratch_shapes=[pltpu.VMEM((2, CLS, rows, 2 * INN), jnp.float32)],
        compiler_params=pltpu.CompilerParams(vmem_limit_bytes=VMEM),
        cost_estimate=pl.CostEstimate(
            flops=count * 3 * 10**9, bytes_accessed=count * 8 * MIB, transcendentals=0
        ),
        name="row_inverse",
    )(parts, nyquist, table)


def nyquist_kernel(planes, own, data, out):
    wide = lambda axis: lax.broadcasted_iota(jnp.int32, (INN, INN), axis)
    tall = lambda axis: lax.broadcasted_iota(jnp.int32, (OUT, INN), axis)
    small = lambda axis: lax.broadcasted_iota(jnp.int32, (OUT, OUT), axis)

    def wave(products, period):
        turn = (products % period).astype(jnp.float32) * (2.0 * math.pi / period)
        return jnp.cos(turn), jnp.sin(turn)

    def exact(left, right):
        return jnp.dot(left, right, preferred_element_type=jnp.float32, precision=lax.Precision.HIGHEST)

    def product(xr, xi, yr, yi):
        return exact(xr, yr) - exact(xi, yi), exact(xr, yi) + exact(xi, yr)

    def rotated(xr, xi, yr, yi):
        return xr * yr - xi * yi, xr * yi + xi * yr

    column = jnp.concatenate([data[i, 0:2, :].astype(jnp.float32) for i in range(8)], axis=0)
    wr, wi = wave(small(0) * small(1), OUT)
    inner_r, inner_i = wave(wide(0) * wide(1), INN)
    vr, vi = wave(tall(0) * tall(1), N)
    ar, ai = rotated(exact(wr, column), exact(-wi, column), vr, -vi)
    yr, yi = product(ar, ai, inner_r, -inner_i)
    fy = signed_fraction(tall(0) + OUT * tall(1))
    (kr, ki), (sr, si) = start_and_step(fy * fy + 0.25)
    block = own[0]
    k = lax.broadcasted_iota(jnp.int32, (8, OUT), 1)
    hr, hi = wave(k * (block // 2), OUT)
    result = []
    for g in range(planes):
        pr, pi = rotated(yr, yi, kr, ki)
        br, bi = rotated(*product(pr, pi, inner_r, inner_i), vr, vi)
        for value in product(hr, hi, br, bi):
            half = jnp.where(block % 2 == 0, value[:, :LANE], value[:, LANE:])
            result.append(half[0:1] * (1.0 / N))
        kr, ki = rotated(kr, ki, sr, si)
    result.append(jnp.zeros((LANE - 2 * planes, LANE), jnp.float32))
    out[...] = jnp.concatenate(result, axis=0).T


def nyquist_column(own, planes, data):
    rows = data.shape[1] - 16
    return pl.pallas_call(
        functools.partial(nyquist_kernel, planes),
        grid_spec=pltpu.PrefetchScalarGridSpec(
            num_scalar_prefetch=1,
            grid=(1,),
            in_specs=[pl.BlockSpec((8, 16, 2 * LANE), lambda i, o: (0, rows // 16, 0))],
            out_specs=pl.BlockSpec((LANE, LANE), lambda i, o: (0, 0)),
        ),
        out_shape=jax.ShapeDtypeStruct((LANE, LANE), jnp.float32),
        cost_estimate=pl.CostEstimate(flops=10**9, bytes_accessed=2**18, transcendentals=0),
        name="nyquist",
    )(own, data)


def focus_of(held, planes, count, out):
    tile = 512
    lane = lax.broadcasted_iota(jnp.int32, (16, tile), 1)
    for i in range(count // 16):
        r = 8 + i * 16
        for t in range(N // tile):
            lanes = slice(t * tile, (t + 1) * tile)
            centre = [held[g, r : r + 16, lanes] for g in range(planes)]
            best = None
            for g in range(planes):
                depth = centre[min(g + 1, planes - 1)] - centre[max(g - 1, 0)]
                down = held[g, r + 1 : r + 17, lanes] - held[g, r - 1 : r + 15, lanes]
                first, last = max(t * tile - 1, 0), min((t + 1) * tile, N - 1)
                right = pltpu.roll(centre[g], tile - 1, 1)
                right = jnp.where(lane == tile - 1, held[g, r : r + 16, last : last + 1], right)
                left = pltpu.roll(centre[g], 1, 1)
                left = jnp.where(lane == 0, held[g, r : r + 16, first : first + 1], left)
                across = right - left
                score = depth * depth + down * down + across * across
                best = score if best is None else jnp.maximum(best, score)
            out[i * 16 : (i + 1) * 16, lanes] = (best * 0.125).astype(jnp.bfloat16)


def inner_focus_kernel(sizes, begin, count, *refs):
    blocks, out, held = refs[: len(sizes)], refs[-2], refs[-1]
    plane = 0
    for block, size in zip(blocks, sizes):
        for g in range(size):
            held[plane, 0 : count + 16, :] = block[g, begin - 16 : begin + count + 16, :].astype(
                jnp.float32
            )[8 : count + 24]
            plane += 1
    focus_of(held, plane, count, out)


def inner_focus(intensities, begin, count):
    sizes = [block.shape[0] for block in intensities]
    return pl.pallas_call(
        functools.partial(inner_focus_kernel, sizes, begin, count),
        out_shape=jax.ShapeDtypeStruct((count, N), jnp.bfloat16),
        scratch_shapes=[pltpu.VMEM((sum(sizes), count + 16, N), jnp.float32)],
        compiler_params=pltpu.CompilerParams(vmem_limit_bytes=VMEM),
        cost_estimate=pl.CostEstimate(flops=10**8, bytes_accessed=6 * MIB, transcendentals=0),
        name="inner_focus",
    )(*intensities)


def outer_focus_kernel(sizes, count, *refs):
    blocks, north, south, out, held = refs[: len(sizes)], refs[-4], refs[-3], refs[-2], refs[-1]
    planes = sum(sizes)
    for side in range(2):
        plane = 0
        for block, size in zip(blocks, sizes):
            rows = block.shape[1]
            for g in range(size):
                if side == 0:
                    held[plane, 8 : 24 + count, :] = block[g, : count + 16, :].astype(jnp.float32)
                    held[plane, 0:8, :] = jnp.broadcast_to(north[plane : plane + 1, :], (8, N))
                else:
                    value = block[g, rows - count - 16 :, :].astype(jnp.float32)
                    held[plane, 0 : count + 8, :] = value[8:]
                    held[plane, count + 8 : count + 16, :] = jnp.broadcast_to(
                        south[plane : plane + 1, :], (8, N)
                    )
                plane += 1
        focus_of(held, planes, count, out.at[side * count : (side + 1) * count])


def outer_focus(intensities, north, south, count):
    sizes = [block.shape[0] for block in intensities]
    return pl.pallas_call(
        functools.partial(outer_focus_kernel, sizes, count),
        out_shape=jax.ShapeDtypeStruct((2 * count, N), jnp.bfloat16),
        scratch_shapes=[pltpu.VMEM((sum(sizes), count + 24, N), jnp.float32)],
        compiler_params=pltpu.CompilerParams(vmem_limit_bytes=VMEM),
        cost_estimate=pl.CostEstimate(flops=10**8, bytes_accessed=6 * MIB, transcendentals=0),
        name="outer_focus",
    )(*intensities, north, south)


def assemble_kernel(own, *refs):
    slot, out = pl.program_id(0), refs[-1]
    inner, outer = refs[:7], refs[7:14]
    part = inner[1].shape[0]
    for s in range(4):

        @pl.when(slot == s)
        def _():
            for both, places in ((inner, (part, 2 * part)), (outer, (0, 3 * part))):
                if s == 0:
                    a, b = both[0][:part], both[0][part:]
                else:
                    a, b = both[s][...], both[3 + s][...]
                out[places[0] : places[0] + part] = a.astype(jnp.float32)
                out[places[1] : places[1] + part] = b.astype(jnp.float32)


def assemble(depth_index, inner, outer):
    part = inner[1].shape[0]
    whole = lambda shape: pl.BlockSpec(shape, lambda s, o: (0, 0))
    specs = [whole((2 * part, N))] + [whole((part, N))] * 6
    return pl.pallas_call(
        assemble_kernel,
        grid_spec=pltpu.PrefetchScalarGridSpec(
            num_scalar_prefetch=1,
            grid=(4,),
            in_specs=specs * 2,
            out_specs=pl.BlockSpec((4 * part, N), lambda s, o: (jnp.bitwise_xor(s, o[0]), 0)),
        ),
        out_shape=jax.ShapeDtypeStruct((16 * part, N), jnp.float32),
        compiler_params=pltpu.CompilerParams(vmem_limit_bytes=VMEM),
        cost_estimate=pl.CostEstimate(flops=10**6, bytes_accessed=12 * MIB, transcendentals=0),
        name="assemble",
    )(depth_index, *inner, *outer)


def exchange_depth(mine):
    half = mine.shape[0] // 2
    a, b = mine[:half], mine[half:]
    over_x = [(i, i ^ 1) for i in range(4)]
    over_y = [(i, i ^ 2) for i in range(4)]
    ax, by = lax.ppermute(a, "depth", over_x), lax.ppermute(b, "depth", over_y)
    ay, axy = lax.ppermute(a, "depth", over_y), lax.ppermute(ax, "depth", over_y)
    bx, byx = lax.ppermute(b, "depth", over_x), lax.ppermute(by, "depth", over_x)
    return mine, ax, ay, axy, bx, by, byx


def half_spectrum_shards(hologram, background):
    rows = hologram.shape[0]
    planes = lax.axis_size("depth") * PL_DEV
    depth, high = lax.axis_index("depth"), lax.axis_index("high")
    low, core = lax.axis_index("low"), lax.axis_index("core")
    as_scalar = lambda value: jnp.reshape(value, (1,)).astype(jnp.int32)
    everyone = ("depth", "high", "low", "core")
    own = rows // 4
    block = ((high * 2 + low) * 2 + core) * 4 + depth

    sections = row_forward(as_scalar(depth), hologram, background)
    data = lax.all_to_all(
        sections.reshape(8, rows + 16, 2 * LANE),
        ("high", "low", "core"),
        split_axis=0,
        concat_axis=0,
        tiled=True,
    )

    group = depth * 2 + core
    slot = low * LANE + jnp.arange(LANE, dtype=jnp.int32)
    special = jnp.where(low == 0, 0, CLS) + OUT * jnp.arange(LANE, dtype=jnp.int32)
    fx = signed_fraction(jnp.where(group == 0, special, group + OUT * slot))
    kernels = propagators(planes, (fx * fx)[None])

    def to_rows(halfway):
        parts = lax.all_to_all(
            halfway.reshape(16, own, -1),
            ("depth", "low", "core"),
            split_axis=0,
            concat_axis=0,
            tiled=True,
        )
        return parts.reshape(4, 2, 2, own, -1)

    halfway, spectrum = first_columns(as_scalar(high), data, kernels)
    parts = [to_rows(halfway)]
    cuts = [(1, 2), (3, planes - 3)]
    for plane, count in cuts:
        halfway = next_columns(as_scalar(high), plane, count, spectrum, kernels)
        if plane > 1:
            halfway, parts[-1] = lax.optimization_barrier((halfway, parts[-1]))
        parts.append(to_rows(halfway))
    middle = nyquist_column(as_scalar(block), planes, data)
    intensities, edges = [], []
    for (plane, count), part in zip([(0, 1)] + cuts, parts):
        intensity, edge = row_inverse(plane, count, part, middle)
        intensities.append(intensity)
        edges.append(edge)

    order = [
        ((d * 2 + h) * 2 + l) * 2 + c
        for h in range(2)
        for l in range(2)
        for c in range(2)
        for d in range(4)
    ]
    down = list(zip(order[:-1], order[1:]))
    up = [(target, source) for source, target in down]
    first = jnp.concatenate([edge[:, 0] for edge in edges])
    last = jnp.concatenate([edge[:, 15] for edge in edges])
    north = lax.ppermute(last, everyone, down)
    south = lax.ppermute(first, everyone, up)
    inner = exchange_depth(inner_focus(intensities, own // 4, own // 2))
    north = jnp.where(block == 0, first, north)
    south = jnp.where(block == N // own - 1, last, south)
    outer = exchange_depth(outer_focus(intensities, north, south, own // 4))
    return assemble(as_scalar(depth), inner, outer)


def solution(mesh):
    spec = P("rows", None)
    if mesh.shape["depth"] == 4 and mesh.shape["rows"] == 8:
        split = Mesh(mesh.devices.reshape(4, 2, 2, 2), ("depth", "high", "low", "core"))
        spec = P(("high", "low", "core"), None)
        body = half_spectrum_shards
    else:
        split, body = mesh, shards
    return jax.shard_map(body, mesh=split, in_specs=(spec, spec), out_specs=spec, check_vma=False)
```

```python
import functools
import math

import jax
import jax.numpy as jnp
import numpy as np
from jax import lax
from jax.experimental import pallas as pl
from jax.experimental.pallas import tpu as pltpu
from jax.sharding import Mesh
from jax.sharding import PartitionSpec as P

N = 4096
RADIX = 64
PL_DEV = 1


wave_number = 0.6
depth_start = 8.0
depth_step = 2.0


def padded_2(block, sides, width):
    for axis, dim in sides:
        count = lax.axis_size(axis)
        forward = [(i, i + 1) for i in range(count - 1)]
        backward = [(target, source) for source, target in forward]
        low = lax.ppermute(
            lax.slice_in_dim(block, block.shape[dim] - width, None, axis=dim), axis, forward
        )
        high = lax.ppermute(lax.slice_in_dim(block, 0, width, axis=dim), axis, backward)
        block = jnp.concatenate([low, block, high], axis=dim)
    return block


def fourier_tables(radix_size, sign_value):
    indices = jnp.arange(radix_size, dtype=jnp.int32)
    products = indices[:, None] * indices[None, :] % radix_size
    angles = products.astype(jnp.float32) * (sign_value * 2.0 * math.pi / radix_size)
    scaling = 1.0 / math.sqrt(radix_size)
    cosine_part = jnp.cos(angles) * scaling
    sine_part = jnp.sin(angles) * scaling
    matrix = jnp.stack([jnp.stack([cosine_part, -sine_part]), jnp.stack([sine_part, cosine_part])])
    return matrix.astype(jnp.bfloat16)


def twiddle_table(radix_size, sign_value):
    indices = jnp.arange(radix_size, dtype=jnp.int32)
    total = radix_size * radix_size
    products = indices[:, None] * indices[None, :] % total
    angles = products.astype(jnp.float32) * (sign_value * 2.0 * math.pi / total)
    return (jnp.cos(angles), jnp.sin(angles))


def rotate(data, cosine_part, sine_part):
    return jnp.stack(
        [data[0] * cosine_part - data[1] * sine_part, data[0] * sine_part + data[1] * cosine_part]
    )


def contract(form, matrix, data):
    return jnp.einsum(form, matrix, data, preferred_element_type=jnp.float32)


def forward_real(data):
    batch_size = data.shape[1]
    shaped = data.reshape(RADIX, RADIX, batch_size)
    matrix = fourier_tables(RADIX, -1.0)
    cosine_part, sine_part = twiddle_table(RADIX, -1.0)
    opening = contract("oka,abm->okbm", matrix[:, 0], shaped)
    sectioned = rotate(opening, cosine_part[:, :, None], sine_part[:, :, None]).astype(jnp.bfloat16)
    closing = contract("ocjb,ckbm->okjm", matrix, sectioned)
    return closing.reshape(2, N, batch_size).astype(jnp.bfloat16)


def forward_first(data):
    batch_size = data.shape[2]
    shaped = data.reshape(2, RADIX, RADIX, batch_size)
    matrix = fourier_tables(RADIX, -1.0)
    cosine_part, sine_part = twiddle_table(RADIX, -1.0)
    opening = contract("ocka,cabm->okbm", matrix, shaped)
    sectioned = rotate(opening, cosine_part[:, :, None], sine_part[:, :, None]).astype(jnp.bfloat16)
    closing = contract("ocjb,ckbm->okjm", matrix, sectioned)
    return closing.reshape(2, N, batch_size).astype(jnp.bfloat16)


def inverse_first(data):
    batch_size = data.shape[2]
    shaped = data.reshape(2, RADIX, RADIX, batch_size)
    matrix = fourier_tables(RADIX, 1.0)
    cosine_part, sine_part = twiddle_table(RADIX, 1.0)
    opening = contract("ocbj,ckjm->okbm", matrix, shaped)
    sectioned = rotate(opening, cosine_part[:, :, None], sine_part[:, :, None]).astype(jnp.bfloat16)
    closing = contract("ocak,ckbm->oabm", matrix, sectioned)
    return closing.reshape(2, N, batch_size)


def frequencies(positions):
    natural = positions // RADIX + RADIX * (positions % RADIX)
    signed_freq = jnp.where(natural >= N // 2, natural - N, natural)
    return signed_freq.astype(jnp.float32) / N


def propagator(freq_whole, freq_own, distance):
    radial = freq_whole[:, None] ** 2 + freq_own[None, :] ** 2
    limit = wave_number * wave_number
    amplitude = jnp.exp(-2.0 * math.pi * distance * jnp.sqrt(jnp.maximum(radial - limit, 0.0)))
    phase_angle = (
        2.0 * math.pi * distance * (jnp.sqrt(jnp.maximum(limit - radial, 0.0)) - wave_number)
    )
    return (amplitude * jnp.cos(phase_angle), amplitude * jnp.sin(phase_angle))


def propagate(spectrum, cosine_part, sine_part):
    return rotate(spectrum.astype(jnp.float32), cosine_part, sine_part).astype(jnp.bfloat16)


def shards(hologram, background):
    row_count = hologram.shape[0]
    contrast = (hologram.astype(jnp.float32) / background.astype(jnp.float32) - 1.0).astype(
        jnp.bfloat16
    )
    along_rows = forward_real(contrast.T)
    columns = lax.all_to_all(
        jnp.swapaxes(along_rows, 1, 2), "rows", split_axis=2, concat_axis=1, tiled=True
    )
    spectrum = forward_first(columns)
    row_index = lax.axis_index("rows")
    own_positions = row_index * row_count + jnp.arange(row_count, dtype=jnp.int32)
    freq_own = frequencies(own_positions)
    freq_whole = frequencies(jnp.arange(N, dtype=jnp.int32))
    depth_index = lax.axis_index("depth")
    distance = depth_start + depth_step * (depth_index * PL_DEV + 0).astype(jnp.float32)
    cosine_part, sine_part = propagator(freq_whole, freq_own, distance)
    propagated = propagate(spectrum, cosine_part, sine_part)
    halfway = inverse_first(propagated).astype(jnp.bfloat16)
    restored = lax.all_to_all(
        jnp.swapaxes(halfway, 1, 2), "rows", split_axis=2, concat_axis=1, tiled=True
    )
    result_field = inverse_first(restored)
    intensities = [
        (result_field[0] * result_field[0] + result_field[1] * result_field[1]).astype(jnp.bfloat16)
    ]
    stacked = jnp.stack(intensities)
    padded = padded_2(stacked, (("depth", 0), ("rows", 2)), 1)
    centre_block = padded[1:-1, :, 1:-1]
    plane_ids = jnp.arange(PL_DEV, dtype=jnp.int32)[:, None, None]
    row_ids = jnp.arange(row_count, dtype=jnp.int32)[None, None, :]
    depth_count = lax.axis_size("depth")
    row_groups = lax.axis_size("rows")
    lower_plane = jnp.where(
        (depth_index == 0) & (plane_ids == 0), centre_block, padded[:-2, :, 1:-1]
    )
    upper_plane = jnp.where(
        (depth_index == depth_count - 1) & (plane_ids == PL_DEV - 1),
        centre_block,
        padded[2:, :, 1:-1],
    )
    north_row = jnp.where((row_index == 0) & (row_ids == 0), centre_block, padded[1:-1, :, :-2])
    south_row = jnp.where(
        (row_index == row_groups - 1) & (row_ids == row_count - 1),
        centre_block,
        padded[1:-1, :, 2:],
    )
    centre = centre_block.astype(jnp.float32)
    east_col = jnp.concatenate([centre[:, 1:], centre[:, -1:]], axis=1)
    west_col = jnp.concatenate([centre[:, :1], centre[:, :-1]], axis=1)
    depth_diff = upper_plane.astype(jnp.float32) - lower_plane.astype(jnp.float32)
    row_diff = south_row.astype(jnp.float32) - north_row.astype(jnp.float32)
    col_diff = east_col - west_col
    scores = (depth_diff * depth_diff + row_diff * row_diff + col_diff * col_diff) / 8.0
    sharpest = jnp.max(scores, axis=0)
    merged = lax.pmax(sharpest.astype(jnp.bfloat16), "depth").astype(sharpest.dtype)
    return merged.T


OUT = 16
INN = 256
CLS = 8
LANE = 128
MIB = 2**20
VMEM = 63 * MIB
SHARED = 36 * MIB


def slot_frequencies():
    table = np.arange(CLS)[:, None] + OUT * np.arange(INN)[None, :]
    half = np.arange(INN // 2)
    table[0] = np.concatenate([OUT * half, CLS + OUT * half])
    return table


def angles(products):
    return 2.0 * np.pi * (products % N) / N


def row_forward_tables():
    freq = slot_frequencies()
    theta = angles(np.arange(INN)[None, :, None] * freq[:, None, :])
    cos, sin = np.cos(theta) / 64.0, np.sin(theta) / 64.0
    top = np.stack([cos, -sin], axis=2)
    low = np.stack([sin, cos], axis=2)
    first = np.arange(INN) < INN // 2
    low[0] = np.where(first, 0.0, top[0])
    top[0] = np.where(first, top[0], 0.0)
    full = np.concatenate([top, low], axis=1)
    full = full.reshape(CLS, 2 * INN, 2, 2, LANE).transpose(0, 1, 3, 2, 4)
    return full.reshape(CLS, 2 * INN, 2 * INN).astype(jnp.bfloat16)


def row_forward_weights():
    turn = 2.0 * np.pi * np.arange(CLS)[:, None] * np.arange(OUT)[None, :] / OUT
    re, im = np.cos(turn), -np.sin(turn)
    im[0] = (-1.0) ** np.arange(OUT)
    return np.stack([re, im], axis=1).reshape(-1).astype(np.float32)


def row_inverse_tables():
    freq = slot_frequencies()
    theta = angles(freq[:, :, None] * np.arange(INN)[None, None, :])
    cos, sin = np.cos(theta) / 32.0, np.sin(theta) / 32.0
    full = np.zeros((CLS, 2, INN, 2, INN))
    full[:, 0, :, 0], full[:, 0, :, 1] = cos, sin
    full[:, 1, :, 0], full[:, 1, :, 1] = -sin, cos
    half = INN // 2
    full[0] = 0.0
    full[0, 0, :half, 0], full[0, 1, :half, 0] = cos[0, :half], -sin[0, :half]
    full[0, 0, half:, 1], full[0, 1, half:, 1] = cos[0, half:], -sin[0, half:]
    full[0, 0, 0, 0] = 1.0 / 64.0
    full[0, 1, 0, 0] = (-1.0) ** np.arange(INN) / 64.0
    full = full.reshape(CLS, 2, 2, LANE, 2 * INN).transpose(0, 2, 1, 3, 4)
    return full.reshape(CLS, 2 * INN, 2 * INN).astype(jnp.bfloat16)


def column_tables():
    turn = 2.0 * np.pi * np.arange(OUT)[:, None] * np.arange(OUT)[None, :] / OUT
    eye = np.eye(16)
    outer_cos, outer_sin = np.kron(np.cos(turn), eye) / 4.0, np.kron(np.sin(turn), eye) / 4.0
    outer = np.concatenate([outer_cos, -outer_sin])
    outer = outer.reshape(-1, 8, 2, 16).swapaxes(1, 2).reshape(outer.shape)
    half_rows = outer_cos.shape[0] // 2
    back = np.stack(
        [
            np.concatenate([outer_cos[i * half_rows :][:half_rows], outer_sin[i * half_rows :][:half_rows]])
            for i in range(2)
        ]
    )
    beyond = np.stack(
        [np.concatenate([outer_cos[a * 16 :][:16], outer_sin[a * 16 :][:16]]) for a in (8, 7)]
    )
    freq = np.arange(OUT)[:, None] + OUT * np.arange(INN)[None, :]
    theta = angles(freq[:, :, None] * np.arange(INN)[None, None, :])
    inner = np.concatenate([np.cos(theta), -np.sin(theta)], axis=1) / 16.0
    theta = theta.transpose(0, 2, 1)
    inner_back = np.concatenate([np.cos(theta), np.sin(theta)], axis=1) / 16.0
    cast = lambda table: table.astype(jnp.bfloat16)
    return cast(outer), cast(inner), cast(inner_back), cast(back), cast(beyond)


def dot(left, right):
    return jnp.dot(left, right, preferred_element_type=jnp.float32)


def split_complex(both, width):
    rows = both.shape[0] // 2
    top, low = both[:rows], both[rows:]
    return top[:, :width] - low[:, width:], top[:, width:] + low[:, :width]


def quarter_kernel(radial):
    gap = wave_number * wave_number - radial
    root = jnp.sqrt(jnp.abs(gap))
    inside = gap > 0.0
    half_pi = 0.5 * math.pi
    angle = half_pi * (jnp.where(inside, root, 0.0) - wave_number)
    decay = jnp.exp(jnp.where(inside, 0.0, -half_pi * root))
    square = angle * angle
    sine = 1.0 / 362880.0
    for c in (-1.0 / 5040.0, 1.0 / 120.0, -1.0 / 6.0, 1.0):
        sine = sine * square + c
    cosine = -1.0 / 3628800.0
    for c in (1.0 / 40320.0, -1.0 / 720.0, 1.0 / 24.0, -0.5, 1.0):
        cosine = cosine * square + c
    return decay * cosine, decay * (sine * angle)


def squared(re, im):
    return (re - im) * (re + im), 2.0 * re * im


def start_and_step(radial):
    value = quarter_kernel(radial)
    distance = 0.25
    step = None
    while distance < depth_start:
        value = squared(*value)
        distance *= 2.0
        if distance == depth_step:
            step = value
    return value, step


def signed_fraction(natural):
    return jnp.where(natural >= N // 2, natural - N, natural).astype(jnp.float32) * (1.0 / N)


def row_forward_kernel(own, weights, holo, back, table, out, acc, held):
    step = pl.program_id(0)
    rows = holo.shape[0]
    group = own[0]
    lane = lax.broadcasted_iota(jnp.int32, (16, INN), 1)
    sign = jnp.where(lane % 2 == 0, 1.0, -1.0).astype(jnp.bfloat16)

    def strip(i, carry):
        here = pl.ds(pl.multiple_of(i * 16, 16), 16)
        sums = [jnp.zeros((16, INN), jnp.float32) for _ in range(5)]
        for a in range(OUT):
            there = pl.ds(a * INN, INN)
            value = holo[here, there].astype(jnp.float32) / back[here, there].astype(jnp.float32)
            value = (value - 1.0).astype(jnp.bfloat16).astype(jnp.float32)
            for q in range(4):
                w = weights[(group * 2 + q // 2) * (2 * OUT) + (q % 2) * OUT + a]
                sums[q] = sums[q] + value * w
            sums[4] = sums[4] + value
        for q in range(4):
            acc[q // 2, here, pl.ds((q % 2) * INN, INN)] = sums[q].astype(jnp.bfloat16)
        acc[2, here, pl.ds(0, INN)] = sums[4].astype(jnp.bfloat16)
        return carry

    lax.fori_loop(0, rows // 16, strip, 0)
    here = pl.ds(pl.multiple_of(step * rows, rows), rows)
    for q in range(2):
        result = dot(acc[q], table[q]).astype(jnp.bfloat16)
        for low in range(2):
            part = result[:, low * 2 * LANE : (low + 1) * 2 * LANE]
            for high in range(2):
                out[high, low, q, here, :] = part
    alternating = lax.dot_general(
        sign, acc[2, :, :INN], (((1,), (1,)), ((), ())), preferred_element_type=jnp.float32
    )
    held[step] = alternating * (1.0 / 64.0)

    @pl.when(step == pl.num_programs(0) - 1)
    def _():
        rows_of = [jnp.concatenate([held[2 * r], held[2 * r + 1]], axis=1) for r in range(2)]
        extra = jnp.where(lax.broadcasted_iota(jnp.int32, (16, INN), 0) == 0, rows_of[0], rows_of[1])
        extra = extra.astype(jnp.bfloat16)
        for high in range(2):
            for low in range(2):
                for q in range(2):
                    out[high, low, q, pl.ds(4 * rows, 16), :] = extra


def row_forward(own, hologram, background):
    rows = hologram.shape[0]
    block = LANE
    table = jnp.asarray(row_forward_tables())
    weights = jnp.asarray(row_forward_weights())
    shape = (2, 2, 2, rows + 16, 2 * LANE)
    return pl.pallas_call(
        row_forward_kernel,
        grid_spec=pltpu.PrefetchScalarGridSpec(
            num_scalar_prefetch=2,
            grid=(rows // block,),
            in_specs=[
                pl.BlockSpec((block, N), lambda i, o, w: (i, 0)),
                pl.BlockSpec((block, N), lambda i, o, w: (i, 0)),
                pl.BlockSpec((2, 2 * INN, 2 * INN), lambda i, o, w: (o[0], 0, 0)),
            ],
            out_specs=pl.BlockSpec(shape, lambda i, o, w: (0, 0, 0, 0, 0)),
            scratch_shapes=[
                pltpu.VMEM((3, block, 2 * INN), jnp.bfloat16),
                pltpu.VMEM((rows // block, 16, LANE), jnp.float32),
            ],
        ),
        out_shape=jax.ShapeDtypeStruct(shape, jnp.bfloat16),
        compiler_params=pltpu.CompilerParams(vmem_limit_bytes=VMEM),
        cost_estimate=pl.CostEstimate(flops=10**10, bytes_accessed=12 * MIB, transcendentals=0),
        name="row_forward",
    )(own, weights, hologram, background, table)


def propagator_kernel(planes, fx2, out):
    step = pl.program_id(0)
    strip = 32
    for i in range(INN // strip):
        rows = slice(i * strip, (i + 1) * strip)
        position = lax.broadcasted_iota(jnp.int32, (strip, LANE), 0) + i * strip
        fy = signed_fraction(step + OUT * position)
        (kr, ki), (sr, si) = start_and_step(fy * fy + fx2[...])
        for g in range(planes):
            out[g, 0, rows, :LANE] = kr
            out[g, 0, rows, LANE:] = ki
            if g + 1 < planes:
                kr, ki = kr * sr - ki * si, kr * si + ki * sr


def propagators(planes, fx2):
    return pl.pallas_call(
        functools.partial(propagator_kernel, planes),
        grid=(OUT,),
        in_specs=[pl.BlockSpec((1, LANE), lambda i: (0, 0))],
        out_specs=pl.BlockSpec((planes, 1, INN, 2 * LANE), lambda i: (0, i, 0, 0)),
        out_shape=jax.ShapeDtypeStruct((planes, OUT, INN, 2 * LANE), jnp.float32),
        compiler_params=pltpu.CompilerParams(vmem_limit_bytes=VMEM),
        cost_estimate=pl.CostEstimate(flops=10**9, bytes_accessed=16 * MIB, transcendentals=10**6),
        name="propagators",
    )(fx2)


PER = 4


def mix_and_open(k, slot, yr, yi, kernels, inner_back, mixed, second):
    width = LANE
    for part in range(2):
        factor = kernels[:, part * width : (part + 1) * width]
        at = part * 2 * width
        mixed[slot, :, at : at + width] = (yr * factor).astype(jnp.bfloat16)
        mixed[slot, :, at + width : at + 2 * width] = (yi * factor).astype(jnp.bfloat16)
    both = dot(inner_back, mixed[slot])
    for part in range(2):
        lanes = slice(part * 2 * width, (part + 1) * 2 * width)
        re, im = split_complex(both[:, lanes], width)
        second[k, :, lanes] = jnp.concatenate([re, im], axis=1).astype(jnp.bfloat16)


def close_columns(half, step, back, beyond, second, out, outside):
    width = LANE
    start = step * PER

    @pl.when(step == 0)
    def _():
        here = pl.ds(pl.multiple_of(half[0] * (INN - 16), 16), 16)
        both = dot(beyond[0], second[:, here, :].reshape(OUT * 16, 4 * width))
        for part in range(2):
            lanes = slice(part * 2 * width, (part + 1) * 2 * width)
            re, im = split_complex(both[:, lanes], width)
            outside[0, :, lanes] = jnp.concatenate([re, im], axis=1).astype(jnp.bfloat16)

    for c in range(PER):
        here = pl.ds(pl.multiple_of((start + c) * 16, 16), 16)
        both = dot(back[0], second[:, here, :].reshape(OUT * 16, 4 * width))
        rows = slice(c * 16, (c + 1) * 16)
        for part in range(2):
            lanes = slice(part * 2 * width, (part + 1) * 2 * width)
            re, im = split_complex(both[:, lanes], width)
            value = jnp.concatenate([re, im], axis=1).astype(jnp.bfloat16)
            value = value.reshape(2, 2, 2, 16, 2 * width)
            for low in range(2):
                for core in range(2):
                    for high in range(2):
                        out[high, 0, low, core, rows, lanes] = value[low, core, high]


def first_columns_kernel(
    half, data, kernels, outer, inner, inner_back, back, beyond,
    out, outside, spectrum, first, mixed, second,
):
    step = pl.program_id(0)
    width = LANE

    @pl.when(step == 0)
    def _():
        for i in range(INN // 16):
            here = slice(i * 16, (i + 1) * 16)
            there = slice(INN + i * 16, INN + (i + 1) * 16)
            block = jnp.concatenate([data[:, here, :], data[:, there, :]], axis=0)
            re, im = split_complex(dot(outer[...], block.reshape(OUT * 16, 2 * width)), width)
            value = jnp.concatenate([re, im], axis=1).astype(jnp.bfloat16)
            first[:, here, :] = value.reshape(OUT, 16, 2 * width)

    @pl.when(step < OUT // PER)
    def _():
        for c in range(PER):
            k = step * PER + c
            yr, yi = split_complex(dot(inner[c], first[k]), width)
            spectrum[c] = jnp.concatenate([yr, yi], axis=1).astype(jnp.bfloat16)
            mix_and_open(k, c, yr, yi, kernels[0, c], inner_back[c], mixed, second)

    @pl.when(step >= OUT // PER)
    def _():
        close_columns(half, step - OUT // PER, back, beyond, second, out, outside)


def next_columns_kernel(
    half, spectrum, kernels, inner_back, back, beyond, out, outside, mixed, second
):
    step = pl.program_id(1)
    width = LANE

    @pl.when(step < OUT // PER)
    def _():
        for c in range(PER):
            values = spectrum[c].astype(jnp.float32)
            yr, yi = values[:, :width], values[:, width:]
            mix_and_open(step * PER + c, c, yr, yi, kernels[0, c], inner_back[c], mixed, second)

    @pl.when(step >= OUT // PER)
    def _():
        close_columns(half, step - OUT // PER, back, beyond, second, out, outside)


STEPS = OUT // PER


def opening_step(s):
    return jnp.minimum(s, STEPS - 1)


def closing_step(s):
    return jnp.maximum(s - STEPS, 0)


def first_columns(half, data, kernels):
    outer, inner, inner_back, back, beyond = (jnp.asarray(t) for t in column_tables())
    rows = data.shape[1] - 16
    opening = lambda i, o: (opening_step(i), 0, 0)
    return pl.pallas_call(
        first_columns_kernel,
        grid_spec=pltpu.PrefetchScalarGridSpec(
            num_scalar_prefetch=1,
            grid=(2 * STEPS,),
            in_specs=[
                pl.BlockSpec((8, rows, 2 * LANE), lambda i, o: (0, 0, 0)),
                pl.BlockSpec((1, PER, INN, 2 * LANE), lambda i, o: (0, opening_step(i), 0, 0)),
                pl.BlockSpec((2 * INN, INN), lambda i, o: (0, 0)),
                pl.BlockSpec((PER, 2 * INN, INN), opening),
                pl.BlockSpec((PER, 2 * INN, INN), opening),
                pl.BlockSpec((1, INN, INN), lambda i, o: (o[0], 0, 0)),
                pl.BlockSpec((1, 32, INN), lambda i, o: (o[0], 0, 0)),
            ],
            out_specs=[
                pl.BlockSpec(
                    (2, 1, 2, 2, PER * 16, 4 * LANE),
                    lambda i, o: (0, closing_step(i) // 2, 0, 0, closing_step(i) % 2, 0),
                ),
                pl.BlockSpec((1, 16, 4 * LANE), lambda i, o: (0, 0, 0)),
                pl.BlockSpec((PER, INN, 2 * LANE), opening),
            ],
            scratch_shapes=[
                pltpu.VMEM((OUT, INN, 2 * LANE), jnp.bfloat16),
                pltpu.VMEM((PER, INN, 4 * LANE), jnp.bfloat16),
                pltpu.VMEM((OUT, INN, 4 * LANE), jnp.bfloat16),
            ],
        ),
        out_shape=[
            jax.ShapeDtypeStruct((2, 2, 2, 2, LANE, 4 * LANE), jnp.bfloat16),
            jax.ShapeDtypeStruct((1, 16, 4 * LANE), jnp.bfloat16),
            jax.ShapeDtypeStruct((OUT, INN, 2 * LANE), jnp.bfloat16),
        ],
        compiler_params=pltpu.CompilerParams(vmem_limit_bytes=VMEM),
        cost_estimate=pl.CostEstimate(flops=10**10, bytes_accessed=20 * MIB, transcendentals=0),
        name="first_columns",
    )(half, data, kernels, outer, inner, inner_back, back, beyond)


def next_columns(half, plane, count, spectrum, kernels):
    inner_back, back, beyond = (jnp.asarray(t) for t in column_tables()[2:])
    opening = lambda g, i, o: (opening_step(i), 0, 0)
    return pl.pallas_call(
        next_columns_kernel,
        grid_spec=pltpu.PrefetchScalarGridSpec(
            num_scalar_prefetch=1,
            grid=(count, 2 * STEPS),
            in_specs=[
                pl.BlockSpec((PER, INN, 2 * LANE), opening),
                pl.BlockSpec(
                    (1, PER, INN, 2 * LANE), lambda g, i, o: (plane + g, opening_step(i), 0, 0)
                ),
                pl.BlockSpec((PER, 2 * INN, INN), opening),
                pl.BlockSpec((1, INN, INN), lambda g, i, o: (o[0], 0, 0)),
                pl.BlockSpec((1, 32, INN), lambda g, i, o: (o[0], 0, 0)),
            ],
            out_specs=[
                pl.BlockSpec(
                    (2, 1, 2, 2, PER * 16, 4 * LANE),
                    lambda g, i, o: (0, closing_step(i) // 2, 0, 0, closing_step(i) % 2, g),
                ),
                pl.BlockSpec((1, 16, 4 * LANE), lambda g, i, o: (g, 0, 0)),
            ],
            scratch_shapes=[
                pltpu.VMEM((PER, INN, 4 * LANE), jnp.bfloat16),
                pltpu.VMEM((OUT, INN, 4 * LANE), jnp.bfloat16),
            ],
        ),
        out_shape=[
            jax.ShapeDtypeStruct((2, 2, 2, 2, LANE, count * 4 * LANE), jnp.bfloat16),
            jax.ShapeDtypeStruct((count, 16, 4 * LANE), jnp.bfloat16),
        ],
        compiler_params=pltpu.CompilerParams(vmem_limit_bytes=VMEM),
        cost_estimate=pl.CostEstimate(
            flops=count * 7 * 10**9, bytes_accessed=count * 16 * MIB, transcendentals=0
        ),
        name="next_columns",
    )(half, spectrum, kernels, inner_back, back, beyond)


def sixteen_points(re, im):
    c = math.sqrt(0.5)
    c1, c3 = math.cos(math.pi / 8), math.cos(3 * math.pi / 8)
    r0, r1, r2, r3, r4, r5, r6, r7 = re
    r8, i1, i2, i3, i4, i5, i6, i7 = im
    sum08, dif08, sum26, dif26 = r0 + r8, r0 - r8, r2 + r6, c * (r2 - r6)
    base = sum08 + r4
    even = [base + sum26, dif08 + dif26, sum08 - r4, dif08 - dif26, base - sum26]
    sum17, dif17, sum35, dif35 = r1 + r7, r1 - r7, r3 + r5, r3 - r5
    odd = [sum17 + sum35, c1 * dif17 + c3 * dif35, c * (sum17 - sum35), c3 * dif17 - c1 * dif35]
    cosines = [even[a] + odd[a] for a in range(4)] + [even[4]]
    cosines += [even[8 - a] - odd[8 - a] for a in range(5, 9)]
    s17, d17, s35, d35 = i1 + i7, i1 - i7, i3 + i5, i3 - i5
    sines_odd = [None, c3 * s17 + c1 * s35, c * (d17 + d35), c1 * s17 - c3 * s35, d17 - d35]
    s26 = c * (i2 + i6)
    sines_even = [None, s26 + i4, i2 - i6, s26 - i4]
    sines = [None] + [sines_odd[a] + sines_even[a] for a in (1, 2, 3)] + [sines_odd[4]]
    sines += [sines_odd[8 - a] - sines_even[8 - a] for a in (5, 6, 7)]
    result = [cosines[0]] + [cosines[a] - sines[a] for a in range(1, 8)] + [cosines[8]]
    return result + [cosines[16 - a] + sines[16 - a] for a in range(9, 16)]


def strip_intensity(opened, here, tile):
    total = None
    for part in range(2):
        re = [opened[part, g, here, tile * LANE : (tile + 1) * LANE] for g in range(CLS)]
        im = [opened[part, g, here, INN + tile * LANE : INN + (tile + 1) * LANE] for g in range(CLS)]
        values = sixteen_points(re, im)
        if total is None:
            total = [v * v for v in values]
        else:
            total = [t + v * v for t, v in zip(total, values)]
    return total


def row_inverse_kernel(plane, parts, nyquist, table, out, edges, opened):
    current = plane + pl.program_id(0)
    rows = parts.shape[3]
    lane = lax.broadcasted_iota(jnp.int32, (rows, LANE), 1)
    for part in range(2):
        at = part * 2 * LANE
        mine = jnp.where(lane == current * 2 + part, nyquist[...], 0.0)
        column = jnp.sum(mine, axis=1, keepdims=True).astype(jnp.bfloat16)
        for group in range(CLS):
            low, high = (parts[group // 2, i, group % 2, :, at : at + 2 * LANE] for i in range(2))
            if group == 0:
                first = jnp.where(lane == 0, column, low[:, LANE:])
                low = jnp.concatenate([low[:, :LANE], first], axis=1)
            opened[part, group] = dot(jnp.concatenate([low, high], axis=1), table[group])

    def strip(i, carry):
        here = pl.ds(pl.multiple_of(i * 16, 16), 16)
        for tile in range(INN // LANE):
            total = strip_intensity(opened, here, tile)
            for a in range(OUT):
                lanes = slice(a * INN + tile * LANE, a * INN + (tile + 1) * LANE)
                out[0, here, lanes] = total[a].astype(jnp.bfloat16)
        return carry

    lax.fori_loop(0, rows // 16, strip, 0)
    edges[0, 0:8, :] = out[0, 0:16, :].astype(jnp.float32)[0:8]
    edges[0, 8:16, :] = out[0, rows - 16 :, :].astype(jnp.float32)[8:16]


def row_inverse(plane, count, parts, nyquist):
    rows = parts.shape[3]
    table = jnp.asarray(row_inverse_tables())
    return pl.pallas_call(
        functools.partial(row_inverse_kernel, plane),
        grid=(count,),
        in_specs=[
            pl.BlockSpec((4, 2, 2, rows, 4 * LANE), lambda g: (0, 0, 0, 0, g)),
            pl.BlockSpec((rows, LANE), lambda g: (0, 0)),
            pl.BlockSpec((CLS, 2 * INN, 2 * INN), lambda g: (0, 0, 0)),
        ],
        out_specs=[
            pl.BlockSpec((1, rows, N), lambda g: (g, 0, 0)),
            pl.BlockSpec((1, 16, N), lambda g: (g, 0, 0)),
        ],
        out_shape=[
            jax.ShapeDtypeStruct((count, rows, N), jnp.bfloat16),
            jax.ShapeDtypeStruct((count, 16, N), jnp.float32),
        ],
        scratch_shapes=[pltpu.VMEM((2, CLS, rows, 2 * INN), jnp.float32)],
        compiler_params=pltpu.CompilerParams(vmem_limit_bytes=VMEM),
        cost_estimate=pl.CostEstimate(
            flops=count * 3 * 10**9, bytes_accessed=count * 8 * MIB, transcendentals=0
        ),
        name="row_inverse",
    )(parts, nyquist, table)


def nyquist_kernel(planes, own, data, out):
    wide = lambda axis: lax.broadcasted_iota(jnp.int32, (INN, INN), axis)
    tall = lambda axis: lax.broadcasted_iota(jnp.int32, (OUT, INN), axis)
    small = lambda axis: lax.broadcasted_iota(jnp.int32, (OUT, OUT), axis)

    def wave(products, period):
        turn = (products % period).astype(jnp.float32) * (2.0 * math.pi / period)
        return jnp.cos(turn), jnp.sin(turn)

    def exact(left, right):
        return jnp.dot(left, right, preferred_element_type=jnp.float32, precision=lax.Precision.HIGHEST)

    def product(xr, xi, yr, yi):
        return exact(xr, yr) - exact(xi, yi), exact(xr, yi) + exact(xi, yr)

    def rotated(xr, xi, yr, yi):
        return xr * yr - xi * yi, xr * yi + xi * yr

    column = jnp.concatenate([data[i, 0:2, :].astype(jnp.float32) for i in range(8)], axis=0)
    wr, wi = wave(small(0) * small(1), OUT)
    inner_r, inner_i = wave(wide(0) * wide(1), INN)
    vr, vi = wave(tall(0) * tall(1), N)
    ar, ai = rotated(exact(wr, column), exact(-wi, column), vr, -vi)
    yr, yi = product(ar, ai, inner_r, -inner_i)
    fy = signed_fraction(tall(0) + OUT * tall(1))
    (kr, ki), (sr, si) = start_and_step(fy * fy + 0.25)
    block, blocks = own[0], own[1]
    k = lax.broadcasted_iota(jnp.int32, (8, OUT), 1)
    section = block // 2 + lax.broadcasted_iota(jnp.int32, (8, OUT), 0) + (OUT - 1)
    hr, hi = wave(k * (section % OUT), OUT)
    even = block % 2 == 0
    lane = lax.broadcasted_iota(jnp.int32, (1, LANE), 1)
    result, beside = [], []
    for g in range(planes):
        pr, pi = rotated(yr, yi, kr, ki)
        br, bi = rotated(*product(pr, pi, inner_r, inner_i), vr, vi)
        for value in product(hr, hi, br, bi):
            value = value * (1.0 / N)
            result.append(jnp.where(even, value[1:2, :LANE], value[1:2, LANE:]))
            above = jnp.where(even, value[0:1, INN - 1 :], value[1:2, LANE - 1 : LANE])
            above = jnp.where(block == 0, value[1:2, 0:1], above)
            below = jnp.where(even, value[1:2, LANE : LANE + 1], value[2:3, 0:1])
            below = jnp.where(block == blocks - 1, value[1:2, INN - 1 :], below)
            beside.append(jnp.where(lane == 0, above, jnp.where(lane == 1, below, 0.0)))
        kr, ki = rotated(kr, ki, sr, si)
    rest = [jnp.zeros((LANE - 2 * planes, LANE), jnp.float32)]
    out[:LANE, :] = jnp.concatenate(result + rest, axis=0).T
    out[LANE:, :] = jnp.concatenate(beside + rest, axis=0).T


def nyquist_column(own, planes, data):
    rows = data.shape[1] - 16
    return pl.pallas_call(
        functools.partial(nyquist_kernel, planes),
        grid_spec=pltpu.PrefetchScalarGridSpec(
            num_scalar_prefetch=1,
            grid=(1,),
            in_specs=[pl.BlockSpec((8, 16, 2 * LANE), lambda i, o: (0, rows // 16, 0))],
            out_specs=pl.BlockSpec((2 * LANE, LANE), lambda i, o: (0, 0)),
        ),
        out_shape=jax.ShapeDtypeStruct((2 * LANE, LANE), jnp.float32),
        compiler_params=pltpu.CompilerParams(vmem_limit_bytes=VMEM),
        cost_estimate=pl.CostEstimate(flops=10**9, bytes_accessed=2**18, transcendentals=0),
        name="nyquist",
    )(own, data)


TILE = 512


def across(centre, tile, west, east):
    lane = lax.broadcasted_iota(jnp.int32, centre.shape, 1)
    right = jnp.where(lane == TILE - 1, east, pltpu.roll(centre, TILE - 1, 1))
    left = jnp.where(lane == 0, west, pltpu.roll(centre, 1, 1))
    return (right - left) * (right - left)


def spatial_term(held, r, t):
    lanes = slice(t * TILE, (t + 1) * TILE)
    centre = held[r : r + 16, lanes]
    down = held[r + 1 : r + 17, lanes] - held[r - 1 : r + 15, lanes]
    first, last = max(t * TILE - 1, 0), min((t + 1) * TILE, N - 1)
    west, east = held[r : r + 16, first : first + 1], held[r : r + 16, last : last + 1]
    return centre, down * down + across(centre, TILE, west, east)


def hold(held, block, rows):
    held[8 : 8 + rows, :] = block.astype(jnp.float32)
    held[7:8, :] = held[8:9, :]
    held[8 + rows : 9 + rows, :] = held[7 + rows : 8 + rows, :]


def early_focus_kernel(first, others, best, spatial, held):
    rows = first.shape[1]
    for g in range(3):
        hold(held.at[g], first[0] if g == 0 else others[g - 1], rows)
    for i in range(rows // 16):
        r = 8 + i * 16
        for t in range(N // TILE):
            lanes = slice(t * TILE, (t + 1) * TILE)
            (c0, s0), (c1, s1), (c2, s2) = (spatial_term(held.at[g], r, t) for g in range(3))
            d0, d1 = c1 - c0, c2 - c0
            score = jnp.maximum(d0 * d0 + s0, d1 * d1 + s1)
            best[r - 8 : r + 8, lanes] = (score * 0.125).astype(jnp.bfloat16)
            spatial[r - 8 : r + 8, lanes] = s2


def early_focus(first, others):
    rows = first.shape[1]
    return pl.pallas_call(
        early_focus_kernel,
        out_shape=[
            jax.ShapeDtypeStruct((rows, N), jnp.bfloat16),
            jax.ShapeDtypeStruct((rows, N), jnp.float32),
        ],
        scratch_shapes=[pltpu.VMEM((3, rows + 16, N), jnp.float32)],
        compiler_params=pltpu.CompilerParams(vmem_limit_bytes=VMEM),
        cost_estimate=pl.CostEstimate(flops=10**9, bytes_accessed=12 * MIB, transcendentals=0),
        name="early_focus",
    )(first, others)


def edge_rows(edges, halo, out_upper, out_lower):
    lane = lax.broadcasted_iota(jnp.int32, (2, N), 1)
    pair = lambda a, b: jnp.concatenate([a, b], axis=0)
    centre = [pair(e[0:1, :], e[15:16, :]) for e in edges]
    best = None
    for g, e in enumerate(edges):
        depth = centre[min(g + 1, 3)] - centre[max(g - 1, 0)]
        above, below = halo[2 * g : 2 * g + 1, :], halo[2 * g + 1 : 2 * g + 2, :]
        down = pair(e[1:2, :], below) - pair(above, e[14:15, :])
        c = centre[g]
        right = jnp.where(lane == N - 1, c, jnp.concatenate([c[:, 1:], c[:, :1]], axis=1))
        left = jnp.where(lane == 0, c, jnp.concatenate([c[:, -1:], c[:, :-1]], axis=1))
        score = depth * depth + down * down + (right - left) * (right - left)
        best = score if best is None else jnp.maximum(best, score)
    best = best * 0.125
    rows = out_upper.shape[0]
    index = lax.broadcasted_iota(jnp.int32, (16, N), 0)
    top = out_upper[0:16, :].astype(jnp.float32)
    out_upper[0:16, :] = jnp.where(index == 0, best[0:1], top).astype(jnp.bfloat16)
    low = out_lower[rows - 16 :, :].astype(jnp.float32)
    out_lower[rows - 16 :, :] = jnp.where(index == 15, best[1:2], low).astype(jnp.bfloat16)


def last_rows_kernel(
    parts, nyquist, table, best, spatial, others, edge0, edge12,
    upper, lower,
    part_buf, table_buf, best_buf, spatial_buf, others_buf, opened, held, halo, edge, sems,
):
    rows = upper.shape[0] * 2
    loads = []
    for group in range(CLS):
        source = parts.at[group // 2, :, group % 2]
        loads.append(pltpu.make_async_copy(source, part_buf.at[group], sems.at[0, group]))
        loads.append(pltpu.make_async_copy(table.at[group], table_buf.at[group], sems.at[1, group]))
    for i, (source, target) in enumerate(
        ((best, best_buf), (spatial, spatial_buf), (others, others_buf))
    ):
        loads.append(pltpu.make_async_copy(source, target, sems.at[2, i]))
    for load in loads:
        load.start()
    lane = lax.broadcasted_iota(jnp.int32, (rows, LANE), 1)
    few_lane = lax.broadcasted_iota(jnp.int32, (16, LANE), 1)
    few_row = lax.broadcasted_iota(jnp.int32, (16, LANE), 0)
    beside = jnp.where(few_row % 2 == 0, nyquist[rows : rows + 1, :], nyquist[rows + 1 : rows + 2, :])
    for group in range(CLS):
        loads[2 * group].wait()
        loads[2 * group + 1].wait()
        for part in range(2):
            at = part * 2 * LANE
            low, high = (part_buf[group, i, :, at : at + 2 * LANE] for i in range(2))
            if group == 0:
                mine = jnp.where(lane == 6 + part, nyquist[:rows, :], 0.0)
                few = jnp.where(few_lane == (few_row // 2) * 2 + part, beside, 0.0)
                column = jnp.sum(jnp.concatenate([mine, few], axis=0), axis=1, keepdims=True)
                column = column.astype(jnp.bfloat16)
                every = lax.broadcasted_iota(jnp.int32, (rows + 16, LANE), 1)
                first = jnp.where(every == 0, column, low[:, LANE:])
                low = jnp.concatenate([low[:, :LANE], first], axis=1)
            opened[part, group] = dot(jnp.concatenate([low, high], axis=1), table_buf[group])

    def strip(i, carry):
        base = pl.multiple_of(i * 8, 8)
        for tile in range(INN // LANE):
            for a, value in enumerate(strip_intensity(opened, pl.ds(base, 8), tile)):
                lanes = slice(a * INN + tile * LANE, a * INN + (tile + 1) * LANE)
                value = value.astype(jnp.bfloat16).astype(jnp.float32)
                held[pl.ds(pl.multiple_of(base + 8, 8), 8), lanes] = value
        return carry

    lax.fori_loop(0, rows // 8 + 1, strip, 0)
    halo[...] = held[8 + rows : 16 + rows, :]
    held[7:8, :] = held[8:9, :]
    held[8 + rows : 9 + rows, :] = held[7 + rows : 8 + rows, :]
    edge[0:8, :] = held[8:16, :]
    edge[8:16, :] = held[rows : rows + 8, :]
    for load in loads[2 * CLS :]:
        load.wait()
    for i in range(rows // 16):
        r = 8 + i * 16
        here = slice(r - 8, r + 8)
        out, at = (upper, r - 8) if 2 * i < rows // 16 else (lower, r - 8 - rows // 2)
        for t in range(N // TILE):
            lanes = slice(t * TILE, (t + 1) * TILE)
            centre, term = spatial_term(held, r, t)
            d2 = centre - others_buf[0, here, lanes].astype(jnp.float32)
            d3 = centre - others_buf[1, here, lanes].astype(jnp.float32)
            score = jnp.maximum(d2 * d2 + spatial_buf[here, lanes], d3 * d3 + term)
            score = jnp.maximum(score * 0.125, best_buf[here, lanes].astype(jnp.float32))
            out[at : at + 16, lanes] = score.astype(jnp.bfloat16)
    edge_rows([edge0.at[0], edge12.at[0], edge12.at[1], edge], halo, upper, lower)


def last_rows(parts, nyquist, best, spatial, others, edge0, edge12):
    rows = best.shape[0]
    table = jnp.asarray(row_inverse_tables())
    vmem, hbm = pl.BlockSpec(memory_space=pltpu.VMEM), pl.BlockSpec(memory_space=pl.ANY)
    bf16, f32 = jnp.bfloat16, jnp.float32
    return pl.pallas_call(
        last_rows_kernel,
        in_specs=[hbm, vmem, hbm, hbm, hbm, hbm, vmem, vmem],
        out_specs=[vmem] * 2,
        out_shape=[jax.ShapeDtypeStruct((rows // 2, N), bf16)] * 2,
        scratch_shapes=[
            pltpu.VMEM((CLS, 2, rows + 16, 4 * LANE), bf16),
            pltpu.VMEM((CLS, 2 * INN, 2 * INN), bf16),
            pltpu.VMEM((rows, N), bf16),
            pltpu.VMEM((rows, N), f32),
            pltpu.VMEM((2, rows, N), bf16),
            pltpu.VMEM((2, CLS, rows + 16, 2 * INN), f32),
            pltpu.VMEM((rows + 16, N), f32),
            pltpu.VMEM((8, N), f32),
            pltpu.VMEM((16, N), f32),
            pltpu.SemaphoreType.DMA((3, CLS)),
        ],
        compiler_params=pltpu.CompilerParams(vmem_limit_bytes=VMEM),
        cost_estimate=pl.CostEstimate(flops=3 * 10**9, bytes_accessed=16 * MIB, transcendentals=0),
        name="last_rows",
    )(parts, nyquist, table, best, spatial, others, edge0, edge12)


def assemble_kernel(own, *refs):
    slot, out = pl.program_id(0), refs[-1]
    half = refs[0].shape[0]
    for s in range(4):

        @pl.when(slot == s)
        def _():
            out[:half] = refs[s][...].astype(jnp.float32)
            out[half:] = refs[4 + s][...].astype(jnp.float32)


def assemble(depth_index, upper, lower):
    half = upper[0].shape[0]
    whole = pl.BlockSpec((half, N), lambda s, o: (0, 0))
    return pl.pallas_call(
        assemble_kernel,
        grid_spec=pltpu.PrefetchScalarGridSpec(
            num_scalar_prefetch=1,
            grid=(4,),
            in_specs=[whole] * 8,
            out_specs=pl.BlockSpec((2 * half, N), lambda s, o: (jnp.bitwise_xor(s, o[0]), 0)),
        ),
        out_shape=jax.ShapeDtypeStruct((8 * half, N), jnp.float32),
        compiler_params=pltpu.CompilerParams(vmem_limit_bytes=SHARED),
        cost_estimate=pl.CostEstimate(flops=10**6, bytes_accessed=12 * MIB, transcendentals=0),
        name="assemble",
    )(depth_index, *upper, *lower)


OVER_X = [(i, i ^ 1) for i in range(4)]
OVER_Y = [(i, i ^ 2) for i in range(4)]


def exchange_depth(a, b):
    ax, by = lax.ppermute(a, "depth", OVER_X), lax.ppermute(b, "depth", OVER_Y)
    ay, axy = lax.ppermute(a, "depth", OVER_Y), lax.ppermute(ax, "depth", OVER_Y)
    bx, byx = lax.ppermute(b, "depth", OVER_X), lax.ppermute(by, "depth", OVER_X)
    return (a, ax, ay, axy), (b, bx, by, byx)


def border_rows(halfway, outside, high):
    lanes = 4 * LANE
    count = halfway.shape[-1] // lanes
    natural = lambda rows: rows.reshape(4, 2, 2, count, lanes).transpose(1, 2, 0, 3, 4).reshape(16, count, lanes)
    first, last = natural(halfway[..., 0, :]), natural(halfway[..., -1, :])
    above = jnp.where(high == 0, first[:1], outside[None, :, 15])
    below = jnp.where(high == 0, outside[None, :, 0], last[-1:])
    above = jnp.concatenate([above, last[:-1]])
    below = jnp.concatenate([first[1:], below])
    both = jnp.stack([above, below], axis=2).reshape(2, 2, 4, 2 * count, lanes)
    return both.transpose(2, 0, 1, 3, 4).reshape(16, 2 * count, lanes)


def half_spectrum_shards(hologram, background):
    rows = hologram.shape[0]
    planes = lax.axis_size("depth") * PL_DEV
    depth, high = lax.axis_index("depth"), lax.axis_index("high")
    low, core = lax.axis_index("low"), lax.axis_index("core")
    as_scalar = lambda value: jnp.reshape(value, (1,)).astype(jnp.int32)
    own = rows // 4
    block = ((high * 2 + low) * 2 + core) * 4 + depth
    place = jnp.stack([block, jnp.int32(N // own)]).astype(jnp.int32)

    sections = row_forward(as_scalar(depth), hologram, background)
    data = lax.all_to_all(
        sections.reshape(8, rows + 16, 2 * LANE),
        ("high", "low", "core"),
        split_axis=0,
        concat_axis=0,
        tiled=True,
    )

    group = depth * 2 + core
    slot = low * LANE + jnp.arange(LANE, dtype=jnp.int32)
    special = jnp.where(low == 0, 0, CLS) + OUT * jnp.arange(LANE, dtype=jnp.int32)
    fx = signed_fraction(jnp.where(group == 0, special, group + OUT * slot))
    kernels = propagators(planes, (fx * fx)[None])

    def to_rows(halfway):
        parts = lax.all_to_all(
            halfway.reshape(16, -1, halfway.shape[-1]),
            ("depth", "low", "core"),
            split_axis=0,
            concat_axis=0,
            tiled=True,
        )
        return parts.reshape(4, 2, 2, -1, halfway.shape[-1])

    halfway, outside, spectrum = first_columns(as_scalar(high), data, kernels)
    parts, borders = [to_rows(halfway)], [border_rows(halfway, outside, high)]
    for plane, count in ((1, 2), (3, 1)):
        halfway, outside = next_columns(as_scalar(high), plane, count, spectrum, kernels)
        borders.append(border_rows(halfway, outside, high))
        halfway = halfway.reshape(16, own, -1)
        if plane == 3:
            below = jnp.concatenate(borders, axis=1)
            below = jnp.pad(below, ((0, 0), (0, 16 - 2 * planes), (0, 0)))
            halfway = jnp.concatenate([halfway, below], axis=1)
        ready = parts[-1]
        if plane == 3:
            first, first_edge = row_inverse(0, 1, parts[0], middle)
            ready = ready, first, first_edge
        elif plane == 1:
            middle = nyquist_column(place, planes, data)
            ready = ready, middle
        halfway, ready = lax.optimization_barrier((halfway, ready))
        if plane == 3:
            parts[-1], first, first_edge = ready
        else:
            parts[-1], middle = ready
        parts.append(to_rows(halfway))
    others, others_edge = row_inverse(1, 2, parts[1], middle)
    best, spatial = early_focus(first, others)
    upper, lower = last_rows(parts[2], middle, best, spatial, others, first_edge, others_edge)
    return assemble(as_scalar(depth), *exchange_depth(upper, lower))


def solution(mesh):
    spec = P("rows", None)
    if mesh.shape["depth"] == 4 and mesh.shape["rows"] == 8:
        split = Mesh(mesh.devices.reshape(4, 2, 2, 2), ("depth", "high", "low", "core"))
        spec = P(("high", "low", "core"), None)
        body = half_spectrum_shards
    else:
        split, body = mesh, shards
    return jax.shard_map(body, mesh=split, in_specs=(spec, spec), out_specs=spec, check_vma=False)
```

```python
import functools
import math

import jax
import jax.numpy as jnp
import numpy as np
from jax import lax
from jax.experimental import pallas as pl
from jax.experimental.pallas import tpu as pltpu
from jax.sharding import Mesh
from jax.sharding import PartitionSpec as P

N = 4096
RADIX = 64
PL_DEV = 1


wave_number = 0.6
depth_start = 8.0
depth_step = 2.0


def padded_2(block, sides, width):
    for axis, dim in sides:
        count = lax.axis_size(axis)
        forward = [(i, i + 1) for i in range(count - 1)]
        backward = [(target, source) for source, target in forward]
        low = lax.ppermute(
            lax.slice_in_dim(block, block.shape[dim] - width, None, axis=dim), axis, forward
        )
        high = lax.ppermute(lax.slice_in_dim(block, 0, width, axis=dim), axis, backward)
        block = jnp.concatenate([low, block, high], axis=dim)
    return block


def fourier_tables(radix_size, sign_value):
    indices = jnp.arange(radix_size, dtype=jnp.int32)
    products = indices[:, None] * indices[None, :] % radix_size
    angles = products.astype(jnp.float32) * (sign_value * 2.0 * math.pi / radix_size)
    scaling = 1.0 / math.sqrt(radix_size)
    cosine_part = jnp.cos(angles) * scaling
    sine_part = jnp.sin(angles) * scaling
    matrix = jnp.stack([jnp.stack([cosine_part, -sine_part]), jnp.stack([sine_part, cosine_part])])
    return matrix.astype(jnp.bfloat16)


def twiddle_table(radix_size, sign_value):
    indices = jnp.arange(radix_size, dtype=jnp.int32)
    total = radix_size * radix_size
    products = indices[:, None] * indices[None, :] % total
    angles = products.astype(jnp.float32) * (sign_value * 2.0 * math.pi / total)
    return (jnp.cos(angles), jnp.sin(angles))


def rotate(data, cosine_part, sine_part):
    return jnp.stack(
        [data[0] * cosine_part - data[1] * sine_part, data[0] * sine_part + data[1] * cosine_part]
    )


def contract(form, matrix, data):
    return jnp.einsum(form, matrix, data, preferred_element_type=jnp.float32)


def forward_real(data):
    batch_size = data.shape[1]
    shaped = data.reshape(RADIX, RADIX, batch_size)
    matrix = fourier_tables(RADIX, -1.0)
    cosine_part, sine_part = twiddle_table(RADIX, -1.0)
    opening = contract("oka,abm->okbm", matrix[:, 0], shaped)
    sectioned = rotate(opening, cosine_part[:, :, None], sine_part[:, :, None]).astype(jnp.bfloat16)
    closing = contract("ocjb,ckbm->okjm", matrix, sectioned)
    return closing.reshape(2, N, batch_size).astype(jnp.bfloat16)


def forward_first(data):
    batch_size = data.shape[2]
    shaped = data.reshape(2, RADIX, RADIX, batch_size)
    matrix = fourier_tables(RADIX, -1.0)
    cosine_part, sine_part = twiddle_table(RADIX, -1.0)
    opening = contract("ocka,cabm->okbm", matrix, shaped)
    sectioned = rotate(opening, cosine_part[:, :, None], sine_part[:, :, None]).astype(jnp.bfloat16)
    closing = contract("ocjb,ckbm->okjm", matrix, sectioned)
    return closing.reshape(2, N, batch_size).astype(jnp.bfloat16)


def inverse_first(data):
    batch_size = data.shape[2]
    shaped = data.reshape(2, RADIX, RADIX, batch_size)
    matrix = fourier_tables(RADIX, 1.0)
    cosine_part, sine_part = twiddle_table(RADIX, 1.0)
    opening = contract("ocbj,ckjm->okbm", matrix, shaped)
    sectioned = rotate(opening, cosine_part[:, :, None], sine_part[:, :, None]).astype(jnp.bfloat16)
    closing = contract("ocak,ckbm->oabm", matrix, sectioned)
    return closing.reshape(2, N, batch_size)


def frequencies(positions):
    natural = positions // RADIX + RADIX * (positions % RADIX)
    signed_freq = jnp.where(natural >= N // 2, natural - N, natural)
    return signed_freq.astype(jnp.float32) / N


def propagator(freq_whole, freq_own, distance):
    radial = freq_whole[:, None] ** 2 + freq_own[None, :] ** 2
    limit = wave_number * wave_number
    amplitude = jnp.exp(-2.0 * math.pi * distance * jnp.sqrt(jnp.maximum(radial - limit, 0.0)))
    phase_angle = (
        2.0 * math.pi * distance * (jnp.sqrt(jnp.maximum(limit - radial, 0.0)) - wave_number)
    )
    return (amplitude * jnp.cos(phase_angle), amplitude * jnp.sin(phase_angle))


def propagate(spectrum, cosine_part, sine_part):
    return rotate(spectrum.astype(jnp.float32), cosine_part, sine_part).astype(jnp.bfloat16)


def shards(hologram, background):
    row_count = hologram.shape[0]
    contrast = (hologram.astype(jnp.float32) / background.astype(jnp.float32) - 1.0).astype(
        jnp.bfloat16
    )
    along_rows = forward_real(contrast.T)
    columns = lax.all_to_all(
        jnp.swapaxes(along_rows, 1, 2), "rows", split_axis=2, concat_axis=1, tiled=True
    )
    spectrum = forward_first(columns)
    row_index = lax.axis_index("rows")
    own_positions = row_index * row_count + jnp.arange(row_count, dtype=jnp.int32)
    freq_own = frequencies(own_positions)
    freq_whole = frequencies(jnp.arange(N, dtype=jnp.int32))
    depth_index = lax.axis_index("depth")
    distance = depth_start + depth_step * (depth_index * PL_DEV + 0).astype(jnp.float32)
    cosine_part, sine_part = propagator(freq_whole, freq_own, distance)
    propagated = propagate(spectrum, cosine_part, sine_part)
    halfway = inverse_first(propagated).astype(jnp.bfloat16)
    restored = lax.all_to_all(
        jnp.swapaxes(halfway, 1, 2), "rows", split_axis=2, concat_axis=1, tiled=True
    )
    result_field = inverse_first(restored)
    intensities = [
        (result_field[0] * result_field[0] + result_field[1] * result_field[1]).astype(jnp.bfloat16)
    ]
    stacked = jnp.stack(intensities)
    padded = padded_2(stacked, (("depth", 0), ("rows", 2)), 1)
    centre_block = padded[1:-1, :, 1:-1]
    plane_ids = jnp.arange(PL_DEV, dtype=jnp.int32)[:, None, None]
    row_ids = jnp.arange(row_count, dtype=jnp.int32)[None, None, :]
    depth_count = lax.axis_size("depth")
    row_groups = lax.axis_size("rows")
    lower_plane = jnp.where(
        (depth_index == 0) & (plane_ids == 0), centre_block, padded[:-2, :, 1:-1]
    )
    upper_plane = jnp.where(
        (depth_index == depth_count - 1) & (plane_ids == PL_DEV - 1),
        centre_block,
        padded[2:, :, 1:-1],
    )
    north_row = jnp.where((row_index == 0) & (row_ids == 0), centre_block, padded[1:-1, :, :-2])
    south_row = jnp.where(
        (row_index == row_groups - 1) & (row_ids == row_count - 1),
        centre_block,
        padded[1:-1, :, 2:],
    )
    centre = centre_block.astype(jnp.float32)
    east_col = jnp.concatenate([centre[:, 1:], centre[:, -1:]], axis=1)
    west_col = jnp.concatenate([centre[:, :1], centre[:, :-1]], axis=1)
    depth_diff = upper_plane.astype(jnp.float32) - lower_plane.astype(jnp.float32)
    row_diff = south_row.astype(jnp.float32) - north_row.astype(jnp.float32)
    col_diff = east_col - west_col
    scores = (depth_diff * depth_diff + row_diff * row_diff + col_diff * col_diff) / 8.0
    sharpest = jnp.max(scores, axis=0)
    merged = lax.pmax(sharpest.astype(jnp.bfloat16), "depth").astype(sharpest.dtype)
    return merged.T


OUT = 16
INN = 256
CLS = 8
LANE = 128
MIB = 2**20
VMEM = 63 * MIB
SHARED = 36 * MIB


def slot_frequencies():
    table = np.arange(CLS)[:, None] + OUT * np.arange(INN)[None, :]
    half = np.arange(INN // 2)
    table[0] = np.concatenate([OUT * half, CLS + OUT * half])
    return table


def angles(products):
    return 2.0 * np.pi * (products % N) / N


def row_forward_tables():
    freq = slot_frequencies()
    theta = angles(np.arange(INN)[None, :, None] * freq[:, None, :])
    cos, sin = np.cos(theta) / 64.0, np.sin(theta) / 64.0
    top = np.stack([cos, -sin], axis=2)
    low = np.stack([sin, cos], axis=2)
    first = np.arange(INN) < INN // 2
    low[0] = np.where(first, 0.0, top[0])
    top[0] = np.where(first, top[0], 0.0)
    full = np.concatenate([top, low], axis=1)
    full = full.reshape(CLS, 2 * INN, 2, 2, LANE).transpose(0, 1, 3, 2, 4)
    return full.reshape(CLS, 2 * INN, 2 * INN).astype(jnp.bfloat16)


def row_forward_weights():
    a = np.arange(1, 5)
    rows = []
    for d in range(CLS // 2):
        even, odd = (2.0 * np.pi * c * a / OUT for c in (2 * d, 2 * d + 1))
        parts = np.cos(even), -np.sin(even[:3]), [float(d == 0)], np.cos(odd[:3]), -np.sin(odd), [0.0]
        rows.append(np.concatenate(parts))
    return np.concatenate(rows).astype(np.float32)


def row_inverse_tables():
    half = np.arange(INN // 2)
    position = np.arange(INN)[None, :]
    full = np.zeros((2, 2, INN, 2, INN))
    for first, place in ((0, 0), (CLS, 1)):
        theta = angles((first + OUT * half)[:, None] * position)
        rows = slice(place * INN // 2, (place + 1) * INN // 2)
        full[0, 0, rows, place], full[0, 1, rows, place] = np.cos(theta), -np.sin(theta)
    full[0, 0, 0, 0] = 0.5
    full[0, 1, 0, 0] = 0.5 * (-1.0) ** np.arange(INN)
    theta = angles(OUT * np.arange(INN)[:, None] * position)
    full[1, 0, :, 0], full[1, 0, :, 1] = np.cos(theta), np.sin(theta)
    full[1, 1, :, 0], full[1, 1, :, 1] = -np.sin(theta), np.cos(theta)
    full = full.reshape(2, 2, 2, LANE, 2 * INN).transpose(0, 2, 1, 3, 4) / 32.0
    turn = angles(np.arange(CLS)[:, None] * position)
    turn = np.concatenate([np.cos(turn), np.sin(turn)]).astype(np.float32)
    return full.reshape(2, 2 * INN, 2 * INN).astype(jnp.bfloat16), turn


def column_tables():
    turn = 2.0 * np.pi * np.arange(OUT)[:, None] * np.arange(OUT)[None, :] / OUT
    eye = np.eye(16)
    outer_cos, outer_sin = np.kron(np.cos(turn), eye) / 4.0, np.kron(np.sin(turn), eye) / 4.0
    complex_form = lambda cos, sin: np.concatenate(
        [np.concatenate([cos, -sin], axis=-1), np.concatenate([sin, cos], axis=-1)], axis=-2
    )
    slabs = lambda table: table.reshape(-1, 8, 2, 16).swapaxes(1, 2).reshape(table.shape)
    outer = complex_form(slabs(outer_cos), slabs(-outer_sin))
    half_rows = outer_cos.shape[0] // 2
    cut = lambda table, begin, size: table[begin : begin + size]
    back = np.stack(
        [
            complex_form(cut(outer_cos, begin, half_rows), cut(outer_sin, begin, half_rows))
            for begin in (0, half_rows)
        ]
    )
    beyond = np.stack(
        [complex_form(cut(outer_cos, a * 16, 16), cut(outer_sin, a * 16, 16)) for a in (8, 7)]
    )
    theta = angles(OUT * np.arange(INN)[:, None] * np.arange(INN)[None, :])
    inner = complex_form(np.cos(theta), -np.sin(theta)) / 16.0
    inner_back = complex_form(np.cos(theta), np.sin(theta)) / 16.0
    turn = angles(np.arange(OUT)[:, None] * np.arange(INN)[None, :])
    by_chunk = turn.reshape(OUT, 16, 16).swapaxes(1, 2).reshape(INN, 16)
    twist = np.zeros((2, INN, LANE), np.float32)
    for i, table in enumerate((by_chunk, turn.T)):
        twist[i, :, :16], twist[i, :, 16:32] = np.cos(table), np.sin(table)
    cast = lambda table: table.astype(jnp.bfloat16)
    return cast(outer), cast(inner), cast(inner_back), cast(back), cast(beyond), twist


def dot(left, right):
    return jnp.dot(left, right, preferred_element_type=jnp.float32)


def split_complex(both, width):
    rows = both.shape[0] // 2
    top, low = both[:rows], both[rows:]
    return top[:, :width] - low[:, width:], top[:, width:] + low[:, :width]


def quarter_kernel(radial):
    gap = wave_number * wave_number - radial
    root = jnp.sqrt(jnp.abs(gap))
    inside = gap > 0.0
    half_pi = 0.5 * math.pi
    angle = half_pi * (jnp.where(inside, root, 0.0) - wave_number)
    decay = jnp.exp(jnp.where(inside, 0.0, -half_pi * root))
    square = angle * angle
    sine = 1.0 / 362880.0
    for c in (-1.0 / 5040.0, 1.0 / 120.0, -1.0 / 6.0, 1.0):
        sine = sine * square + c
    cosine = -1.0 / 3628800.0
    for c in (1.0 / 40320.0, -1.0 / 720.0, 1.0 / 24.0, -0.5, 1.0):
        cosine = cosine * square + c
    return decay * cosine, decay * (sine * angle)


def squared(re, im):
    return (re - im) * (re + im), 2.0 * re * im


def start_and_step(radial):
    value = quarter_kernel(radial)
    distance = 0.25
    step = None
    while distance < depth_start:
        value = squared(*value)
        distance *= 2.0
        if distance == depth_step:
            step = value
    return value, step


def signed_fraction(natural):
    return jnp.where(natural >= N // 2, natural - N, natural).astype(jnp.float32) * (1.0 / N)


CHUNK = 64


def sixteen_sums(term, w):
    c0, c8 = term(0), term(8)
    plus, minus = c0 + c8, c0 - c8
    c4, c12 = term(4), term(12)
    e4, o4 = c4 + c12, c4 - c12
    total = plus + e4
    eighth = total
    re_even = plus + w(3) * e4
    im_even = None
    re_odd, im_odd = minus, w(14) * o4
    for a in (1, 2, 3):
        p, q, r, s = term(a), term(16 - a), term(8 - a), term(8 + a)
        e, o, f, h = p + q, p - q, r + s, r - s
        both = e + f
        total = total + both
        eighth = eighth - both if a % 2 else eighth + both
        re_even = re_even + w(a - 1) * both
        term_im = w(3 + a) * (o - h)
        im_even = term_im if im_even is None else im_even + term_im
        re_odd = re_odd + w(7 + a) * (e - f)
        im_odd = im_odd + w(10 + a) * (o + h)
    return re_even, im_even + w(7) * eighth, re_odd, im_odd, total


def row_forward_kernel(
    own, weights, holo, back, table, out, holo_buf, back_buf, table_buf, acc, result, held, sems
):
    rows = holo.shape[0]
    group = own[0]
    chunks = rows // CHUNK
    loads = []
    for i in range(chunks):
        here = pl.ds(i * CHUNK, CHUNK)
        loads.append(
            (
                pltpu.make_async_copy(holo.at[here], holo_buf.at[here], sems.at[0, i]),
                pltpu.make_async_copy(back.at[here], back_buf.at[here], sems.at[1, i]),
            )
        )
        for load in loads[-1]:
            load.start()
        if i == 0:
            tables = pltpu.make_async_copy(table.at[pl.ds(2 * group, 2)], table_buf, sems.at[4, 0])
            tables.start()
    lane = lax.broadcasted_iota(jnp.int32, (16, INN), 1)
    sign = jnp.where(lane % 2 == 0, 1.0, -1.0).astype(jnp.bfloat16)
    stores = []
    for chunk in range(chunks):
        for load in loads[chunk]:
            load.wait()

        def strip(i, carry):
            here = pl.ds(pl.multiple_of(chunk * CHUNK + i * 16, 16), 16)

            def term(a):
                there = pl.ds(a * INN, INN)
                below = back_buf[here, there].astype(jnp.float32)
                inverse = pl.reciprocal(below, approx=True)
                inverse = inverse * (2.0 - below * inverse)
                inverse = inverse * (2.0 - below * inverse)
                value = holo_buf[here, there].astype(jnp.float32) * inverse
                return (value - 1.0).astype(jnp.bfloat16).astype(jnp.float32)

            sums = sixteen_sums(term, lambda n: weights[group * 16 + n])
            for q in range(4):
                acc[q // 2, here, pl.ds((q % 2) * INN, INN)] = sums[q].astype(jnp.bfloat16)
            acc[2, here, pl.ds(0, INN)] = sums[4].astype(jnp.bfloat16)
            return carry

        lax.fori_loop(0, CHUNK // 16, strip, 0)
        batch = rows // 2 // CHUNK
        if chunk % batch != batch - 1:
            continue
        if chunk < batch:
            tables.wait()
        begin, end = (chunk + 1 - batch) * CHUNK, (chunk + 1) * CHUNK
        for q in range(2):
            both = dot(acc[q, begin:end], table_buf[q]).astype(jnp.bfloat16)
            for low in range(2):
                part = both[:, low * 2 * LANE : (low + 1) * 2 * LANE]
                result[low, q, begin:end, :] = part
        held[chunk // batch] = lax.dot_general(
            sign,
            acc[2, begin:end, :INN],
            (((1,), (1,)), ((), ())),
            preferred_element_type=jnp.float32,
        )
        here = pl.ds(begin, end - begin)
        if chunk == chunks - 1:
            index = lax.broadcasted_iota(jnp.int32, (16, INN), 0)
            extra = jnp.where(index == 0, held[0], held[1]) * (1.0 / 64.0)
            for low in range(2):
                for q in range(2):
                    result[low, q, rows:, :] = extra.astype(jnp.bfloat16)
            here = pl.ds(begin, end - begin + 16)
        for high in range(2):
            source, target = result.at[:, :, here, :], out.at[high, :, :, here, :]
            stores.append(pltpu.make_async_copy(source, target, sems.at[2 + high, chunk]))
            stores[-1].start()
    for store in stores:
        store.wait()


def row_forward(own, hologram, background):
    rows = hologram.shape[0]
    table = jnp.asarray(row_forward_tables())
    weights = jnp.asarray(row_forward_weights())
    hbm = pl.BlockSpec(memory_space=pl.ANY)
    chunks = rows // CHUNK
    return pl.pallas_call(
        row_forward_kernel,
        grid_spec=pltpu.PrefetchScalarGridSpec(
            num_scalar_prefetch=2,
            grid=(1,),
            in_specs=[hbm] * 3,
            out_specs=hbm,
            scratch_shapes=[
                pltpu.VMEM((rows, N), jnp.bfloat16),
                pltpu.VMEM((rows, N), jnp.bfloat16),
                pltpu.VMEM((2, 2 * INN, 2 * INN), jnp.bfloat16),
                pltpu.VMEM((3, rows, 2 * INN), jnp.bfloat16),
                pltpu.VMEM((2, 2, rows + 16, 2 * LANE), jnp.bfloat16),
                pltpu.VMEM((2, 16, INN), jnp.float32),
                pltpu.SemaphoreType.DMA((5, chunks)),
            ],
        ),
        out_shape=jax.ShapeDtypeStruct((2, 2, 2, rows + 16, 2 * LANE), jnp.bfloat16),
        compiler_params=pltpu.CompilerParams(vmem_limit_bytes=VMEM),
        cost_estimate=pl.CostEstimate(flops=10**10, bytes_accessed=12 * MIB, transcendentals=0),
        name="row_forward",
    )(own, weights, hologram, background, table)


def propagator_kernel(planes, fx2, out):
    step = pl.program_id(0)
    strip = 32
    for i in range(INN // strip):
        rows = slice(i * strip, (i + 1) * strip)
        position = lax.broadcasted_iota(jnp.int32, (strip, LANE), 0) + i * strip
        fy = signed_fraction(step + OUT * position)
        (kr, ki), (sr, si) = start_and_step(fy * fy + fx2[...])
        for g in range(planes):
            out[g, 0, rows, :LANE] = kr.astype(jnp.bfloat16)
            out[g, 0, rows, LANE:] = ki.astype(jnp.bfloat16)
            if g + 1 < planes:
                kr, ki = kr * sr - ki * si, kr * si + ki * sr


def propagators(planes, fx2):
    return pl.pallas_call(
        functools.partial(propagator_kernel, planes),
        grid=(OUT,),
        in_specs=[pl.BlockSpec((1, LANE), lambda i: (0, 0))],
        out_specs=pl.BlockSpec((planes, 1, INN, 2 * LANE), lambda i: (0, i, 0, 0)),
        out_shape=jax.ShapeDtypeStruct((planes, OUT, INN, 2 * LANE), jnp.bfloat16),
        compiler_params=pltpu.CompilerParams(vmem_limit_bytes=VMEM),
        cost_estimate=pl.CostEstimate(flops=10**9, bytes_accessed=16 * MIB, transcendentals=10**6),
        name="propagators",
    )(fx2)


PAIRS = OUT // 2


def mix_and_open(pair, both, kernels, inner_back, twist, mixed, second):
    wide = 2 * LANE
    for k in range(2):
        yr, yi = (both[p * INN : (p + 1) * INN, k * LANE : (k + 1) * LANE] for p in range(2))
        for part in range(2):
            factor = kernels[k, :, part * LANE : (part + 1) * LANE].astype(jnp.float32)
            lanes = slice(k * wide + part * LANE, k * wide + (part + 1) * LANE)
            mixed[:INN, lanes] = (yr * factor).astype(jnp.bfloat16)
            mixed[INN:, lanes] = (yi * factor).astype(jnp.bfloat16)
    opened = dot(inner_back[...], mixed[...])
    for k in range(2):
        at = pair * 2 + k
        re, im = (opened[p * INN : (p + 1) * INN, k * wide : (k + 1) * wide] for p in range(2))
        cos, sin = twist[1, :, at : at + 1], twist[1, :, 16 + at : 17 + at]
        second[0, at] = (re * cos - im * sin).astype(jnp.bfloat16)
        second[1, at] = (re * sin + im * cos).astype(jnp.bfloat16)


def outer_block(second, here):
    return second[:, :, here, :].reshape(2 * OUT * 16, 2 * LANE)


def spread(both):
    rows = both.shape[0] // 2
    re, im = both[:rows], both[rows:]
    return [re[:, :LANE], im[:, :LANE], re[:, LANE:], im[:, LANE:]]


def open_outside(half, beyond, second, outside):
    here = pl.ds(pl.multiple_of(half[0] * (INN - 16), 16), 16)
    both = dot(beyond, outer_block(second, here)).astype(jnp.bfloat16)
    for i, value in enumerate(spread(both)):
        outside[:, i * LANE : (i + 1) * LANE] = value


def close_chunk(here, back, second, store):
    both = dot(back, outer_block(second, here)).astype(jnp.bfloat16)
    for i, value in enumerate(spread(both)):
        value = value.reshape(2, 2, 2, 16, LANE)
        for low in range(2):
            for core in range(2):
                for high in range(2):
                    store(high, low, core, slice(i * LANE, (i + 1) * LANE), value[low, core, high])


def first_columns_kernel(
    half, data, kernels, outer_in, inner_in, inner_back_in, back_in, beyond_in, twist_in,
    out, spectrum, outside,
    data_buf, kernel_buf, outer, inner, inner_back, back, beyond, twist,
    out_buf, spectrum_buf, first, mixed, second, sems,
):
    rows = data_buf.shape[1]
    early = [
        pltpu.make_async_copy(source, target, sems.at[3, i])
        for i, (source, target) in enumerate(
            (
                (data.at[:, pl.ds(0, rows), :], data_buf),
                (outer_in, outer),
                (twist_in, twist),
                (inner_in, inner),
                (inner_back_in, inner_back),
                (back_in.at[half[0]], back),
                (beyond_in.at[half[0]], beyond),
            )
        )
    ]
    for load in early:
        load.start()
    loads = []
    for pair in range(PAIRS):
        here = pl.ds(2 * pair, 2)
        loads.append(
            pltpu.make_async_copy(kernels.at[0, here], kernel_buf.at[here], sems.at[1, pair])
        )
        loads[-1].start()
    for load in early[:3]:
        load.wait()
    for i in range(0, INN // 16, 2):
        pieces = []
        for part in range(2):
            lanes = slice(part * LANE, (part + 1) * LANE)
            for parity in range(2):
                at = parity * INN + i * 16
                block = data_buf[:, at : at + 32, lanes]
                block = jnp.concatenate([block[:, :16], block[:, 16:]], axis=2)
                pieces.append(block.reshape(OUT // 2 * 16, 2 * LANE))
        both = dot(outer[...], jnp.concatenate(pieces, axis=0))
        for c in range(2):
            re, im = (both[p * INN : (p + 1) * INN, c * LANE : (c + 1) * LANE] for p in range(2))
            cos, sin = (twist[0, :, t + i + c : t + i + c + 1] for t in (0, 16))
            here = slice((i + c) * 16, (i + c + 1) * 16)
            for part, value in enumerate((re * cos + im * sin, im * cos - re * sin)):
                value = value.astype(jnp.bfloat16).reshape(PAIRS, 2, 16, LANE)
                first[:, part, here, :LANE] = value[:, 0]
                first[:, part, here, LANE:] = value[:, 1]
    stores = []

    def transform(pair):
        both = dot(inner[...], first[pair].reshape(2 * INN, 2 * LANE))
        spectrum_buf[pair] = both.astype(jnp.bfloat16)
        stores.append(pltpu.make_async_copy(spectrum_buf.at[pair], spectrum.at[pair], sems.at[2, pair]))
        stores[-1].start()
        return both

    early[3].wait()
    both = transform(0)
    early[4].wait()
    for pair in range(PAIRS):
        following = transform(pair + 1) if pair + 1 < PAIRS else None
        loads[pair].wait()
        now = kernel_buf.at[pl.ds(2 * pair, 2)]
        mix_and_open(pair, both, now, inner_back, twist, mixed.at[pair % 2], second)
        both = following
    for load in early[5:]:
        load.wait()
    open_outside(half, beyond[...], second, outside.at[0])
    for chunk in range(INN // 16):
        side, rows = chunk // 8, slice(chunk % 8 * 16, chunk % 8 * 16 + 16)

        def store(high, low, core, lanes, value):
            out_buf[side, high, low, core, rows, lanes] = value

        close_chunk(slice(chunk * 16, chunk * 16 + 16), back[...], second, store)
        if chunk % 4 == 3:
            here = pl.ds((chunk % 8 - 3) * 16, 64)
            source = out_buf.at[side, :, :, :, here, :]
            target = out.at[:, side, :, :, here, :]
            stores.append(pltpu.make_async_copy(source, target, sems.at[0, chunk // 4]))
            stores[-1].start()
    for copy in stores:
        copy.wait()


def next_columns_kernel(
    half, spectrum, kernels, inner_back, back, beyond, twist, out, outside, mixed, second
):
    step = pl.program_id(1)
    for s in range(2):

        @pl.when(step == s)
        def _():
            for i in range(PAIRS // 2):
                pair = s * (PAIRS // 2) + i
                both = spectrum[i].astype(jnp.float32)
                now = kernels.at[0, pl.ds(2 * i, 2)]
                mix_and_open(pair, both, now, inner_back, twist, mixed.at[i % 2], second)
            if s == 1:
                open_outside(half, beyond[0], second, outside.at[0])

    @pl.when(step >= 2)
    def _():
        for c in range(8):
            rows = slice(c * 16, (c + 1) * 16)

            def store(high, low, core, lanes, value):
                out[high, 0, low, core, rows, lanes] = value

            start = pl.multiple_of(((step - 2) * 8 + c) * 16, 16)
            close_chunk(pl.ds(start, 16), back[0], second, store)


def first_columns(half, data, kernels):
    tables = [jnp.asarray(t) for t in column_tables()]
    rows = data.shape[1] - 16
    bf16, f32 = jnp.bfloat16, jnp.float32
    hbm = pl.BlockSpec(memory_space=pl.ANY)
    return pl.pallas_call(
        first_columns_kernel,
        grid_spec=pltpu.PrefetchScalarGridSpec(
            num_scalar_prefetch=1,
            grid=(1,),
            in_specs=[hbm] * 8,
            out_specs=[hbm, hbm, pl.BlockSpec((1, 16, 4 * LANE), lambda i, o: (0, 0, 0))],
            scratch_shapes=[
                pltpu.VMEM((8, rows, 2 * LANE), bf16),
                pltpu.VMEM((OUT, INN, 2 * LANE), bf16),
                pltpu.VMEM((2 * INN, 2 * INN), bf16),
                pltpu.VMEM((2 * INN, 2 * INN), bf16),
                pltpu.VMEM((2 * INN, 2 * INN), bf16),
                pltpu.VMEM((INN, 2 * INN), bf16),
                pltpu.VMEM((32, 2 * INN), bf16),
                pltpu.VMEM((2, INN, LANE), f32),
                pltpu.VMEM((2, 2, 2, 2, LANE, 4 * LANE), bf16),
                pltpu.VMEM((PAIRS, 2 * INN, 2 * LANE), bf16),
                pltpu.VMEM((PAIRS, 2, INN, 2 * LANE), bf16),
                pltpu.VMEM((2, 2 * INN, 4 * LANE), bf16),
                pltpu.VMEM((2, OUT, INN, 2 * LANE), bf16),
                pltpu.SemaphoreType.DMA((4, PAIRS)),
            ],
        ),
        out_shape=[
            jax.ShapeDtypeStruct((2, 2, 2, 2, LANE, 4 * LANE), bf16),
            jax.ShapeDtypeStruct((PAIRS, 2 * INN, 2 * LANE), bf16),
            jax.ShapeDtypeStruct((1, 16, 4 * LANE), bf16),
        ],
        compiler_params=pltpu.CompilerParams(vmem_limit_bytes=VMEM),
        cost_estimate=pl.CostEstimate(flops=10**10, bytes_accessed=16 * MIB, transcendentals=0),
        name="first_columns",
    )(half, data, kernels, *tables)


def next_columns(half, plane, count, spectrum, kernels):
    tables = [jnp.asarray(t) for t in column_tables()[2:]]
    opening = lambda i: jnp.minimum(i, 1)
    closing = lambda i: jnp.maximum(i - 2, 0)
    own = lambda g, i, o: (o[0], 0, 0)
    return pl.pallas_call(
        next_columns_kernel,
        grid_spec=pltpu.PrefetchScalarGridSpec(
            num_scalar_prefetch=1,
            grid=(count, 4),
            in_specs=[
                pl.BlockSpec((PAIRS // 2, 2 * INN, 2 * LANE), lambda g, i, o: (opening(i), 0, 0)),
                pl.BlockSpec(
                    (1, OUT // 2, INN, 2 * LANE), lambda g, i, o: (plane + g, opening(i), 0, 0)
                ),
                pl.BlockSpec((2 * INN, 2 * INN), lambda g, i, o: (0, 0)),
                pl.BlockSpec((1, INN, 2 * INN), own),
                pl.BlockSpec((1, 32, 2 * INN), own),
                pl.BlockSpec((2, INN, LANE), lambda g, i, o: (0, 0, 0)),
            ],
            out_specs=[
                pl.BlockSpec(
                    (2, 1, 2, 2, LANE, 4 * LANE), lambda g, i, o: (0, closing(i), 0, 0, 0, g)
                ),
                pl.BlockSpec((1, 16, 4 * LANE), lambda g, i, o: (g, 0, 0)),
            ],
            scratch_shapes=[
                pltpu.VMEM((2, 2 * INN, 4 * LANE), jnp.bfloat16),
                pltpu.VMEM((2, OUT, INN, 2 * LANE), jnp.bfloat16),
            ],
        ),
        out_shape=[
            jax.ShapeDtypeStruct((2, 2, 2, 2, LANE, count * 4 * LANE), jnp.bfloat16),
            jax.ShapeDtypeStruct((count, 16, 4 * LANE), jnp.bfloat16),
        ],
        compiler_params=pltpu.CompilerParams(vmem_limit_bytes=VMEM),
        cost_estimate=pl.CostEstimate(
            flops=count * 7 * 10**9, bytes_accessed=count * 16 * MIB, transcendentals=0
        ),
        name="next_columns",
    )(half, spectrum, kernels, *tables)


def sixteen_points(re, im):
    c = math.sqrt(0.5)
    c1, c3 = math.cos(math.pi / 8), math.cos(3 * math.pi / 8)
    r0, r1, r2, r3, r4, r5, r6, r7 = re
    r8, i1, i2, i3, i4, i5, i6, i7 = im
    sum08, dif08, sum26, dif26 = r0 + r8, r0 - r8, r2 + r6, c * (r2 - r6)
    base = sum08 + r4
    even = [base + sum26, dif08 + dif26, sum08 - r4, dif08 - dif26, base - sum26]
    sum17, dif17, sum35, dif35 = r1 + r7, r1 - r7, r3 + r5, r3 - r5
    odd = [sum17 + sum35, c1 * dif17 + c3 * dif35, c * (sum17 - sum35), c3 * dif17 - c1 * dif35]
    cosines = [even[a] + odd[a] for a in range(4)] + [even[4]]
    cosines += [even[8 - a] - odd[8 - a] for a in range(5, 9)]
    s17, d17, s35, d35 = i1 + i7, i1 - i7, i3 + i5, i3 - i5
    sines_odd = [None, c3 * s17 + c1 * s35, c * (d17 + d35), c1 * s17 - c3 * s35, d17 - d35]
    s26 = c * (i2 + i6)
    sines_even = [None, s26 + i4, i2 - i6, s26 - i4]
    sines = [None] + [sines_odd[a] + sines_even[a] for a in (1, 2, 3)] + [sines_odd[4]]
    sines += [sines_odd[8 - a] - sines_even[8 - a] for a in (5, 6, 7)]
    result = [cosines[0]] + [cosines[a] - sines[a] for a in range(1, 8)] + [cosines[8]]
    return result + [cosines[16 - a] + sines[16 - a] for a in range(9, 16)]


def open_rows(group, block, table, turn):
    both = dot(block, table[min(group, 1)])
    if group == 0:
        return both
    re, im = both[:, :INN], both[:, INN:]
    cos, sin = turn[group : group + 1, :], turn[CLS + group : CLS + group + 1, :]
    return jnp.concatenate([re * cos - im * sin, re * sin + im * cos], axis=1)


def open_class(group, low, high, columns, table, turn, opened):
    blocks = []
    for part in range(2):
        lanes = slice(part * 2 * LANE, (part + 1) * 2 * LANE)
        first, rest = low[:, lanes], high[:, lanes]
        if group == 0:
            lane = lax.broadcasted_iota(jnp.int32, (first.shape[0], LANE), 1)
            im = jnp.where(lane == 0, columns[part], first[:, LANE:])
            first = jnp.concatenate([first[:, :LANE], im], axis=1)
        blocks.append(jnp.concatenate([first, rest], axis=1))
    rows = blocks[0].shape[0]
    both = open_rows(group, jnp.concatenate(blocks, axis=0), table, turn)
    for part in range(2):
        opened[part, group] = both[part * rows : (part + 1) * rows]


def strip_intensity(opened, here, tile):
    total = None
    for part in range(2):
        re = [opened[part, g, here, tile * LANE : (tile + 1) * LANE] for g in range(CLS)]
        im = [opened[part, g, here, INN + tile * LANE : INN + (tile + 1) * LANE] for g in range(CLS)]
        values = sixteen_points(re, im)
        if total is None:
            total = [v * v for v in values]
        else:
            total = [t + v * v for t, v in zip(total, values)]
    return total


def row_inverse_kernel(plane, parts, nyquist, table, turn, out, edges, opened):
    current = plane + pl.program_id(0)
    rows = parts.shape[3]
    lane = lax.broadcasted_iota(jnp.int32, (rows, LANE), 1)
    columns = []
    for part in range(2):
        mine = jnp.where(lane == current * 2 + part, nyquist[...], 0.0)
        columns.append(jnp.sum(mine, axis=1, keepdims=True).astype(jnp.bfloat16))
    for group in range(CLS):
        low, high = (parts[group // 2, i, group % 2] for i in range(2))
        open_class(group, low, high, columns, table, turn, opened)

    def strip(i, carry):
        here = pl.ds(pl.multiple_of(i * 16, 16), 16)
        for tile in range(INN // LANE):
            total = strip_intensity(opened, here, tile)
            for a in range(OUT):
                lanes = slice(a * INN + tile * LANE, a * INN + (tile + 1) * LANE)
                out[0, here, lanes] = total[a].astype(jnp.bfloat16)
        return carry

    lax.fori_loop(0, rows // 16, strip, 0)
    edges[0, 0:8, :] = out[0, 0:16, :].astype(jnp.float32)[0:8]
    edges[0, 8:16, :] = out[0, rows - 16 :, :].astype(jnp.float32)[8:16]


def row_inverse(plane, count, parts, nyquist):
    rows = parts.shape[3]
    table, turn = (jnp.asarray(t) for t in row_inverse_tables())
    return pl.pallas_call(
        functools.partial(row_inverse_kernel, plane),
        grid=(count,),
        in_specs=[
            pl.BlockSpec((4, 2, 2, rows, 4 * LANE), lambda g: (0, 0, 0, 0, g)),
            pl.BlockSpec((rows, LANE), lambda g: (0, 0)),
            pl.BlockSpec((2, 2 * INN, 2 * INN), lambda g: (0, 0, 0)),
            pl.BlockSpec((2 * CLS, INN), lambda g: (0, 0)),
        ],
        out_specs=[
            pl.BlockSpec((1, rows, N), lambda g: (g, 0, 0)),
            pl.BlockSpec((1, 16, N), lambda g: (g, 0, 0)),
        ],
        out_shape=[
            jax.ShapeDtypeStruct((count, rows, N), jnp.bfloat16),
            jax.ShapeDtypeStruct((count, 16, N), jnp.float32),
        ],
        scratch_shapes=[pltpu.VMEM((2, CLS, rows, 2 * INN), jnp.float32)],
        compiler_params=pltpu.CompilerParams(vmem_limit_bytes=VMEM),
        cost_estimate=pl.CostEstimate(
            flops=count * 3 * 10**9, bytes_accessed=count * 8 * MIB, transcendentals=0
        ),
        name="row_inverse",
    )(parts, nyquist, table, turn)


def nyquist_kernel(planes, own, data, out):
    wide = lambda axis: lax.broadcasted_iota(jnp.int32, (INN, INN), axis)
    tall = lambda axis: lax.broadcasted_iota(jnp.int32, (OUT, INN), axis)
    small = lambda axis: lax.broadcasted_iota(jnp.int32, (OUT, OUT), axis)

    def wave(products, period):
        turn = (products % period).astype(jnp.float32) * (2.0 * math.pi / period)
        return jnp.cos(turn), jnp.sin(turn)

    def exact(left, right):
        return jnp.dot(left, right, preferred_element_type=jnp.float32, precision=lax.Precision.HIGHEST)

    def product(xr, xi, yr, yi):
        return exact(xr, yr) - exact(xi, yi), exact(xr, yi) + exact(xi, yr)

    def rotated(xr, xi, yr, yi):
        return xr * yr - xi * yi, xr * yi + xi * yr

    column = jnp.concatenate([data[i, 0:2, :].astype(jnp.float32) for i in range(8)], axis=0)
    wr, wi = wave(small(0) * small(1), OUT)
    inner_r, inner_i = wave(wide(0) * wide(1), INN)
    vr, vi = wave(tall(0) * tall(1), N)
    ar, ai = rotated(exact(wr, column), exact(-wi, column), vr, -vi)
    yr, yi = product(ar, ai, inner_r, -inner_i)
    fy = signed_fraction(tall(0) + OUT * tall(1))
    (kr, ki), (sr, si) = start_and_step(fy * fy + 0.25)
    block, blocks = own[0], own[1]
    k = lax.broadcasted_iota(jnp.int32, (8, OUT), 1)
    section = block // 2 + lax.broadcasted_iota(jnp.int32, (8, OUT), 0) + (OUT - 1)
    hr, hi = wave(k * (section % OUT), OUT)
    even = block % 2 == 0
    lane = lax.broadcasted_iota(jnp.int32, (1, LANE), 1)
    result, beside = [], []
    for g in range(planes):
        pr, pi = rotated(yr, yi, kr, ki)
        br, bi = rotated(*product(pr, pi, inner_r, inner_i), vr, vi)
        for value in product(hr, hi, br, bi):
            value = value * (1.0 / N)
            result.append(jnp.where(even, value[1:2, :LANE], value[1:2, LANE:]))
            above = jnp.where(even, value[0:1, INN - 1 :], value[1:2, LANE - 1 : LANE])
            above = jnp.where(block == 0, value[1:2, 0:1], above)
            below = jnp.where(even, value[1:2, LANE : LANE + 1], value[2:3, 0:1])
            below = jnp.where(block == blocks - 1, value[1:2, INN - 1 :], below)
            beside.append(jnp.where(lane == 0, above, jnp.where(lane == 1, below, 0.0)))
        kr, ki = rotated(kr, ki, sr, si)
    rest = [jnp.zeros((LANE - 2 * planes, LANE), jnp.float32)]
    out[:LANE, :] = jnp.concatenate(result + rest, axis=0).T
    out[LANE:, :] = jnp.concatenate(beside + rest, axis=0).T


def nyquist_column(own, planes, data):
    rows = data.shape[1] - 16
    return pl.pallas_call(
        functools.partial(nyquist_kernel, planes),
        grid_spec=pltpu.PrefetchScalarGridSpec(
            num_scalar_prefetch=1,
            grid=(1,),
            in_specs=[pl.BlockSpec((8, 16, 2 * LANE), lambda i, o: (0, rows // 16, 0))],
            out_specs=pl.BlockSpec((2 * LANE, LANE), lambda i, o: (0, 0)),
        ),
        out_shape=jax.ShapeDtypeStruct((2 * LANE, LANE), jnp.float32),
        compiler_params=pltpu.CompilerParams(vmem_limit_bytes=VMEM),
        cost_estimate=pl.CostEstimate(flops=10**9, bytes_accessed=2**18, transcendentals=0),
        name="nyquist",
    )(own, data)


TILE = 512


def across(centre, tile, west, east):
    lane = lax.broadcasted_iota(jnp.int32, centre.shape, 1)
    right = jnp.where(lane == TILE - 1, east, pltpu.roll(centre, TILE - 1, 1))
    left = jnp.where(lane == 0, west, pltpu.roll(centre, 1, 1))
    return (right - left) * (right - left)


def spatial_term(held, r, t):
    lanes = slice(t * TILE, (t + 1) * TILE)
    around = held[pl.ds(pl.multiple_of(r - 8, 8), 32), lanes]
    centre, down = around[8:24], around[9:25] - around[7:23]
    first, last = max(t * TILE - 1, 0), min((t + 1) * TILE, N - 1)
    here = pl.ds(r, 16)
    west, east = held[here, first : first + 1], held[here, last : last + 1]
    return centre, down * down + across(centre, TILE, west, east)


def hold(held, block, rows):
    held[8 : 8 + rows, :] = block.astype(jnp.float32)
    held[7:8, :] = held[8:9, :]
    held[8 + rows : 9 + rows, :] = held[7 + rows : 8 + rows, :]


def early_focus_kernel(first, others, best, spatial, held):
    rows = first.shape[1]
    for g in range(3):
        hold(held.at[g], first[0] if g == 0 else others[g - 1], rows)

    def strip(i, carry):
        r = pl.multiple_of(8 + i * 16, 8)
        here = pl.ds(pl.multiple_of(i * 16, 16), 16)
        for t in range(N // TILE):
            lanes = slice(t * TILE, (t + 1) * TILE)
            (c0, s0), (c1, s1), (c2, s2) = (spatial_term(held.at[g], r, t) for g in range(3))
            d0, d1 = c1 - c0, c2 - c0
            score = jnp.maximum(d0 * d0 + s0, d1 * d1 + s1)
            best[here, lanes] = (score * 0.125).astype(jnp.bfloat16)
            spatial[here, lanes] = s2.astype(jnp.bfloat16)
        return carry

    lax.fori_loop(0, rows // 16, strip, 0)


def early_focus(first, others):
    rows = first.shape[1]
    return pl.pallas_call(
        early_focus_kernel,
        out_shape=[
            jax.ShapeDtypeStruct((rows, N), jnp.bfloat16),
            jax.ShapeDtypeStruct((rows, N), jnp.bfloat16),
        ],
        scratch_shapes=[pltpu.VMEM((3, rows + 16, N), jnp.float32)],
        compiler_params=pltpu.CompilerParams(vmem_limit_bytes=VMEM),
        cost_estimate=pl.CostEstimate(flops=10**9, bytes_accessed=12 * MIB, transcendentals=0),
        name="early_focus",
    )(first, others)


def edge_rows(edges, halo):
    lane = lax.broadcasted_iota(jnp.int32, (2, N), 1)
    pair = lambda a, b: jnp.concatenate([a, b], axis=0)
    centre = [pair(e[0:1, :], e[15:16, :]) for e in edges]
    best = None
    for g, e in enumerate(edges):
        depth = centre[min(g + 1, 3)] - centre[max(g - 1, 0)]
        above, below = halo[2 * g : 2 * g + 1, :], halo[2 * g + 1 : 2 * g + 2, :]
        down = pair(e[1:2, :], below) - pair(above, e[14:15, :])
        c = centre[g]
        right = jnp.where(lane == N - 1, c, jnp.concatenate([c[:, 1:], c[:, :1]], axis=1))
        left = jnp.where(lane == 0, c, jnp.concatenate([c[:, -1:], c[:, :-1]], axis=1))
        score = depth * depth + down * down + (right - left) * (right - left)
        best = score if best is None else jnp.maximum(best, score)
    return best * 0.125


def last_rows_kernel(
    parts, best, spatial, others, nyquist_in, table_in, turn_in, edge0_in, edge12_in,
    upper_out, lower_out,
    both, nyquist, table, turn, edge0, edge12, part_buf, best_buf, spatial_buf, others_buf, opened, held, halo, edge, sems,
):
    rows = both.shape[0]
    loads = []
    for group in range(CLS):
        source = parts.at[group // 2, :, group % 2]
        loads.append(pltpu.make_async_copy(source, part_buf.at[group], sems.at[0, group]))
    late = (best, best_buf), (spatial, spatial_buf), (others, others_buf)
    late += (edge0_in, edge0), (edge12_in, edge12)
    for i, (source, target) in enumerate(late):
        loads.append(pltpu.make_async_copy(source, target, sems.at[1, i]))
    early = (nyquist_in, nyquist), (table_in, table), (turn_in, turn)
    early = [pltpu.make_async_copy(a, b, sems.at[2, i]) for i, (a, b) in enumerate(early)]
    for load in early + loads:
        load.start()
    for load in early:
        load.wait()
    lane = lax.broadcasted_iota(jnp.int32, (rows, LANE), 1)
    few_lane = lax.broadcasted_iota(jnp.int32, (16, LANE), 1)
    few_row = lax.broadcasted_iota(jnp.int32, (16, LANE), 0)
    beside = jnp.where(few_row % 2 == 0, nyquist[rows : rows + 1, :], nyquist[rows + 1 : rows + 2, :])
    columns = []
    for part in range(2):
        mine = jnp.where(lane == 6 + part, nyquist[:rows, :], 0.0)
        few = jnp.where(few_lane == (few_row // 2) * 2 + part, beside, 0.0)
        column = jnp.sum(jnp.concatenate([mine, few], axis=0), axis=1, keepdims=True)
        columns.append(column.astype(jnp.bfloat16))
    for group in range(CLS):
        loads[group].wait()
        low, high = part_buf[group, 0], part_buf[group, 1]
        open_class(group, low, high, columns, table, turn, opened)

    def strip(i, carry):
        base = pl.multiple_of(i * 8, 8)
        for tile in range(INN // LANE):
            for a, value in enumerate(strip_intensity(opened, pl.ds(base, 8), tile)):
                lanes = slice(a * INN + tile * LANE, a * INN + (tile + 1) * LANE)
                value = value.astype(jnp.bfloat16).astype(jnp.float32)
                held[pl.ds(pl.multiple_of(base + 8, 8), 8), lanes] = value
        return carry

    lax.fori_loop(0, rows // 8 + 1, strip, 0)
    halo[...] = held[8 + rows : 16 + rows, :]
    held[7:8, :] = held[8:9, :]
    held[8 + rows : 9 + rows, :] = held[7 + rows : 8 + rows, :]
    edge[0:8, :] = held[8:16, :]
    edge[8:16, :] = held[rows : rows + 8, :]
    for load in loads[CLS:]:
        load.wait()
    ends = edge_rows([edge0.at[0], edge12.at[0], edge12.at[1], edge], halo)

    def measure(i, carry):
        r = pl.multiple_of(8 + i * 16, 8)
        here = pl.ds(pl.multiple_of(i * 16, 16), 16)
        for t in range(N // TILE):
            lanes = slice(t * TILE, (t + 1) * TILE)
            centre, term = spatial_term(held, r, t)
            d2 = centre - others_buf[0, here, lanes].astype(jnp.float32)
            d3 = centre - others_buf[1, here, lanes].astype(jnp.float32)
            score = jnp.maximum(d2 * d2 + spatial_buf[here, lanes].astype(jnp.float32), d3 * d3 + term)
            score = jnp.maximum(score * 0.125, best_buf[here, lanes].astype(jnp.float32))
            both[here, lanes] = score.astype(jnp.bfloat16)
        return carry

    half = rows // 2
    stores = []
    for side, out in enumerate((upper_out, lower_out)):
        lax.fori_loop(side * (half // 16), (side + 1) * (half // 16), measure, 0)
        here = slice(0, 16) if side == 0 else slice(rows - 16, rows)
        index = lax.broadcasted_iota(jnp.int32, (16, N), 0)
        value = jnp.where(index == 15 * side, ends[side : side + 1], both[here].astype(jnp.float32))
        both[here] = value.astype(jnp.bfloat16)
        source = both.at[pl.ds(side * half, half)]
        stores.append(pltpu.make_async_copy(source, out, sems.at[2, 3 + side]))
        stores[-1].start()
    for store in stores:
        store.wait()


def last_rows(parts, nyquist, best, spatial, others, edge0, edge12):
    rows = best.shape[0]
    table, turn = (jnp.asarray(t) for t in row_inverse_tables())
    hbm = pl.BlockSpec(memory_space=pl.ANY)
    bf16, f32 = jnp.bfloat16, jnp.float32
    return pl.pallas_call(
        last_rows_kernel,
        in_specs=[hbm] * 9,
        out_specs=[hbm] * 2,
        out_shape=[jax.ShapeDtypeStruct((rows // 2, N), bf16)] * 2,
        scratch_shapes=[
            pltpu.VMEM((rows, N), bf16),
            pltpu.VMEM((2 * LANE, LANE), f32),
            pltpu.VMEM((2, 2 * INN, 2 * INN), bf16),
            pltpu.VMEM((2 * CLS, INN), f32),
            pltpu.VMEM((1, 16, N), f32),
            pltpu.VMEM((2, 16, N), f32),
            pltpu.VMEM((CLS, 2, rows + 16, 4 * LANE), bf16),
            pltpu.VMEM((rows, N), bf16),
            pltpu.VMEM((rows, N), bf16),
            pltpu.VMEM((2, rows, N), bf16),
            pltpu.VMEM((2, CLS, rows + 16, 2 * INN), f32),
            pltpu.VMEM((rows + 16, N), f32),
            pltpu.VMEM((8, N), f32),
            pltpu.VMEM((16, N), f32),
            pltpu.SemaphoreType.DMA((3, CLS)),
        ],
        compiler_params=pltpu.CompilerParams(vmem_limit_bytes=VMEM),
        cost_estimate=pl.CostEstimate(flops=3 * 10**9, bytes_accessed=16 * MIB, transcendentals=0),
        name="last_rows",
    )(parts, best, spatial, others, nyquist, table, turn, edge0, edge12)


def assemble_kernel(own, *refs):
    slot, out = pl.program_id(0), refs[-1]
    half = refs[0].shape[0]
    for s in range(4):

        @pl.when(slot == s)
        def _():
            out[:half] = refs[s][...].astype(jnp.float32)
            out[half:] = refs[4 + s][...].astype(jnp.float32)


def assemble(depth_index, upper, lower):
    half = upper[0].shape[0]
    whole = pl.BlockSpec((half, N), lambda s, o: (0, 0))
    return pl.pallas_call(
        assemble_kernel,
        grid_spec=pltpu.PrefetchScalarGridSpec(
            num_scalar_prefetch=1,
            grid=(4,),
            in_specs=[whole] * 8,
            out_specs=pl.BlockSpec((2 * half, N), lambda s, o: (jnp.bitwise_xor(s, o[0]), 0)),
        ),
        out_shape=jax.ShapeDtypeStruct((8 * half, N), jnp.float32),
        compiler_params=pltpu.CompilerParams(vmem_limit_bytes=SHARED),
        cost_estimate=pl.CostEstimate(flops=10**6, bytes_accessed=12 * MIB, transcendentals=0),
        name="assemble",
    )(depth_index, *upper, *lower)


OVER_X = [(i, i ^ 1) for i in range(4)]
OVER_Y = [(i, i ^ 2) for i in range(4)]


def exchange_depth(a, b):
    ax, by = lax.ppermute(a, "depth", OVER_X), lax.ppermute(b, "depth", OVER_Y)
    ay, axy = lax.ppermute(a, "depth", OVER_Y), lax.ppermute(ax, "depth", OVER_Y)
    bx, byx = lax.ppermute(b, "depth", OVER_X), lax.ppermute(by, "depth", OVER_X)
    return (a, ax, ay, axy), (b, bx, by, byx)


def border_rows(halfway, outside, high):
    lanes = 4 * LANE
    count = halfway.shape[-1] // lanes
    natural = lambda rows: rows.reshape(4, 2, 2, count, lanes).transpose(1, 2, 0, 3, 4).reshape(16, count, lanes)
    first, last = natural(halfway[..., 0, :]), natural(halfway[..., -1, :])
    above = jnp.where(high == 0, first[:1], outside[None, :, 15])
    below = jnp.where(high == 0, outside[None, :, 0], last[-1:])
    above = jnp.concatenate([above, last[:-1]])
    below = jnp.concatenate([first[1:], below])
    both = jnp.stack([above, below], axis=2).reshape(2, 2, 4, 2 * count, lanes)
    return both.transpose(2, 0, 1, 3, 4).reshape(16, 2 * count, lanes)


def half_spectrum_shards(hologram, background):
    rows = hologram.shape[0]
    planes = lax.axis_size("depth") * PL_DEV
    depth, high = lax.axis_index("depth"), lax.axis_index("high")
    low, core = lax.axis_index("low"), lax.axis_index("core")
    as_scalar = lambda value: jnp.reshape(value, (1,)).astype(jnp.int32)
    own = rows // 4
    block = ((high * 2 + low) * 2 + core) * 4 + depth
    place = jnp.stack([block, jnp.int32(N // own)]).astype(jnp.int32)

    sections = row_forward(as_scalar(depth), hologram, background)
    data = lax.all_to_all(
        sections.reshape(8, rows + 16, 2 * LANE),
        ("high", "low", "core"),
        split_axis=0,
        concat_axis=0,
        tiled=True,
    )

    group = depth * 2 + core
    slot = low * LANE + jnp.arange(LANE, dtype=jnp.int32)
    special = jnp.where(low == 0, 0, CLS) + OUT * jnp.arange(LANE, dtype=jnp.int32)
    fx = signed_fraction(jnp.where(group == 0, special, group + OUT * slot))
    kernels = propagators(planes, (fx * fx)[None])

    def to_rows(halfway):
        parts = lax.all_to_all(
            halfway.reshape(16, -1, halfway.shape[-1]),
            ("depth", "low", "core"),
            split_axis=0,
            concat_axis=0,
            tiled=True,
        )
        return parts.reshape(4, 2, 2, -1, halfway.shape[-1])

    halfway, spectrum, outside = first_columns(as_scalar(high), data, kernels)
    parts, borders = [to_rows(halfway)], [border_rows(halfway, outside, high)]
    for plane, count in ((1, 2), (3, 1)):
        halfway, outside = next_columns(as_scalar(high), plane, count, spectrum, kernels)
        borders.append(border_rows(halfway, outside, high))
        halfway = halfway.reshape(16, own, -1)
        if plane == 3:
            below = jnp.concatenate(borders, axis=1)
            below = jnp.pad(below, ((0, 0), (0, 16 - 2 * planes), (0, 0)))
            halfway = jnp.concatenate([halfway, below], axis=1)
        ready = parts[-1]
        if plane == 3:
            first, first_edge = row_inverse(0, 1, parts[0], middle)
            ready = ready, first, first_edge
        elif plane == 1:
            middle = nyquist_column(place, planes, data)
            ready = ready, middle
        halfway, ready = lax.optimization_barrier((halfway, ready))
        if plane == 3:
            parts[-1], first, first_edge = ready
        else:
            parts[-1], middle = ready
        parts.append(to_rows(halfway))
    others, others_edge = row_inverse(1, 2, parts[1], middle)
    best, spatial = early_focus(first, others)
    upper, lower = last_rows(parts[2], middle, best, spatial, others, first_edge, others_edge)
    return assemble(as_scalar(depth), *exchange_depth(upper, lower))


def solution(mesh):
    spec = P("rows", None)
    if mesh.shape["depth"] == 4 and mesh.shape["rows"] == 8:
        split = Mesh(mesh.devices.reshape(4, 2, 2, 2), ("depth", "high", "low", "core"))
        spec = P(("high", "low", "core"), None)
        body = half_spectrum_shards
    else:
        split, body = mesh, shards
    return jax.shard_map(body, mesh=split, in_specs=(spec, spec), out_specs=spec, check_vma=False)
```

```python
import functools
import math

import jax
import jax.numpy as jnp
import numpy as np
from jax import lax
from jax.experimental import pallas as pl
from jax.experimental.pallas import tpu as pltpu
from jax.sharding import Mesh
from jax.sharding import PartitionSpec as P

N = 4096
RADIX = 64
PL_DEV = 1


wave_number = 0.6
depth_start = 8.0
depth_step = 2.0


def padded_2(block, sides, width):
    for axis, dim in sides:
        count = lax.axis_size(axis)
        forward = [(i, i + 1) for i in range(count - 1)]
        backward = [(target, source) for source, target in forward]
        low = lax.ppermute(
            lax.slice_in_dim(block, block.shape[dim] - width, None, axis=dim), axis, forward
        )
        high = lax.ppermute(lax.slice_in_dim(block, 0, width, axis=dim), axis, backward)
        block = jnp.concatenate([low, block, high], axis=dim)
    return block


def fourier_tables(radix_size, sign_value):
    indices = jnp.arange(radix_size, dtype=jnp.int32)
    products = indices[:, None] * indices[None, :] % radix_size
    angles = products.astype(jnp.float32) * (sign_value * 2.0 * math.pi / radix_size)
    scaling = 1.0 / math.sqrt(radix_size)
    cosine_part = jnp.cos(angles) * scaling
    sine_part = jnp.sin(angles) * scaling
    matrix = jnp.stack([jnp.stack([cosine_part, -sine_part]), jnp.stack([sine_part, cosine_part])])
    return matrix.astype(jnp.bfloat16)


def twiddle_table(radix_size, sign_value):
    indices = jnp.arange(radix_size, dtype=jnp.int32)
    total = radix_size * radix_size
    products = indices[:, None] * indices[None, :] % total
    angles = products.astype(jnp.float32) * (sign_value * 2.0 * math.pi / total)
    return (jnp.cos(angles), jnp.sin(angles))


def rotate(data, cosine_part, sine_part):
    return jnp.stack(
        [data[0] * cosine_part - data[1] * sine_part, data[0] * sine_part + data[1] * cosine_part]
    )


def contract(form, matrix, data):
    return jnp.einsum(form, matrix, data, preferred_element_type=jnp.float32)


def forward_real(data):
    batch_size = data.shape[1]
    shaped = data.reshape(RADIX, RADIX, batch_size)
    matrix = fourier_tables(RADIX, -1.0)
    cosine_part, sine_part = twiddle_table(RADIX, -1.0)
    opening = contract("oka,abm->okbm", matrix[:, 0], shaped)
    sectioned = rotate(opening, cosine_part[:, :, None], sine_part[:, :, None]).astype(jnp.bfloat16)
    closing = contract("ocjb,ckbm->okjm", matrix, sectioned)
    return closing.reshape(2, N, batch_size).astype(jnp.bfloat16)


def forward_first(data):
    batch_size = data.shape[2]
    shaped = data.reshape(2, RADIX, RADIX, batch_size)
    matrix = fourier_tables(RADIX, -1.0)
    cosine_part, sine_part = twiddle_table(RADIX, -1.0)
    opening = contract("ocka,cabm->okbm", matrix, shaped)
    sectioned = rotate(opening, cosine_part[:, :, None], sine_part[:, :, None]).astype(jnp.bfloat16)
    closing = contract("ocjb,ckbm->okjm", matrix, sectioned)
    return closing.reshape(2, N, batch_size).astype(jnp.bfloat16)


def inverse_first(data):
    batch_size = data.shape[2]
    shaped = data.reshape(2, RADIX, RADIX, batch_size)
    matrix = fourier_tables(RADIX, 1.0)
    cosine_part, sine_part = twiddle_table(RADIX, 1.0)
    opening = contract("ocbj,ckjm->okbm", matrix, shaped)
    sectioned = rotate(opening, cosine_part[:, :, None], sine_part[:, :, None]).astype(jnp.bfloat16)
    closing = contract("ocak,ckbm->oabm", matrix, sectioned)
    return closing.reshape(2, N, batch_size)


def frequencies(positions):
    natural = positions // RADIX + RADIX * (positions % RADIX)
    signed_freq = jnp.where(natural >= N // 2, natural - N, natural)
    return signed_freq.astype(jnp.float32) / N


def propagator(freq_whole, freq_own, distance):
    radial = freq_whole[:, None] ** 2 + freq_own[None, :] ** 2
    limit = wave_number * wave_number
    amplitude = jnp.exp(-2.0 * math.pi * distance * jnp.sqrt(jnp.maximum(radial - limit, 0.0)))
    phase_angle = (
        2.0 * math.pi * distance * (jnp.sqrt(jnp.maximum(limit - radial, 0.0)) - wave_number)
    )
    return (amplitude * jnp.cos(phase_angle), amplitude * jnp.sin(phase_angle))


def propagate(spectrum, cosine_part, sine_part):
    return rotate(spectrum.astype(jnp.float32), cosine_part, sine_part).astype(jnp.bfloat16)


def shards(hologram, background):
    row_count = hologram.shape[0]
    contrast = (hologram.astype(jnp.float32) / background.astype(jnp.float32) - 1.0).astype(
        jnp.bfloat16
    )
    along_rows = forward_real(contrast.T)
    columns = lax.all_to_all(
        jnp.swapaxes(along_rows, 1, 2), "rows", split_axis=2, concat_axis=1, tiled=True
    )
    spectrum = forward_first(columns)
    row_index = lax.axis_index("rows")
    own_positions = row_index * row_count + jnp.arange(row_count, dtype=jnp.int32)
    freq_own = frequencies(own_positions)
    freq_whole = frequencies(jnp.arange(N, dtype=jnp.int32))
    depth_index = lax.axis_index("depth")
    distance = depth_start + depth_step * (depth_index * PL_DEV + 0).astype(jnp.float32)
    cosine_part, sine_part = propagator(freq_whole, freq_own, distance)
    propagated = propagate(spectrum, cosine_part, sine_part)
    halfway = inverse_first(propagated).astype(jnp.bfloat16)
    restored = lax.all_to_all(
        jnp.swapaxes(halfway, 1, 2), "rows", split_axis=2, concat_axis=1, tiled=True
    )
    result_field = inverse_first(restored)
    intensities = [
        (result_field[0] * result_field[0] + result_field[1] * result_field[1]).astype(jnp.bfloat16)
    ]
    stacked = jnp.stack(intensities)
    padded = padded_2(stacked, (("depth", 0), ("rows", 2)), 1)
    centre_block = padded[1:-1, :, 1:-1]
    plane_ids = jnp.arange(PL_DEV, dtype=jnp.int32)[:, None, None]
    row_ids = jnp.arange(row_count, dtype=jnp.int32)[None, None, :]
    depth_count = lax.axis_size("depth")
    row_groups = lax.axis_size("rows")
    lower_plane = jnp.where(
        (depth_index == 0) & (plane_ids == 0), centre_block, padded[:-2, :, 1:-1]
    )
    upper_plane = jnp.where(
        (depth_index == depth_count - 1) & (plane_ids == PL_DEV - 1),
        centre_block,
        padded[2:, :, 1:-1],
    )
    north_row = jnp.where((row_index == 0) & (row_ids == 0), centre_block, padded[1:-1, :, :-2])
    south_row = jnp.where(
        (row_index == row_groups - 1) & (row_ids == row_count - 1),
        centre_block,
        padded[1:-1, :, 2:],
    )
    centre = centre_block.astype(jnp.float32)
    east_col = jnp.concatenate([centre[:, 1:], centre[:, -1:]], axis=1)
    west_col = jnp.concatenate([centre[:, :1], centre[:, :-1]], axis=1)
    depth_diff = upper_plane.astype(jnp.float32) - lower_plane.astype(jnp.float32)
    row_diff = south_row.astype(jnp.float32) - north_row.astype(jnp.float32)
    col_diff = east_col - west_col
    scores = (depth_diff * depth_diff + row_diff * row_diff + col_diff * col_diff) / 8.0
    sharpest = jnp.max(scores, axis=0)
    merged = lax.pmax(sharpest.astype(jnp.bfloat16), "depth").astype(sharpest.dtype)
    return merged.T


OUT = 16
INN = 256
CLS = 8
LANE = 128
MIB = 2**20
VMEM = 63 * MIB
SHARED = 36 * MIB


def slot_frequencies():
    table = np.arange(CLS)[:, None] + OUT * np.arange(INN)[None, :]
    half = np.arange(INN // 2)
    table[0] = np.concatenate([OUT * half, CLS + OUT * half])
    return table


def angles(products):
    return 2.0 * np.pi * (products % N) / N


def row_forward_tables():
    freq = slot_frequencies()
    theta = angles(np.arange(INN)[None, :, None] * freq[:, None, :])
    cos, sin = np.cos(theta) / 64.0, np.sin(theta) / 64.0
    top = np.stack([cos, -sin], axis=2)
    low = np.stack([sin, cos], axis=2)
    first = np.arange(INN) < INN // 2
    low[0] = np.where(first, 0.0, top[0])
    top[0] = np.where(first, top[0], 0.0)
    full = np.concatenate([top, low], axis=1)
    full = full.reshape(CLS, 2 * INN, 2, 2, LANE).transpose(0, 1, 3, 2, 4)
    return full.reshape(CLS, 2 * INN, 2 * INN).astype(jnp.bfloat16)


def row_forward_weights():
    a = np.arange(1, 5)
    rows = []
    for d in range(CLS // 2):
        even, odd = (2.0 * np.pi * c * a / OUT for c in (2 * d, 2 * d + 1))
        parts = np.cos(even), -np.sin(even[:3]), [float(d == 0)], np.cos(odd[:3]), -np.sin(odd), [0.0]
        rows.append(np.concatenate(parts))
    return np.concatenate(rows).astype(np.float32)


def row_inverse_tables():
    half = np.arange(INN // 2)
    position = np.arange(INN)[None, :]
    full = np.zeros((2, 2, INN, 2, INN))
    for first, place in ((0, 0), (CLS, 1)):
        theta = angles((first + OUT * half)[:, None] * position)
        rows = slice(place * INN // 2, (place + 1) * INN // 2)
        full[0, 0, rows, place], full[0, 1, rows, place] = np.cos(theta), -np.sin(theta)
    full[0, 0, 0, 0] = 0.5
    full[0, 1, 0, 0] = 0.5 * (-1.0) ** np.arange(INN)
    theta = angles(OUT * np.arange(INN)[:, None] * position)
    full[1, 0, :, 0], full[1, 0, :, 1] = np.cos(theta), np.sin(theta)
    full[1, 1, :, 0], full[1, 1, :, 1] = -np.sin(theta), np.cos(theta)
    full = full.reshape(2, 2, 2, LANE, 2 * INN).transpose(0, 2, 1, 3, 4) / 32.0
    turn = angles(np.arange(CLS)[:, None] * position)
    turn = np.concatenate([np.cos(turn), np.sin(turn)]).astype(np.float32)
    return full.reshape(2, 2 * INN, 2 * INN).astype(jnp.bfloat16), turn


def column_tables():
    turn = 2.0 * np.pi * np.arange(OUT)[:, None] * np.arange(OUT)[None, :] / OUT
    eye = np.eye(16)
    outer_cos, outer_sin = np.kron(np.cos(turn), eye) / 4.0, np.kron(np.sin(turn), eye) / 4.0
    complex_form = lambda cos, sin: np.concatenate(
        [np.concatenate([cos, -sin], axis=-1), np.concatenate([sin, cos], axis=-1)], axis=-2
    )
    slabs = lambda table: table.reshape(-1, 8, 2, 16).swapaxes(1, 2).reshape(table.shape)
    outer = complex_form(slabs(outer_cos), slabs(-outer_sin))
    half_rows = outer_cos.shape[0] // 2
    cut = lambda table, begin, size: table[begin : begin + size]
    back = np.stack(
        [
            complex_form(cut(outer_cos, begin, half_rows), cut(outer_sin, begin, half_rows))
            for begin in (0, half_rows)
        ]
    )
    beyond = np.stack(
        [complex_form(cut(outer_cos, a * 16, 16), cut(outer_sin, a * 16, 16)) for a in (8, 7)]
    )
    theta = angles(OUT * np.arange(INN)[:, None] * np.arange(INN)[None, :])
    inner = complex_form(np.cos(theta), -np.sin(theta)) / 16.0
    inner_back = complex_form(np.cos(theta), np.sin(theta)) / 16.0
    turn = angles(np.arange(OUT)[:, None] * np.arange(INN)[None, :])
    by_chunk = turn.reshape(OUT, 16, 16).swapaxes(1, 2).reshape(INN, 16)
    twist = np.zeros((2, INN, LANE), np.float32)
    for i, table in enumerate((by_chunk, turn.T)):
        twist[i, :, :16], twist[i, :, 16:32] = np.cos(table), np.sin(table)
    cast = lambda table: table.astype(jnp.bfloat16)
    return cast(outer), cast(inner), cast(inner_back), cast(back), cast(beyond), twist


def dot(left, right):
    return jnp.dot(left, right, preferred_element_type=jnp.float32)


def split_complex(both, width):
    rows = both.shape[0] // 2
    top, low = both[:rows], both[rows:]
    return top[:, :width] - low[:, width:], top[:, width:] + low[:, :width]


def quarter_kernel(radial):
    gap = wave_number * wave_number - radial
    root = jnp.sqrt(jnp.abs(gap))
    inside = gap > 0.0
    half_pi = 0.5 * math.pi
    angle = half_pi * (jnp.where(inside, root, 0.0) - wave_number)
    decay = jnp.exp(jnp.where(inside, 0.0, -half_pi * root))
    square = angle * angle
    sine = 1.0 / 362880.0
    for c in (-1.0 / 5040.0, 1.0 / 120.0, -1.0 / 6.0, 1.0):
        sine = sine * square + c
    cosine = -1.0 / 3628800.0
    for c in (1.0 / 40320.0, -1.0 / 720.0, 1.0 / 24.0, -0.5, 1.0):
        cosine = cosine * square + c
    return decay * cosine, decay * (sine * angle)


def squared(re, im):
    return (re - im) * (re + im), 2.0 * re * im


def start_and_step(radial):
    value = quarter_kernel(radial)
    distance = 0.25
    step = None
    while distance < depth_start:
        value = squared(*value)
        distance *= 2.0
        if distance == depth_step:
            step = value
    return value, step


def signed_fraction(natural):
    return jnp.where(natural >= N // 2, natural - N, natural).astype(jnp.float32) * (1.0 / N)


CHUNK = 64


def sixteen_sums(term, w):
    c0, c8 = term(0), term(8)
    plus, minus = c0 + c8, c0 - c8
    c4, c12 = term(4), term(12)
    e4, o4 = c4 + c12, c4 - c12
    total = plus + e4
    eighth = total
    re_even = plus + w(3) * e4
    im_even = None
    re_odd, im_odd = minus, w(14) * o4
    for a in (1, 2, 3):
        p, q, r, s = term(a), term(16 - a), term(8 - a), term(8 + a)
        e, o, f, h = p + q, p - q, r + s, r - s
        both = e + f
        total = total + both
        eighth = eighth - both if a % 2 else eighth + both
        re_even = re_even + w(a - 1) * both
        term_im = w(3 + a) * (o - h)
        im_even = term_im if im_even is None else im_even + term_im
        re_odd = re_odd + w(7 + a) * (e - f)
        im_odd = im_odd + w(10 + a) * (o + h)
    return re_even, im_even + w(7) * eighth, re_odd, im_odd, total


def row_forward_kernel(
    own, weights, holo, back, table, out, holo_buf, back_buf, table_buf, acc, result, held, sems
):
    rows = holo.shape[0]
    group = own[0]
    chunks = rows // CHUNK
    loads = []
    for i in range(chunks):
        here = pl.ds(i * CHUNK, CHUNK)
        loads.append(
            (
                pltpu.make_async_copy(holo.at[here], holo_buf.at[here], sems.at[0, i]),
                pltpu.make_async_copy(back.at[here], back_buf.at[here], sems.at[1, i]),
            )
        )
        for load in loads[-1]:
            load.start()
        if i == 0:
            tables = pltpu.make_async_copy(table.at[pl.ds(2 * group, 2)], table_buf, sems.at[4, 0])
            tables.start()
    lane = lax.broadcasted_iota(jnp.int32, (16, INN), 1)
    sign = jnp.where(lane % 2 == 0, 1.0, -1.0).astype(jnp.bfloat16)
    stores = []
    for chunk in range(chunks):
        for load in loads[chunk]:
            load.wait()

        def strip(i, carry):
            here = pl.ds(pl.multiple_of(chunk * CHUNK + i * 16, 16), 16)

            def term(a):
                there = pl.ds(a * INN, INN)
                below = back_buf[here, there].astype(jnp.float32)
                inverse = pl.reciprocal(below, approx=True)
                inverse = inverse * (2.0 - below * inverse)
                value = holo_buf[here, there].astype(jnp.float32) * inverse
                return (value - 1.0).astype(jnp.bfloat16).astype(jnp.float32)

            sums = sixteen_sums(term, lambda n: weights[group * 16 + n])
            for q in range(4):
                acc[q // 2, here, pl.ds((q % 2) * INN, INN)] = sums[q].astype(jnp.bfloat16)
            acc[2, here, pl.ds(0, INN)] = sums[4].astype(jnp.bfloat16)
            return carry

        lax.fori_loop(0, CHUNK // 16, strip, 0)
        batch = rows // 2 // CHUNK
        if chunk % batch != batch - 1:
            continue
        if chunk < batch:
            tables.wait()
        begin, end = (chunk + 1 - batch) * CHUNK, (chunk + 1) * CHUNK
        for q in range(2):
            both = dot(acc[q, begin:end], table_buf[q]).astype(jnp.bfloat16)
            for low in range(2):
                part = both[:, low * 2 * LANE : (low + 1) * 2 * LANE]
                result[low, q, begin:end, :] = part
        held[chunk // batch] = lax.dot_general(
            sign,
            acc[2, begin:end, :INN],
            (((1,), (1,)), ((), ())),
            preferred_element_type=jnp.float32,
        )
        here = pl.ds(begin, end - begin)
        if chunk == chunks - 1:
            index = lax.broadcasted_iota(jnp.int32, (16, INN), 0)
            extra = jnp.where(index == 0, held[0], held[1]) * (1.0 / 64.0)
            for low in range(2):
                for q in range(2):
                    result[low, q, rows:, :] = extra.astype(jnp.bfloat16)
            here = pl.ds(begin, end - begin + 16)
        for high in range(2):
            source, target = result.at[:, :, here, :], out.at[high, :, :, here, :]
            stores.append(pltpu.make_async_copy(source, target, sems.at[2 + high, chunk]))
            stores[-1].start()
    for store in stores:
        store.wait()


def row_forward(own, hologram, background):
    rows = hologram.shape[0]
    table = jnp.asarray(row_forward_tables())
    weights = jnp.asarray(row_forward_weights())
    hbm = pl.BlockSpec(memory_space=pl.ANY)
    chunks = rows // CHUNK
    return pl.pallas_call(
        row_forward_kernel,
        grid_spec=pltpu.PrefetchScalarGridSpec(
            num_scalar_prefetch=2,
            grid=(1,),
            in_specs=[hbm] * 3,
            out_specs=hbm,
            scratch_shapes=[
                pltpu.VMEM((rows, N), jnp.bfloat16),
                pltpu.VMEM((rows, N), jnp.bfloat16),
                pltpu.VMEM((2, 2 * INN, 2 * INN), jnp.bfloat16),
                pltpu.VMEM((3, rows, 2 * INN), jnp.bfloat16),
                pltpu.VMEM((2, 2, rows + 16, 2 * LANE), jnp.bfloat16),
                pltpu.VMEM((2, 16, INN), jnp.float32),
                pltpu.SemaphoreType.DMA((5, chunks)),
            ],
        ),
        out_shape=jax.ShapeDtypeStruct((2, 2, 2, rows + 16, 2 * LANE), jnp.bfloat16),
        compiler_params=pltpu.CompilerParams(vmem_limit_bytes=VMEM),
        cost_estimate=pl.CostEstimate(flops=10**10, bytes_accessed=12 * MIB, transcendentals=0),
        name="row_forward",
    )(own, weights, hologram, background, table)


def propagator_kernel(planes, fx2, out):
    step = pl.program_id(0)
    strip = 32
    for i in range(INN // strip):
        rows = slice(i * strip, (i + 1) * strip)
        position = lax.broadcasted_iota(jnp.int32, (strip, LANE), 0) + i * strip
        fy = signed_fraction(step + OUT * position)
        (kr, ki), (sr, si) = start_and_step(fy * fy + fx2[...])
        for g in range(planes):
            out[g, 0, rows, :LANE] = kr.astype(jnp.bfloat16)
            out[g, 0, rows, LANE:] = ki.astype(jnp.bfloat16)
            if g + 1 < planes:
                kr, ki = kr * sr - ki * si, kr * si + ki * sr


def propagators(planes, fx2):
    return pl.pallas_call(
        functools.partial(propagator_kernel, planes),
        grid=(OUT,),
        in_specs=[pl.BlockSpec((1, LANE), lambda i: (0, 0))],
        out_specs=pl.BlockSpec((planes, 1, INN, 2 * LANE), lambda i: (0, i, 0, 0)),
        out_shape=jax.ShapeDtypeStruct((planes, OUT, INN, 2 * LANE), jnp.bfloat16),
        compiler_params=pltpu.CompilerParams(vmem_limit_bytes=VMEM),
        cost_estimate=pl.CostEstimate(flops=10**9, bytes_accessed=16 * MIB, transcendentals=10**6),
        name="propagators",
    )(fx2)


PAIRS = OUT // 2


def mix_and_open(pair, both, kernels, inner_back, twist, mixed, second):
    wide = 2 * LANE
    for k in range(2):
        yr, yi = (both[p * INN : (p + 1) * INN, k * LANE : (k + 1) * LANE] for p in range(2))
        for part in range(2):
            factor = kernels[k, :, part * LANE : (part + 1) * LANE].astype(jnp.float32)
            lanes = slice(k * wide + part * LANE, k * wide + (part + 1) * LANE)
            mixed[:INN, lanes] = (yr * factor).astype(jnp.bfloat16)
            mixed[INN:, lanes] = (yi * factor).astype(jnp.bfloat16)
    opened = dot(inner_back[...], mixed[...])
    for k in range(2):
        at = pair * 2 + k
        re, im = (opened[p * INN : (p + 1) * INN, k * wide : (k + 1) * wide] for p in range(2))
        cos, sin = twist[1, :, at : at + 1], twist[1, :, 16 + at : 17 + at]
        second[0, at] = (re * cos - im * sin).astype(jnp.bfloat16)
        second[1, at] = (re * sin + im * cos).astype(jnp.bfloat16)


def outer_block(second, here):
    return second[:, :, here, :].reshape(2 * OUT * 16, 2 * LANE)


def spread(both):
    rows = both.shape[0] // 2
    re, im = both[:rows], both[rows:]
    return [re[:, :LANE], im[:, :LANE], re[:, LANE:], im[:, LANE:]]


def open_outside(half, beyond, second, outside):
    here = pl.ds(pl.multiple_of(half[0] * (INN - 16), 16), 16)
    both = dot(beyond, outer_block(second, here)).astype(jnp.bfloat16)
    for i, value in enumerate(spread(both)):
        outside[:, i * LANE : (i + 1) * LANE] = value


def close_chunk(here, back, second, store):
    both = dot(back, outer_block(second, here)).astype(jnp.bfloat16)
    for i, value in enumerate(spread(both)):
        value = value.reshape(2, 2, 2, 16, LANE)
        for low in range(2):
            for core in range(2):
                for high in range(2):
                    store(high, low, core, slice(i * LANE, (i + 1) * LANE), value[low, core, high])


def first_columns_kernel(
    half, data, kernels, outer_in, inner_in, inner_back_in, back_in, beyond_in, twist_in,
    out, spectrum, outside,
    data_buf, kernel_buf, outer, inner, inner_back, back, beyond, twist,
    out_buf, spectrum_buf, first, mixed, second, sems,
):
    rows = data_buf.shape[1]
    early = [
        pltpu.make_async_copy(source, target, sems.at[3, i])
        for i, (source, target) in enumerate(
            (
                (data.at[:, pl.ds(0, rows), :], data_buf),
                (outer_in, outer),
                (twist_in, twist),
                (inner_in, inner),
                (inner_back_in, inner_back),
                (back_in.at[half[0]], back),
                (beyond_in.at[half[0]], beyond),
            )
        )
    ]
    for load in early:
        load.start()
    loads = []
    for pair in range(PAIRS):
        here = pl.ds(2 * pair, 2)
        loads.append(
            pltpu.make_async_copy(kernels.at[0, here], kernel_buf.at[here], sems.at[1, pair])
        )
        loads[-1].start()
    for load in early[:3]:
        load.wait()
    for i in range(0, INN // 16, 2):
        pieces = []
        for part in range(2):
            lanes = slice(part * LANE, (part + 1) * LANE)
            for parity in range(2):
                at = parity * INN + i * 16
                block = data_buf[:, at : at + 32, lanes]
                block = jnp.concatenate([block[:, :16], block[:, 16:]], axis=2)
                pieces.append(block.reshape(OUT // 2 * 16, 2 * LANE))
        both = dot(outer[...], jnp.concatenate(pieces, axis=0))
        for c in range(2):
            re, im = (both[p * INN : (p + 1) * INN, c * LANE : (c + 1) * LANE] for p in range(2))
            cos, sin = (twist[0, :, t + i + c : t + i + c + 1] for t in (0, 16))
            here = slice((i + c) * 16, (i + c + 1) * 16)
            for part, value in enumerate((re * cos + im * sin, im * cos - re * sin)):
                value = value.astype(jnp.bfloat16).reshape(PAIRS, 2, 16, LANE)
                first[:, part, here, :LANE] = value[:, 0]
                first[:, part, here, LANE:] = value[:, 1]
    stores = []

    def transform(pair):
        both = dot(inner[...], first[pair].reshape(2 * INN, 2 * LANE))
        spectrum_buf[pair] = both.astype(jnp.bfloat16)
        stores.append(pltpu.make_async_copy(spectrum_buf.at[pair], spectrum.at[pair], sems.at[2, pair]))
        stores[-1].start()
        return both

    early[3].wait()
    both = transform(0)
    early[4].wait()
    for pair in range(PAIRS):
        following = transform(pair + 1) if pair + 1 < PAIRS else None
        loads[pair].wait()
        now = kernel_buf.at[pl.ds(2 * pair, 2)]
        mix_and_open(pair, both, now, inner_back, twist, mixed.at[pair % 2], second)
        both = following
    for load in early[5:]:
        load.wait()
    open_outside(half, beyond[...], second, outside.at[0])
    for chunk in range(INN // 16):
        side, rows = chunk // 8, slice(chunk % 8 * 16, chunk % 8 * 16 + 16)

        def store(high, low, core, lanes, value):
            out_buf[side, high, low, core, rows, lanes] = value

        close_chunk(slice(chunk * 16, chunk * 16 + 16), back[...], second, store)
        if chunk % 4 == 3:
            here = pl.ds((chunk % 8 - 3) * 16, 64)
            source = out_buf.at[side, :, :, :, here, :]
            target = out.at[:, side, :, :, here, :]
            stores.append(pltpu.make_async_copy(source, target, sems.at[0, chunk // 4]))
            stores[-1].start()
    for copy in stores:
        copy.wait()


def next_columns_kernel(
    half, spectrum, kernels, inner_back, back, beyond, twist, out, outside, mixed, second
):
    step = pl.program_id(1)
    for s in range(2):

        @pl.when(step == s)
        def _():
            for i in range(PAIRS // 2):
                pair = s * (PAIRS // 2) + i
                both = spectrum[i].astype(jnp.float32)
                now = kernels.at[0, pl.ds(2 * i, 2)]
                mix_and_open(pair, both, now, inner_back, twist, mixed.at[i % 2], second)
            if s == 1:
                open_outside(half, beyond[0], second, outside.at[0])

    @pl.when(step >= 2)
    def _():
        for c in range(8):
            rows = slice(c * 16, (c + 1) * 16)

            def store(high, low, core, lanes, value):
                out[high, 0, low, core, rows, lanes] = value

            start = pl.multiple_of(((step - 2) * 8 + c) * 16, 16)
            close_chunk(pl.ds(start, 16), back[0], second, store)


def first_columns(half, data, kernels):
    tables = [jnp.asarray(t) for t in column_tables()]
    rows = data.shape[1] - 16
    bf16, f32 = jnp.bfloat16, jnp.float32
    hbm = pl.BlockSpec(memory_space=pl.ANY)
    return pl.pallas_call(
        first_columns_kernel,
        grid_spec=pltpu.PrefetchScalarGridSpec(
            num_scalar_prefetch=1,
            grid=(1,),
            in_specs=[hbm] * 8,
            out_specs=[hbm, hbm, pl.BlockSpec((1, 16, 4 * LANE), lambda i, o: (0, 0, 0))],
            scratch_shapes=[
                pltpu.VMEM((8, rows, 2 * LANE), bf16),
                pltpu.VMEM((OUT, INN, 2 * LANE), bf16),
                pltpu.VMEM((2 * INN, 2 * INN), bf16),
                pltpu.VMEM((2 * INN, 2 * INN), bf16),
                pltpu.VMEM((2 * INN, 2 * INN), bf16),
                pltpu.VMEM((INN, 2 * INN), bf16),
                pltpu.VMEM((32, 2 * INN), bf16),
                pltpu.VMEM((2, INN, LANE), f32),
                pltpu.VMEM((2, 2, 2, 2, LANE, 4 * LANE), bf16),
                pltpu.VMEM((PAIRS, 2 * INN, 2 * LANE), bf16),
                pltpu.VMEM((PAIRS, 2, INN, 2 * LANE), bf16),
                pltpu.VMEM((2, 2 * INN, 4 * LANE), bf16),
                pltpu.VMEM((2, OUT, INN, 2 * LANE), bf16),
                pltpu.SemaphoreType.DMA((4, PAIRS)),
            ],
        ),
        out_shape=[
            jax.ShapeDtypeStruct((2, 2, 2, 2, LANE, 4 * LANE), bf16),
            jax.ShapeDtypeStruct((PAIRS, 2 * INN, 2 * LANE), bf16),
            jax.ShapeDtypeStruct((1, 16, 4 * LANE), bf16),
        ],
        compiler_params=pltpu.CompilerParams(vmem_limit_bytes=VMEM),
        cost_estimate=pl.CostEstimate(flops=10**10, bytes_accessed=16 * MIB, transcendentals=0),
        name="first_columns",
    )(half, data, kernels, *tables)


def next_columns(half, plane, count, spectrum, kernels):
    tables = [jnp.asarray(t) for t in column_tables()[2:]]
    opening = lambda i: jnp.minimum(i, 1)
    closing = lambda i: jnp.maximum(i - 2, 0)
    own = lambda g, i, o: (o[0], 0, 0)
    return pl.pallas_call(
        next_columns_kernel,
        grid_spec=pltpu.PrefetchScalarGridSpec(
            num_scalar_prefetch=1,
            grid=(count, 4),
            in_specs=[
                pl.BlockSpec((PAIRS // 2, 2 * INN, 2 * LANE), lambda g, i, o: (opening(i), 0, 0)),
                pl.BlockSpec(
                    (1, OUT // 2, INN, 2 * LANE), lambda g, i, o: (plane + g, opening(i), 0, 0)
                ),
                pl.BlockSpec((2 * INN, 2 * INN), lambda g, i, o: (0, 0)),
                pl.BlockSpec((1, INN, 2 * INN), own),
                pl.BlockSpec((1, 32, 2 * INN), own),
                pl.BlockSpec((2, INN, LANE), lambda g, i, o: (0, 0, 0)),
            ],
            out_specs=[
                pl.BlockSpec(
                    (2, 1, 2, 2, LANE, 4 * LANE), lambda g, i, o: (0, closing(i), 0, 0, 0, g)
                ),
                pl.BlockSpec((1, 16, 4 * LANE), lambda g, i, o: (g, 0, 0)),
            ],
            scratch_shapes=[
                pltpu.VMEM((2, 2 * INN, 4 * LANE), jnp.bfloat16),
                pltpu.VMEM((2, OUT, INN, 2 * LANE), jnp.bfloat16),
            ],
        ),
        out_shape=[
            jax.ShapeDtypeStruct((2, 2, 2, 2, LANE, count * 4 * LANE), jnp.bfloat16),
            jax.ShapeDtypeStruct((count, 16, 4 * LANE), jnp.bfloat16),
        ],
        compiler_params=pltpu.CompilerParams(vmem_limit_bytes=VMEM),
        cost_estimate=pl.CostEstimate(
            flops=count * 7 * 10**9, bytes_accessed=count * 16 * MIB, transcendentals=0
        ),
        name="next_columns",
    )(half, spectrum, kernels, *tables)


def sixteen_points(re, im):
    c = math.sqrt(0.5)
    c1, c3 = math.cos(math.pi / 8), math.cos(3 * math.pi / 8)
    r0, r1, r2, r3, r4, r5, r6, r7 = re
    r8, i1, i2, i3, i4, i5, i6, i7 = im
    sum08, dif08, sum26, dif26 = r0 + r8, r0 - r8, r2 + r6, c * (r2 - r6)
    base = sum08 + r4
    even = [base + sum26, dif08 + dif26, sum08 - r4, dif08 - dif26, base - sum26]
    sum17, dif17, sum35, dif35 = r1 + r7, r1 - r7, r3 + r5, r3 - r5
    odd = [sum17 + sum35, c1 * dif17 + c3 * dif35, c * (sum17 - sum35), c3 * dif17 - c1 * dif35]
    cosines = [even[a] + odd[a] for a in range(4)] + [even[4]]
    cosines += [even[8 - a] - odd[8 - a] for a in range(5, 9)]
    s17, d17, s35, d35 = i1 + i7, i1 - i7, i3 + i5, i3 - i5
    sines_odd = [None, c3 * s17 + c1 * s35, c * (d17 + d35), c1 * s17 - c3 * s35, d17 - d35]
    s26 = c * (i2 + i6)
    sines_even = [None, s26 + i4, i2 - i6, s26 - i4]
    sines = [None] + [sines_odd[a] + sines_even[a] for a in (1, 2, 3)] + [sines_odd[4]]
    sines += [sines_odd[8 - a] - sines_even[8 - a] for a in (5, 6, 7)]
    result = [cosines[0]] + [cosines[a] - sines[a] for a in range(1, 8)] + [cosines[8]]
    return result + [cosines[16 - a] + sines[16 - a] for a in range(9, 16)]


def open_rows(group, block, table, turn):
    both = dot(block, table[min(group, 1)])
    if group == 0:
        return both
    re, im = both[:, :INN], both[:, INN:]
    cos, sin = turn[group : group + 1, :], turn[CLS + group : CLS + group + 1, :]
    return jnp.concatenate([re * cos - im * sin, re * sin + im * cos], axis=1)


def open_class(group, low, high, columns, table, turn, opened):
    blocks = []
    for part in range(2):
        lanes = slice(part * 2 * LANE, (part + 1) * 2 * LANE)
        first, rest = low[:, lanes], high[:, lanes]
        if group == 0:
            lane = lax.broadcasted_iota(jnp.int32, (first.shape[0], LANE), 1)
            im = jnp.where(lane == 0, columns[part], first[:, LANE:])
            first = jnp.concatenate([first[:, :LANE], im], axis=1)
        blocks.append(jnp.concatenate([first, rest], axis=1))
    rows = blocks[0].shape[0]
    both = open_rows(group, jnp.concatenate(blocks, axis=0), table, turn)
    for part in range(2):
        opened[part, group] = both[part * rows : (part + 1) * rows]


def strip_intensity(opened, here, tile):
    total = None
    for part in range(2):
        re = [opened[part, g, here, tile * LANE : (tile + 1) * LANE] for g in range(CLS)]
        im = [opened[part, g, here, INN + tile * LANE : INN + (tile + 1) * LANE] for g in range(CLS)]
        values = sixteen_points(re, im)
        if total is None:
            total = [v * v for v in values]
        else:
            total = [t + v * v for t, v in zip(total, values)]
    return total


def row_inverse_kernel(plane, parts, nyquist, table, turn, out, edges, opened):
    current = plane + pl.program_id(0)
    rows = parts.shape[3]
    lane = lax.broadcasted_iota(jnp.int32, (rows, LANE), 1)
    columns = []
    for part in range(2):
        mine = jnp.where(lane == current * 2 + part, nyquist[...], 0.0)
        columns.append(jnp.sum(mine, axis=1, keepdims=True).astype(jnp.bfloat16))
    for group in range(CLS):
        low, high = (parts[group // 2, i, group % 2] for i in range(2))
        open_class(group, low, high, columns, table, turn, opened)

    def strip(i, carry):
        here = pl.ds(pl.multiple_of(i * 16, 16), 16)
        for tile in range(INN // LANE):
            total = strip_intensity(opened, here, tile)
            for a in range(OUT):
                lanes = slice(a * INN + tile * LANE, a * INN + (tile + 1) * LANE)
                out[0, here, lanes] = total[a].astype(jnp.bfloat16)
        return carry

    lax.fori_loop(0, rows // 16, strip, 0)
    edges[0, 0:8, :] = out[0, 0:16, :].astype(jnp.float32)[0:8]
    edges[0, 8:16, :] = out[0, rows - 16 :, :].astype(jnp.float32)[8:16]


def row_inverse(plane, count, parts, nyquist):
    rows = parts.shape[3]
    table, turn = (jnp.asarray(t) for t in row_inverse_tables())
    return pl.pallas_call(
        functools.partial(row_inverse_kernel, plane),
        grid=(count,),
        in_specs=[
            pl.BlockSpec((4, 2, 2, rows, 4 * LANE), lambda g: (0, 0, 0, 0, g)),
            pl.BlockSpec((rows, LANE), lambda g: (0, 0)),
            pl.BlockSpec((2, 2 * INN, 2 * INN), lambda g: (0, 0, 0)),
            pl.BlockSpec((2 * CLS, INN), lambda g: (0, 0)),
        ],
        out_specs=[
            pl.BlockSpec((1, rows, N), lambda g: (g, 0, 0)),
            pl.BlockSpec((1, 16, N), lambda g: (g, 0, 0)),
        ],
        out_shape=[
            jax.ShapeDtypeStruct((count, rows, N), jnp.bfloat16),
            jax.ShapeDtypeStruct((count, 16, N), jnp.float32),
        ],
        scratch_shapes=[pltpu.VMEM((2, CLS, rows, 2 * INN), jnp.float32)],
        compiler_params=pltpu.CompilerParams(vmem_limit_bytes=VMEM),
        cost_estimate=pl.CostEstimate(
            flops=count * 3 * 10**9, bytes_accessed=count * 8 * MIB, transcendentals=0
        ),
        name="row_inverse",
    )(parts, nyquist, table, turn)


def nyquist_kernel(planes, own, data, out):
    wide = lambda axis: lax.broadcasted_iota(jnp.int32, (INN, INN), axis)
    tall = lambda axis: lax.broadcasted_iota(jnp.int32, (OUT, INN), axis)
    small = lambda axis: lax.broadcasted_iota(jnp.int32, (OUT, OUT), axis)

    def wave(products, period):
        turn = (products % period).astype(jnp.float32) * (2.0 * math.pi / period)
        return jnp.cos(turn), jnp.sin(turn)

    def exact(left, right):
        return jnp.dot(left, right, preferred_element_type=jnp.float32, precision=lax.Precision.HIGHEST)

    def product(xr, xi, yr, yi):
        return exact(xr, yr) - exact(xi, yi), exact(xr, yi) + exact(xi, yr)

    def rotated(xr, xi, yr, yi):
        return xr * yr - xi * yi, xr * yi + xi * yr

    column = jnp.concatenate([data[i, 0:2, :].astype(jnp.float32) for i in range(8)], axis=0)
    wr, wi = wave(small(0) * small(1), OUT)
    inner_r, inner_i = wave(wide(0) * wide(1), INN)
    vr, vi = wave(tall(0) * tall(1), N)
    ar, ai = rotated(exact(wr, column), exact(-wi, column), vr, -vi)
    yr, yi = product(ar, ai, inner_r, -inner_i)
    fy = signed_fraction(tall(0) + OUT * tall(1))
    (kr, ki), (sr, si) = start_and_step(fy * fy + 0.25)
    block, blocks = own[0], own[1]
    k = lax.broadcasted_iota(jnp.int32, (8, OUT), 1)
    section = block // 2 + lax.broadcasted_iota(jnp.int32, (8, OUT), 0) + (OUT - 1)
    hr, hi = wave(k * (section % OUT), OUT)
    even = block % 2 == 0
    lane = lax.broadcasted_iota(jnp.int32, (1, LANE), 1)
    result, beside = [], []
    for g in range(planes):
        pr, pi = rotated(yr, yi, kr, ki)
        br, bi = rotated(*product(pr, pi, inner_r, inner_i), vr, vi)
        for value in product(hr, hi, br, bi):
            value = value * (1.0 / N)
            result.append(jnp.where(even, value[1:2, :LANE], value[1:2, LANE:]))
            above = jnp.where(even, value[0:1, INN - 1 :], value[1:2, LANE - 1 : LANE])
            above = jnp.where(block == 0, value[1:2, 0:1], above)
            below = jnp.where(even, value[1:2, LANE : LANE + 1], value[2:3, 0:1])
            below = jnp.where(block == blocks - 1, value[1:2, INN - 1 :], below)
            beside.append(jnp.where(lane == 0, above, jnp.where(lane == 1, below, 0.0)))
        kr, ki = rotated(kr, ki, sr, si)
    rest = [jnp.zeros((LANE - 2 * planes, LANE), jnp.float32)]
    out[:LANE, :] = jnp.concatenate(result + rest, axis=0).T
    out[LANE:, :] = jnp.concatenate(beside + rest, axis=0).T


def nyquist_column(own, planes, data):
    rows = data.shape[1] - 16
    return pl.pallas_call(
        functools.partial(nyquist_kernel, planes),
        grid_spec=pltpu.PrefetchScalarGridSpec(
            num_scalar_prefetch=1,
            grid=(1,),
            in_specs=[pl.BlockSpec((8, 16, 2 * LANE), lambda i, o: (0, rows // 16, 0))],
            out_specs=pl.BlockSpec((2 * LANE, LANE), lambda i, o: (0, 0)),
        ),
        out_shape=jax.ShapeDtypeStruct((2 * LANE, LANE), jnp.float32),
        compiler_params=pltpu.CompilerParams(vmem_limit_bytes=VMEM),
        cost_estimate=pl.CostEstimate(flops=10**9, bytes_accessed=2**18, transcendentals=0),
        name="nyquist",
    )(own, data)


TILE = 512


def across(centre, tile, west, east):
    lane = lax.broadcasted_iota(jnp.int32, centre.shape, 1)
    right = jnp.where(lane == TILE - 1, east, pltpu.roll(centre, TILE - 1, 1))
    left = jnp.where(lane == 0, west, pltpu.roll(centre, 1, 1))
    return (right - left) * (right - left)


def spatial_term(held, r, t):
    lanes = slice(t * TILE, (t + 1) * TILE)
    around = held[pl.ds(pl.multiple_of(r - 8, 8), 32), lanes]
    centre, down = around[8:24], around[9:25] - around[7:23]
    first, last = max(t * TILE - 1, 0), min((t + 1) * TILE, N - 1)
    here = pl.ds(r, 16)
    west, east = held[here, first : first + 1], held[here, last : last + 1]
    return centre, down * down + across(centre, TILE, west, east)


def hold(held, block, rows):
    held[8 : 8 + rows, :] = block.astype(jnp.float32)
    held[7:8, :] = held[8:9, :]
    held[8 + rows : 9 + rows, :] = held[7 + rows : 8 + rows, :]


def early_focus_kernel(first, others, best, spatial, held):
    rows = first.shape[1]
    for g in range(3):
        hold(held.at[g], first[0] if g == 0 else others[g - 1], rows)

    def strip(i, carry):
        r = pl.multiple_of(8 + i * 16, 8)
        here = pl.ds(pl.multiple_of(i * 16, 16), 16)
        for t in range(N // TILE):
            lanes = slice(t * TILE, (t + 1) * TILE)
            (c0, s0), (c1, s1), (c2, s2) = (spatial_term(held.at[g], r, t) for g in range(3))
            d0, d1 = c1 - c0, c2 - c0
            score = jnp.maximum(d0 * d0 + s0, d1 * d1 + s1)
            best[here, lanes] = (score * 0.125).astype(jnp.bfloat16)
            spatial[here, lanes] = s2.astype(jnp.bfloat16)
        return carry

    lax.fori_loop(0, rows // 16, strip, 0)


def early_focus(first, others):
    rows = first.shape[1]
    return pl.pallas_call(
        early_focus_kernel,
        out_shape=[
            jax.ShapeDtypeStruct((rows, N), jnp.bfloat16),
            jax.ShapeDtypeStruct((rows, N), jnp.bfloat16),
        ],
        scratch_shapes=[pltpu.VMEM((3, rows + 16, N), jnp.float32)],
        compiler_params=pltpu.CompilerParams(vmem_limit_bytes=VMEM),
        cost_estimate=pl.CostEstimate(flops=10**9, bytes_accessed=12 * MIB, transcendentals=0),
        name="early_focus",
    )(first, others)


def edge_rows(edges, halo):
    lane = lax.broadcasted_iota(jnp.int32, (2, N), 1)
    pair = lambda a, b: jnp.concatenate([a, b], axis=0)
    centre = [pair(e[0:1, :], e[15:16, :]) for e in edges]
    best = None
    for g, e in enumerate(edges):
        depth = centre[min(g + 1, 3)] - centre[max(g - 1, 0)]
        above, below = halo[2 * g : 2 * g + 1, :], halo[2 * g + 1 : 2 * g + 2, :]
        down = pair(e[1:2, :], below) - pair(above, e[14:15, :])
        c = centre[g]
        right = jnp.where(lane == N - 1, c, jnp.concatenate([c[:, 1:], c[:, :1]], axis=1))
        left = jnp.where(lane == 0, c, jnp.concatenate([c[:, -1:], c[:, :-1]], axis=1))
        score = depth * depth + down * down + (right - left) * (right - left)
        best = score if best is None else jnp.maximum(best, score)
    return best * 0.125


def last_rows_kernel(
    parts, best, spatial, others, nyquist_in, table_in, turn_in, edge0_in, edge12_in,
    upper_out, lower_out,
    both, nyquist, table, turn, edge0, edge12, part_buf, best_buf, spatial_buf, others_buf, opened, held, halo, edge, sems,
):
    rows = both.shape[0]
    loads = []
    for group in range(CLS):
        source = parts.at[group // 2, :, group % 2]
        loads.append(pltpu.make_async_copy(source, part_buf.at[group], sems.at[0, group]))
    late = (best, best_buf), (spatial, spatial_buf), (others, others_buf)
    late += (edge0_in, edge0), (edge12_in, edge12)
    for i, (source, target) in enumerate(late):
        loads.append(pltpu.make_async_copy(source, target, sems.at[1, i]))
    early = (nyquist_in, nyquist), (table_in, table), (turn_in, turn)
    early = [pltpu.make_async_copy(a, b, sems.at[2, i]) for i, (a, b) in enumerate(early)]
    for load in early + loads:
        load.start()
    for load in early:
        load.wait()
    lane = lax.broadcasted_iota(jnp.int32, (rows, LANE), 1)
    few_lane = lax.broadcasted_iota(jnp.int32, (16, LANE), 1)
    few_row = lax.broadcasted_iota(jnp.int32, (16, LANE), 0)
    beside = jnp.where(few_row % 2 == 0, nyquist[rows : rows + 1, :], nyquist[rows + 1 : rows + 2, :])
    columns = []
    for part in range(2):
        mine = jnp.where(lane == 6 + part, nyquist[:rows, :], 0.0)
        few = jnp.where(few_lane == (few_row // 2) * 2 + part, beside, 0.0)
        column = jnp.sum(jnp.concatenate([mine, few], axis=0), axis=1, keepdims=True)
        columns.append(column.astype(jnp.bfloat16))
    for group in range(CLS):
        loads[group].wait()
        low, high = part_buf[group, 0], part_buf[group, 1]
        open_class(group, low, high, columns, table, turn, opened)

    def strip(i, carry):
        base = pl.multiple_of(i * 8, 8)
        for tile in range(INN // LANE):
            for a, value in enumerate(strip_intensity(opened, pl.ds(base, 8), tile)):
                lanes = slice(a * INN + tile * LANE, a * INN + (tile + 1) * LANE)
                value = value.astype(jnp.bfloat16).astype(jnp.float32)
                held[pl.ds(pl.multiple_of(base + 8, 8), 8), lanes] = value
        return carry

    lax.fori_loop(0, rows // 8 + 1, strip, 0)
    halo[...] = held[8 + rows : 16 + rows, :]
    held[7:8, :] = held[8:9, :]
    held[8 + rows : 9 + rows, :] = held[7 + rows : 8 + rows, :]
    edge[0:8, :] = held[8:16, :]
    edge[8:16, :] = held[rows : rows + 8, :]
    for load in loads[CLS:]:
        load.wait()
    ends = edge_rows([edge0.at[0], edge12.at[0], edge12.at[1], edge], halo)

    def measure(i, carry):
        r = pl.multiple_of(8 + i * 16, 8)
        here = pl.ds(pl.multiple_of(i * 16, 16), 16)
        for t in range(N // TILE):
            lanes = slice(t * TILE, (t + 1) * TILE)
            centre, term = spatial_term(held, r, t)
            d2 = centre - others_buf[0, here, lanes].astype(jnp.float32)
            d3 = centre - others_buf[1, here, lanes].astype(jnp.float32)
            score = jnp.maximum(d2 * d2 + spatial_buf[here, lanes].astype(jnp.float32), d3 * d3 + term)
            score = jnp.maximum(score * 0.125, best_buf[here, lanes].astype(jnp.float32))
            both[here, lanes] = score.astype(jnp.bfloat16)
        return carry

    half = rows // 2
    stores = []
    for side, out in enumerate((upper_out, lower_out)):
        lax.fori_loop(side * (half // 16), (side + 1) * (half // 16), measure, 0)
        here = slice(0, 16) if side == 0 else slice(rows - 16, rows)
        index = lax.broadcasted_iota(jnp.int32, (16, N), 0)
        value = jnp.where(index == 15 * side, ends[side : side + 1], both[here].astype(jnp.float32))
        both[here] = value.astype(jnp.bfloat16)
        source = both.at[pl.ds(side * half, half)]
        stores.append(pltpu.make_async_copy(source, out, sems.at[2, 3 + side]))
        stores[-1].start()
    for store in stores:
        store.wait()


def last_rows(parts, nyquist, best, spatial, others, edge0, edge12):
    rows = best.shape[0]
    table, turn = (jnp.asarray(t) for t in row_inverse_tables())
    hbm = pl.BlockSpec(memory_space=pl.ANY)
    bf16, f32 = jnp.bfloat16, jnp.float32
    return pl.pallas_call(
        last_rows_kernel,
        in_specs=[hbm] * 9,
        out_specs=[hbm] * 2,
        out_shape=[jax.ShapeDtypeStruct((rows // 2, N), bf16)] * 2,
        scratch_shapes=[
            pltpu.VMEM((rows, N), bf16),
            pltpu.VMEM((2 * LANE, LANE), f32),
            pltpu.VMEM((2, 2 * INN, 2 * INN), bf16),
            pltpu.VMEM((2 * CLS, INN), f32),
            pltpu.VMEM((1, 16, N), f32),
            pltpu.VMEM((2, 16, N), f32),
            pltpu.VMEM((CLS, 2, rows + 16, 4 * LANE), bf16),
            pltpu.VMEM((rows, N), bf16),
            pltpu.VMEM((rows, N), bf16),
            pltpu.VMEM((2, rows, N), bf16),
            pltpu.VMEM((2, CLS, rows + 16, 2 * INN), f32),
            pltpu.VMEM((rows + 16, N), f32),
            pltpu.VMEM((8, N), f32),
            pltpu.VMEM((16, N), f32),
            pltpu.SemaphoreType.DMA((3, CLS)),
        ],
        compiler_params=pltpu.CompilerParams(vmem_limit_bytes=VMEM),
        cost_estimate=pl.CostEstimate(flops=3 * 10**9, bytes_accessed=16 * MIB, transcendentals=0),
        name="last_rows",
    )(parts, best, spatial, others, nyquist, table, turn, edge0, edge12)


def assemble_kernel(own, *refs):
    slot, out = pl.program_id(0), refs[-1]
    half = refs[0].shape[0]
    for s in range(3):

        @pl.when(slot == s)
        def _():
            out[:half] = refs[s][...].astype(jnp.float32)
            out[half:] = refs[3 + s][...].astype(jnp.float32)


def assemble(depth_index, upper, lower):
    half = upper[0].shape[0]
    whole = pl.BlockSpec((half, N), lambda s, o: (0, 0))
    return pl.pallas_call(
        assemble_kernel,
        grid_spec=pltpu.PrefetchScalarGridSpec(
            num_scalar_prefetch=1,
            grid=(3,),
            in_specs=[whole] * 6,
            out_specs=pl.BlockSpec((2 * half, N), lambda s, o: (jnp.bitwise_xor(s, o[0]), 0)),
        ),
        out_shape=jax.ShapeDtypeStruct((8 * half, N), jnp.float32),
        compiler_params=pltpu.CompilerParams(vmem_limit_bytes=20 * MIB),
        cost_estimate=pl.CostEstimate(flops=10**6, bytes_accessed=10 * MIB, transcendentals=0),
        name="assemble",
    )(depth_index, *upper, *lower)


def complete_kernel(own, upper, lower, whole, out):
    half = lower.shape[0] // 2
    step = pl.program_id(0)
    for s, ref in enumerate((upper, lower)):
        for part in range(2):

            @pl.when(step == 2 * s + part)
            def _():
                out[...] = ref[part * half : (part + 1) * half].astype(jnp.float32)


def complete(depth_index, upper, lower, whole):
    half = upper.shape[0]
    both = pl.BlockSpec((half, N), lambda i, o: (0, 0))
    place = lambda i, o: (jnp.bitwise_xor(3, o[0]) * 4 + i, 0)
    return pl.pallas_call(
        complete_kernel,
        grid_spec=pltpu.PrefetchScalarGridSpec(
            num_scalar_prefetch=1,
            grid=(4,),
            in_specs=[both, both, pl.BlockSpec(memory_space=pl.ANY)],
            out_specs=pl.BlockSpec((half // 2, N), place),
        ),
        out_shape=jax.ShapeDtypeStruct(whole.shape, jnp.float32),
        input_output_aliases={3: 0},
        compiler_params=pltpu.CompilerParams(vmem_limit_bytes=20 * MIB),
        cost_estimate=pl.CostEstimate(flops=10**6, bytes_accessed=3 * MIB, transcendentals=0),
        name="complete",
    )(depth_index, upper, lower, whole)


OVER_X = [(i, i ^ 1) for i in range(4)]
OVER_Y = [(i, i ^ 2) for i in range(4)]


def exchange_depth(a, b):
    ax, by = lax.ppermute(a, "depth", OVER_X), lax.ppermute(b, "depth", OVER_Y)
    ay, axy = lax.ppermute(a, "depth", OVER_Y), lax.ppermute(ax, "depth", OVER_Y)
    bx, byx = lax.ppermute(b, "depth", OVER_X), lax.ppermute(by, "depth", OVER_X)
    return (a, ax, ay, axy), (b, bx, by, byx)


def border_rows(halfway, outside, high):
    lanes = 4 * LANE
    count = halfway.shape[-1] // lanes
    natural = lambda rows: rows.reshape(4, 2, 2, count, lanes).transpose(1, 2, 0, 3, 4).reshape(16, count, lanes)
    first, last = natural(halfway[..., 0, :]), natural(halfway[..., -1, :])
    above = jnp.where(high == 0, first[:1], outside[None, :, 15])
    below = jnp.where(high == 0, outside[None, :, 0], last[-1:])
    above = jnp.concatenate([above, last[:-1]])
    below = jnp.concatenate([first[1:], below])
    both = jnp.stack([above, below], axis=2).reshape(2, 2, 4, 2 * count, lanes)
    return both.transpose(2, 0, 1, 3, 4).reshape(16, 2 * count, lanes)


def half_spectrum_shards(hologram, background):
    rows = hologram.shape[0]
    planes = lax.axis_size("depth") * PL_DEV
    depth, high = lax.axis_index("depth"), lax.axis_index("high")
    low, core = lax.axis_index("low"), lax.axis_index("core")
    as_scalar = lambda value: jnp.reshape(value, (1,)).astype(jnp.int32)
    own = rows // 4
    block = ((high * 2 + low) * 2 + core) * 4 + depth
    place = jnp.stack([block, jnp.int32(N // own)]).astype(jnp.int32)

    sections = row_forward(as_scalar(depth), hologram, background)
    data = lax.all_to_all(
        sections.reshape(8, rows + 16, 2 * LANE),
        ("high", "low", "core"),
        split_axis=0,
        concat_axis=0,
        tiled=True,
    )

    group = depth * 2 + core
    slot = low * LANE + jnp.arange(LANE, dtype=jnp.int32)
    special = jnp.where(low == 0, 0, CLS) + OUT * jnp.arange(LANE, dtype=jnp.int32)
    fx = signed_fraction(jnp.where(group == 0, special, group + OUT * slot))
    kernels = propagators(planes, (fx * fx)[None])

    def to_rows(halfway):
        parts = lax.all_to_all(
            halfway.reshape(16, -1, halfway.shape[-1]),
            ("depth", "low", "core"),
            split_axis=0,
            concat_axis=0,
            tiled=True,
        )
        return parts.reshape(4, 2, 2, -1, halfway.shape[-1])

    halfway, spectrum, outside = first_columns(as_scalar(high), data, kernels)
    parts, borders = [to_rows(halfway)], [border_rows(halfway, outside, high)]
    for plane, count in ((1, 2), (3, 1)):
        halfway, outside = next_columns(as_scalar(high), plane, count, spectrum, kernels)
        borders.append(border_rows(halfway, outside, high))
        halfway = halfway.reshape(16, own, -1)
        if plane == 3:
            below = jnp.concatenate(borders, axis=1)
            below = jnp.pad(below, ((0, 0), (0, 16 - 2 * planes), (0, 0)))
            halfway = jnp.concatenate([halfway, below], axis=1)
        ready = parts[-1]
        if plane == 3:
            first, first_edge = row_inverse(0, 1, parts[0], middle)
            ready = ready, first, first_edge
        elif plane == 1:
            middle = nyquist_column(place, planes, data)
            ready = ready, middle
        halfway, ready = lax.optimization_barrier((halfway, ready))
        if plane == 3:
            parts[-1], first, first_edge = ready
        else:
            parts[-1], middle = ready
        parts.append(to_rows(halfway))
    others, others_edge = row_inverse(1, 2, parts[1], middle)
    best, spatial = early_focus(first, others)
    upper, lower = last_rows(parts[2], middle, best, spatial, others, first_edge, others_edge)
    upper, lower = exchange_depth(upper, lower)
    whole = assemble(as_scalar(depth), upper[:3], lower[:3])
    return complete(as_scalar(depth), upper[3], lower[3], whole)


def solution(mesh):
    spec = P("rows", None)
    if mesh.shape["depth"] == 4 and mesh.shape["rows"] == 8:
        split = Mesh(mesh.devices.reshape(4, 2, 2, 2), ("depth", "high", "low", "core"))
        spec = P(("high", "low", "core"), None)
        body = half_spectrum_shards
    else:
        split, body = mesh, shards
    return jax.shard_map(body, mesh=split, in_specs=(spec, spec), out_specs=spec, check_vma=False)
```

```python
import functools
import math

import jax
import jax.numpy as jnp
import numpy as np
from jax import lax
from jax.experimental import pallas as pl
from jax.experimental.pallas import tpu as pltpu
from jax.sharding import Mesh
from jax.sharding import PartitionSpec as P

N = 4096
RADIX = 64
PL_DEV = 1


wave_number = 0.6
depth_start = 8.0
depth_step = 2.0


def padded_2(block, sides, width):
    for axis, dim in sides:
        count = lax.axis_size(axis)
        forward = [(i, i + 1) for i in range(count - 1)]
        backward = [(target, source) for source, target in forward]
        low = lax.ppermute(
            lax.slice_in_dim(block, block.shape[dim] - width, None, axis=dim), axis, forward
        )
        high = lax.ppermute(lax.slice_in_dim(block, 0, width, axis=dim), axis, backward)
        block = jnp.concatenate([low, block, high], axis=dim)
    return block


def fourier_tables(radix_size, sign_value):
    indices = jnp.arange(radix_size, dtype=jnp.int32)
    products = indices[:, None] * indices[None, :] % radix_size
    angles = products.astype(jnp.float32) * (sign_value * 2.0 * math.pi / radix_size)
    scaling = 1.0 / math.sqrt(radix_size)
    cosine_part = jnp.cos(angles) * scaling
    sine_part = jnp.sin(angles) * scaling
    matrix = jnp.stack([jnp.stack([cosine_part, -sine_part]), jnp.stack([sine_part, cosine_part])])
    return matrix.astype(jnp.bfloat16)


def twiddle_table(radix_size, sign_value):
    indices = jnp.arange(radix_size, dtype=jnp.int32)
    total = radix_size * radix_size
    products = indices[:, None] * indices[None, :] % total
    angles = products.astype(jnp.float32) * (sign_value * 2.0 * math.pi / total)
    return (jnp.cos(angles), jnp.sin(angles))


def rotate(data, cosine_part, sine_part):
    return jnp.stack(
        [data[0] * cosine_part - data[1] * sine_part, data[0] * sine_part + data[1] * cosine_part]
    )


def contract(form, matrix, data):
    return jnp.einsum(form, matrix, data, preferred_element_type=jnp.float32)


def forward_real(data):
    batch_size = data.shape[1]
    shaped = data.reshape(RADIX, RADIX, batch_size)
    matrix = fourier_tables(RADIX, -1.0)
    cosine_part, sine_part = twiddle_table(RADIX, -1.0)
    opening = contract("oka,abm->okbm", matrix[:, 0], shaped)
    sectioned = rotate(opening, cosine_part[:, :, None], sine_part[:, :, None]).astype(jnp.bfloat16)
    closing = contract("ocjb,ckbm->okjm", matrix, sectioned)
    return closing.reshape(2, N, batch_size).astype(jnp.bfloat16)


def forward_first(data):
    batch_size = data.shape[2]
    shaped = data.reshape(2, RADIX, RADIX, batch_size)
    matrix = fourier_tables(RADIX, -1.0)
    cosine_part, sine_part = twiddle_table(RADIX, -1.0)
    opening = contract("ocka,cabm->okbm", matrix, shaped)
    sectioned = rotate(opening, cosine_part[:, :, None], sine_part[:, :, None]).astype(jnp.bfloat16)
    closing = contract("ocjb,ckbm->okjm", matrix, sectioned)
    return closing.reshape(2, N, batch_size).astype(jnp.bfloat16)


def inverse_first(data):
    batch_size = data.shape[2]
    shaped = data.reshape(2, RADIX, RADIX, batch_size)
    matrix = fourier_tables(RADIX, 1.0)
    cosine_part, sine_part = twiddle_table(RADIX, 1.0)
    opening = contract("ocbj,ckjm->okbm", matrix, shaped)
    sectioned = rotate(opening, cosine_part[:, :, None], sine_part[:, :, None]).astype(jnp.bfloat16)
    closing = contract("ocak,ckbm->oabm", matrix, sectioned)
    return closing.reshape(2, N, batch_size)


def frequencies(positions):
    natural = positions // RADIX + RADIX * (positions % RADIX)
    signed_freq = jnp.where(natural >= N // 2, natural - N, natural)
    return signed_freq.astype(jnp.float32) / N


def propagator(freq_whole, freq_own, distance):
    radial = freq_whole[:, None] ** 2 + freq_own[None, :] ** 2
    limit = wave_number * wave_number
    amplitude = jnp.exp(-2.0 * math.pi * distance * jnp.sqrt(jnp.maximum(radial - limit, 0.0)))
    phase_angle = (
        2.0 * math.pi * distance * (jnp.sqrt(jnp.maximum(limit - radial, 0.0)) - wave_number)
    )
    return (amplitude * jnp.cos(phase_angle), amplitude * jnp.sin(phase_angle))


def propagate(spectrum, cosine_part, sine_part):
    return rotate(spectrum.astype(jnp.float32), cosine_part, sine_part).astype(jnp.bfloat16)


def shards(hologram, background):
    row_count = hologram.shape[0]
    contrast = (hologram.astype(jnp.float32) / background.astype(jnp.float32) - 1.0).astype(
        jnp.bfloat16
    )
    along_rows = forward_real(contrast.T)
    columns = lax.all_to_all(
        jnp.swapaxes(along_rows, 1, 2), "rows", split_axis=2, concat_axis=1, tiled=True
    )
    spectrum = forward_first(columns)
    row_index = lax.axis_index("rows")
    own_positions = row_index * row_count + jnp.arange(row_count, dtype=jnp.int32)
    freq_own = frequencies(own_positions)
    freq_whole = frequencies(jnp.arange(N, dtype=jnp.int32))
    depth_index = lax.axis_index("depth")
    distance = depth_start + depth_step * (depth_index * PL_DEV + 0).astype(jnp.float32)
    cosine_part, sine_part = propagator(freq_whole, freq_own, distance)
    propagated = propagate(spectrum, cosine_part, sine_part)
    halfway = inverse_first(propagated).astype(jnp.bfloat16)
    restored = lax.all_to_all(
        jnp.swapaxes(halfway, 1, 2), "rows", split_axis=2, concat_axis=1, tiled=True
    )
    result_field = inverse_first(restored)
    intensities = [
        (result_field[0] * result_field[0] + result_field[1] * result_field[1]).astype(jnp.bfloat16)
    ]
    stacked = jnp.stack(intensities)
    padded = padded_2(stacked, (("depth", 0), ("rows", 2)), 1)
    centre_block = padded[1:-1, :, 1:-1]
    plane_ids = jnp.arange(PL_DEV, dtype=jnp.int32)[:, None, None]
    row_ids = jnp.arange(row_count, dtype=jnp.int32)[None, None, :]
    depth_count = lax.axis_size("depth")
    row_groups = lax.axis_size("rows")
    lower_plane = jnp.where(
        (depth_index == 0) & (plane_ids == 0), centre_block, padded[:-2, :, 1:-1]
    )
    upper_plane = jnp.where(
        (depth_index == depth_count - 1) & (plane_ids == PL_DEV - 1),
        centre_block,
        padded[2:, :, 1:-1],
    )
    north_row = jnp.where((row_index == 0) & (row_ids == 0), centre_block, padded[1:-1, :, :-2])
    south_row = jnp.where(
        (row_index == row_groups - 1) & (row_ids == row_count - 1),
        centre_block,
        padded[1:-1, :, 2:],
    )
    centre = centre_block.astype(jnp.float32)
    east_col = jnp.concatenate([centre[:, 1:], centre[:, -1:]], axis=1)
    west_col = jnp.concatenate([centre[:, :1], centre[:, :-1]], axis=1)
    depth_diff = upper_plane.astype(jnp.float32) - lower_plane.astype(jnp.float32)
    row_diff = south_row.astype(jnp.float32) - north_row.astype(jnp.float32)
    col_diff = east_col - west_col
    scores = (depth_diff * depth_diff + row_diff * row_diff + col_diff * col_diff) / 8.0
    sharpest = jnp.max(scores, axis=0)
    merged = lax.pmax(sharpest.astype(jnp.bfloat16), "depth").astype(sharpest.dtype)
    return merged.T


OUT = 16
INN = 256
CLS = 8
LANE = 128
MIB = 2**20
VMEM = 63 * MIB
SHARED = 36 * MIB


def slot_frequencies():
    table = np.arange(CLS)[:, None] + OUT * np.arange(INN)[None, :]
    half = np.arange(INN // 2)
    table[0] = np.concatenate([OUT * half, CLS + OUT * half])
    return table


def angles(products):
    return 2.0 * np.pi * (products % N) / N


def row_forward_tables():
    freq = slot_frequencies()
    theta = angles(np.arange(INN)[None, :, None] * freq[:, None, :])
    cos, sin = np.cos(theta) / 64.0, np.sin(theta) / 64.0
    top = np.stack([cos, -sin], axis=2)
    low = np.stack([sin, cos], axis=2)
    first = np.arange(INN) < INN // 2
    low[0] = np.where(first, 0.0, top[0])
    top[0] = np.where(first, top[0], 0.0)
    full = np.concatenate([top, low], axis=1)
    full = full.reshape(CLS, 2 * INN, 2, 2, LANE).transpose(0, 1, 3, 2, 4)
    return full.reshape(CLS, 2 * INN, 2 * INN).astype(jnp.bfloat16)


def row_forward_weights():
    a = np.arange(1, 5)
    rows = []
    for d in range(CLS // 2):
        even, odd = (2.0 * np.pi * c * a / OUT for c in (2 * d, 2 * d + 1))
        parts = np.cos(even), -np.sin(even[:3]), [float(d == 0)], np.cos(odd[:3]), -np.sin(odd), [0.0]
        rows.append(np.concatenate(parts))
    return np.concatenate(rows).astype(np.float32)


def row_inverse_tables():
    half = np.arange(INN // 2)
    position = np.arange(INN)[None, :]
    full = np.zeros((2, 2, INN, 2, INN))
    for first, place in ((0, 0), (CLS, 1)):
        theta = angles((first + OUT * half)[:, None] * position)
        rows = slice(place * INN // 2, (place + 1) * INN // 2)
        full[0, 0, rows, place], full[0, 1, rows, place] = np.cos(theta), -np.sin(theta)
    full[0, 0, 0, 0] = 0.5
    full[0, 1, 0, 0] = 0.5 * (-1.0) ** np.arange(INN)
    theta = angles(OUT * np.arange(INN)[:, None] * position)
    full[1, 0, :, 0], full[1, 0, :, 1] = np.cos(theta), np.sin(theta)
    full[1, 1, :, 0], full[1, 1, :, 1] = -np.sin(theta), np.cos(theta)
    full = full.reshape(2, 2, 2, LANE, 2 * INN).transpose(0, 2, 1, 3, 4) / 32.0
    turn = angles(np.arange(CLS)[:, None] * position)
    turn = np.concatenate([np.cos(turn), np.sin(turn)]).astype(np.float32)
    return full.reshape(2, 2 * INN, 2 * INN).astype(jnp.bfloat16), turn


def column_tables():
    turn = 2.0 * np.pi * np.arange(OUT)[:, None] * np.arange(OUT)[None, :] / OUT
    eye = np.eye(16)
    outer_cos, outer_sin = np.kron(np.cos(turn), eye) / 4.0, np.kron(np.sin(turn), eye) / 4.0
    complex_form = lambda cos, sin: np.concatenate(
        [np.concatenate([cos, -sin], axis=-1), np.concatenate([sin, cos], axis=-1)], axis=-2
    )
    slabs = lambda table: table.reshape(-1, 8, 2, 16).swapaxes(1, 2).reshape(table.shape)
    outer = complex_form(slabs(outer_cos), slabs(-outer_sin))
    half_rows = outer_cos.shape[0] // 2
    cut = lambda table, begin, size: table[begin : begin + size]
    back = np.stack(
        [
            complex_form(cut(outer_cos, begin, half_rows), cut(outer_sin, begin, half_rows))
            for begin in (0, half_rows)
        ]
    )
    beyond = np.stack(
        [complex_form(cut(outer_cos, a * 16, 16), cut(outer_sin, a * 16, 16)) for a in (8, 7)]
    )
    theta = angles(OUT * np.arange(INN)[:, None] * np.arange(INN)[None, :])
    inner = complex_form(np.cos(theta), -np.sin(theta)) / 16.0
    inner_back = complex_form(np.cos(theta), np.sin(theta)) / 16.0
    turn = angles(np.arange(OUT)[:, None] * np.arange(INN)[None, :])
    by_chunk = turn.reshape(OUT, 16, 16).swapaxes(1, 2).reshape(INN, 16)
    twist = np.zeros((2, INN, LANE), np.float32)
    for i, table in enumerate((by_chunk, turn.T)):
        twist[i, :, :16], twist[i, :, 16:32] = np.cos(table), np.sin(table)
    cast = lambda table: table.astype(jnp.bfloat16)
    return cast(outer), cast(inner), cast(inner_back), cast(back), cast(beyond), twist


def dot(left, right):
    return jnp.dot(left, right, preferred_element_type=jnp.float32)


def split_complex(both, width):
    rows = both.shape[0] // 2
    top, low = both[:rows], both[rows:]
    return top[:, :width] - low[:, width:], top[:, width:] + low[:, :width]


def quarter_kernel(radial):
    gap = wave_number * wave_number - radial
    root = jnp.sqrt(jnp.abs(gap))
    inside = gap > 0.0
    half_pi = 0.5 * math.pi
    angle = half_pi * (jnp.where(inside, root, 0.0) - wave_number)
    decay = jnp.exp(jnp.where(inside, 0.0, -half_pi * root))
    square = angle * angle
    sine = 1.0 / 362880.0
    for c in (-1.0 / 5040.0, 1.0 / 120.0, -1.0 / 6.0, 1.0):
        sine = sine * square + c
    cosine = -1.0 / 3628800.0
    for c in (1.0 / 40320.0, -1.0 / 720.0, 1.0 / 24.0, -0.5, 1.0):
        cosine = cosine * square + c
    return decay * cosine, decay * (sine * angle)


def squared(re, im):
    return (re - im) * (re + im), 2.0 * re * im


def start_and_step(radial):
    value = quarter_kernel(radial)
    distance = 0.25
    step = None
    while distance < depth_start:
        value = squared(*value)
        distance *= 2.0
        if distance == depth_step:
            step = value
    return value, step


def signed_fraction(natural):
    return jnp.where(natural >= N // 2, natural - N, natural).astype(jnp.float32) * (1.0 / N)


CHUNK = 64
BATCHES = ((0,), (1, 2), (3, 4), (5, 6, 7))


def sixteen_sums(term, w):
    c0, c8 = term(0), term(8)
    plus, minus = c0 + c8, c0 - c8
    c4, c12 = term(4), term(12)
    e4, o4 = c4 + c12, c4 - c12
    total = plus + e4
    eighth = total
    re_even = plus + w(3) * e4
    im_even = None
    re_odd, im_odd = minus, w(14) * o4
    for a in (1, 2, 3):
        p, q, r, s = term(a), term(16 - a), term(8 - a), term(8 + a)
        e, o, f, h = p + q, p - q, r + s, r - s
        both = e + f
        total = total + both
        eighth = eighth - both if a % 2 else eighth + both
        re_even = re_even + w(a - 1) * both
        term_im = w(3 + a) * (o - h)
        im_even = term_im if im_even is None else im_even + term_im
        re_odd = re_odd + w(7 + a) * (e - f)
        im_odd = im_odd + w(10 + a) * (o + h)
    return re_even, im_even + w(7) * eighth, re_odd, im_odd, total


def row_forward_kernel(
    own, weights, holo, back, table, out, holo_buf, back_buf, table_buf, acc, result, held, sems
):
    rows = holo.shape[0]
    group = own[0]
    chunks = rows // CHUNK
    loads = []
    for i in range(chunks):
        here = pl.ds(i * CHUNK, CHUNK)
        loads.append(
            (
                pltpu.make_async_copy(holo.at[here], holo_buf.at[here], sems.at[0, i]),
                pltpu.make_async_copy(back.at[here], back_buf.at[here], sems.at[1, i]),
            )
        )
        for load in loads[-1]:
            load.start()
        if i == 0:
            tables = pltpu.make_async_copy(table.at[pl.ds(2 * group, 2)], table_buf, sems.at[4, 0])
            tables.start()
    lane = lax.broadcasted_iota(jnp.int32, (16, INN), 1)
    sign = jnp.where(lane % 2 == 0, 1.0, -1.0).astype(jnp.bfloat16)
    stores = []
    for chunk in range(chunks):
        for load in loads[chunk]:
            load.wait()

        def strip(i, carry):
            here = pl.ds(pl.multiple_of(chunk * CHUNK + i * 16, 16), 16)

            def term(a):
                there = pl.ds(a * INN, INN)
                below = back_buf[here, there].astype(jnp.float32)
                inverse = pl.reciprocal(below, approx=True)
                inverse = inverse * (2.0 - below * inverse)
                value = holo_buf[here, there].astype(jnp.float32) * inverse
                return (value - 1.0).astype(jnp.bfloat16).astype(jnp.float32)

            sums = sixteen_sums(term, lambda n: weights[group * 16 + n])
            for q in range(4):
                acc[q // 2, here, pl.ds((q % 2) * INN, INN)] = sums[q].astype(jnp.bfloat16)
            acc[2, here, pl.ds(0, INN)] = sums[4].astype(jnp.bfloat16)
            return carry

        lax.fori_loop(0, CHUNK // 16, strip, 0)
        batch = rows // 2 // CHUNK
        if chunk % batch != batch - 1:
            continue
        if chunk < batch:
            tables.wait()
        begin, end = (chunk + 1 - batch) * CHUNK, (chunk + 1) * CHUNK
        for q in range(2):
            both = dot(acc[q, begin:end], table_buf[q]).astype(jnp.bfloat16)
            for low in range(2):
                part = both[:, low * 2 * LANE : (low + 1) * 2 * LANE]
                result[low, q, begin:end, :] = part
        held[chunk // batch] = lax.dot_general(
            sign,
            acc[2, begin:end, :INN],
            (((1,), (1,)), ((), ())),
            preferred_element_type=jnp.float32,
        )
        here = pl.ds(begin, end - begin)
        if chunk == chunks - 1:
            index = lax.broadcasted_iota(jnp.int32, (16, INN), 0)
            extra = jnp.where(index == 0, held[0], held[1]) * (1.0 / 64.0)
            for low in range(2):
                for q in range(2):
                    result[low, q, rows:, :] = extra.astype(jnp.bfloat16)
            here = pl.ds(begin, end - begin + 16)
        for high in range(2):
            source, target = result.at[:, :, here, :], out.at[high, :, :, here, :]
            stores.append(pltpu.make_async_copy(source, target, sems.at[2 + high, chunk]))
            stores[-1].start()
    for store in stores:
        store.wait()


def row_forward(own, hologram, background):
    rows = hologram.shape[0]
    table = jnp.asarray(row_forward_tables())
    weights = jnp.asarray(row_forward_weights())
    hbm = pl.BlockSpec(memory_space=pl.ANY)
    chunks = rows // CHUNK
    return pl.pallas_call(
        row_forward_kernel,
        grid_spec=pltpu.PrefetchScalarGridSpec(
            num_scalar_prefetch=2,
            grid=(1,),
            in_specs=[hbm] * 3,
            out_specs=hbm,
            scratch_shapes=[
                pltpu.VMEM((rows, N), jnp.bfloat16),
                pltpu.VMEM((rows, N), jnp.bfloat16),
                pltpu.VMEM((2, 2 * INN, 2 * INN), jnp.bfloat16),
                pltpu.VMEM((3, rows, 2 * INN), jnp.bfloat16),
                pltpu.VMEM((2, 2, rows + 16, 2 * LANE), jnp.bfloat16),
                pltpu.VMEM((2, 16, INN), jnp.float32),
                pltpu.SemaphoreType.DMA((5, chunks)),
            ],
        ),
        out_shape=jax.ShapeDtypeStruct((2, 2, 2, rows + 16, 2 * LANE), jnp.bfloat16),
        compiler_params=pltpu.CompilerParams(vmem_limit_bytes=VMEM),
        cost_estimate=pl.CostEstimate(flops=10**10, bytes_accessed=12 * MIB, transcendentals=0),
        name="row_forward",
    )(own, weights, hologram, background, table)


def propagator_kernel(planes, fx2, out):
    step = pl.program_id(0)
    strip = 32
    for i in range(INN // strip):
        rows = slice(i * strip, (i + 1) * strip)
        position = lax.broadcasted_iota(jnp.int32, (strip, LANE), 0) + i * strip
        fy = signed_fraction(step + OUT * position)
        (kr, ki), (sr, si) = start_and_step(fy * fy + fx2[...])
        for g in range(planes):
            out[g, 0, rows, :LANE] = kr.astype(jnp.bfloat16)
            out[g, 0, rows, LANE:] = ki.astype(jnp.bfloat16)
            if g + 1 < planes:
                kr, ki = kr * sr - ki * si, kr * si + ki * sr


def propagators(planes, fx2):
    return pl.pallas_call(
        functools.partial(propagator_kernel, planes),
        grid=(OUT,),
        in_specs=[pl.BlockSpec((1, LANE), lambda i: (0, 0))],
        out_specs=pl.BlockSpec((planes, 1, INN, 2 * LANE), lambda i: (0, i, 0, 0)),
        out_shape=jax.ShapeDtypeStruct((planes, OUT, INN, 2 * LANE), jnp.bfloat16),
        compiler_params=pltpu.CompilerParams(vmem_limit_bytes=VMEM),
        cost_estimate=pl.CostEstimate(flops=10**9, bytes_accessed=16 * MIB, transcendentals=10**6),
        name="propagators",
    )(fx2)


PAIRS = OUT // 2


def mix_and_open(pair, both, kernels, inner_back, twist, mixed, second):
    wide = 2 * LANE
    for k in range(2):
        yr, yi = (both[p * INN : (p + 1) * INN, k * LANE : (k + 1) * LANE] for p in range(2))
        for part in range(2):
            factor = kernels[k, :, part * LANE : (part + 1) * LANE].astype(jnp.float32)
            lanes = slice(k * wide + part * LANE, k * wide + (part + 1) * LANE)
            mixed[:INN, lanes] = (yr * factor).astype(jnp.bfloat16)
            mixed[INN:, lanes] = (yi * factor).astype(jnp.bfloat16)
    opened = dot(inner_back[...], mixed[...])
    for k in range(2):
        at = pair * 2 + k
        re, im = (opened[p * INN : (p + 1) * INN, k * wide : (k + 1) * wide] for p in range(2))
        cos, sin = twist[1, :, at : at + 1], twist[1, :, 16 + at : 17 + at]
        second[0, at] = (re * cos - im * sin).astype(jnp.bfloat16)
        second[1, at] = (re * sin + im * cos).astype(jnp.bfloat16)


def outer_block(second, here):
    return second[:, :, here, :].reshape(2 * OUT * 16, 2 * LANE)


def spread(both):
    rows = both.shape[0] // 2
    re, im = both[:rows], both[rows:]
    return [re[:, :LANE], im[:, :LANE], re[:, LANE:], im[:, LANE:]]


def open_outside(half, beyond, second, outside):
    here = pl.ds(pl.multiple_of(half[0] * (INN - 16), 16), 16)
    both = dot(beyond, outer_block(second, here)).astype(jnp.bfloat16)
    for i, value in enumerate(spread(both)):
        outside[:, i * LANE : (i + 1) * LANE] = value


def close_chunk(here, back, second, store):
    both = dot(back, outer_block(second, here)).astype(jnp.bfloat16)
    for i, value in enumerate(spread(both)):
        value = value.reshape(2, 2, 2, 16, LANE)
        for low in range(2):
            for core in range(2):
                for high in range(2):
                    store(high, low, core, slice(i * LANE, (i + 1) * LANE), value[low, core, high])


def first_columns_kernel(
    half, data, kernels, outer_in, inner_in, inner_back_in, back_in, beyond_in, twist_in,
    out, spectrum, outside,
    data_buf, kernel_buf, outer, inner, inner_back, back, beyond, twist,
    out_buf, spectrum_buf, first, mixed, second, sems,
):
    rows = data_buf.shape[1]
    early = [
        pltpu.make_async_copy(source, target, sems.at[3, i])
        for i, (source, target) in enumerate(
            (
                (data.at[:, pl.ds(0, rows), :], data_buf),
                (outer_in, outer),
                (twist_in, twist),
                (inner_in, inner),
                (inner_back_in, inner_back),
                (back_in.at[half[0]], back),
                (beyond_in.at[half[0]], beyond),
            )
        )
    ]
    for load in early:
        load.start()
    loads = []
    for pair in range(PAIRS):
        here = pl.ds(2 * pair, 2)
        loads.append(
            pltpu.make_async_copy(kernels.at[0, here], kernel_buf.at[here], sems.at[1, pair])
        )
        loads[-1].start()
    for load in early[:3]:
        load.wait()
    for i in range(0, INN // 16, 2):
        pieces = []
        for part in range(2):
            lanes = slice(part * LANE, (part + 1) * LANE)
            for parity in range(2):
                at = parity * INN + i * 16
                block = data_buf[:, at : at + 32, lanes]
                block = jnp.concatenate([block[:, :16], block[:, 16:]], axis=2)
                pieces.append(block.reshape(OUT // 2 * 16, 2 * LANE))
        both = dot(outer[...], jnp.concatenate(pieces, axis=0))
        for c in range(2):
            re, im = (both[p * INN : (p + 1) * INN, c * LANE : (c + 1) * LANE] for p in range(2))
            cos, sin = (twist[0, :, t + i + c : t + i + c + 1] for t in (0, 16))
            here = slice((i + c) * 16, (i + c + 1) * 16)
            for part, value in enumerate((re * cos + im * sin, im * cos - re * sin)):
                value = value.astype(jnp.bfloat16).reshape(PAIRS, 2, 16, LANE)
                first[:, part, here, :LANE] = value[:, 0]
                first[:, part, here, LANE:] = value[:, 1]
    stores = []

    def transform(pair):
        block = jnp.concatenate(
            [first[pair + i].reshape(2 * INN, 2 * LANE) for i in range(2)], axis=1
        )
        both = dot(inner[...], block)
        result = []
        for i in range(2):
            result.append(both[:, i * 2 * LANE : (i + 1) * 2 * LANE])
            spectrum_buf[pair + i] = result[i].astype(jnp.bfloat16)
        here = pl.ds(pair, 2)
        copy = pltpu.make_async_copy(spectrum_buf.at[here], spectrum.at[here], sems.at[2, pair])
        stores.append(copy)
        copy.start()
        return result

    early[3].wait()
    both = transform(0)
    early[4].wait()
    for pair in range(PAIRS):
        if pair % 2 == 0:
            now_both = both
            both = transform(pair + 2) if pair + 2 < PAIRS else None
        loads[pair].wait()
        now = kernel_buf.at[pl.ds(2 * pair, 2)]
        mix_and_open(pair, now_both[pair % 2], now, inner_back, twist, mixed.at[pair % 2], second)
    for load in early[5:]:
        load.wait()
    open_outside(half, beyond[...], second, outside.at[0])
    for chunk in range(INN // 16):
        side, rows = chunk // 8, slice(chunk % 8 * 16, chunk % 8 * 16 + 16)

        def store(high, low, core, lanes, value):
            out_buf[side, high, low, core, rows, lanes] = value

        close_chunk(slice(chunk * 16, chunk * 16 + 16), back[...], second, store)
        if chunk % 4 == 3:
            here = pl.ds((chunk % 8 - 3) * 16, 64)
            source = out_buf.at[side, :, :, :, here, :]
            target = out.at[:, side, :, :, here, :]
            stores.append(pltpu.make_async_copy(source, target, sems.at[0, chunk // 4]))
            stores[-1].start()
    for copy in stores:
        copy.wait()


def next_columns_kernel(
    half, spectrum, kernels, inner_back, back, beyond, twist, out, outside, mixed, second
):
    step = pl.program_id(1)
    for s in range(2):

        @pl.when(step == s)
        def _():
            for i in range(PAIRS // 2):
                pair = s * (PAIRS // 2) + i
                both = spectrum[i].astype(jnp.float32)
                now = kernels.at[0, pl.ds(2 * i, 2)]
                mix_and_open(pair, both, now, inner_back, twist, mixed.at[i % 2], second)
            if s == 1:
                open_outside(half, beyond[0], second, outside.at[0])

    @pl.when(step >= 2)
    def _():
        for c in range(8):
            rows = slice(c * 16, (c + 1) * 16)

            def store(high, low, core, lanes, value):
                out[high, 0, low, core, rows, lanes] = value

            start = pl.multiple_of(((step - 2) * 8 + c) * 16, 16)
            close_chunk(pl.ds(start, 16), back[0], second, store)


def first_columns(half, data, kernels):
    tables = [jnp.asarray(t) for t in column_tables()]
    rows = data.shape[1] - 16
    bf16, f32 = jnp.bfloat16, jnp.float32
    hbm = pl.BlockSpec(memory_space=pl.ANY)
    return pl.pallas_call(
        first_columns_kernel,
        grid_spec=pltpu.PrefetchScalarGridSpec(
            num_scalar_prefetch=1,
            grid=(1,),
            in_specs=[hbm] * 8,
            out_specs=[hbm, hbm, pl.BlockSpec((1, 16, 4 * LANE), lambda i, o: (0, 0, 0))],
            scratch_shapes=[
                pltpu.VMEM((8, rows, 2 * LANE), bf16),
                pltpu.VMEM((OUT, INN, 2 * LANE), bf16),
                pltpu.VMEM((2 * INN, 2 * INN), bf16),
                pltpu.VMEM((2 * INN, 2 * INN), bf16),
                pltpu.VMEM((2 * INN, 2 * INN), bf16),
                pltpu.VMEM((INN, 2 * INN), bf16),
                pltpu.VMEM((32, 2 * INN), bf16),
                pltpu.VMEM((2, INN, LANE), f32),
                pltpu.VMEM((2, 2, 2, 2, LANE, 4 * LANE), bf16),
                pltpu.VMEM((PAIRS, 2 * INN, 2 * LANE), bf16),
                pltpu.VMEM((PAIRS, 2, INN, 2 * LANE), bf16),
                pltpu.VMEM((2, 2 * INN, 4 * LANE), bf16),
                pltpu.VMEM((2, OUT, INN, 2 * LANE), bf16),
                pltpu.SemaphoreType.DMA((4, PAIRS)),
            ],
        ),
        out_shape=[
            jax.ShapeDtypeStruct((2, 2, 2, 2, LANE, 4 * LANE), bf16),
            jax.ShapeDtypeStruct((PAIRS, 2 * INN, 2 * LANE), bf16),
            jax.ShapeDtypeStruct((1, 16, 4 * LANE), bf16),
        ],
        compiler_params=pltpu.CompilerParams(vmem_limit_bytes=VMEM),
        cost_estimate=pl.CostEstimate(flops=10**10, bytes_accessed=16 * MIB, transcendentals=0),
        name="first_columns",
    )(half, data, kernels, *tables)


def next_columns(half, plane, count, spectrum, kernels):
    tables = [jnp.asarray(t) for t in column_tables()[2:]]
    opening = lambda i: jnp.minimum(i, 1)
    closing = lambda i: jnp.maximum(i - 2, 0)
    own = lambda g, i, o: (o[0], 0, 0)
    return pl.pallas_call(
        next_columns_kernel,
        grid_spec=pltpu.PrefetchScalarGridSpec(
            num_scalar_prefetch=1,
            grid=(count, 4),
            in_specs=[
                pl.BlockSpec((PAIRS // 2, 2 * INN, 2 * LANE), lambda g, i, o: (opening(i), 0, 0)),
                pl.BlockSpec(
                    (1, OUT // 2, INN, 2 * LANE), lambda g, i, o: (plane + g, opening(i), 0, 0)
                ),
                pl.BlockSpec((2 * INN, 2 * INN), lambda g, i, o: (0, 0)),
                pl.BlockSpec((1, INN, 2 * INN), own),
                pl.BlockSpec((1, 32, 2 * INN), own),
                pl.BlockSpec((2, INN, LANE), lambda g, i, o: (0, 0, 0)),
            ],
            out_specs=[
                pl.BlockSpec(
                    (2, 1, 2, 2, LANE, 4 * LANE), lambda g, i, o: (0, closing(i), 0, 0, 0, g)
                ),
                pl.BlockSpec((1, 16, 4 * LANE), lambda g, i, o: (g, 0, 0)),
            ],
            scratch_shapes=[
                pltpu.VMEM((2, 2 * INN, 4 * LANE), jnp.bfloat16),
                pltpu.VMEM((2, OUT, INN, 2 * LANE), jnp.bfloat16),
            ],
        ),
        out_shape=[
            jax.ShapeDtypeStruct((2, 2, 2, 2, LANE, count * 4 * LANE), jnp.bfloat16),
            jax.ShapeDtypeStruct((count, 16, 4 * LANE), jnp.bfloat16),
        ],
        compiler_params=pltpu.CompilerParams(vmem_limit_bytes=VMEM),
        cost_estimate=pl.CostEstimate(
            flops=count * 7 * 10**9, bytes_accessed=count * 16 * MIB, transcendentals=0
        ),
        name="next_columns",
    )(half, spectrum, kernels, *tables)


def sixteen_points(re, im):
    c = math.sqrt(0.5)
    c1, c3 = math.cos(math.pi / 8), math.cos(3 * math.pi / 8)
    r0, r1, r2, r3, r4, r5, r6, r7 = re
    r8, i1, i2, i3, i4, i5, i6, i7 = im
    sum08, dif08, sum26, dif26 = r0 + r8, r0 - r8, r2 + r6, c * (r2 - r6)
    base = sum08 + r4
    even = [base + sum26, dif08 + dif26, sum08 - r4, dif08 - dif26, base - sum26]
    sum17, dif17, sum35, dif35 = r1 + r7, r1 - r7, r3 + r5, r3 - r5
    odd = [sum17 + sum35, c1 * dif17 + c3 * dif35, c * (sum17 - sum35), c3 * dif17 - c1 * dif35]
    cosines = [even[a] + odd[a] for a in range(4)] + [even[4]]
    cosines += [even[8 - a] - odd[8 - a] for a in range(5, 9)]
    s17, d17, s35, d35 = i1 + i7, i1 - i7, i3 + i5, i3 - i5
    sines_odd = [None, c3 * s17 + c1 * s35, c * (d17 + d35), c1 * s17 - c3 * s35, d17 - d35]
    s26 = c * (i2 + i6)
    sines_even = [None, s26 + i4, i2 - i6, s26 - i4]
    sines = [None] + [sines_odd[a] + sines_even[a] for a in (1, 2, 3)] + [sines_odd[4]]
    sines += [sines_odd[8 - a] - sines_even[8 - a] for a in (5, 6, 7)]
    result = [cosines[0]] + [cosines[a] - sines[a] for a in range(1, 8)] + [cosines[8]]
    return result + [cosines[16 - a] + sines[16 - a] for a in range(9, 16)]


def open_rows(group, both, turn):
    if group == 0:
        return both
    re, im = both[:, :INN], both[:, INN:]
    cos, sin = turn[group : group + 1, :], turn[CLS + group : CLS + group + 1, :]
    return jnp.concatenate([re * cos - im * sin, re * sin + im * cos], axis=1)


def open_classes(groups, halves, columns, table, turn, opened):
    blocks = []
    for group, (low, high) in zip(groups, halves):
        for part in range(2):
            lanes = slice(part * 2 * LANE, (part + 1) * 2 * LANE)
            first, rest = low[:, lanes], high[:, lanes]
            if group == 0:
                lane = lax.broadcasted_iota(jnp.int32, (first.shape[0], LANE), 1)
                im = jnp.where(lane == 0, columns[part], first[:, LANE:])
                first = jnp.concatenate([first[:, :LANE], im], axis=1)
            blocks.append(jnp.concatenate([first, rest], axis=1))
    rows = blocks[0].shape[0]
    both = dot(jnp.concatenate(blocks, axis=0), table[min(groups[0], 1)])
    for i, group in enumerate(groups):
        for part in range(2):
            at = (2 * i + part) * rows
            opened[part, group] = open_rows(group, both[at : at + rows], turn)


def strip_intensity(opened, here, tile):
    total = None
    for part in range(2):
        re = [opened[part, g, here, tile * LANE : (tile + 1) * LANE] for g in range(CLS)]
        im = [opened[part, g, here, INN + tile * LANE : INN + (tile + 1) * LANE] for g in range(CLS)]
        values = sixteen_points(re, im)
        if total is None:
            total = [v * v for v in values]
        else:
            total = [t + v * v for t, v in zip(total, values)]
    return total


def row_inverse_kernel(plane, parts, nyquist, table, turn, out, edges, opened):
    current = plane + pl.program_id(0)
    rows = parts.shape[3]
    lane = lax.broadcasted_iota(jnp.int32, (rows, LANE), 1)
    columns = []
    for part in range(2):
        mine = jnp.where(lane == current * 2 + part, nyquist[...], 0.0)
        columns.append(jnp.sum(mine, axis=1, keepdims=True).astype(jnp.bfloat16))
    for groups in BATCHES:
        halves = [[parts[g // 2, i, g % 2] for i in range(2)] for g in groups]
        open_classes(groups, halves, columns, table, turn, opened)

    def strip(i, carry):
        here = pl.ds(pl.multiple_of(i * 16, 16), 16)
        for tile in range(INN // LANE):
            total = strip_intensity(opened, here, tile)
            for a in range(OUT):
                lanes = slice(a * INN + tile * LANE, a * INN + (tile + 1) * LANE)
                out[0, here, lanes] = total[a].astype(jnp.bfloat16)
        return carry

    lax.fori_loop(0, rows // 16, strip, 0)
    edges[0, 0:8, :] = out[0, 0:16, :].astype(jnp.float32)[0:8]
    edges[0, 8:16, :] = out[0, rows - 16 :, :].astype(jnp.float32)[8:16]


def row_inverse(plane, count, parts, nyquist):
    rows = parts.shape[3]
    table, turn = (jnp.asarray(t) for t in row_inverse_tables())
    return pl.pallas_call(
        functools.partial(row_inverse_kernel, plane),
        grid=(count,),
        in_specs=[
            pl.BlockSpec((4, 2, 2, rows, 4 * LANE), lambda g: (0, 0, 0, 0, g)),
            pl.BlockSpec((rows, LANE), lambda g: (0, 0)),
            pl.BlockSpec((2, 2 * INN, 2 * INN), lambda g: (0, 0, 0)),
            pl.BlockSpec((2 * CLS, INN), lambda g: (0, 0)),
        ],
        out_specs=[
            pl.BlockSpec((1, rows, N), lambda g: (g, 0, 0)),
            pl.BlockSpec((1, 16, N), lambda g: (g, 0, 0)),
        ],
        out_shape=[
            jax.ShapeDtypeStruct((count, rows, N), jnp.bfloat16),
            jax.ShapeDtypeStruct((count, 16, N), jnp.float32),
        ],
        scratch_shapes=[pltpu.VMEM((2, CLS, rows, 2 * INN), jnp.float32)],
        compiler_params=pltpu.CompilerParams(vmem_limit_bytes=VMEM),
        cost_estimate=pl.CostEstimate(
            flops=count * 3 * 10**9, bytes_accessed=count * 8 * MIB, transcendentals=0
        ),
        name="row_inverse",
    )(parts, nyquist, table, turn)


def nyquist_kernel(planes, own, data, out):
    wide = lambda axis: lax.broadcasted_iota(jnp.int32, (INN, INN), axis)
    tall = lambda axis: lax.broadcasted_iota(jnp.int32, (OUT, INN), axis)
    small = lambda axis: lax.broadcasted_iota(jnp.int32, (OUT, OUT), axis)

    def wave(products, period):
        turn = (products % period).astype(jnp.float32) * (2.0 * math.pi / period)
        return jnp.cos(turn), jnp.sin(turn)

    def exact(left, right):
        return jnp.dot(left, right, preferred_element_type=jnp.float32, precision=lax.Precision.HIGHEST)

    def product(xr, xi, yr, yi):
        return exact(xr, yr) - exact(xi, yi), exact(xr, yi) + exact(xi, yr)

    def rotated(xr, xi, yr, yi):
        return xr * yr - xi * yi, xr * yi + xi * yr

    column = jnp.concatenate([data[i, 0:2, :].astype(jnp.float32) for i in range(8)], axis=0)
    wr, wi = wave(small(0) * small(1), OUT)
    inner_r, inner_i = wave(wide(0) * wide(1), INN)
    vr, vi = wave(tall(0) * tall(1), N)
    ar, ai = rotated(exact(wr, column), exact(-wi, column), vr, -vi)
    yr, yi = product(ar, ai, inner_r, -inner_i)
    fy = signed_fraction(tall(0) + OUT * tall(1))
    (kr, ki), (sr, si) = start_and_step(fy * fy + 0.25)
    block, blocks = own[0], own[1]
    k = lax.broadcasted_iota(jnp.int32, (8, OUT), 1)
    section = block // 2 + lax.broadcasted_iota(jnp.int32, (8, OUT), 0) + (OUT - 1)
    hr, hi = wave(k * (section % OUT), OUT)
    even = block % 2 == 0
    lane = lax.broadcasted_iota(jnp.int32, (1, LANE), 1)
    result, beside = [], []
    for g in range(planes):
        pr, pi = rotated(yr, yi, kr, ki)
        br, bi = rotated(*product(pr, pi, inner_r, inner_i), vr, vi)
        for value in product(hr, hi, br, bi):
            value = value * (1.0 / N)
            result.append(jnp.where(even, value[1:2, :LANE], value[1:2, LANE:]))
            above = jnp.where(even, value[0:1, INN - 1 :], value[1:2, LANE - 1 : LANE])
            above = jnp.where(block == 0, value[1:2, 0:1], above)
            below = jnp.where(even, value[1:2, LANE : LANE + 1], value[2:3, 0:1])
            below = jnp.where(block == blocks - 1, value[1:2, INN - 1 :], below)
            beside.append(jnp.where(lane == 0, above, jnp.where(lane == 1, below, 0.0)))
        kr, ki = rotated(kr, ki, sr, si)
    rest = [jnp.zeros((LANE - 2 * planes, LANE), jnp.float32)]
    out[:LANE, :] = jnp.concatenate(result + rest, axis=0).T
    out[LANE:, :] = jnp.concatenate(beside + rest, axis=0).T


def nyquist_column(own, planes, data):
    rows = data.shape[1] - 16
    return pl.pallas_call(
        functools.partial(nyquist_kernel, planes),
        grid_spec=pltpu.PrefetchScalarGridSpec(
            num_scalar_prefetch=1,
            grid=(1,),
            in_specs=[pl.BlockSpec((8, 16, 2 * LANE), lambda i, o: (0, rows // 16, 0))],
            out_specs=pl.BlockSpec((2 * LANE, LANE), lambda i, o: (0, 0)),
        ),
        out_shape=jax.ShapeDtypeStruct((2 * LANE, LANE), jnp.float32),
        compiler_params=pltpu.CompilerParams(vmem_limit_bytes=VMEM),
        cost_estimate=pl.CostEstimate(flops=10**9, bytes_accessed=2**18, transcendentals=0),
        name="nyquist",
    )(own, data)


TILE = 512


def across(centre, tile, west, east):
    lane = lax.broadcasted_iota(jnp.int32, centre.shape, 1)
    right = jnp.where(lane == TILE - 1, east, pltpu.roll(centre, TILE - 1, 1))
    left = jnp.where(lane == 0, west, pltpu.roll(centre, 1, 1))
    return (right - left) * (right - left)


def spatial_term(held, r, t):
    lanes = slice(t * TILE, (t + 1) * TILE)
    around = held[pl.ds(pl.multiple_of(r - 8, 8), 32), lanes]
    centre, down = around[8:24], around[9:25] - around[7:23]
    first, last = max(t * TILE - 1, 0), min((t + 1) * TILE, N - 1)
    here = pl.ds(r, 16)
    west, east = held[here, first : first + 1], held[here, last : last + 1]
    return centre, down * down + across(centre, TILE, west, east)


def hold(held, block, rows):
    held[8 : 8 + rows, :] = block.astype(jnp.float32)
    held[7:8, :] = held[8:9, :]
    held[8 + rows : 9 + rows, :] = held[7 + rows : 8 + rows, :]


def early_focus_kernel(first, others, best, spatial, held):
    rows = first.shape[1]
    for g in range(3):
        hold(held.at[g], first[0] if g == 0 else others[g - 1], rows)

    def strip(i, carry):
        r = pl.multiple_of(8 + i * 16, 8)
        here = pl.ds(pl.multiple_of(i * 16, 16), 16)
        for t in range(N // TILE):
            lanes = slice(t * TILE, (t + 1) * TILE)
            (c0, s0), (c1, s1), (c2, s2) = (spatial_term(held.at[g], r, t) for g in range(3))
            d0, d1 = c1 - c0, c2 - c0
            score = jnp.maximum(d0 * d0 + s0, d1 * d1 + s1)
            best[here, lanes] = (score * 0.125).astype(jnp.bfloat16)
            spatial[here, lanes] = s2.astype(jnp.bfloat16)
        return carry

    lax.fori_loop(0, rows // 16, strip, 0)


def early_focus(first, others):
    rows = first.shape[1]
    return pl.pallas_call(
        early_focus_kernel,
        out_shape=[
            jax.ShapeDtypeStruct((rows, N), jnp.bfloat16),
            jax.ShapeDtypeStruct((rows, N), jnp.bfloat16),
        ],
        scratch_shapes=[pltpu.VMEM((3, rows + 16, N), jnp.float32)],
        compiler_params=pltpu.CompilerParams(vmem_limit_bytes=VMEM),
        cost_estimate=pl.CostEstimate(flops=10**9, bytes_accessed=12 * MIB, transcendentals=0),
        name="early_focus",
    )(first, others)


def edge_rows(edges, halo):
    lane = lax.broadcasted_iota(jnp.int32, (2, N), 1)
    pair = lambda a, b: jnp.concatenate([a, b], axis=0)
    centre = [pair(e[0:1, :], e[15:16, :]) for e in edges]
    best = None
    for g, e in enumerate(edges):
        depth = centre[min(g + 1, 3)] - centre[max(g - 1, 0)]
        above, below = halo[2 * g : 2 * g + 1, :], halo[2 * g + 1 : 2 * g + 2, :]
        down = pair(e[1:2, :], below) - pair(above, e[14:15, :])
        c = centre[g]
        right = jnp.where(lane == N - 1, c, jnp.concatenate([c[:, 1:], c[:, :1]], axis=1))
        left = jnp.where(lane == 0, c, jnp.concatenate([c[:, -1:], c[:, :-1]], axis=1))
        score = depth * depth + down * down + (right - left) * (right - left)
        best = score if best is None else jnp.maximum(best, score)
    return best * 0.125


def last_rows_kernel(
    parts, best, spatial, others, nyquist_in, table_in, turn_in, edge0_in, edge12_in,
    upper_out, lower_out,
    both, nyquist, table, turn, edge0, edge12, part_buf, best_buf, spatial_buf, others_buf, opened, held, halo, edge, sems,
):
    rows = both.shape[0]
    loads = []
    for group in range(CLS):
        source = parts.at[group // 2, :, group % 2]
        loads.append(pltpu.make_async_copy(source, part_buf.at[group], sems.at[0, group]))
    late = (best, best_buf), (spatial, spatial_buf), (others, others_buf)
    late += (edge0_in, edge0), (edge12_in, edge12)
    for i, (source, target) in enumerate(late):
        loads.append(pltpu.make_async_copy(source, target, sems.at[1, i]))
    early = (nyquist_in, nyquist), (table_in, table), (turn_in, turn)
    early = [pltpu.make_async_copy(a, b, sems.at[2, i]) for i, (a, b) in enumerate(early)]
    for load in early + loads:
        load.start()
    for load in early:
        load.wait()
    lane = lax.broadcasted_iota(jnp.int32, (rows, LANE), 1)
    few_lane = lax.broadcasted_iota(jnp.int32, (16, LANE), 1)
    few_row = lax.broadcasted_iota(jnp.int32, (16, LANE), 0)
    beside = jnp.where(few_row % 2 == 0, nyquist[rows : rows + 1, :], nyquist[rows + 1 : rows + 2, :])
    columns = []
    for part in range(2):
        mine = jnp.where(lane == 6 + part, nyquist[:rows, :], 0.0)
        few = jnp.where(few_lane == (few_row // 2) * 2 + part, beside, 0.0)
        column = jnp.sum(jnp.concatenate([mine, few], axis=0), axis=1, keepdims=True)
        columns.append(column.astype(jnp.bfloat16))
    for groups in BATCHES:
        for group in groups:
            loads[group].wait()
        halves = [[part_buf[g, i] for i in range(2)] for g in groups]
        open_classes(groups, halves, columns, table, turn, opened)

    def strip(i, carry):
        base = pl.multiple_of(i * 8, 8)
        for tile in range(INN // LANE):
            for a, value in enumerate(strip_intensity(opened, pl.ds(base, 8), tile)):
                lanes = slice(a * INN + tile * LANE, a * INN + (tile + 1) * LANE)
                value = value.astype(jnp.bfloat16).astype(jnp.float32)
                held[pl.ds(pl.multiple_of(base + 8, 8), 8), lanes] = value
        return carry

    lax.fori_loop(0, rows // 8 + 1, strip, 0)
    halo[...] = held[8 + rows : 16 + rows, :]
    held[7:8, :] = held[8:9, :]
    held[8 + rows : 9 + rows, :] = held[7 + rows : 8 + rows, :]
    edge[0:8, :] = held[8:16, :]
    edge[8:16, :] = held[rows : rows + 8, :]
    for load in loads[CLS:]:
        load.wait()
    ends = edge_rows([edge0.at[0], edge12.at[0], edge12.at[1], edge], halo)

    def measure(i, carry):
        r = pl.multiple_of(8 + i * 16, 8)
        here = pl.ds(pl.multiple_of(i * 16, 16), 16)
        for t in range(N // TILE):
            lanes = slice(t * TILE, (t + 1) * TILE)
            centre, term = spatial_term(held, r, t)
            d2 = centre - others_buf[0, here, lanes].astype(jnp.float32)
            d3 = centre - others_buf[1, here, lanes].astype(jnp.float32)
            score = jnp.maximum(d2 * d2 + spatial_buf[here, lanes].astype(jnp.float32), d3 * d3 + term)
            score = jnp.maximum(score * 0.125, best_buf[here, lanes].astype(jnp.float32))
            both[here, lanes] = score.astype(jnp.bfloat16)
        return carry

    half = rows // 2
    stores = []
    for side, out in enumerate((upper_out, lower_out)):
        lax.fori_loop(side * (half // 16), (side + 1) * (half // 16), measure, 0)
        here = slice(0, 16) if side == 0 else slice(rows - 16, rows)
        index = lax.broadcasted_iota(jnp.int32, (16, N), 0)
        value = jnp.where(index == 15 * side, ends[side : side + 1], both[here].astype(jnp.float32))
        both[here] = value.astype(jnp.bfloat16)
        source = both.at[pl.ds(side * half, half)]
        stores.append(pltpu.make_async_copy(source, out, sems.at[2, 3 + side]))
        stores[-1].start()
    for store in stores:
        store.wait()


def last_rows(parts, nyquist, best, spatial, others, edge0, edge12):
    rows = best.shape[0]
    table, turn = (jnp.asarray(t) for t in row_inverse_tables())
    hbm = pl.BlockSpec(memory_space=pl.ANY)
    bf16, f32 = jnp.bfloat16, jnp.float32
    return pl.pallas_call(
        last_rows_kernel,
        in_specs=[hbm] * 9,
        out_specs=[hbm] * 2,
        out_shape=[jax.ShapeDtypeStruct((rows // 2, N), bf16)] * 2,
        scratch_shapes=[
            pltpu.VMEM((rows, N), bf16),
            pltpu.VMEM((2 * LANE, LANE), f32),
            pltpu.VMEM((2, 2 * INN, 2 * INN), bf16),
            pltpu.VMEM((2 * CLS, INN), f32),
            pltpu.VMEM((1, 16, N), f32),
            pltpu.VMEM((2, 16, N), f32),
            pltpu.VMEM((CLS, 2, rows + 16, 4 * LANE), bf16),
            pltpu.VMEM((rows, N), bf16),
            pltpu.VMEM((rows, N), bf16),
            pltpu.VMEM((2, rows, N), bf16),
            pltpu.VMEM((2, CLS, rows + 16, 2 * INN), f32),
            pltpu.VMEM((rows + 16, N), f32),
            pltpu.VMEM((8, N), f32),
            pltpu.VMEM((16, N), f32),
            pltpu.SemaphoreType.DMA((3, CLS)),
        ],
        compiler_params=pltpu.CompilerParams(vmem_limit_bytes=VMEM),
        cost_estimate=pl.CostEstimate(flops=3 * 10**9, bytes_accessed=16 * MIB, transcendentals=0),
        name="last_rows",
    )(parts, best, spatial, others, nyquist, table, turn, edge0, edge12)


def assemble_kernel(own, *refs):
    slot, out = pl.program_id(0), refs[-1]
    half = refs[0].shape[0]
    for s in range(3):

        @pl.when(slot == s)
        def _():
            out[:half] = refs[s][...].astype(jnp.float32)
            out[half:] = refs[3 + s][...].astype(jnp.float32)


def assemble(depth_index, upper, lower):
    half = upper[0].shape[0]
    whole = pl.BlockSpec((half, N), lambda s, o: (0, 0))
    return pl.pallas_call(
        assemble_kernel,
        grid_spec=pltpu.PrefetchScalarGridSpec(
            num_scalar_prefetch=1,
            grid=(3,),
            in_specs=[whole] * 6,
            out_specs=pl.BlockSpec((2 * half, N), lambda s, o: (jnp.bitwise_xor(s, o[0]), 0)),
        ),
        out_shape=jax.ShapeDtypeStruct((8 * half, N), jnp.float32),
        compiler_params=pltpu.CompilerParams(vmem_limit_bytes=20 * MIB),
        cost_estimate=pl.CostEstimate(flops=10**6, bytes_accessed=10 * MIB, transcendentals=0),
        name="assemble",
    )(depth_index, *upper, *lower)


def complete_kernel(own, upper, lower, whole, out):
    half = lower.shape[0] // 2
    step = pl.program_id(0)
    for s, ref in enumerate((upper, lower)):
        for part in range(2):

            @pl.when(step == 2 * s + part)
            def _():
                out[...] = ref[part * half : (part + 1) * half].astype(jnp.float32)


def complete(depth_index, upper, lower, whole):
    half = upper.shape[0]
    both = pl.BlockSpec((half, N), lambda i, o: (0, 0))
    place = lambda i, o: (jnp.bitwise_xor(3, o[0]) * 4 + i, 0)
    return pl.pallas_call(
        complete_kernel,
        grid_spec=pltpu.PrefetchScalarGridSpec(
            num_scalar_prefetch=1,
            grid=(4,),
            in_specs=[both, both, pl.BlockSpec(memory_space=pl.ANY)],
            out_specs=pl.BlockSpec((half // 2, N), place),
        ),
        out_shape=jax.ShapeDtypeStruct(whole.shape, jnp.float32),
        input_output_aliases={3: 0},
        compiler_params=pltpu.CompilerParams(vmem_limit_bytes=20 * MIB),
        cost_estimate=pl.CostEstimate(flops=10**6, bytes_accessed=3 * MIB, transcendentals=0),
        name="complete",
    )(depth_index, upper, lower, whole)


OVER_X = [(i, i ^ 1) for i in range(4)]
OVER_Y = [(i, i ^ 2) for i in range(4)]


def exchange_depth(a, b):
    ax, by = lax.ppermute(a, "depth", OVER_X), lax.ppermute(b, "depth", OVER_Y)
    ay, axy = lax.ppermute(a, "depth", OVER_Y), lax.ppermute(ax, "depth", OVER_Y)
    bx, byx = lax.ppermute(b, "depth", OVER_X), lax.ppermute(by, "depth", OVER_X)
    return (a, ax, ay, axy), (b, bx, by, byx)


def border_rows(halfway, outside, high):
    lanes = 4 * LANE
    count = halfway.shape[-1] // lanes
    natural = lambda rows: rows.reshape(4, 2, 2, count, lanes).transpose(1, 2, 0, 3, 4).reshape(16, count, lanes)
    first, last = natural(halfway[..., 0, :]), natural(halfway[..., -1, :])
    above = jnp.where(high == 0, first[:1], outside[None, :, 15])
    below = jnp.where(high == 0, outside[None, :, 0], last[-1:])
    above = jnp.concatenate([above, last[:-1]])
    below = jnp.concatenate([first[1:], below])
    both = jnp.stack([above, below], axis=2).reshape(2, 2, 4, 2 * count, lanes)
    return both.transpose(2, 0, 1, 3, 4).reshape(16, 2 * count, lanes)


def half_spectrum_shards(hologram, background):
    rows = hologram.shape[0]
    planes = lax.axis_size("depth") * PL_DEV
    depth, high = lax.axis_index("depth"), lax.axis_index("high")
    low, core = lax.axis_index("low"), lax.axis_index("core")
    as_scalar = lambda value: jnp.reshape(value, (1,)).astype(jnp.int32)
    own = rows // 4
    block = ((high * 2 + low) * 2 + core) * 4 + depth
    place = jnp.stack([block, jnp.int32(N // own)]).astype(jnp.int32)

    sections = row_forward(as_scalar(depth), hologram, background)
    data = lax.all_to_all(
        sections.reshape(8, rows + 16, 2 * LANE),
        ("high", "low", "core"),
        split_axis=0,
        concat_axis=0,
        tiled=True,
    )

    group = depth * 2 + core
    slot = low * LANE + jnp.arange(LANE, dtype=jnp.int32)
    special = jnp.where(low == 0, 0, CLS) + OUT * jnp.arange(LANE, dtype=jnp.int32)
    fx = signed_fraction(jnp.where(group == 0, special, group + OUT * slot))
    kernels = propagators(planes, (fx * fx)[None])

    def to_rows(halfway):
        parts = lax.all_to_all(
            halfway.reshape(16, -1, halfway.shape[-1]),
            ("depth", "low", "core"),
            split_axis=0,
            concat_axis=0,
            tiled=True,
        )
        return parts.reshape(4, 2, 2, -1, halfway.shape[-1])

    halfway, spectrum, outside = first_columns(as_scalar(high), data, kernels)
    parts, borders = [to_rows(halfway)], [border_rows(halfway, outside, high)]
    for plane, count in ((1, 2), (3, 1)):
        halfway, outside = next_columns(as_scalar(high), plane, count, spectrum, kernels)
        borders.append(border_rows(halfway, outside, high))
        halfway = halfway.reshape(16, own, -1)
        if plane == 3:
            below = jnp.concatenate(borders, axis=1)
            below = jnp.pad(below, ((0, 0), (0, 16 - 2 * planes), (0, 0)))
            halfway = jnp.concatenate([halfway, below], axis=1)
        ready = parts[-1]
        if plane == 3:
            first, first_edge = row_inverse(0, 1, parts[0], middle)
            ready = ready, first, first_edge
        elif plane == 1:
            middle = nyquist_column(place, planes, data)
            ready = ready, middle
        halfway, ready = lax.optimization_barrier((halfway, ready))
        if plane == 3:
            parts[-1], first, first_edge = ready
        else:
            parts[-1], middle = ready
        parts.append(to_rows(halfway))
    others, others_edge = row_inverse(1, 2, parts[1], middle)
    best, spatial = early_focus(first, others)
    upper, lower = last_rows(parts[2], middle, best, spatial, others, first_edge, others_edge)
    upper, lower = exchange_depth(upper, lower)
    whole = assemble(as_scalar(depth), upper[:3], lower[:3])
    return complete(as_scalar(depth), upper[3], lower[3], whole)


def solution(mesh):
    spec = P("rows", None)
    if mesh.shape["depth"] == 4 and mesh.shape["rows"] == 8:
        split = Mesh(mesh.devices.reshape(4, 2, 2, 2), ("depth", "high", "low", "core"))
        spec = P(("high", "low", "core"), None)
        body = half_spectrum_shards
    else:
        split, body = mesh, shards
    return jax.shard_map(body, mesh=split, in_specs=(spec, spec), out_specs=spec, check_vma=False)
```

```python
import functools
import math

import jax
import jax.numpy as jnp
import numpy as np
from jax import lax
from jax.experimental import pallas as pl
from jax.experimental.pallas import tpu as pltpu
from jax.sharding import Mesh
from jax.sharding import PartitionSpec as P

N = 4096
RADIX = 64
PL_DEV = 1


wave_number = 0.6
depth_start = 8.0
depth_step = 2.0


def padded_2(block, sides, width):
    for axis, dim in sides:
        count = lax.axis_size(axis)
        forward = [(i, i + 1) for i in range(count - 1)]
        backward = [(target, source) for source, target in forward]
        low = lax.ppermute(
            lax.slice_in_dim(block, block.shape[dim] - width, None, axis=dim), axis, forward
        )
        high = lax.ppermute(lax.slice_in_dim(block, 0, width, axis=dim), axis, backward)
        block = jnp.concatenate([low, block, high], axis=dim)
    return block


def fourier_tables(radix_size, sign_value):
    indices = jnp.arange(radix_size, dtype=jnp.int32)
    products = indices[:, None] * indices[None, :] % radix_size
    angles = products.astype(jnp.float32) * (sign_value * 2.0 * math.pi / radix_size)
    scaling = 1.0 / math.sqrt(radix_size)
    cosine_part = jnp.cos(angles) * scaling
    sine_part = jnp.sin(angles) * scaling
    matrix = jnp.stack([jnp.stack([cosine_part, -sine_part]), jnp.stack([sine_part, cosine_part])])
    return matrix.astype(jnp.bfloat16)


def twiddle_table(radix_size, sign_value):
    indices = jnp.arange(radix_size, dtype=jnp.int32)
    total = radix_size * radix_size
    products = indices[:, None] * indices[None, :] % total
    angles = products.astype(jnp.float32) * (sign_value * 2.0 * math.pi / total)
    return (jnp.cos(angles), jnp.sin(angles))


def rotate(data, cosine_part, sine_part):
    return jnp.stack(
        [data[0] * cosine_part - data[1] * sine_part, data[0] * sine_part + data[1] * cosine_part]
    )


def contract(form, matrix, data):
    return jnp.einsum(form, matrix, data, preferred_element_type=jnp.float32)


def forward_real(data):
    batch_size = data.shape[1]
    shaped = data.reshape(RADIX, RADIX, batch_size)
    matrix = fourier_tables(RADIX, -1.0)
    cosine_part, sine_part = twiddle_table(RADIX, -1.0)
    opening = contract("oka,abm->okbm", matrix[:, 0], shaped)
    sectioned = rotate(opening, cosine_part[:, :, None], sine_part[:, :, None]).astype(jnp.bfloat16)
    closing = contract("ocjb,ckbm->okjm", matrix, sectioned)
    return closing.reshape(2, N, batch_size).astype(jnp.bfloat16)


def forward_first(data):
    batch_size = data.shape[2]
    shaped = data.reshape(2, RADIX, RADIX, batch_size)
    matrix = fourier_tables(RADIX, -1.0)
    cosine_part, sine_part = twiddle_table(RADIX, -1.0)
    opening = contract("ocka,cabm->okbm", matrix, shaped)
    sectioned = rotate(opening, cosine_part[:, :, None], sine_part[:, :, None]).astype(jnp.bfloat16)
    closing = contract("ocjb,ckbm->okjm", matrix, sectioned)
    return closing.reshape(2, N, batch_size).astype(jnp.bfloat16)


def inverse_first(data):
    batch_size = data.shape[2]
    shaped = data.reshape(2, RADIX, RADIX, batch_size)
    matrix = fourier_tables(RADIX, 1.0)
    cosine_part, sine_part = twiddle_table(RADIX, 1.0)
    opening = contract("ocbj,ckjm->okbm", matrix, shaped)
    sectioned = rotate(opening, cosine_part[:, :, None], sine_part[:, :, None]).astype(jnp.bfloat16)
    closing = contract("ocak,ckbm->oabm", matrix, sectioned)
    return closing.reshape(2, N, batch_size)


def frequencies(positions):
    natural = positions // RADIX + RADIX * (positions % RADIX)
    signed_freq = jnp.where(natural >= N // 2, natural - N, natural)
    return signed_freq.astype(jnp.float32) / N


def propagator(freq_whole, freq_own, distance):
    radial = freq_whole[:, None] ** 2 + freq_own[None, :] ** 2
    limit = wave_number * wave_number
    amplitude = jnp.exp(-2.0 * math.pi * distance * jnp.sqrt(jnp.maximum(radial - limit, 0.0)))
    phase_angle = (
        2.0 * math.pi * distance * (jnp.sqrt(jnp.maximum(limit - radial, 0.0)) - wave_number)
    )
    return (amplitude * jnp.cos(phase_angle), amplitude * jnp.sin(phase_angle))


def propagate(spectrum, cosine_part, sine_part):
    return rotate(spectrum.astype(jnp.float32), cosine_part, sine_part).astype(jnp.bfloat16)


def shards(hologram, background):
    row_count = hologram.shape[0]
    contrast = (hologram.astype(jnp.float32) / background.astype(jnp.float32) - 1.0).astype(
        jnp.bfloat16
    )
    along_rows = forward_real(contrast.T)
    columns = lax.all_to_all(
        jnp.swapaxes(along_rows, 1, 2), "rows", split_axis=2, concat_axis=1, tiled=True
    )
    spectrum = forward_first(columns)
    row_index = lax.axis_index("rows")
    own_positions = row_index * row_count + jnp.arange(row_count, dtype=jnp.int32)
    freq_own = frequencies(own_positions)
    freq_whole = frequencies(jnp.arange(N, dtype=jnp.int32))
    depth_index = lax.axis_index("depth")
    distance = depth_start + depth_step * (depth_index * PL_DEV + 0).astype(jnp.float32)
    cosine_part, sine_part = propagator(freq_whole, freq_own, distance)
    propagated = propagate(spectrum, cosine_part, sine_part)
    halfway = inverse_first(propagated).astype(jnp.bfloat16)
    restored = lax.all_to_all(
        jnp.swapaxes(halfway, 1, 2), "rows", split_axis=2, concat_axis=1, tiled=True
    )
    result_field = inverse_first(restored)
    intensities = [
        (result_field[0] * result_field[0] + result_field[1] * result_field[1]).astype(jnp.bfloat16)
    ]
    stacked = jnp.stack(intensities)
    padded = padded_2(stacked, (("depth", 0), ("rows", 2)), 1)
    centre_block = padded[1:-1, :, 1:-1]
    plane_ids = jnp.arange(PL_DEV, dtype=jnp.int32)[:, None, None]
    row_ids = jnp.arange(row_count, dtype=jnp.int32)[None, None, :]
    depth_count = lax.axis_size("depth")
    row_groups = lax.axis_size("rows")
    lower_plane = jnp.where(
        (depth_index == 0) & (plane_ids == 0), centre_block, padded[:-2, :, 1:-1]
    )
    upper_plane = jnp.where(
        (depth_index == depth_count - 1) & (plane_ids == PL_DEV - 1),
        centre_block,
        padded[2:, :, 1:-1],
    )
    north_row = jnp.where((row_index == 0) & (row_ids == 0), centre_block, padded[1:-1, :, :-2])
    south_row = jnp.where(
        (row_index == row_groups - 1) & (row_ids == row_count - 1),
        centre_block,
        padded[1:-1, :, 2:],
    )
    centre = centre_block.astype(jnp.float32)
    east_col = jnp.concatenate([centre[:, 1:], centre[:, -1:]], axis=1)
    west_col = jnp.concatenate([centre[:, :1], centre[:, :-1]], axis=1)
    depth_diff = upper_plane.astype(jnp.float32) - lower_plane.astype(jnp.float32)
    row_diff = south_row.astype(jnp.float32) - north_row.astype(jnp.float32)
    col_diff = east_col - west_col
    scores = (depth_diff * depth_diff + row_diff * row_diff + col_diff * col_diff) / 8.0
    sharpest = jnp.max(scores, axis=0)
    merged = lax.pmax(sharpest.astype(jnp.bfloat16), "depth").astype(sharpest.dtype)
    return merged.T


OUT = 16
INN = 256
CLS = 8
LANE = 128
MIB = 2**20
VMEM = 63 * MIB
SHARED = 36 * MIB


def slot_frequencies():
    table = np.arange(CLS)[:, None] + OUT * np.arange(INN)[None, :]
    half = np.arange(INN // 2)
    table[0] = np.concatenate([OUT * half, CLS + OUT * half])
    return table


def angles(products):
    return 2.0 * np.pi * (products % N) / N


def row_forward_tables():
    freq = slot_frequencies()
    theta = angles(np.arange(INN)[None, :, None] * freq[:, None, :])
    cos, sin = np.cos(theta) / 64.0, np.sin(theta) / 64.0
    top = np.stack([cos, -sin], axis=2)
    low = np.stack([sin, cos], axis=2)
    first = np.arange(INN) < INN // 2
    low[0] = np.where(first, 0.0, top[0])
    top[0] = np.where(first, top[0], 0.0)
    full = np.concatenate([top, low], axis=1)
    full = full.reshape(CLS, 2 * INN, 2, 2, LANE).transpose(0, 1, 3, 2, 4)
    return full.reshape(CLS, 2 * INN, 2 * INN).astype(jnp.bfloat16)


def row_forward_weights():
    a = np.arange(1, 5)
    rows = []
    for d in range(CLS // 2):
        even, odd = (2.0 * np.pi * c * a / OUT for c in (2 * d, 2 * d + 1))
        parts = np.cos(even), -np.sin(even[:3]), [float(d == 0)], np.cos(odd[:3]), -np.sin(odd), [0.0]
        rows.append(np.concatenate(parts))
    return np.concatenate(rows).astype(np.float32)


def row_inverse_tables():
    half = np.arange(INN // 2)
    position = np.arange(INN)[None, :]
    full = np.zeros((2, 2, INN, 2, INN))
    for first, place in ((0, 0), (CLS, 1)):
        theta = angles((first + OUT * half)[:, None] * position)
        rows = slice(place * INN // 2, (place + 1) * INN // 2)
        full[0, 0, rows, place], full[0, 1, rows, place] = np.cos(theta), -np.sin(theta)
    full[0, 0, 0, 0] = 0.5
    full[0, 1, 0, 0] = 0.5 * (-1.0) ** np.arange(INN)
    theta = angles(OUT * np.arange(INN)[:, None] * position)
    full[1, 0, :, 0], full[1, 0, :, 1] = np.cos(theta), np.sin(theta)
    full[1, 1, :, 0], full[1, 1, :, 1] = -np.sin(theta), np.cos(theta)
    full = full.reshape(2, 2, 2, LANE, 2 * INN).transpose(0, 2, 1, 3, 4) / 32.0
    turn = angles(np.arange(CLS)[:, None] * position)
    turn = np.concatenate([np.cos(turn), np.sin(turn)]).astype(np.float32)
    return full.reshape(2, 2 * INN, 2 * INN).astype(jnp.bfloat16), turn


def column_tables():
    turn = 2.0 * np.pi * np.arange(OUT)[:, None] * np.arange(OUT)[None, :] / OUT
    eye = np.eye(16)
    outer_cos, outer_sin = np.kron(np.cos(turn), eye) / 4.0, np.kron(np.sin(turn), eye) / 4.0
    complex_form = lambda cos, sin: np.concatenate(
        [np.concatenate([cos, -sin], axis=-1), np.concatenate([sin, cos], axis=-1)], axis=-2
    )
    slabs = lambda table: table.reshape(-1, 8, 2, 16).swapaxes(1, 2).reshape(table.shape)
    outer = complex_form(slabs(outer_cos), slabs(-outer_sin))
    half_rows = outer_cos.shape[0] // 2
    cut = lambda table, begin, size: table[begin : begin + size]
    back = np.stack(
        [
            complex_form(cut(outer_cos, begin, half_rows), cut(outer_sin, begin, half_rows))
            for begin in (0, half_rows)
        ]
    )
    beyond = np.stack(
        [complex_form(cut(outer_cos, a * 16, 16), cut(outer_sin, a * 16, 16)) for a in (8, 7)]
    )
    theta = angles(OUT * np.arange(INN)[:, None] * np.arange(INN)[None, :])
    inner = complex_form(np.cos(theta), -np.sin(theta)) / 16.0
    inner_back = complex_form(np.cos(theta), np.sin(theta)) / 16.0
    turn = angles(np.arange(OUT)[:, None] * np.arange(INN)[None, :])
    by_chunk = turn.reshape(OUT, 16, 16).swapaxes(1, 2).reshape(INN, 16)
    twist = np.zeros((2, INN, LANE), np.float32)
    for i, table in enumerate((by_chunk, turn.T)):
        twist[i, :, :16], twist[i, :, 16:32] = np.cos(table), np.sin(table)
    cast = lambda table: table.astype(jnp.bfloat16)
    return cast(outer), cast(inner), cast(inner_back), cast(back), cast(beyond), twist


def dot(left, right):
    return jnp.dot(left, right, preferred_element_type=jnp.float32)


def split_complex(both, width):
    rows = both.shape[0] // 2
    top, low = both[:rows], both[rows:]
    return top[:, :width] - low[:, width:], top[:, width:] + low[:, :width]


def quarter_kernel(radial):
    gap = wave_number * wave_number - radial
    root = jnp.sqrt(jnp.abs(gap))
    inside = gap > 0.0
    half_pi = 0.5 * math.pi
    angle = half_pi * (jnp.where(inside, root, 0.0) - wave_number)
    decay = jnp.exp(jnp.where(inside, 0.0, -half_pi * root))
    square = angle * angle
    sine = 1.0 / 362880.0
    for c in (-1.0 / 5040.0, 1.0 / 120.0, -1.0 / 6.0, 1.0):
        sine = sine * square + c
    cosine = -1.0 / 3628800.0
    for c in (1.0 / 40320.0, -1.0 / 720.0, 1.0 / 24.0, -0.5, 1.0):
        cosine = cosine * square + c
    return decay * cosine, decay * (sine * angle)


def squared(re, im):
    return (re - im) * (re + im), 2.0 * re * im


def start_and_step(radial):
    value = quarter_kernel(radial)
    distance = 0.25
    step = None
    while distance < depth_start:
        value = squared(*value)
        distance *= 2.0
        if distance == depth_step:
            step = value
    return value, step


def signed_fraction(natural):
    return jnp.where(natural >= N // 2, natural - N, natural).astype(jnp.float32) * (1.0 / N)


CHUNK = 64
BATCHES = ((0,), (1, 2), (3, 4), (5, 6, 7))


def sixteen_sums(term, w):
    c0, c8 = term(0), term(8)
    plus, minus = c0 + c8, c0 - c8
    c4, c12 = term(4), term(12)
    e4, o4 = c4 + c12, c4 - c12
    total = plus + e4
    eighth = total
    re_even = plus + w(3) * e4
    im_even = None
    re_odd, im_odd = minus, w(14) * o4
    for a in (1, 2, 3):
        p, q, r, s = term(a), term(16 - a), term(8 - a), term(8 + a)
        e, o, f, h = p + q, p - q, r + s, r - s
        both = e + f
        total = total + both
        eighth = eighth - both if a % 2 else eighth + both
        re_even = re_even + w(a - 1) * both
        term_im = w(3 + a) * (o - h)
        im_even = term_im if im_even is None else im_even + term_im
        re_odd = re_odd + w(7 + a) * (e - f)
        im_odd = im_odd + w(10 + a) * (o + h)
    return re_even, im_even + w(7) * eighth, re_odd, im_odd, total


def row_forward_kernel(
    own, weights, holo, back, table, out, holo_buf, back_buf, table_buf, acc, result, held, sems
):
    rows = holo.shape[0]
    group = own[0]
    chunks = rows // CHUNK
    loads = []
    for i in range(chunks):
        here = pl.ds(i * CHUNK, CHUNK)
        loads.append(
            (
                pltpu.make_async_copy(holo.at[here], holo_buf.at[here], sems.at[0, i]),
                pltpu.make_async_copy(back.at[here], back_buf.at[here], sems.at[1, i]),
            )
        )
        for load in loads[-1]:
            load.start()
        if i == 0:
            tables = pltpu.make_async_copy(table.at[pl.ds(2 * group, 2)], table_buf, sems.at[4, 0])
            tables.start()
    lane = lax.broadcasted_iota(jnp.int32, (16, INN), 1)
    sign = jnp.where(lane % 2 == 0, 1.0, -1.0).astype(jnp.bfloat16)
    stores = []
    for chunk in range(chunks):
        for load in loads[chunk]:
            load.wait()

        def strip(i, carry):
            here = pl.ds(pl.multiple_of(chunk * CHUNK + i * 16, 16), 16)

            def term(a):
                there = pl.ds(a * INN, INN)
                below = back_buf[here, there].astype(jnp.float32)
                inverse = pl.reciprocal(below, approx=True)
                inverse = inverse * (2.0 - below * inverse)
                value = holo_buf[here, there].astype(jnp.float32) * inverse
                return value - 1.0

            sums = sixteen_sums(term, lambda n: weights[group * 16 + n])
            for q in range(4):
                acc[q // 2, here, pl.ds((q % 2) * INN, INN)] = sums[q].astype(jnp.bfloat16)
            acc[2, here, pl.ds(0, INN)] = sums[4].astype(jnp.bfloat16)
            return carry

        lax.fori_loop(0, CHUNK // 16, strip, 0)
        batch = rows // 2 // CHUNK
        if chunk % batch != batch - 1:
            continue
        if chunk < batch:
            tables.wait()
        begin, end = (chunk + 1 - batch) * CHUNK, (chunk + 1) * CHUNK
        for q in range(2):
            both = dot(acc[q, begin:end], table_buf[q]).astype(jnp.bfloat16)
            for low in range(2):
                part = both[:, low * 2 * LANE : (low + 1) * 2 * LANE]
                result[low, q, begin:end, :] = part
        held[chunk // batch] = lax.dot_general(
            sign,
            acc[2, begin:end, :INN],
            (((1,), (1,)), ((), ())),
            preferred_element_type=jnp.float32,
        )
        here = pl.ds(begin, end - begin)
        if chunk == chunks - 1:
            index = lax.broadcasted_iota(jnp.int32, (16, INN), 0)
            extra = jnp.where(index == 0, held[0], held[1]) * (1.0 / 64.0)
            for low in range(2):
                for q in range(2):
                    result[low, q, rows:, :] = extra.astype(jnp.bfloat16)
            here = pl.ds(begin, end - begin + 16)
        for high in range(2):
            source, target = result.at[:, :, here, :], out.at[high, :, :, here, :]
            stores.append(pltpu.make_async_copy(source, target, sems.at[2 + high, chunk]))
            stores[-1].start()
    for store in stores:
        store.wait()


def row_forward(own, hologram, background):
    rows = hologram.shape[0]
    table = jnp.asarray(row_forward_tables())
    weights = jnp.asarray(row_forward_weights())
    hbm = pl.BlockSpec(memory_space=pl.ANY)
    chunks = rows // CHUNK
    return pl.pallas_call(
        row_forward_kernel,
        grid_spec=pltpu.PrefetchScalarGridSpec(
            num_scalar_prefetch=2,
            grid=(1,),
            in_specs=[hbm] * 3,
            out_specs=hbm,
            scratch_shapes=[
                pltpu.VMEM((rows, N), jnp.bfloat16),
                pltpu.VMEM((rows, N), jnp.bfloat16),
                pltpu.VMEM((2, 2 * INN, 2 * INN), jnp.bfloat16),
                pltpu.VMEM((3, rows, 2 * INN), jnp.bfloat16),
                pltpu.VMEM((2, 2, rows + 16, 2 * LANE), jnp.bfloat16),
                pltpu.VMEM((2, 16, INN), jnp.float32),
                pltpu.SemaphoreType.DMA((5, chunks)),
            ],
        ),
        out_shape=jax.ShapeDtypeStruct((2, 2, 2, rows + 16, 2 * LANE), jnp.bfloat16),
        compiler_params=pltpu.CompilerParams(vmem_limit_bytes=VMEM),
        cost_estimate=pl.CostEstimate(flops=10**10, bytes_accessed=12 * MIB, transcendentals=0),
        name="row_forward",
    )(own, weights, hologram, background, table)


def propagator_kernel(planes, fx2, out):
    step = pl.program_id(0)
    strip = 32
    for i in range(INN // strip):
        rows = slice(i * strip, (i + 1) * strip)
        position = lax.broadcasted_iota(jnp.int32, (strip, LANE), 0) + i * strip
        fy = signed_fraction(step + OUT * position)
        (kr, ki), (sr, si) = start_and_step(fy * fy + fx2[...])
        for g in range(planes):
            out[g, 0, rows, :LANE] = kr.astype(jnp.bfloat16)
            out[g, 0, rows, LANE:] = ki.astype(jnp.bfloat16)
            if g + 1 < planes:
                kr, ki = kr * sr - ki * si, kr * si + ki * sr


def propagators(planes, fx2):
    return pl.pallas_call(
        functools.partial(propagator_kernel, planes),
        grid=(OUT,),
        in_specs=[pl.BlockSpec((1, LANE), lambda i: (0, 0))],
        out_specs=pl.BlockSpec((planes, 1, INN, 2 * LANE), lambda i: (0, i, 0, 0)),
        out_shape=jax.ShapeDtypeStruct((planes, OUT, INN, 2 * LANE), jnp.bfloat16),
        compiler_params=pltpu.CompilerParams(vmem_limit_bytes=VMEM),
        cost_estimate=pl.CostEstimate(flops=10**9, bytes_accessed=16 * MIB, transcendentals=10**6),
        name="propagators",
    )(fx2)


PAIRS = OUT // 2


def mix_and_open(pair, both, kernels, inner_back, twist, mixed, second):
    wide = 2 * LANE
    for k in range(2):
        yr, yi = (both[p * INN : (p + 1) * INN, k * LANE : (k + 1) * LANE] for p in range(2))
        for part in range(2):
            factor = kernels[k, :, part * LANE : (part + 1) * LANE].astype(jnp.float32)
            lanes = slice(k * wide + part * LANE, k * wide + (part + 1) * LANE)
            mixed[:INN, lanes] = (yr * factor).astype(jnp.bfloat16)
            mixed[INN:, lanes] = (yi * factor).astype(jnp.bfloat16)
    opened = dot(inner_back[...], mixed[...])
    for k in range(2):
        at = pair * 2 + k
        re, im = (opened[p * INN : (p + 1) * INN, k * wide : (k + 1) * wide] for p in range(2))
        cos, sin = twist[1, :, at : at + 1], twist[1, :, 16 + at : 17 + at]
        second[0, at] = (re * cos - im * sin).astype(jnp.bfloat16)
        second[1, at] = (re * sin + im * cos).astype(jnp.bfloat16)


def outer_block(second, here):
    return second[:, :, here, :].reshape(2 * OUT * 16, 2 * LANE)


def spread(both):
    rows = both.shape[0] // 2
    re, im = both[:rows], both[rows:]
    return [re[:, :LANE], im[:, :LANE], re[:, LANE:], im[:, LANE:]]


def open_outside(half, beyond, second, outside):
    here = pl.ds(pl.multiple_of(half[0] * (INN - 16), 16), 16)
    both = dot(beyond, outer_block(second, here)).astype(jnp.bfloat16)
    for i, value in enumerate(spread(both)):
        outside[:, i * LANE : (i + 1) * LANE] = value


def close_chunk(here, back, second, store):
    both = dot(back, outer_block(second, here)).astype(jnp.bfloat16)
    for i, value in enumerate(spread(both)):
        value = value.reshape(2, 2, 2, 16, LANE)
        for low in range(2):
            for core in range(2):
                for high in range(2):
                    store(high, low, core, slice(i * LANE, (i + 1) * LANE), value[low, core, high])


def first_columns_kernel(
    half, data, kernels, outer_in, inner_in, inner_back_in, back_in, beyond_in, twist_in,
    out, spectrum, outside,
    data_buf, kernel_buf, outer, inner, inner_back, back, beyond, twist,
    out_buf, spectrum_buf, first, mixed, second, sems,
):
    rows = data_buf.shape[1]
    early = [
        pltpu.make_async_copy(source, target, sems.at[3, i])
        for i, (source, target) in enumerate(
            (
                (data.at[:, pl.ds(0, rows), :], data_buf),
                (outer_in, outer),
                (twist_in, twist),
                (inner_in, inner),
                (inner_back_in, inner_back),
                (back_in.at[half[0]], back),
                (beyond_in.at[half[0]], beyond),
            )
        )
    ]
    for load in early:
        load.start()
    loads = []
    for pair in range(PAIRS):
        here = pl.ds(2 * pair, 2)
        loads.append(
            pltpu.make_async_copy(kernels.at[0, here], kernel_buf.at[here], sems.at[1, pair])
        )
        loads[-1].start()
    for load in early[:3]:
        load.wait()
    for i in range(0, INN // 16, 2):
        pieces = []
        for part in range(2):
            lanes = slice(part * LANE, (part + 1) * LANE)
            for parity in range(2):
                at = parity * INN + i * 16
                block = data_buf[:, at : at + 32, lanes]
                block = jnp.concatenate([block[:, :16], block[:, 16:]], axis=2)
                pieces.append(block.reshape(OUT // 2 * 16, 2 * LANE))
        both = dot(outer[...], jnp.concatenate(pieces, axis=0))
        for c in range(2):
            re, im = (both[p * INN : (p + 1) * INN, c * LANE : (c + 1) * LANE] for p in range(2))
            cos, sin = (twist[0, :, t + i + c : t + i + c + 1] for t in (0, 16))
            here = slice((i + c) * 16, (i + c + 1) * 16)
            for part, value in enumerate((re * cos + im * sin, im * cos - re * sin)):
                value = value.astype(jnp.bfloat16).reshape(PAIRS, 2, 16, LANE)
                first[:, part, here, :LANE] = value[:, 0]
                first[:, part, here, LANE:] = value[:, 1]
    stores = []

    def transform(pair):
        block = jnp.concatenate(
            [first[pair + i].reshape(2 * INN, 2 * LANE) for i in range(2)], axis=1
        )
        both = dot(inner[...], block)
        result = []
        for i in range(2):
            result.append(both[:, i * 2 * LANE : (i + 1) * 2 * LANE])
            spectrum_buf[pair + i] = result[i].astype(jnp.bfloat16)
        here = pl.ds(pair, 2)
        copy = pltpu.make_async_copy(spectrum_buf.at[here], spectrum.at[here], sems.at[2, pair])
        stores.append(copy)
        copy.start()
        return result

    early[3].wait()
    both = transform(0)
    early[4].wait()
    for pair in range(PAIRS):
        if pair % 2 == 0:
            now_both = both
            both = transform(pair + 2) if pair + 2 < PAIRS else None
        loads[pair].wait()
        now = kernel_buf.at[pl.ds(2 * pair, 2)]
        mix_and_open(pair, now_both[pair % 2], now, inner_back, twist, mixed.at[pair % 2], second)
    for load in early[5:]:
        load.wait()
    open_outside(half, beyond[...], second, outside.at[0])
    for chunk in range(INN // 16):
        side, rows = chunk // 8, slice(chunk % 8 * 16, chunk % 8 * 16 + 16)

        def store(high, low, core, lanes, value):
            out_buf[side, high, low, core, rows, lanes] = value

        close_chunk(slice(chunk * 16, chunk * 16 + 16), back[...], second, store)
        if chunk % 4 == 3:
            here = pl.ds((chunk % 8 - 3) * 16, 64)
            source = out_buf.at[side, :, :, :, here, :]
            target = out.at[:, side, :, :, here, :]
            stores.append(pltpu.make_async_copy(source, target, sems.at[0, chunk // 4]))
            stores[-1].start()
    for copy in stores:
        copy.wait()


def next_columns_kernel(
    half, spectrum, kernels, inner_back, back, beyond, twist, out, outside, mixed, second
):
    step = pl.program_id(1)
    for s in range(2):

        @pl.when(step == s)
        def _():
            for i in range(PAIRS // 2):
                pair = s * (PAIRS // 2) + i
                both = spectrum[i].astype(jnp.float32)
                now = kernels.at[0, pl.ds(2 * i, 2)]
                mix_and_open(pair, both, now, inner_back, twist, mixed.at[i % 2], second)
            if s == 1:
                open_outside(half, beyond[0], second, outside.at[0])

    @pl.when(step >= 2)
    def _():
        for c in range(8):
            rows = slice(c * 16, (c + 1) * 16)

            def store(high, low, core, lanes, value):
                out[high, 0, low, core, rows, lanes] = value

            start = pl.multiple_of(((step - 2) * 8 + c) * 16, 16)
            close_chunk(pl.ds(start, 16), back[0], second, store)


def first_columns(half, data, kernels):
    tables = [jnp.asarray(t) for t in column_tables()]
    rows = data.shape[1] - 16
    bf16, f32 = jnp.bfloat16, jnp.float32
    hbm = pl.BlockSpec(memory_space=pl.ANY)
    return pl.pallas_call(
        first_columns_kernel,
        grid_spec=pltpu.PrefetchScalarGridSpec(
            num_scalar_prefetch=1,
            grid=(1,),
            in_specs=[hbm] * 8,
            out_specs=[hbm, hbm, pl.BlockSpec((1, 16, 4 * LANE), lambda i, o: (0, 0, 0))],
            scratch_shapes=[
                pltpu.VMEM((8, rows, 2 * LANE), bf16),
                pltpu.VMEM((OUT, INN, 2 * LANE), bf16),
                pltpu.VMEM((2 * INN, 2 * INN), bf16),
                pltpu.VMEM((2 * INN, 2 * INN), bf16),
                pltpu.VMEM((2 * INN, 2 * INN), bf16),
                pltpu.VMEM((INN, 2 * INN), bf16),
                pltpu.VMEM((32, 2 * INN), bf16),
                pltpu.VMEM((2, INN, LANE), f32),
                pltpu.VMEM((2, 2, 2, 2, LANE, 4 * LANE), bf16),
                pltpu.VMEM((PAIRS, 2 * INN, 2 * LANE), bf16),
                pltpu.VMEM((PAIRS, 2, INN, 2 * LANE), bf16),
                pltpu.VMEM((2, 2 * INN, 4 * LANE), bf16),
                pltpu.VMEM((2, OUT, INN, 2 * LANE), bf16),
                pltpu.SemaphoreType.DMA((4, PAIRS)),
            ],
        ),
        out_shape=[
            jax.ShapeDtypeStruct((2, 2, 2, 2, LANE, 4 * LANE), bf16),
            jax.ShapeDtypeStruct((PAIRS, 2 * INN, 2 * LANE), bf16),
            jax.ShapeDtypeStruct((1, 16, 4 * LANE), bf16),
        ],
        compiler_params=pltpu.CompilerParams(vmem_limit_bytes=VMEM),
        cost_estimate=pl.CostEstimate(flops=10**10, bytes_accessed=16 * MIB, transcendentals=0),
        name="first_columns",
    )(half, data, kernels, *tables)


def next_columns(half, plane, count, spectrum, kernels):
    tables = [jnp.asarray(t) for t in column_tables()[2:]]
    opening = lambda i: jnp.minimum(i, 1)
    closing = lambda i: jnp.maximum(i - 2, 0)
    own = lambda g, i, o: (o[0], 0, 0)
    return pl.pallas_call(
        next_columns_kernel,
        grid_spec=pltpu.PrefetchScalarGridSpec(
            num_scalar_prefetch=1,
            grid=(count, 4),
            in_specs=[
                pl.BlockSpec((PAIRS // 2, 2 * INN, 2 * LANE), lambda g, i, o: (opening(i), 0, 0)),
                pl.BlockSpec(
                    (1, OUT // 2, INN, 2 * LANE), lambda g, i, o: (plane + g, opening(i), 0, 0)
                ),
                pl.BlockSpec((2 * INN, 2 * INN), lambda g, i, o: (0, 0)),
                pl.BlockSpec((1, INN, 2 * INN), own),
                pl.BlockSpec((1, 32, 2 * INN), own),
                pl.BlockSpec((2, INN, LANE), lambda g, i, o: (0, 0, 0)),
            ],
            out_specs=[
                pl.BlockSpec(
                    (2, 1, 2, 2, LANE, 4 * LANE), lambda g, i, o: (0, closing(i), 0, 0, 0, g)
                ),
                pl.BlockSpec((1, 16, 4 * LANE), lambda g, i, o: (g, 0, 0)),
            ],
            scratch_shapes=[
                pltpu.VMEM((2, 2 * INN, 4 * LANE), jnp.bfloat16),
                pltpu.VMEM((2, OUT, INN, 2 * LANE), jnp.bfloat16),
            ],
        ),
        out_shape=[
            jax.ShapeDtypeStruct((2, 2, 2, 2, LANE, count * 4 * LANE), jnp.bfloat16),
            jax.ShapeDtypeStruct((count, 16, 4 * LANE), jnp.bfloat16),
        ],
        compiler_params=pltpu.CompilerParams(vmem_limit_bytes=VMEM),
        cost_estimate=pl.CostEstimate(
            flops=count * 7 * 10**9, bytes_accessed=count * 16 * MIB, transcendentals=0
        ),
        name="next_columns",
    )(half, spectrum, kernels, *tables)


def sixteen_points(re, im):
    c = math.sqrt(0.5)
    c1, c3 = math.cos(math.pi / 8), math.cos(3 * math.pi / 8)
    r0, r1, r2, r3, r4, r5, r6, r7 = re
    r8, i1, i2, i3, i4, i5, i6, i7 = im
    sum08, dif08, sum26, dif26 = r0 + r8, r0 - r8, r2 + r6, c * (r2 - r6)
    base = sum08 + r4
    even = [base + sum26, dif08 + dif26, sum08 - r4, dif08 - dif26, base - sum26]
    sum17, dif17, sum35, dif35 = r1 + r7, r1 - r7, r3 + r5, r3 - r5
    odd = [sum17 + sum35, c1 * dif17 + c3 * dif35, c * (sum17 - sum35), c3 * dif17 - c1 * dif35]
    cosines = [even[a] + odd[a] for a in range(4)] + [even[4]]
    cosines += [even[8 - a] - odd[8 - a] for a in range(5, 9)]
    s17, d17, s35, d35 = i1 + i7, i1 - i7, i3 + i5, i3 - i5
    sines_odd = [None, c3 * s17 + c1 * s35, c * (d17 + d35), c1 * s17 - c3 * s35, d17 - d35]
    s26 = c * (i2 + i6)
    sines_even = [None, s26 + i4, i2 - i6, s26 - i4]
    sines = [None] + [sines_odd[a] + sines_even[a] for a in (1, 2, 3)] + [sines_odd[4]]
    sines += [sines_odd[8 - a] - sines_even[8 - a] for a in (5, 6, 7)]
    result = [cosines[0]] + [cosines[a] - sines[a] for a in range(1, 8)] + [cosines[8]]
    return result + [cosines[16 - a] + sines[16 - a] for a in range(9, 16)]


def open_rows(group, both, turn):
    if group == 0:
        return both
    re, im = both[:, :INN], both[:, INN:]
    cos, sin = turn[group : group + 1, :], turn[CLS + group : CLS + group + 1, :]
    return jnp.concatenate([re * cos - im * sin, re * sin + im * cos], axis=1)


def open_classes(groups, halves, columns, table, turn, opened):
    blocks = []
    for group, (low, high) in zip(groups, halves):
        for part in range(2):
            lanes = slice(part * 2 * LANE, (part + 1) * 2 * LANE)
            first, rest = low[:, lanes], high[:, lanes]
            if group == 0:
                lane = lax.broadcasted_iota(jnp.int32, (first.shape[0], LANE), 1)
                im = jnp.where(lane == 0, columns[part], first[:, LANE:])
                first = jnp.concatenate([first[:, :LANE], im], axis=1)
            blocks.append(jnp.concatenate([first, rest], axis=1))
    rows = blocks[0].shape[0]
    both = dot(jnp.concatenate(blocks, axis=0), table[min(groups[0], 1)])
    for i, group in enumerate(groups):
        for part in range(2):
            at = (2 * i + part) * rows
            opened[part, group] = open_rows(group, both[at : at + rows], turn)


def strip_intensity(opened, here, tile):
    total = None
    for part in range(2):
        re = [opened[part, g, here, tile * LANE : (tile + 1) * LANE] for g in range(CLS)]
        im = [opened[part, g, here, INN + tile * LANE : INN + (tile + 1) * LANE] for g in range(CLS)]
        values = sixteen_points(re, im)
        if total is None:
            total = [v * v for v in values]
        else:
            total = [t + v * v for t, v in zip(total, values)]
    return total


def row_inverse_kernel(plane, parts, nyquist, table, turn, out, edges, opened):
    current = plane + pl.program_id(0)
    rows = parts.shape[3]
    lane = lax.broadcasted_iota(jnp.int32, (rows, LANE), 1)
    columns = []
    for part in range(2):
        mine = jnp.where(lane == current * 2 + part, nyquist[...], 0.0)
        columns.append(jnp.sum(mine, axis=1, keepdims=True).astype(jnp.bfloat16))
    for groups in BATCHES:
        halves = [[parts[g // 2, i, g % 2] for i in range(2)] for g in groups]
        open_classes(groups, halves, columns, table, turn, opened)

    def strip(i, carry):
        here = pl.ds(pl.multiple_of(i * 16, 16), 16)
        for tile in range(INN // LANE):
            total = strip_intensity(opened, here, tile)
            for a in range(OUT):
                lanes = slice(a * INN + tile * LANE, a * INN + (tile + 1) * LANE)
                out[0, here, lanes] = total[a].astype(jnp.bfloat16)
        return carry

    lax.fori_loop(0, rows // 16, strip, 0)
    edges[0, 0:8, :] = out[0, 0:16, :].astype(jnp.float32)[0:8]
    edges[0, 8:16, :] = out[0, rows - 16 :, :].astype(jnp.float32)[8:16]


def row_inverse(plane, count, parts, nyquist):
    rows = parts.shape[3]
    table, turn = (jnp.asarray(t) for t in row_inverse_tables())
    return pl.pallas_call(
        functools.partial(row_inverse_kernel, plane),
        grid=(count,),
        in_specs=[
            pl.BlockSpec((4, 2, 2, rows, 4 * LANE), lambda g: (0, 0, 0, 0, g)),
            pl.BlockSpec((rows, LANE), lambda g: (0, 0)),
            pl.BlockSpec((2, 2 * INN, 2 * INN), lambda g: (0, 0, 0)),
            pl.BlockSpec((2 * CLS, INN), lambda g: (0, 0)),
        ],
        out_specs=[
            pl.BlockSpec((1, rows, N), lambda g: (g, 0, 0)),
            pl.BlockSpec((1, 16, N), lambda g: (g, 0, 0)),
        ],
        out_shape=[
            jax.ShapeDtypeStruct((count, rows, N), jnp.bfloat16),
            jax.ShapeDtypeStruct((count, 16, N), jnp.float32),
        ],
        scratch_shapes=[pltpu.VMEM((2, CLS, rows, 2 * INN), jnp.float32)],
        compiler_params=pltpu.CompilerParams(vmem_limit_bytes=VMEM),
        cost_estimate=pl.CostEstimate(
            flops=count * 3 * 10**9, bytes_accessed=count * 8 * MIB, transcendentals=0
        ),
        name="row_inverse",
    )(parts, nyquist, table, turn)


def nyquist_kernel(planes, own, data, out):
    wide = lambda axis: lax.broadcasted_iota(jnp.int32, (INN, INN), axis)
    tall = lambda axis: lax.broadcasted_iota(jnp.int32, (OUT, INN), axis)
    small = lambda axis: lax.broadcasted_iota(jnp.int32, (OUT, OUT), axis)

    def wave(products, period):
        turn = (products % period).astype(jnp.float32) * (2.0 * math.pi / period)
        return jnp.cos(turn), jnp.sin(turn)

    def exact(left, right):
        return jnp.dot(left, right, preferred_element_type=jnp.float32, precision=lax.Precision.HIGHEST)

    def product(xr, xi, yr, yi):
        return exact(xr, yr) - exact(xi, yi), exact(xr, yi) + exact(xi, yr)

    def rotated(xr, xi, yr, yi):
        return xr * yr - xi * yi, xr * yi + xi * yr

    column = jnp.concatenate([data[i, 0:2, :].astype(jnp.float32) for i in range(8)], axis=0)
    wr, wi = wave(small(0) * small(1), OUT)
    inner_r, inner_i = wave(wide(0) * wide(1), INN)
    vr, vi = wave(tall(0) * tall(1), N)
    ar, ai = rotated(exact(wr, column), exact(-wi, column), vr, -vi)
    yr, yi = product(ar, ai, inner_r, -inner_i)
    fy = signed_fraction(tall(0) + OUT * tall(1))
    (kr, ki), (sr, si) = start_and_step(fy * fy + 0.25)
    block, blocks = own[0], own[1]
    k = lax.broadcasted_iota(jnp.int32, (8, OUT), 1)
    section = block // 2 + lax.broadcasted_iota(jnp.int32, (8, OUT), 0) + (OUT - 1)
    hr, hi = wave(k * (section % OUT), OUT)
    even = block % 2 == 0
    lane = lax.broadcasted_iota(jnp.int32, (1, LANE), 1)
    result, beside = [], []
    for g in range(planes):
        pr, pi = rotated(yr, yi, kr, ki)
        br, bi = rotated(*product(pr, pi, inner_r, inner_i), vr, vi)
        for value in product(hr, hi, br, bi):
            value = value * (1.0 / N)
            result.append(jnp.where(even, value[1:2, :LANE], value[1:2, LANE:]))
            above = jnp.where(even, value[0:1, INN - 1 :], value[1:2, LANE - 1 : LANE])
            above = jnp.where(block == 0, value[1:2, 0:1], above)
            below = jnp.where(even, value[1:2, LANE : LANE + 1], value[2:3, 0:1])
            below = jnp.where(block == blocks - 1, value[1:2, INN - 1 :], below)
            beside.append(jnp.where(lane == 0, above, jnp.where(lane == 1, below, 0.0)))
        kr, ki = rotated(kr, ki, sr, si)
    rest = [jnp.zeros((LANE - 2 * planes, LANE), jnp.float32)]
    out[:LANE, :] = jnp.concatenate(result + rest, axis=0).T
    out[LANE:, :] = jnp.concatenate(beside + rest, axis=0).T


def nyquist_column(own, planes, data):
    rows = data.shape[1] - 16
    return pl.pallas_call(
        functools.partial(nyquist_kernel, planes),
        grid_spec=pltpu.PrefetchScalarGridSpec(
            num_scalar_prefetch=1,
            grid=(1,),
            in_specs=[pl.BlockSpec((8, 16, 2 * LANE), lambda i, o: (0, rows // 16, 0))],
            out_specs=pl.BlockSpec((2 * LANE, LANE), lambda i, o: (0, 0)),
        ),
        out_shape=jax.ShapeDtypeStruct((2 * LANE, LANE), jnp.float32),
        compiler_params=pltpu.CompilerParams(vmem_limit_bytes=VMEM),
        cost_estimate=pl.CostEstimate(flops=10**9, bytes_accessed=2**18, transcendentals=0),
        name="nyquist",
    )(own, data)


TILE = 512


def across(centre, tile, west, east):
    lane = lax.broadcasted_iota(jnp.int32, centre.shape, 1)
    right = jnp.where(lane == TILE - 1, east, pltpu.roll(centre, TILE - 1, 1))
    left = jnp.where(lane == 0, west, pltpu.roll(centre, 1, 1))
    return (right - left) * (right - left)


def spatial_term(held, r, t):
    lanes = slice(t * TILE, (t + 1) * TILE)
    around = held[pl.ds(pl.multiple_of(r - 8, 8), 32), lanes]
    centre, down = around[8:24], around[9:25] - around[7:23]
    first, last = max(t * TILE - 1, 0), min((t + 1) * TILE, N - 1)
    here = pl.ds(r, 16)
    west, east = held[here, first : first + 1], held[here, last : last + 1]
    return centre, down * down + across(centre, TILE, west, east)


def hold(held, block, rows):
    held[8 : 8 + rows, :] = block.astype(jnp.float32)
    held[7:8, :] = held[8:9, :]
    held[8 + rows : 9 + rows, :] = held[7 + rows : 8 + rows, :]


def early_focus_kernel(first, others, best, spatial, held):
    rows = first.shape[1]
    for g in range(3):
        hold(held.at[g], first[0] if g == 0 else others[g - 1], rows)

    def strip(i, carry):
        r = pl.multiple_of(8 + i * 16, 8)
        here = pl.ds(pl.multiple_of(i * 16, 16), 16)
        for t in range(N // TILE):
            lanes = slice(t * TILE, (t + 1) * TILE)
            (c0, s0), (c1, s1), (c2, s2) = (spatial_term(held.at[g], r, t) for g in range(3))
            d0, d1 = c1 - c0, c2 - c0
            score = jnp.maximum(d0 * d0 + s0, d1 * d1 + s1)
            best[here, lanes] = (score * 0.125).astype(jnp.bfloat16)
            spatial[here, lanes] = s2.astype(jnp.bfloat16)
        return carry

    lax.fori_loop(0, rows // 16, strip, 0)


def early_focus(first, others):
    rows = first.shape[1]
    return pl.pallas_call(
        early_focus_kernel,
        out_shape=[
            jax.ShapeDtypeStruct((rows, N), jnp.bfloat16),
            jax.ShapeDtypeStruct((rows, N), jnp.bfloat16),
        ],
        scratch_shapes=[pltpu.VMEM((3, rows + 16, N), jnp.float32)],
        compiler_params=pltpu.CompilerParams(vmem_limit_bytes=VMEM),
        cost_estimate=pl.CostEstimate(flops=10**9, bytes_accessed=12 * MIB, transcendentals=0),
        name="early_focus",
    )(first, others)


def edge_rows(edges, halo):
    lane = lax.broadcasted_iota(jnp.int32, (2, N), 1)
    pair = lambda a, b: jnp.concatenate([a, b], axis=0)
    centre = [pair(e[0:1, :], e[15:16, :]) for e in edges]
    best = None
    for g, e in enumerate(edges):
        depth = centre[min(g + 1, 3)] - centre[max(g - 1, 0)]
        above, below = halo[2 * g : 2 * g + 1, :], halo[2 * g + 1 : 2 * g + 2, :]
        down = pair(e[1:2, :], below) - pair(above, e[14:15, :])
        c = centre[g]
        right = jnp.where(lane == N - 1, c, jnp.concatenate([c[:, 1:], c[:, :1]], axis=1))
        left = jnp.where(lane == 0, c, jnp.concatenate([c[:, -1:], c[:, :-1]], axis=1))
        score = depth * depth + down * down + (right - left) * (right - left)
        best = score if best is None else jnp.maximum(best, score)
    return best * 0.125


def last_rows_kernel(
    parts, best, spatial, others, nyquist_in, table_in, turn_in, edge0_in, edge12_in,
    upper_out, lower_out,
    both, nyquist, table, turn, edge0, edge12, part_buf, best_buf, spatial_buf, others_buf, opened, held, halo, edge, sems,
):
    rows = both.shape[0]
    loads = []
    for group in range(CLS):
        source = parts.at[group // 2, :, group % 2]
        loads.append(pltpu.make_async_copy(source, part_buf.at[group], sems.at[0, group]))
    late = (best, best_buf), (spatial, spatial_buf), (others, others_buf)
    late += (edge0_in, edge0), (edge12_in, edge12)
    for i, (source, target) in enumerate(late):
        loads.append(pltpu.make_async_copy(source, target, sems.at[1, i]))
    early = (nyquist_in, nyquist), (table_in, table), (turn_in, turn)
    early = [pltpu.make_async_copy(a, b, sems.at[2, i]) for i, (a, b) in enumerate(early)]
    for load in early + loads:
        load.start()
    for load in early:
        load.wait()
    lane = lax.broadcasted_iota(jnp.int32, (rows, LANE), 1)
    few_lane = lax.broadcasted_iota(jnp.int32, (16, LANE), 1)
    few_row = lax.broadcasted_iota(jnp.int32, (16, LANE), 0)
    beside = jnp.where(few_row % 2 == 0, nyquist[rows : rows + 1, :], nyquist[rows + 1 : rows + 2, :])
    columns = []
    for part in range(2):
        mine = jnp.where(lane == 6 + part, nyquist[:rows, :], 0.0)
        few = jnp.where(few_lane == (few_row // 2) * 2 + part, beside, 0.0)
        column = jnp.sum(jnp.concatenate([mine, few], axis=0), axis=1, keepdims=True)
        columns.append(column.astype(jnp.bfloat16))
    for groups in BATCHES:
        for group in groups:
            loads[group].wait()
        halves = [[part_buf[g, i] for i in range(2)] for g in groups]
        open_classes(groups, halves, columns, table, turn, opened)

    def strip(i, carry):
        base = pl.multiple_of(i * 8, 8)
        for tile in range(INN // LANE):
            for a, value in enumerate(strip_intensity(opened, pl.ds(base, 8), tile)):
                lanes = slice(a * INN + tile * LANE, a * INN + (tile + 1) * LANE)
                value = value.astype(jnp.bfloat16).astype(jnp.float32)
                held[pl.ds(pl.multiple_of(base + 8, 8), 8), lanes] = value
        return carry

    lax.fori_loop(0, rows // 8 + 1, strip, 0)
    halo[...] = held[8 + rows : 16 + rows, :]
    held[7:8, :] = held[8:9, :]
    held[8 + rows : 9 + rows, :] = held[7 + rows : 8 + rows, :]
    edge[0:8, :] = held[8:16, :]
    edge[8:16, :] = held[rows : rows + 8, :]
    for load in loads[CLS:]:
        load.wait()
    ends = edge_rows([edge0.at[0], edge12.at[0], edge12.at[1], edge], halo)

    def measure(i, carry):
        r = pl.multiple_of(8 + i * 16, 8)
        here = pl.ds(pl.multiple_of(i * 16, 16), 16)
        for t in range(N // TILE):
            lanes = slice(t * TILE, (t + 1) * TILE)
            centre, term = spatial_term(held, r, t)
            d2 = centre - others_buf[0, here, lanes].astype(jnp.float32)
            d3 = centre - others_buf[1, here, lanes].astype(jnp.float32)
            score = jnp.maximum(d2 * d2 + spatial_buf[here, lanes].astype(jnp.float32), d3 * d3 + term)
            score = jnp.maximum(score * 0.125, best_buf[here, lanes].astype(jnp.float32))
            both[here, lanes] = score.astype(jnp.bfloat16)
        return carry

    half = rows // 2
    stores = []
    for side, out in enumerate((upper_out, lower_out)):
        lax.fori_loop(side * (half // 16), (side + 1) * (half // 16), measure, 0)
        here = slice(0, 16) if side == 0 else slice(rows - 16, rows)
        index = lax.broadcasted_iota(jnp.int32, (16, N), 0)
        value = jnp.where(index == 15 * side, ends[side : side + 1], both[here].astype(jnp.float32))
        both[here] = value.astype(jnp.bfloat16)
        source = both.at[pl.ds(side * half, half)]
        stores.append(pltpu.make_async_copy(source, out, sems.at[2, 3 + side]))
        stores[-1].start()
    for store in stores:
        store.wait()


def last_rows(parts, nyquist, best, spatial, others, edge0, edge12):
    rows = best.shape[0]
    table, turn = (jnp.asarray(t) for t in row_inverse_tables())
    hbm = pl.BlockSpec(memory_space=pl.ANY)
    bf16, f32 = jnp.bfloat16, jnp.float32
    return pl.pallas_call(
        last_rows_kernel,
        in_specs=[hbm] * 9,
        out_specs=[hbm] * 2,
        out_shape=[jax.ShapeDtypeStruct((rows // 2, N), bf16)] * 2,
        scratch_shapes=[
            pltpu.VMEM((rows, N), bf16),
            pltpu.VMEM((2 * LANE, LANE), f32),
            pltpu.VMEM((2, 2 * INN, 2 * INN), bf16),
            pltpu.VMEM((2 * CLS, INN), f32),
            pltpu.VMEM((1, 16, N), f32),
            pltpu.VMEM((2, 16, N), f32),
            pltpu.VMEM((CLS, 2, rows + 16, 4 * LANE), bf16),
            pltpu.VMEM((rows, N), bf16),
            pltpu.VMEM((rows, N), bf16),
            pltpu.VMEM((2, rows, N), bf16),
            pltpu.VMEM((2, CLS, rows + 16, 2 * INN), f32),
            pltpu.VMEM((rows + 16, N), f32),
            pltpu.VMEM((8, N), f32),
            pltpu.VMEM((16, N), f32),
            pltpu.SemaphoreType.DMA((3, CLS)),
        ],
        compiler_params=pltpu.CompilerParams(vmem_limit_bytes=VMEM),
        cost_estimate=pl.CostEstimate(flops=3 * 10**9, bytes_accessed=16 * MIB, transcendentals=0),
        name="last_rows",
    )(parts, best, spatial, others, nyquist, table, turn, edge0, edge12)


def assemble_kernel(own, *refs):
    slot, out = pl.program_id(0), refs[-1]
    half = refs[0].shape[0]
    for s in range(3):

        @pl.when(slot == s)
        def _():
            out[:half] = refs[s][...].astype(jnp.float32)
            out[half:] = refs[3 + s][...].astype(jnp.float32)


def assemble(depth_index, upper, lower):
    half = upper[0].shape[0]
    whole = pl.BlockSpec((half, N), lambda s, o: (0, 0))
    return pl.pallas_call(
        assemble_kernel,
        grid_spec=pltpu.PrefetchScalarGridSpec(
            num_scalar_prefetch=1,
            grid=(3,),
            in_specs=[whole] * 6,
            out_specs=pl.BlockSpec((2 * half, N), lambda s, o: (jnp.bitwise_xor(s, o[0]), 0)),
        ),
        out_shape=jax.ShapeDtypeStruct((8 * half, N), jnp.float32),
        compiler_params=pltpu.CompilerParams(vmem_limit_bytes=20 * MIB),
        cost_estimate=pl.CostEstimate(flops=10**6, bytes_accessed=10 * MIB, transcendentals=0),
        name="assemble",
    )(depth_index, *upper, *lower)


def complete_kernel(own, upper, lower, whole, out):
    half = lower.shape[0] // 2
    step = pl.program_id(0)
    for s, ref in enumerate((upper, lower)):
        for part in range(2):

            @pl.when(step == 2 * s + part)
            def _():
                out[...] = ref[part * half : (part + 1) * half].astype(jnp.float32)


def complete(depth_index, upper, lower, whole):
    half = upper.shape[0]
    both = pl.BlockSpec((half, N), lambda i, o: (0, 0))
    place = lambda i, o: (jnp.bitwise_xor(3, o[0]) * 4 + i, 0)
    return pl.pallas_call(
        complete_kernel,
        grid_spec=pltpu.PrefetchScalarGridSpec(
            num_scalar_prefetch=1,
            grid=(4,),
            in_specs=[both, both, pl.BlockSpec(memory_space=pl.ANY)],
            out_specs=pl.BlockSpec((half // 2, N), place),
        ),
        out_shape=jax.ShapeDtypeStruct(whole.shape, jnp.float32),
        input_output_aliases={3: 0},
        compiler_params=pltpu.CompilerParams(vmem_limit_bytes=20 * MIB),
        cost_estimate=pl.CostEstimate(flops=10**6, bytes_accessed=3 * MIB, transcendentals=0),
        name="complete",
    )(depth_index, upper, lower, whole)


OVER_X = [(i, i ^ 1) for i in range(4)]
OVER_Y = [(i, i ^ 2) for i in range(4)]


def exchange_depth(a, b):
    ax, by = lax.ppermute(a, "depth", OVER_X), lax.ppermute(b, "depth", OVER_Y)
    ay, axy = lax.ppermute(a, "depth", OVER_Y), lax.ppermute(ax, "depth", OVER_Y)
    bx, byx = lax.ppermute(b, "depth", OVER_X), lax.ppermute(by, "depth", OVER_X)
    return (a, ax, ay, axy), (b, bx, by, byx)


def border_rows(halfway, outside, high):
    lanes = 4 * LANE
    count = halfway.shape[-1] // lanes
    natural = lambda rows: rows.reshape(4, 2, 2, count, lanes).transpose(1, 2, 0, 3, 4).reshape(16, count, lanes)
    first, last = natural(halfway[..., 0, :]), natural(halfway[..., -1, :])
    above = jnp.where(high == 0, first[:1], outside[None, :, 15])
    below = jnp.where(high == 0, outside[None, :, 0], last[-1:])
    above = jnp.concatenate([above, last[:-1]])
    below = jnp.concatenate([first[1:], below])
    both = jnp.stack([above, below], axis=2).reshape(2, 2, 4, 2 * count, lanes)
    return both.transpose(2, 0, 1, 3, 4).reshape(16, 2 * count, lanes)


def half_spectrum_shards(hologram, background):
    rows = hologram.shape[0]
    planes = lax.axis_size("depth") * PL_DEV
    depth, high = lax.axis_index("depth"), lax.axis_index("high")
    low, core = lax.axis_index("low"), lax.axis_index("core")
    as_scalar = lambda value: jnp.reshape(value, (1,)).astype(jnp.int32)
    own = rows // 4
    block = ((high * 2 + low) * 2 + core) * 4 + depth
    place = jnp.stack([block, jnp.int32(N // own)]).astype(jnp.int32)

    sections = row_forward(as_scalar(depth), hologram, background)
    data = lax.all_to_all(
        sections.reshape(8, rows + 16, 2 * LANE),
        ("high", "low", "core"),
        split_axis=0,
        concat_axis=0,
        tiled=True,
    )

    group = depth * 2 + core
    slot = low * LANE + jnp.arange(LANE, dtype=jnp.int32)
    special = jnp.where(low == 0, 0, CLS) + OUT * jnp.arange(LANE, dtype=jnp.int32)
    fx = signed_fraction(jnp.where(group == 0, special, group + OUT * slot))
    kernels = propagators(planes, (fx * fx)[None])

    def to_rows(halfway):
        parts = lax.all_to_all(
            halfway.reshape(16, -1, halfway.shape[-1]),
            ("depth", "low", "core"),
            split_axis=0,
            concat_axis=0,
            tiled=True,
        )
        return parts.reshape(4, 2, 2, -1, halfway.shape[-1])

    halfway, spectrum, outside = first_columns(as_scalar(high), data, kernels)
    parts, borders = [to_rows(halfway)], [border_rows(halfway, outside, high)]
    for plane, count in ((1, 2), (3, 1)):
        halfway, outside = next_columns(as_scalar(high), plane, count, spectrum, kernels)
        borders.append(border_rows(halfway, outside, high))
        halfway = halfway.reshape(16, own, -1)
        if plane == 3:
            below = jnp.concatenate(borders, axis=1)
            below = jnp.pad(below, ((0, 0), (0, 16 - 2 * planes), (0, 0)))
            halfway = jnp.concatenate([halfway, below], axis=1)
        ready = parts[-1]
        if plane == 3:
            first, first_edge = row_inverse(0, 1, parts[0], middle)
            ready = ready, first, first_edge
        elif plane == 1:
            middle = nyquist_column(place, planes, data)
            ready = ready, middle
        halfway, ready = lax.optimization_barrier((halfway, ready))
        if plane == 3:
            parts[-1], first, first_edge = ready
        else:
            parts[-1], middle = ready
        parts.append(to_rows(halfway))
    others, others_edge = row_inverse(1, 2, parts[1], middle)
    best, spatial = early_focus(first, others)
    upper, lower = last_rows(parts[2], middle, best, spatial, others, first_edge, others_edge)
    upper, lower = exchange_depth(upper, lower)
    whole = assemble(as_scalar(depth), upper[:3], lower[:3])
    return complete(as_scalar(depth), upper[3], lower[3], whole)


def solution(mesh):
    spec = P("rows", None)
    if mesh.shape["depth"] == 4 and mesh.shape["rows"] == 8:
        split = Mesh(mesh.devices.reshape(4, 2, 2, 2), ("depth", "high", "low", "core"))
        spec = P(("high", "low", "core"), None)
        body = half_spectrum_shards
    else:
        split, body = mesh, shards
    return jax.shard_map(body, mesh=split, in_specs=(spec, spec), out_specs=spec, check_vma=False)
```

```python
import functools
import math

import jax
import jax.numpy as jnp
import numpy as np
from jax import lax
from jax.experimental import pallas as pl
from jax.experimental.pallas import tpu as pltpu
from jax.sharding import Mesh
from jax.sharding import PartitionSpec as P

N = 4096
RADIX = 64
PL_DEV = 1


wave_number = 0.6
depth_start = 8.0
depth_step = 2.0


def padded_2(block, sides, width):
    for axis, dim in sides:
        count = lax.axis_size(axis)
        forward = [(i, i + 1) for i in range(count - 1)]
        backward = [(target, source) for source, target in forward]
        low = lax.ppermute(
            lax.slice_in_dim(block, block.shape[dim] - width, None, axis=dim), axis, forward
        )
        high = lax.ppermute(lax.slice_in_dim(block, 0, width, axis=dim), axis, backward)
        block = jnp.concatenate([low, block, high], axis=dim)
    return block


def fourier_tables(radix_size, sign_value):
    indices = jnp.arange(radix_size, dtype=jnp.int32)
    products = indices[:, None] * indices[None, :] % radix_size
    angles = products.astype(jnp.float32) * (sign_value * 2.0 * math.pi / radix_size)
    scaling = 1.0 / math.sqrt(radix_size)
    cosine_part = jnp.cos(angles) * scaling
    sine_part = jnp.sin(angles) * scaling
    matrix = jnp.stack([jnp.stack([cosine_part, -sine_part]), jnp.stack([sine_part, cosine_part])])
    return matrix.astype(jnp.bfloat16)


def twiddle_table(radix_size, sign_value):
    indices = jnp.arange(radix_size, dtype=jnp.int32)
    total = radix_size * radix_size
    products = indices[:, None] * indices[None, :] % total
    angles = products.astype(jnp.float32) * (sign_value * 2.0 * math.pi / total)
    return (jnp.cos(angles), jnp.sin(angles))


def rotate(data, cosine_part, sine_part):
    return jnp.stack(
        [data[0] * cosine_part - data[1] * sine_part, data[0] * sine_part + data[1] * cosine_part]
    )


def contract(form, matrix, data):
    return jnp.einsum(form, matrix, data, preferred_element_type=jnp.float32)


def forward_real(data):
    batch_size = data.shape[1]
    shaped = data.reshape(RADIX, RADIX, batch_size)
    matrix = fourier_tables(RADIX, -1.0)
    cosine_part, sine_part = twiddle_table(RADIX, -1.0)
    opening = contract("oka,abm->okbm", matrix[:, 0], shaped)
    sectioned = rotate(opening, cosine_part[:, :, None], sine_part[:, :, None]).astype(jnp.bfloat16)
    closing = contract("ocjb,ckbm->okjm", matrix, sectioned)
    return closing.reshape(2, N, batch_size).astype(jnp.bfloat16)


def forward_first(data):
    batch_size = data.shape[2]
    shaped = data.reshape(2, RADIX, RADIX, batch_size)
    matrix = fourier_tables(RADIX, -1.0)
    cosine_part, sine_part = twiddle_table(RADIX, -1.0)
    opening = contract("ocka,cabm->okbm", matrix, shaped)
    sectioned = rotate(opening, cosine_part[:, :, None], sine_part[:, :, None]).astype(jnp.bfloat16)
    closing = contract("ocjb,ckbm->okjm", matrix, sectioned)
    return closing.reshape(2, N, batch_size).astype(jnp.bfloat16)


def inverse_first(data):
    batch_size = data.shape[2]
    shaped = data.reshape(2, RADIX, RADIX, batch_size)
    matrix = fourier_tables(RADIX, 1.0)
    cosine_part, sine_part = twiddle_table(RADIX, 1.0)
    opening = contract("ocbj,ckjm->okbm", matrix, shaped)
    sectioned = rotate(opening, cosine_part[:, :, None], sine_part[:, :, None]).astype(jnp.bfloat16)
    closing = contract("ocak,ckbm->oabm", matrix, sectioned)
    return closing.reshape(2, N, batch_size)


def frequencies(positions):
    natural = positions // RADIX + RADIX * (positions % RADIX)
    signed_freq = jnp.where(natural >= N // 2, natural - N, natural)
    return signed_freq.astype(jnp.float32) / N


def propagator(freq_whole, freq_own, distance):
    radial = freq_whole[:, None] ** 2 + freq_own[None, :] ** 2
    limit = wave_number * wave_number
    amplitude = jnp.exp(-2.0 * math.pi * distance * jnp.sqrt(jnp.maximum(radial - limit, 0.0)))
    phase_angle = (
        2.0 * math.pi * distance * (jnp.sqrt(jnp.maximum(limit - radial, 0.0)) - wave_number)
    )
    return (amplitude * jnp.cos(phase_angle), amplitude * jnp.sin(phase_angle))


def propagate(spectrum, cosine_part, sine_part):
    return rotate(spectrum.astype(jnp.float32), cosine_part, sine_part).astype(jnp.bfloat16)


def shards(hologram, background):
    row_count = hologram.shape[0]
    contrast = (hologram.astype(jnp.float32) / background.astype(jnp.float32) - 1.0).astype(
        jnp.bfloat16
    )
    along_rows = forward_real(contrast.T)
    columns = lax.all_to_all(
        jnp.swapaxes(along_rows, 1, 2), "rows", split_axis=2, concat_axis=1, tiled=True
    )
    spectrum = forward_first(columns)
    row_index = lax.axis_index("rows")
    own_positions = row_index * row_count + jnp.arange(row_count, dtype=jnp.int32)
    freq_own = frequencies(own_positions)
    freq_whole = frequencies(jnp.arange(N, dtype=jnp.int32))
    depth_index = lax.axis_index("depth")
    distance = depth_start + depth_step * (depth_index * PL_DEV + 0).astype(jnp.float32)
    cosine_part, sine_part = propagator(freq_whole, freq_own, distance)
    propagated = propagate(spectrum, cosine_part, sine_part)
    halfway = inverse_first(propagated).astype(jnp.bfloat16)
    restored = lax.all_to_all(
        jnp.swapaxes(halfway, 1, 2), "rows", split_axis=2, concat_axis=1, tiled=True
    )
    result_field = inverse_first(restored)
    intensities = [
        (result_field[0] * result_field[0] + result_field[1] * result_field[1]).astype(jnp.bfloat16)
    ]
    stacked = jnp.stack(intensities)
    padded = padded_2(stacked, (("depth", 0), ("rows", 2)), 1)
    centre_block = padded[1:-1, :, 1:-1]
    plane_ids = jnp.arange(PL_DEV, dtype=jnp.int32)[:, None, None]
    row_ids = jnp.arange(row_count, dtype=jnp.int32)[None, None, :]
    depth_count = lax.axis_size("depth")
    row_groups = lax.axis_size("rows")
    lower_plane = jnp.where(
        (depth_index == 0) & (plane_ids == 0), centre_block, padded[:-2, :, 1:-1]
    )
    upper_plane = jnp.where(
        (depth_index == depth_count - 1) & (plane_ids == PL_DEV - 1),
        centre_block,
        padded[2:, :, 1:-1],
    )
    north_row = jnp.where((row_index == 0) & (row_ids == 0), centre_block, padded[1:-1, :, :-2])
    south_row = jnp.where(
        (row_index == row_groups - 1) & (row_ids == row_count - 1),
        centre_block,
        padded[1:-1, :, 2:],
    )
    centre = centre_block.astype(jnp.float32)
    east_col = jnp.concatenate([centre[:, 1:], centre[:, -1:]], axis=1)
    west_col = jnp.concatenate([centre[:, :1], centre[:, :-1]], axis=1)
    depth_diff = upper_plane.astype(jnp.float32) - lower_plane.astype(jnp.float32)
    row_diff = south_row.astype(jnp.float32) - north_row.astype(jnp.float32)
    col_diff = east_col - west_col
    scores = (depth_diff * depth_diff + row_diff * row_diff + col_diff * col_diff) / 8.0
    sharpest = jnp.max(scores, axis=0)
    merged = lax.pmax(sharpest.astype(jnp.bfloat16), "depth").astype(sharpest.dtype)
    return merged.T


OUT = 16
INN = 256
CLS = 8
LANE = 128
MIB = 2**20
VMEM = 63 * MIB
SHARED = 36 * MIB


def slot_frequencies():
    table = np.arange(CLS)[:, None] + OUT * np.arange(INN)[None, :]
    half = np.arange(INN // 2)
    table[0] = np.concatenate([OUT * half, CLS + OUT * half])
    return table


def angles(products):
    return 2.0 * np.pi * (products % N) / N


def row_forward_tables():
    freq = slot_frequencies()
    theta = angles(np.arange(INN)[None, :, None] * freq[:, None, :])
    cos, sin = np.cos(theta) / 64.0, np.sin(theta) / 64.0
    top = np.stack([cos, -sin], axis=2)
    low = np.stack([sin, cos], axis=2)
    first = np.arange(INN) < INN // 2
    low[0] = np.where(first, 0.0, top[0])
    top[0] = np.where(first, top[0], 0.0)
    full = np.concatenate([top, low], axis=1)
    full = full.reshape(CLS, 2 * INN, 2, 2, LANE).transpose(0, 1, 3, 2, 4)
    return full.reshape(CLS, 2 * INN, 2 * INN).astype(jnp.bfloat16)


def row_forward_weights():
    a = np.arange(1, 5)
    rows = []
    for d in range(CLS // 2):
        even, odd = (2.0 * np.pi * c * a / OUT for c in (2 * d, 2 * d + 1))
        parts = np.cos(even), -np.sin(even[:3]), [float(d == 0)], np.cos(odd[:3]), -np.sin(odd), [0.0]
        rows.append(np.concatenate(parts))
    return np.concatenate(rows).astype(np.float32)


def row_inverse_tables():
    half = np.arange(INN // 2)
    position = np.arange(INN)[None, :]
    full = np.zeros((2, 2, INN, 2, INN))
    for first, place in ((0, 0), (CLS, 1)):
        theta = angles((first + OUT * half)[:, None] * position)
        rows = slice(place * INN // 2, (place + 1) * INN // 2)
        full[0, 0, rows, place], full[0, 1, rows, place] = np.cos(theta), -np.sin(theta)
    full[0, 0, 0, 0] = 0.5
    full[0, 1, 0, 0] = 0.5 * (-1.0) ** np.arange(INN)
    theta = angles(OUT * np.arange(INN)[:, None] * position)
    full[1, 0, :, 0], full[1, 0, :, 1] = np.cos(theta), np.sin(theta)
    full[1, 1, :, 0], full[1, 1, :, 1] = -np.sin(theta), np.cos(theta)
    full = full.reshape(2, 2, 2, LANE, 2 * INN).transpose(0, 2, 1, 3, 4) / 32.0
    turn = angles(np.arange(CLS)[:, None] * position)
    turn = np.concatenate([np.cos(turn), np.sin(turn)]).astype(np.float32)
    return full.reshape(2, 2 * INN, 2 * INN).astype(jnp.bfloat16), turn


def column_tables():
    turn = 2.0 * np.pi * np.arange(OUT)[:, None] * np.arange(OUT)[None, :] / OUT
    eye = np.eye(16)
    outer_cos, outer_sin = np.kron(np.cos(turn), eye) / 4.0, np.kron(np.sin(turn), eye) / 4.0
    complex_form = lambda cos, sin: np.concatenate(
        [np.concatenate([cos, -sin], axis=-1), np.concatenate([sin, cos], axis=-1)], axis=-2
    )
    slabs = lambda table: table.reshape(-1, 8, 2, 16).swapaxes(1, 2).reshape(table.shape)
    outer = complex_form(slabs(outer_cos), slabs(-outer_sin))
    half_rows = outer_cos.shape[0] // 2
    cut = lambda table, begin, size: table[begin : begin + size]
    back = np.stack(
        [
            complex_form(cut(outer_cos, begin, half_rows), cut(outer_sin, begin, half_rows))
            for begin in (0, half_rows)
        ]
    )
    beyond = np.stack(
        [complex_form(cut(outer_cos, a * 16, 16), cut(outer_sin, a * 16, 16)) for a in (8, 7)]
    )
    theta = angles(OUT * np.arange(INN)[:, None] * np.arange(INN)[None, :])
    inner = complex_form(np.cos(theta), -np.sin(theta)) / 16.0
    inner_back = complex_form(np.cos(theta), np.sin(theta)) / 16.0
    turn = angles(np.arange(OUT)[:, None] * np.arange(INN)[None, :])
    by_chunk = turn.reshape(OUT, 16, 16).swapaxes(1, 2).reshape(INN, 16)
    twist = np.zeros((2, INN, LANE), np.float32)
    for i, table in enumerate((by_chunk, turn.T)):
        twist[i, :, :16], twist[i, :, 16:32] = np.cos(table), np.sin(table)
    cast = lambda table: table.astype(jnp.bfloat16)
    return cast(outer), cast(inner), cast(inner_back), cast(back), cast(beyond), twist


def dot(left, right):
    return jnp.dot(left, right, preferred_element_type=jnp.float32)


def split_complex(both, width):
    rows = both.shape[0] // 2
    top, low = both[:rows], both[rows:]
    return top[:, :width] - low[:, width:], top[:, width:] + low[:, :width]


def quarter_kernel(radial):
    gap = wave_number * wave_number - radial
    root = jnp.sqrt(jnp.abs(gap))
    inside = gap > 0.0
    half_pi = 0.5 * math.pi
    angle = half_pi * (jnp.where(inside, root, 0.0) - wave_number)
    decay = jnp.exp(jnp.where(inside, 0.0, -half_pi * root))
    square = angle * angle
    sine = 1.0 / 362880.0
    for c in (-1.0 / 5040.0, 1.0 / 120.0, -1.0 / 6.0, 1.0):
        sine = sine * square + c
    cosine = -1.0 / 3628800.0
    for c in (1.0 / 40320.0, -1.0 / 720.0, 1.0 / 24.0, -0.5, 1.0):
        cosine = cosine * square + c
    return decay * cosine, decay * (sine * angle)


def squared(re, im):
    return (re - im) * (re + im), 2.0 * re * im


def start_and_step(radial):
    value = quarter_kernel(radial)
    distance = 0.25
    step = None
    while distance < depth_start:
        value = squared(*value)
        distance *= 2.0
        if distance == depth_step:
            step = value
    return value, step


def signed_fraction(natural):
    return jnp.where(natural >= N // 2, natural - N, natural).astype(jnp.float32) * (1.0 / N)


CHUNK = 64
BATCHES = ((1, 2), (3, 4), (5, 6, 7), (0,))


def sixteen_sums(term, w):
    c0, c8 = term(0), term(8)
    plus, minus = c0 + c8, c0 - c8
    c4, c12 = term(4), term(12)
    e4, o4 = c4 + c12, c4 - c12
    total = plus + e4
    eighth = total
    re_even = plus + w(3) * e4
    im_even = None
    re_odd, im_odd = minus, w(14) * o4
    for a in (1, 2, 3):
        p, q, r, s = term(a), term(16 - a), term(8 - a), term(8 + a)
        e, o, f, h = p + q, p - q, r + s, r - s
        both = e + f
        total = total + both
        eighth = eighth - both if a % 2 else eighth + both
        re_even = re_even + w(a - 1) * both
        term_im = w(3 + a) * (o - h)
        im_even = term_im if im_even is None else im_even + term_im
        re_odd = re_odd + w(7 + a) * (e - f)
        im_odd = im_odd + w(10 + a) * (o + h)
    return re_even, im_even + w(7) * eighth, re_odd, im_odd, total


def row_forward_kernel(
    own, weights, holo, back, table, out, holo_buf, back_buf, table_buf, acc, result, held, sems
):
    rows = holo.shape[0]
    group = own[0]
    chunks = rows // CHUNK
    loads = []
    for i in range(chunks):
        here = pl.ds(i * CHUNK, CHUNK)
        loads.append(
            (
                pltpu.make_async_copy(holo.at[here], holo_buf.at[here], sems.at[0, i]),
                pltpu.make_async_copy(back.at[here], back_buf.at[here], sems.at[1, i]),
            )
        )
        for load in loads[-1]:
            load.start()
        if i == 0:
            tables = pltpu.make_async_copy(table.at[pl.ds(2 * group, 2)], table_buf, sems.at[4, 0])
            tables.start()
    lane = lax.broadcasted_iota(jnp.int32, (16, INN), 1)
    sign = jnp.where(lane % 2 == 0, 1.0, -1.0).astype(jnp.bfloat16)
    stores = []
    for chunk in range(chunks):
        for load in loads[chunk]:
            load.wait()

        def strip(i, carry):
            here = pl.ds(pl.multiple_of(chunk * CHUNK + i * 16, 16), 16)

            def term(a):
                there = pl.ds(a * INN, INN)
                below = back_buf[here, there].astype(jnp.float32)
                inverse = pl.reciprocal(below, approx=True)
                inverse = inverse * (2.0 - below * inverse)
                value = holo_buf[here, there].astype(jnp.float32) * inverse
                return (value - 1.0).astype(jnp.bfloat16).astype(jnp.float32)

            sums = sixteen_sums(term, lambda n: weights[group * 16 + n])
            for q in range(4):
                acc[q // 2, here, pl.ds((q % 2) * INN, INN)] = sums[q].astype(jnp.bfloat16)
            acc[2, here, pl.ds(0, INN)] = sums[4].astype(jnp.bfloat16)
            return carry

        lax.fori_loop(0, CHUNK // 16, strip, 0)
        batch = rows // 2 // CHUNK
        if chunk % batch != batch - 1:
            continue
        if chunk < batch:
            tables.wait()
        begin, end = (chunk + 1 - batch) * CHUNK, (chunk + 1) * CHUNK
        for q in range(2):
            both = dot(acc[q, begin:end], table_buf[q]).astype(jnp.bfloat16)
            for low in range(2):
                part = both[:, low * 2 * LANE : (low + 1) * 2 * LANE]
                result[low, q, begin:end, :] = part
        held[chunk // batch] = lax.dot_general(
            sign,
            acc[2, begin:end, :INN],
            (((1,), (1,)), ((), ())),
            preferred_element_type=jnp.float32,
        )
        here = pl.ds(begin, end - begin)
        if chunk == chunks - 1:
            index = lax.broadcasted_iota(jnp.int32, (16, INN), 0)
            extra = jnp.where(index == 0, held[0], held[1]) * (1.0 / 64.0)
            for low in range(2):
                for q in range(2):
                    result[low, q, rows:, :] = extra.astype(jnp.bfloat16)
            here = pl.ds(begin, end - begin + 16)
        for high in range(2):
            source, target = result.at[:, :, here, :], out.at[high, :, :, here, :]
            stores.append(pltpu.make_async_copy(source, target, sems.at[2 + high, chunk]))
            stores[-1].start()
    for store in stores:
        store.wait()


def row_forward(own, hologram, background):
    rows = hologram.shape[0]
    table = jnp.asarray(row_forward_tables())
    weights = jnp.asarray(row_forward_weights())
    hbm = pl.BlockSpec(memory_space=pl.ANY)
    chunks = rows // CHUNK
    return pl.pallas_call(
        row_forward_kernel,
        grid_spec=pltpu.PrefetchScalarGridSpec(
            num_scalar_prefetch=2,
            grid=(1,),
            in_specs=[hbm] * 3,
            out_specs=hbm,
            scratch_shapes=[
                pltpu.VMEM((rows, N), jnp.bfloat16),
                pltpu.VMEM((rows, N), jnp.bfloat16),
                pltpu.VMEM((2, 2 * INN, 2 * INN), jnp.bfloat16),
                pltpu.VMEM((3, rows, 2 * INN), jnp.bfloat16),
                pltpu.VMEM((2, 2, rows + 16, 2 * LANE), jnp.bfloat16),
                pltpu.VMEM((2, 16, INN), jnp.float32),
                pltpu.SemaphoreType.DMA((5, chunks)),
            ],
        ),
        out_shape=jax.ShapeDtypeStruct((2, 2, 2, rows + 16, 2 * LANE), jnp.bfloat16),
        compiler_params=pltpu.CompilerParams(vmem_limit_bytes=VMEM),
        cost_estimate=pl.CostEstimate(flops=10**10, bytes_accessed=12 * MIB, transcendentals=0),
        name="row_forward",
    )(own, weights, hologram, background, table)


def propagator_kernel(planes, fx2, out):
    step = pl.program_id(0)
    strip = 32
    for i in range(INN // strip):
        rows = slice(i * strip, (i + 1) * strip)
        position = lax.broadcasted_iota(jnp.int32, (strip, LANE), 0) + i * strip
        fy = signed_fraction(step + OUT * position)
        (kr, ki), (sr, si) = start_and_step(fy * fy + fx2[...])
        for g in range(planes):
            out[g, 0, rows, :LANE] = kr.astype(jnp.bfloat16)
            out[g, 0, rows, LANE:] = ki.astype(jnp.bfloat16)
            if g + 1 < planes:
                kr, ki = kr * sr - ki * si, kr * si + ki * sr


def propagators(planes, fx2):
    return pl.pallas_call(
        functools.partial(propagator_kernel, planes),
        grid=(OUT,),
        in_specs=[pl.BlockSpec((1, LANE), lambda i: (0, 0))],
        out_specs=pl.BlockSpec((planes, 1, INN, 2 * LANE), lambda i: (0, i, 0, 0)),
        out_shape=jax.ShapeDtypeStruct((planes, OUT, INN, 2 * LANE), jnp.bfloat16),
        compiler_params=pltpu.CompilerParams(vmem_limit_bytes=VMEM),
        cost_estimate=pl.CostEstimate(flops=10**9, bytes_accessed=16 * MIB, transcendentals=10**6),
        name="propagators",
    )(fx2)


PAIRS = OUT // 2


def mix_and_open(pair, both, kernels, inner_back, twist, mixed, second):
    wide = 2 * LANE
    for k in range(2):
        yr, yi = (both[p * INN : (p + 1) * INN, k * LANE : (k + 1) * LANE] for p in range(2))
        for part in range(2):
            factor = kernels[k, :, part * LANE : (part + 1) * LANE].astype(jnp.float32)
            lanes = slice(k * wide + part * LANE, k * wide + (part + 1) * LANE)
            mixed[:INN, lanes] = (yr * factor).astype(jnp.bfloat16)
            mixed[INN:, lanes] = (yi * factor).astype(jnp.bfloat16)
    opened = dot(inner_back[...], mixed[...])
    for k in range(2):
        at = pair * 2 + k
        re, im = (opened[p * INN : (p + 1) * INN, k * wide : (k + 1) * wide] for p in range(2))
        cos, sin = twist[1, :, at : at + 1], twist[1, :, 16 + at : 17 + at]
        second[0, at] = (re * cos - im * sin).astype(jnp.bfloat16)
        second[1, at] = (re * sin + im * cos).astype(jnp.bfloat16)


def outer_block(second, here):
    return second[:, :, here, :].reshape(2 * OUT * 16, 2 * LANE)


def spread(both):
    rows = both.shape[0] // 2
    re, im = both[:rows], both[rows:]
    return [re[:, :LANE], im[:, :LANE], re[:, LANE:], im[:, LANE:]]


def open_outside(half, beyond, second, outside):
    here = pl.ds(pl.multiple_of(half[0] * (INN - 16), 16), 16)
    both = dot(beyond, outer_block(second, here)).astype(jnp.bfloat16)
    for i, value in enumerate(spread(both)):
        outside[:, i * LANE : (i + 1) * LANE] = value


def close_chunk(here, back, second, store):
    both = dot(back, outer_block(second, here)).astype(jnp.bfloat16)
    for i, value in enumerate(spread(both)):
        value = value.reshape(2, 2, 2, 16, LANE)
        for low in range(2):
            for core in range(2):
                for high in range(2):
                    store(high, low, core, slice(i * LANE, (i + 1) * LANE), value[low, core, high])


def first_columns_kernel(
    half, data, kernels, outer_in, inner_in, inner_back_in, back_in, beyond_in, twist_in,
    out, spectrum, outside,
    data_buf, kernel_buf, outer, inner, inner_back, back, beyond, twist,
    out_buf, spectrum_buf, first, mixed, second, sems,
):
    rows = data_buf.shape[1]
    early = [
        pltpu.make_async_copy(source, target, sems.at[3, i])
        for i, (source, target) in enumerate(
            (
                (data.at[:, pl.ds(0, rows), :], data_buf),
                (outer_in, outer),
                (twist_in, twist),
                (inner_in, inner),
                (inner_back_in, inner_back),
                (back_in.at[half[0]], back),
                (beyond_in.at[half[0]], beyond),
            )
        )
    ]
    for load in early:
        load.start()
    loads = []
    for pair in range(PAIRS):
        here = pl.ds(2 * pair, 2)
        loads.append(
            pltpu.make_async_copy(kernels.at[0, here], kernel_buf.at[here], sems.at[1, pair])
        )
        loads[-1].start()
    for load in early[:3]:
        load.wait()
    for i in range(0, INN // 16, 2):
        pieces = []
        for part in range(2):
            lanes = slice(part * LANE, (part + 1) * LANE)
            for parity in range(2):
                at = parity * INN + i * 16
                block = data_buf[:, at : at + 32, lanes]
                block = jnp.concatenate([block[:, :16], block[:, 16:]], axis=2)
                pieces.append(block.reshape(OUT // 2 * 16, 2 * LANE))
        both = dot(outer[...], jnp.concatenate(pieces, axis=0))
        for c in range(2):
            re, im = (both[p * INN : (p + 1) * INN, c * LANE : (c + 1) * LANE] for p in range(2))
            cos, sin = (twist[0, :, t + i + c : t + i + c + 1] for t in (0, 16))
            here = slice((i + c) * 16, (i + c + 1) * 16)
            for part, value in enumerate((re * cos + im * sin, im * cos - re * sin)):
                value = value.astype(jnp.bfloat16).reshape(PAIRS, 2, 16, LANE)
                first[:, part, here, :LANE] = value[:, 0]
                first[:, part, here, LANE:] = value[:, 1]
    stores = []

    def transform(pair):
        block = jnp.concatenate(
            [first[pair + i].reshape(2 * INN, 2 * LANE) for i in range(2)], axis=1
        )
        both = dot(inner[...], block)
        result = []
        for i in range(2):
            result.append(both[:, i * 2 * LANE : (i + 1) * 2 * LANE])
            spectrum_buf[pair + i] = result[i].astype(jnp.bfloat16)
        here = pl.ds(pair, 2)
        copy = pltpu.make_async_copy(spectrum_buf.at[here], spectrum.at[here], sems.at[2, pair])
        stores.append(copy)
        copy.start()
        return result

    early[3].wait()
    both = transform(0)
    early[4].wait()
    for pair in range(PAIRS):
        if pair % 2 == 0:
            now_both = both
            both = transform(pair + 2) if pair + 2 < PAIRS else None
        loads[pair].wait()
        now = kernel_buf.at[pl.ds(2 * pair, 2)]
        mix_and_open(pair, now_both[pair % 2], now, inner_back, twist, mixed.at[pair % 2], second)
    for load in early[5:]:
        load.wait()
    open_outside(half, beyond[...], second, outside.at[0])
    for chunk in range(INN // 16):
        side, rows = chunk // 8, slice(chunk % 8 * 16, chunk % 8 * 16 + 16)

        def store(high, low, core, lanes, value):
            out_buf[side, high, low, core, rows, lanes] = value

        close_chunk(slice(chunk * 16, chunk * 16 + 16), back[...], second, store)
        if chunk % 4 == 3:
            here = pl.ds((chunk % 8 - 3) * 16, 64)
            source = out_buf.at[side, :, :, :, here, :]
            target = out.at[:, side, :, :, here, :]
            stores.append(pltpu.make_async_copy(source, target, sems.at[0, chunk // 4]))
            stores[-1].start()
    for copy in stores:
        copy.wait()


def next_columns_kernel(
    half, spectrum, kernels, inner_back, back, beyond, twist, out, outside, mixed, second
):
    step = pl.program_id(1)
    for s in range(2):

        @pl.when(step == s)
        def _():
            for i in range(PAIRS // 2):
                pair = s * (PAIRS // 2) + i
                both = spectrum[i].astype(jnp.float32)
                now = kernels.at[0, pl.ds(2 * i, 2)]
                mix_and_open(pair, both, now, inner_back, twist, mixed.at[i % 2], second)
            if s == 1:
                open_outside(half, beyond[0], second, outside.at[0])

    @pl.when(step >= 2)
    def _():
        for c in range(8):
            rows = slice(c * 16, (c + 1) * 16)

            def store(high, low, core, lanes, value):
                out[high, 0, low, core, rows, lanes] = value

            start = pl.multiple_of(((step - 2) * 8 + c) * 16, 16)
            close_chunk(pl.ds(start, 16), back[0], second, store)


def first_columns(half, data, kernels):
    tables = [jnp.asarray(t) for t in column_tables()]
    rows = data.shape[1] - 16
    bf16, f32 = jnp.bfloat16, jnp.float32
    hbm = pl.BlockSpec(memory_space=pl.ANY)
    return pl.pallas_call(
        first_columns_kernel,
        grid_spec=pltpu.PrefetchScalarGridSpec(
            num_scalar_prefetch=1,
            grid=(1,),
            in_specs=[hbm] * 8,
            out_specs=[hbm, hbm, pl.BlockSpec((1, 16, 4 * LANE), lambda i, o: (0, 0, 0))],
            scratch_shapes=[
                pltpu.VMEM((8, rows, 2 * LANE), bf16),
                pltpu.VMEM((OUT, INN, 2 * LANE), bf16),
                pltpu.VMEM((2 * INN, 2 * INN), bf16),
                pltpu.VMEM((2 * INN, 2 * INN), bf16),
                pltpu.VMEM((2 * INN, 2 * INN), bf16),
                pltpu.VMEM((INN, 2 * INN), bf16),
                pltpu.VMEM((32, 2 * INN), bf16),
                pltpu.VMEM((2, INN, LANE), f32),
                pltpu.VMEM((2, 2, 2, 2, LANE, 4 * LANE), bf16),
                pltpu.VMEM((PAIRS, 2 * INN, 2 * LANE), bf16),
                pltpu.VMEM((PAIRS, 2, INN, 2 * LANE), bf16),
                pltpu.VMEM((2, 2 * INN, 4 * LANE), bf16),
                pltpu.VMEM((2, OUT, INN, 2 * LANE), bf16),
                pltpu.SemaphoreType.DMA((4, PAIRS)),
            ],
        ),
        out_shape=[
            jax.ShapeDtypeStruct((2, 2, 2, 2, LANE, 4 * LANE), bf16),
            jax.ShapeDtypeStruct((PAIRS, 2 * INN, 2 * LANE), bf16),
            jax.ShapeDtypeStruct((1, 16, 4 * LANE), bf16),
        ],
        compiler_params=pltpu.CompilerParams(vmem_limit_bytes=VMEM),
        cost_estimate=pl.CostEstimate(flops=10**10, bytes_accessed=16 * MIB, transcendentals=0),
        name="first_columns",
    )(half, data, kernels, *tables)


def next_columns(half, plane, count, spectrum, kernels):
    tables = [jnp.asarray(t) for t in column_tables()[2:]]
    opening = lambda i: jnp.minimum(i, 1)
    closing = lambda i: jnp.maximum(i - 2, 0)
    own = lambda g, i, o: (o[0], 0, 0)
    return pl.pallas_call(
        next_columns_kernel,
        grid_spec=pltpu.PrefetchScalarGridSpec(
            num_scalar_prefetch=1,
            grid=(count, 4),
            in_specs=[
                pl.BlockSpec((PAIRS // 2, 2 * INN, 2 * LANE), lambda g, i, o: (opening(i), 0, 0)),
                pl.BlockSpec(
                    (1, OUT // 2, INN, 2 * LANE), lambda g, i, o: (plane + g, opening(i), 0, 0)
                ),
                pl.BlockSpec((2 * INN, 2 * INN), lambda g, i, o: (0, 0)),
                pl.BlockSpec((1, INN, 2 * INN), own),
                pl.BlockSpec((1, 32, 2 * INN), own),
                pl.BlockSpec((2, INN, LANE), lambda g, i, o: (0, 0, 0)),
            ],
            out_specs=[
                pl.BlockSpec(
                    (2, 1, 2, 2, LANE, 4 * LANE), lambda g, i, o: (0, closing(i), 0, 0, 0, g)
                ),
                pl.BlockSpec((1, 16, 4 * LANE), lambda g, i, o: (g, 0, 0)),
            ],
            scratch_shapes=[
                pltpu.VMEM((2, 2 * INN, 4 * LANE), jnp.bfloat16),
                pltpu.VMEM((2, OUT, INN, 2 * LANE), jnp.bfloat16),
            ],
        ),
        out_shape=[
            jax.ShapeDtypeStruct((2, 2, 2, 2, LANE, count * 4 * LANE), jnp.bfloat16),
            jax.ShapeDtypeStruct((count, 16, 4 * LANE), jnp.bfloat16),
        ],
        compiler_params=pltpu.CompilerParams(vmem_limit_bytes=VMEM),
        cost_estimate=pl.CostEstimate(
            flops=count * 7 * 10**9, bytes_accessed=count * 16 * MIB, transcendentals=0
        ),
        name="next_columns",
    )(half, spectrum, kernels, *tables)


def sixteen_points(re, im):
    c = math.sqrt(0.5)
    c1, c3 = math.cos(math.pi / 8), math.cos(3 * math.pi / 8)
    r0, r1, r2, r3, r4, r5, r6, r7 = re
    r8, i1, i2, i3, i4, i5, i6, i7 = im
    sum08, dif08, sum26, dif26 = r0 + r8, r0 - r8, r2 + r6, c * (r2 - r6)
    base = sum08 + r4
    even = [base + sum26, dif08 + dif26, sum08 - r4, dif08 - dif26, base - sum26]
    sum17, dif17, sum35, dif35 = r1 + r7, r1 - r7, r3 + r5, r3 - r5
    odd = [sum17 + sum35, c1 * dif17 + c3 * dif35, c * (sum17 - sum35), c3 * dif17 - c1 * dif35]
    cosines = [even[a] + odd[a] for a in range(4)] + [even[4]]
    cosines += [even[8 - a] - odd[8 - a] for a in range(5, 9)]
    s17, d17, s35, d35 = i1 + i7, i1 - i7, i3 + i5, i3 - i5
    sines_odd = [None, c3 * s17 + c1 * s35, c * (d17 + d35), c1 * s17 - c3 * s35, d17 - d35]
    s26 = c * (i2 + i6)
    sines_even = [None, s26 + i4, i2 - i6, s26 - i4]
    sines = [None] + [sines_odd[a] + sines_even[a] for a in (1, 2, 3)] + [sines_odd[4]]
    sines += [sines_odd[8 - a] - sines_even[8 - a] for a in (5, 6, 7)]
    result = [cosines[0]] + [cosines[a] - sines[a] for a in range(1, 8)] + [cosines[8]]
    return result + [cosines[16 - a] + sines[16 - a] for a in range(9, 16)]


def open_rows(group, both, turn):
    if group == 0:
        return both
    re, im = both[:, :INN], both[:, INN:]
    cos, sin = turn[group : group + 1, :], turn[CLS + group : CLS + group + 1, :]
    return jnp.concatenate([re * cos - im * sin, re * sin + im * cos], axis=1)


def open_classes(groups, halves, columns, table, turn, opened):
    blocks = []
    for group, (low, high) in zip(groups, halves):
        for part in range(2):
            lanes = slice(part * 2 * LANE, (part + 1) * 2 * LANE)
            first, rest = low[:, lanes], high[:, lanes]
            if group == 0:
                lane = lax.broadcasted_iota(jnp.int32, (first.shape[0], LANE), 1)
                im = jnp.where(lane == 0, columns[part], first[:, LANE:])
                first = jnp.concatenate([first[:, :LANE], im], axis=1)
            blocks.append(jnp.concatenate([first, rest], axis=1))
    rows = blocks[0].shape[0]
    both = dot(jnp.concatenate(blocks, axis=0), table[min(groups[0], 1)])
    for i, group in enumerate(groups):
        for part in range(2):
            at = (2 * i + part) * rows
            opened[part, group] = open_rows(group, both[at : at + rows], turn)


def strip_intensity(opened, here, tile):
    total = None
    for part in range(2):
        re = [opened[part, g, here, tile * LANE : (tile + 1) * LANE] for g in range(CLS)]
        im = [opened[part, g, here, INN + tile * LANE : INN + (tile + 1) * LANE] for g in range(CLS)]
        values = sixteen_points(re, im)
        if total is None:
            total = [v * v for v in values]
        else:
            total = [t + v * v for t, v in zip(total, values)]
    return total


def row_inverse_kernel(plane, parts, nyquist, table, turn, out, edges, opened):
    current = plane + pl.program_id(0)
    rows = parts.shape[3]
    lane = lax.broadcasted_iota(jnp.int32, (rows, LANE), 1)
    columns = []
    for part in range(2):
        mine = jnp.where(lane == current * 2 + part, nyquist[...], 0.0)
        columns.append(jnp.sum(mine, axis=1, keepdims=True).astype(jnp.bfloat16))
    for groups in BATCHES:
        halves = [[parts[g // 2, i, g % 2] for i in range(2)] for g in groups]
        open_classes(groups, halves, columns, table, turn, opened)

    def strip(i, carry):
        here = pl.ds(pl.multiple_of(i * 16, 16), 16)
        for tile in range(INN // LANE):
            total = strip_intensity(opened, here, tile)
            for a in range(OUT):
                lanes = slice(a * INN + tile * LANE, a * INN + (tile + 1) * LANE)
                out[0, here, lanes] = total[a].astype(jnp.bfloat16)
        return carry

    lax.fori_loop(0, rows // 16, strip, 0)
    edges[0, 0:8, :] = out[0, 0:16, :].astype(jnp.float32)[0:8]
    edges[0, 8:16, :] = out[0, rows - 16 :, :].astype(jnp.float32)[8:16]


def row_inverse(plane, count, parts, nyquist):
    rows = parts.shape[3]
    table, turn = (jnp.asarray(t) for t in row_inverse_tables())
    return pl.pallas_call(
        functools.partial(row_inverse_kernel, plane),
        grid=(count,),
        in_specs=[
            pl.BlockSpec((4, 2, 2, rows, 4 * LANE), lambda g: (0, 0, 0, 0, g)),
            pl.BlockSpec((rows, LANE), lambda g: (0, 0)),
            pl.BlockSpec((2, 2 * INN, 2 * INN), lambda g: (0, 0, 0)),
            pl.BlockSpec((2 * CLS, INN), lambda g: (0, 0)),
        ],
        out_specs=[
            pl.BlockSpec((1, rows, N), lambda g: (g, 0, 0)),
            pl.BlockSpec((1, 16, N), lambda g: (g, 0, 0)),
        ],
        out_shape=[
            jax.ShapeDtypeStruct((count, rows, N), jnp.bfloat16),
            jax.ShapeDtypeStruct((count, 16, N), jnp.float32),
        ],
        scratch_shapes=[pltpu.VMEM((2, CLS, rows, 2 * INN), jnp.float32)],
        compiler_params=pltpu.CompilerParams(vmem_limit_bytes=VMEM),
        cost_estimate=pl.CostEstimate(
            flops=count * 3 * 10**9, bytes_accessed=count * 8 * MIB, transcendentals=0
        ),
        name="row_inverse",
    )(parts, nyquist, table, turn)


def nyquist_kernel(planes, own, data, out):
    wide = lambda axis: lax.broadcasted_iota(jnp.int32, (INN, INN), axis)
    tall = lambda axis: lax.broadcasted_iota(jnp.int32, (OUT, INN), axis)
    small = lambda axis: lax.broadcasted_iota(jnp.int32, (OUT, OUT), axis)

    def wave(products, period):
        turn = (products % period).astype(jnp.float32) * (2.0 * math.pi / period)
        return jnp.cos(turn), jnp.sin(turn)

    def exact(left, right):
        return jnp.dot(left, right, preferred_element_type=jnp.float32, precision=lax.Precision.HIGHEST)

    def product(xr, xi, yr, yi):
        return exact(xr, yr) - exact(xi, yi), exact(xr, yi) + exact(xi, yr)

    def rotated(xr, xi, yr, yi):
        return xr * yr - xi * yi, xr * yi + xi * yr

    column = jnp.concatenate([data[i, 0:2, :].astype(jnp.float32) for i in range(8)], axis=0)
    wr, wi = wave(small(0) * small(1), OUT)
    inner_r, inner_i = wave(wide(0) * wide(1), INN)
    vr, vi = wave(tall(0) * tall(1), N)
    ar, ai = rotated(exact(wr, column), exact(-wi, column), vr, -vi)
    yr, yi = product(ar, ai, inner_r, -inner_i)
    fy = signed_fraction(tall(0) + OUT * tall(1))
    (kr, ki), (sr, si) = start_and_step(fy * fy + 0.25)
    block, blocks = own[0], own[1]
    k = lax.broadcasted_iota(jnp.int32, (8, OUT), 1)
    section = block // 2 + lax.broadcasted_iota(jnp.int32, (8, OUT), 0) + (OUT - 1)
    hr, hi = wave(k * (section % OUT), OUT)
    even = block % 2 == 0
    lane = lax.broadcasted_iota(jnp.int32, (1, LANE), 1)
    result, beside = [], []
    for g in range(planes):
        pr, pi = rotated(yr, yi, kr, ki)
        br, bi = rotated(*product(pr, pi, inner_r, inner_i), vr, vi)
        for value in product(hr, hi, br, bi):
            value = value * (1.0 / N)
            result.append(jnp.where(even, value[1:2, :LANE], value[1:2, LANE:]))
            above = jnp.where(even, value[0:1, INN - 1 :], value[1:2, LANE - 1 : LANE])
            above = jnp.where(block == 0, value[1:2, 0:1], above)
            below = jnp.where(even, value[1:2, LANE : LANE + 1], value[2:3, 0:1])
            below = jnp.where(block == blocks - 1, value[1:2, INN - 1 :], below)
            beside.append(jnp.where(lane == 0, above, jnp.where(lane == 1, below, 0.0)))
        kr, ki = rotated(kr, ki, sr, si)
    rest = [jnp.zeros((LANE - 2 * planes, LANE), jnp.float32)]
    out[:LANE, :] = jnp.concatenate(result + rest, axis=0).T
    out[LANE:, :] = jnp.concatenate(beside + rest, axis=0).T


def nyquist_column(own, planes, data):
    rows = data.shape[1] - 16
    return pl.pallas_call(
        functools.partial(nyquist_kernel, planes),
        grid_spec=pltpu.PrefetchScalarGridSpec(
            num_scalar_prefetch=1,
            grid=(1,),
            in_specs=[pl.BlockSpec((8, 16, 2 * LANE), lambda i, o: (0, rows // 16, 0))],
            out_specs=pl.BlockSpec((2 * LANE, LANE), lambda i, o: (0, 0)),
        ),
        out_shape=jax.ShapeDtypeStruct((2 * LANE, LANE), jnp.float32),
        compiler_params=pltpu.CompilerParams(vmem_limit_bytes=VMEM),
        cost_estimate=pl.CostEstimate(flops=10**9, bytes_accessed=2**18, transcendentals=0),
        name="nyquist",
    )(own, data)


TILE = 512


def across(centre, tile, west, east):
    lane = lax.broadcasted_iota(jnp.int32, centre.shape, 1)
    right = jnp.where(lane == TILE - 1, east, pltpu.roll(centre, TILE - 1, 1))
    left = jnp.where(lane == 0, west, pltpu.roll(centre, 1, 1))
    return (right - left) * (right - left)


def spatial_term(held, r, t):
    lanes = slice(t * TILE, (t + 1) * TILE)
    around = held[pl.ds(pl.multiple_of(r - 8, 8), 32), lanes]
    centre, down = around[8:24], around[9:25] - around[7:23]
    first, last = max(t * TILE - 1, 0), min((t + 1) * TILE, N - 1)
    here = pl.ds(r, 16)
    west, east = held[here, first : first + 1], held[here, last : last + 1]
    return centre, down * down + across(centre, TILE, west, east)


def hold(held, block, rows):
    held[8 : 8 + rows, :] = block.astype(jnp.float32)
    held[7:8, :] = held[8:9, :]
    held[8 + rows : 9 + rows, :] = held[7 + rows : 8 + rows, :]


def early_focus_kernel(first, others, best, spatial, held):
    rows = first.shape[1]
    for g in range(3):
        hold(held.at[g], first[0] if g == 0 else others[g - 1], rows)

    def strip(i, carry):
        r = pl.multiple_of(8 + i * 16, 8)
        here = pl.ds(pl.multiple_of(i * 16, 16), 16)
        for t in range(N // TILE):
            lanes = slice(t * TILE, (t + 1) * TILE)
            (c0, s0), (c1, s1), (c2, s2) = (spatial_term(held.at[g], r, t) for g in range(3))
            d0, d1 = c1 - c0, c2 - c0
            score = jnp.maximum(d0 * d0 + s0, d1 * d1 + s1)
            best[here, lanes] = (score * 0.125).astype(jnp.bfloat16)
            spatial[here, lanes] = s2.astype(jnp.bfloat16)
        return carry

    lax.fori_loop(0, rows // 16, strip, 0)


def early_focus(first, others):
    rows = first.shape[1]
    return pl.pallas_call(
        early_focus_kernel,
        out_shape=[
            jax.ShapeDtypeStruct((rows, N), jnp.bfloat16),
            jax.ShapeDtypeStruct((rows, N), jnp.bfloat16),
        ],
        scratch_shapes=[pltpu.VMEM((3, rows + 16, N), jnp.float32)],
        compiler_params=pltpu.CompilerParams(vmem_limit_bytes=VMEM),
        cost_estimate=pl.CostEstimate(flops=10**9, bytes_accessed=12 * MIB, transcendentals=0),
        name="early_focus",
    )(first, others)


def edge_rows(edges, halo):
    lane = lax.broadcasted_iota(jnp.int32, (2, N), 1)
    pair = lambda a, b: jnp.concatenate([a, b], axis=0)
    centre = [pair(e[0:1, :], e[15:16, :]) for e in edges]
    best = None
    for g, e in enumerate(edges):
        depth = centre[min(g + 1, 3)] - centre[max(g - 1, 0)]
        above, below = halo[2 * g : 2 * g + 1, :], halo[2 * g + 1 : 2 * g + 2, :]
        down = pair(e[1:2, :], below) - pair(above, e[14:15, :])
        c = centre[g]
        right = jnp.where(lane == N - 1, c, jnp.concatenate([c[:, 1:], c[:, :1]], axis=1))
        left = jnp.where(lane == 0, c, jnp.concatenate([c[:, -1:], c[:, :-1]], axis=1))
        score = depth * depth + down * down + (right - left) * (right - left)
        best = score if best is None else jnp.maximum(best, score)
    return best * 0.125


def last_rows_kernel(
    parts, best, spatial, others, nyquist_in, table_in, turn_in, edge0_in, edge12_in,
    upper_out, lower_out,
    both, nyquist, table, turn, edge0, edge12, part_buf, best_buf, spatial_buf, others_buf, opened, held, halo, edge, sems,
):
    rows = both.shape[0]
    loads = []
    for group in range(CLS):
        source = parts.at[group // 2, :, group % 2]
        loads.append(pltpu.make_async_copy(source, part_buf.at[group], sems.at[0, group]))
    late = (best, best_buf), (spatial, spatial_buf), (others, others_buf)
    late += (edge0_in, edge0), (edge12_in, edge12)
    for i, (source, target) in enumerate(late):
        loads.append(pltpu.make_async_copy(source, target, sems.at[1, i]))
    early = (turn_in, turn), (table_in.at[1], table.at[1])
    early += (table_in.at[0], table.at[0]), (nyquist_in, nyquist)
    early = [pltpu.make_async_copy(a, b, sems.at[2, i]) for i, (a, b) in enumerate(early)]
    for load in early[:2] + loads[1:CLS] + early[2:] + loads[:1] + loads[CLS:]:
        load.start()
    for load in early[:2]:
        load.wait()
    lane = lax.broadcasted_iota(jnp.int32, (rows, LANE), 1)
    few_lane = lax.broadcasted_iota(jnp.int32, (16, LANE), 1)
    few_row = lax.broadcasted_iota(jnp.int32, (16, LANE), 0)
    columns = []
    for groups in BATCHES:
        for group in groups:
            loads[group].wait()
        if groups[0] == 0:
            for load in early[2:]:
                load.wait()
            beside = jnp.where(few_row % 2 == 0, nyquist[rows : rows + 1, :], nyquist[rows + 1 : rows + 2, :])
            for part in range(2):
                mine = jnp.where(lane == 6 + part, nyquist[:rows, :], 0.0)
                few = jnp.where(few_lane == (few_row // 2) * 2 + part, beside, 0.0)
                column = jnp.sum(jnp.concatenate([mine, few], axis=0), axis=1, keepdims=True)
                columns.append(column.astype(jnp.bfloat16))
        halves = [[part_buf[g, i] for i in range(2)] for g in groups]
        open_classes(groups, halves, columns, table, turn, opened)

    def strip(i, carry):
        base = pl.multiple_of(i * 8, 8)
        for tile in range(INN // LANE):
            for a, value in enumerate(strip_intensity(opened, pl.ds(base, 8), tile)):
                lanes = slice(a * INN + tile * LANE, a * INN + (tile + 1) * LANE)
                value = value.astype(jnp.bfloat16).astype(jnp.float32)
                held[pl.ds(pl.multiple_of(base + 8, 8), 8), lanes] = value
        return carry

    lax.fori_loop(0, rows // 8 + 1, strip, 0)
    halo[...] = held[8 + rows : 16 + rows, :]
    held[7:8, :] = held[8:9, :]
    held[8 + rows : 9 + rows, :] = held[7 + rows : 8 + rows, :]
    edge[0:8, :] = held[8:16, :]
    edge[8:16, :] = held[rows : rows + 8, :]
    for load in loads[CLS:]:
        load.wait()
    ends = edge_rows([edge0.at[0], edge12.at[0], edge12.at[1], edge], halo)

    def measure(i, carry):
        r = pl.multiple_of(8 + i * 16, 8)
        here = pl.ds(pl.multiple_of(i * 16, 16), 16)
        for t in range(N // TILE):
            lanes = slice(t * TILE, (t + 1) * TILE)
            centre, term = spatial_term(held, r, t)
            d2 = centre - others_buf[0, here, lanes].astype(jnp.float32)
            d3 = centre - others_buf[1, here, lanes].astype(jnp.float32)
            score = jnp.maximum(d2 * d2 + spatial_buf[here, lanes].astype(jnp.float32), d3 * d3 + term)
            score = jnp.maximum(score * 0.125, best_buf[here, lanes].astype(jnp.float32))
            both[here, lanes] = score.astype(jnp.bfloat16)
        return carry

    half = rows // 2
    stores = []
    for side, out in enumerate((upper_out, lower_out)):
        lax.fori_loop(side * (half // 16), (side + 1) * (half // 16), measure, 0)
        here = slice(0, 16) if side == 0 else slice(rows - 16, rows)
        index = lax.broadcasted_iota(jnp.int32, (16, N), 0)
        value = jnp.where(index == 15 * side, ends[side : side + 1], both[here].astype(jnp.float32))
        both[here] = value.astype(jnp.bfloat16)
        source = both.at[pl.ds(side * half, half)]
        stores.append(pltpu.make_async_copy(source, out, sems.at[2, 4 + side]))
        stores[-1].start()
    for store in stores:
        store.wait()


def last_rows(parts, nyquist, best, spatial, others, edge0, edge12):
    rows = best.shape[0]
    table, turn = (jnp.asarray(t) for t in row_inverse_tables())
    hbm = pl.BlockSpec(memory_space=pl.ANY)
    bf16, f32 = jnp.bfloat16, jnp.float32
    return pl.pallas_call(
        last_rows_kernel,
        in_specs=[hbm] * 9,
        out_specs=[hbm] * 2,
        out_shape=[jax.ShapeDtypeStruct((rows // 2, N), bf16)] * 2,
        scratch_shapes=[
            pltpu.VMEM((rows, N), bf16),
            pltpu.VMEM((2 * LANE, LANE), f32),
            pltpu.VMEM((2, 2 * INN, 2 * INN), bf16),
            pltpu.VMEM((2 * CLS, INN), f32),
            pltpu.VMEM((1, 16, N), f32),
            pltpu.VMEM((2, 16, N), f32),
            pltpu.VMEM((CLS, 2, rows + 16, 4 * LANE), bf16),
            pltpu.VMEM((rows, N), bf16),
            pltpu.VMEM((rows, N), bf16),
            pltpu.VMEM((2, rows, N), bf16),
            pltpu.VMEM((2, CLS, rows + 16, 2 * INN), f32),
            pltpu.VMEM((rows + 16, N), f32),
            pltpu.VMEM((8, N), f32),
            pltpu.VMEM((16, N), f32),
            pltpu.SemaphoreType.DMA((3, CLS)),
        ],
        compiler_params=pltpu.CompilerParams(vmem_limit_bytes=VMEM),
        cost_estimate=pl.CostEstimate(flops=3 * 10**9, bytes_accessed=16 * MIB, transcendentals=0),
        name="last_rows",
    )(parts, best, spatial, others, nyquist, table, turn, edge0, edge12)


def assemble_kernel(own, *refs):
    slot, out = pl.program_id(0), refs[-1]
    half = refs[0].shape[0]
    for s in range(3):

        @pl.when(slot == s)
        def _():
            out[:half] = refs[s][...].astype(jnp.float32)
            out[half:] = refs[3 + s][...].astype(jnp.float32)


def assemble(depth_index, upper, lower):
    half = upper[0].shape[0]
    whole = pl.BlockSpec((half, N), lambda s, o: (0, 0))
    return pl.pallas_call(
        assemble_kernel,
        grid_spec=pltpu.PrefetchScalarGridSpec(
            num_scalar_prefetch=1,
            grid=(3,),
            in_specs=[whole] * 6,
            out_specs=pl.BlockSpec((2 * half, N), lambda s, o: (jnp.bitwise_xor(s, o[0]), 0)),
        ),
        out_shape=jax.ShapeDtypeStruct((8 * half, N), jnp.float32),
        compiler_params=pltpu.CompilerParams(vmem_limit_bytes=20 * MIB),
        cost_estimate=pl.CostEstimate(flops=10**6, bytes_accessed=10 * MIB, transcendentals=0),
        name="assemble",
    )(depth_index, *upper, *lower)


def complete_kernel(own, upper, lower, whole, out):
    step = pl.program_id(0)
    for s, ref in enumerate((upper, lower)):

        @pl.when(step == s)
        def _():
            out[...] = ref[...].astype(jnp.float32)


def complete(depth_index, upper, lower, whole):
    half = upper.shape[0]
    both = pl.BlockSpec((half, N), lambda i, o: (0, 0))
    place = lambda i, o: (jnp.bitwise_xor(3, o[0]) * 2 + i, 0)
    return pl.pallas_call(
        complete_kernel,
        grid_spec=pltpu.PrefetchScalarGridSpec(
            num_scalar_prefetch=1,
            grid=(2,),
            in_specs=[both, both, pl.BlockSpec(memory_space=pl.ANY)],
            out_specs=pl.BlockSpec((half, N), place),
        ),
        out_shape=jax.ShapeDtypeStruct(whole.shape, jnp.float32),
        input_output_aliases={3: 0},
        compiler_params=pltpu.CompilerParams(vmem_limit_bytes=20 * MIB),
        cost_estimate=pl.CostEstimate(flops=10**6, bytes_accessed=3 * MIB, transcendentals=0),
        name="complete",
    )(depth_index, upper, lower, whole)


OVER_X = [(i, i ^ 1) for i in range(4)]
OVER_Y = [(i, i ^ 2) for i in range(4)]


def exchange_depth(a, b):
    ax, by = lax.ppermute(a, "depth", OVER_X), lax.ppermute(b, "depth", OVER_Y)
    ay, axy = lax.ppermute(a, "depth", OVER_Y), lax.ppermute(ax, "depth", OVER_Y)
    bx, byx = lax.ppermute(b, "depth", OVER_X), lax.ppermute(by, "depth", OVER_X)
    return (a, ax, ay, axy), (b, bx, by, byx)


def border_rows(halfway, outside, high):
    lanes = 4 * LANE
    count = halfway.shape[-1] // lanes
    natural = lambda rows: rows.reshape(4, 2, 2, count, lanes).transpose(1, 2, 0, 3, 4).reshape(16, count, lanes)
    first, last = natural(halfway[..., 0, :]), natural(halfway[..., -1, :])
    above = jnp.where(high == 0, first[:1], outside[None, :, 15])
    below = jnp.where(high == 0, outside[None, :, 0], last[-1:])
    above = jnp.concatenate([above, last[:-1]])
    below = jnp.concatenate([first[1:], below])
    both = jnp.stack([above, below], axis=2).reshape(2, 2, 4, 2 * count, lanes)
    return both.transpose(2, 0, 1, 3, 4).reshape(16, 2 * count, lanes)


def half_spectrum_shards(hologram, background):
    rows = hologram.shape[0]
    planes = lax.axis_size("depth") * PL_DEV
    depth, high = lax.axis_index("depth"), lax.axis_index("high")
    low, core = lax.axis_index("low"), lax.axis_index("core")
    as_scalar = lambda value: jnp.reshape(value, (1,)).astype(jnp.int32)
    own = rows // 4
    block = ((high * 2 + low) * 2 + core) * 4 + depth
    place = jnp.stack([block, jnp.int32(N // own)]).astype(jnp.int32)

    sections = row_forward(as_scalar(depth), hologram, background)
    data = lax.all_to_all(
        sections.reshape(8, rows + 16, 2 * LANE),
        ("high", "low", "core"),
        split_axis=0,
        concat_axis=0,
        tiled=True,
    )

    group = depth * 2 + core
    slot = low * LANE + jnp.arange(LANE, dtype=jnp.int32)
    special = jnp.where(low == 0, 0, CLS) + OUT * jnp.arange(LANE, dtype=jnp.int32)
    fx = signed_fraction(jnp.where(group == 0, special, group + OUT * slot))
    kernels = propagators(planes, (fx * fx)[None])

    def to_rows(halfway):
        parts = lax.all_to_all(
            halfway.reshape(16, -1, halfway.shape[-1]),
            ("depth", "low", "core"),
            split_axis=0,
            concat_axis=0,
            tiled=True,
        )
        return parts.reshape(4, 2, 2, -1, halfway.shape[-1])

    halfway, spectrum, outside = first_columns(as_scalar(high), data, kernels)
    parts, borders = [to_rows(halfway)], [border_rows(halfway, outside, high)]
    for plane, count in ((1, 2), (3, 1)):
        halfway, outside = next_columns(as_scalar(high), plane, count, spectrum, kernels)
        borders.append(border_rows(halfway, outside, high))
        halfway = halfway.reshape(16, own, -1)
        if plane == 3:
            below = jnp.concatenate(borders, axis=1)
            below = jnp.pad(below, ((0, 0), (0, 16 - 2 * planes), (0, 0)))
            halfway = jnp.concatenate([halfway, below], axis=1)
        ready = parts[-1]
        if plane == 3:
            first, first_edge = row_inverse(0, 1, parts[0], middle)
            ready = ready, first, first_edge
        elif plane == 1:
            middle = nyquist_column(place, planes, data)
            ready = ready, middle
        halfway, ready = lax.optimization_barrier((halfway, ready))
        if plane == 3:
            parts[-1], first, first_edge = ready
        else:
            parts[-1], middle = ready
        parts.append(to_rows(halfway))
    others, others_edge = row_inverse(1, 2, parts[1], middle)
    best, spatial = early_focus(first, others)
    upper, lower = last_rows(parts[2], middle, best, spatial, others, first_edge, others_edge)
    upper, lower = exchange_depth(upper, lower)
    whole = assemble(as_scalar(depth), upper[:3], lower[:3])
    return complete(as_scalar(depth), upper[3], lower[3], whole)


def solution(mesh):
    spec = P("rows", None)
    if mesh.shape["depth"] == 4 and mesh.shape["rows"] == 8:
        split = Mesh(mesh.devices.reshape(4, 2, 2, 2), ("depth", "high", "low", "core"))
        spec = P(("high", "low", "core"), None)
        body = half_spectrum_shards
    else:
        split, body = mesh, shards
    return jax.shard_map(body, mesh=split, in_specs=(spec, spec), out_specs=spec, check_vma=False)
```

```python
import functools
import math

import jax
import jax.numpy as jnp
import numpy as np
from jax import lax
from jax.experimental import pallas as pl
from jax.experimental.pallas import tpu as pltpu
from jax.sharding import Mesh
from jax.sharding import PartitionSpec as P

N = 4096
RADIX = 64
PL_DEV = 1


wave_number = 0.6
depth_start = 8.0
depth_step = 2.0


def padded_2(block, sides, width):
    for axis, dim in sides:
        count = lax.axis_size(axis)
        forward = [(i, i + 1) for i in range(count - 1)]
        backward = [(target, source) for source, target in forward]
        low = lax.ppermute(
            lax.slice_in_dim(block, block.shape[dim] - width, None, axis=dim), axis, forward
        )
        high = lax.ppermute(lax.slice_in_dim(block, 0, width, axis=dim), axis, backward)
        block = jnp.concatenate([low, block, high], axis=dim)
    return block


def fourier_tables(radix_size, sign_value):
    indices = jnp.arange(radix_size, dtype=jnp.int32)
    products = indices[:, None] * indices[None, :] % radix_size
    angles = products.astype(jnp.float32) * (sign_value * 2.0 * math.pi / radix_size)
    scaling = 1.0 / math.sqrt(radix_size)
    cosine_part = jnp.cos(angles) * scaling
    sine_part = jnp.sin(angles) * scaling
    matrix = jnp.stack([jnp.stack([cosine_part, -sine_part]), jnp.stack([sine_part, cosine_part])])
    return matrix.astype(jnp.bfloat16)


def twiddle_table(radix_size, sign_value):
    indices = jnp.arange(radix_size, dtype=jnp.int32)
    total = radix_size * radix_size
    products = indices[:, None] * indices[None, :] % total
    angles = products.astype(jnp.float32) * (sign_value * 2.0 * math.pi / total)
    return (jnp.cos(angles), jnp.sin(angles))


def rotate(data, cosine_part, sine_part):
    return jnp.stack(
        [data[0] * cosine_part - data[1] * sine_part, data[0] * sine_part + data[1] * cosine_part]
    )


def contract(form, matrix, data):
    return jnp.einsum(form, matrix, data, preferred_element_type=jnp.float32)


def forward_real(data):
    batch_size = data.shape[1]
    shaped = data.reshape(RADIX, RADIX, batch_size)
    matrix = fourier_tables(RADIX, -1.0)
    cosine_part, sine_part = twiddle_table(RADIX, -1.0)
    opening = contract("oka,abm->okbm", matrix[:, 0], shaped)
    sectioned = rotate(opening, cosine_part[:, :, None], sine_part[:, :, None]).astype(jnp.bfloat16)
    closing = contract("ocjb,ckbm->okjm", matrix, sectioned)
    return closing.reshape(2, N, batch_size).astype(jnp.bfloat16)


def forward_first(data):
    batch_size = data.shape[2]
    shaped = data.reshape(2, RADIX, RADIX, batch_size)
    matrix = fourier_tables(RADIX, -1.0)
    cosine_part, sine_part = twiddle_table(RADIX, -1.0)
    opening = contract("ocka,cabm->okbm", matrix, shaped)
    sectioned = rotate(opening, cosine_part[:, :, None], sine_part[:, :, None]).astype(jnp.bfloat16)
    closing = contract("ocjb,ckbm->okjm", matrix, sectioned)
    return closing.reshape(2, N, batch_size).astype(jnp.bfloat16)


def inverse_first(data):
    batch_size = data.shape[2]
    shaped = data.reshape(2, RADIX, RADIX, batch_size)
    matrix = fourier_tables(RADIX, 1.0)
    cosine_part, sine_part = twiddle_table(RADIX, 1.0)
    opening = contract("ocbj,ckjm->okbm", matrix, shaped)
    sectioned = rotate(opening, cosine_part[:, :, None], sine_part[:, :, None]).astype(jnp.bfloat16)
    closing = contract("ocak,ckbm->oabm", matrix, sectioned)
    return closing.reshape(2, N, batch_size)


def frequencies(positions):
    natural = positions // RADIX + RADIX * (positions % RADIX)
    signed_freq = jnp.where(natural >= N // 2, natural - N, natural)
    return signed_freq.astype(jnp.float32) / N


def propagator(freq_whole, freq_own, distance):
    radial = freq_whole[:, None] ** 2 + freq_own[None, :] ** 2
    limit = wave_number * wave_number
    amplitude = jnp.exp(-2.0 * math.pi * distance * jnp.sqrt(jnp.maximum(radial - limit, 0.0)))
    phase_angle = (
        2.0 * math.pi * distance * (jnp.sqrt(jnp.maximum(limit - radial, 0.0)) - wave_number)
    )
    return (amplitude * jnp.cos(phase_angle), amplitude * jnp.sin(phase_angle))


def propagate(spectrum, cosine_part, sine_part):
    return rotate(spectrum.astype(jnp.float32), cosine_part, sine_part).astype(jnp.bfloat16)


def shards(hologram, background):
    row_count = hologram.shape[0]
    contrast = (hologram.astype(jnp.float32) / background.astype(jnp.float32) - 1.0).astype(
        jnp.bfloat16
    )
    along_rows = forward_real(contrast.T)
    columns = lax.all_to_all(
        jnp.swapaxes(along_rows, 1, 2), "rows", split_axis=2, concat_axis=1, tiled=True
    )
    spectrum = forward_first(columns)
    row_index = lax.axis_index("rows")
    own_positions = row_index * row_count + jnp.arange(row_count, dtype=jnp.int32)
    freq_own = frequencies(own_positions)
    freq_whole = frequencies(jnp.arange(N, dtype=jnp.int32))
    depth_index = lax.axis_index("depth")
    distance = depth_start + depth_step * (depth_index * PL_DEV + 0).astype(jnp.float32)
    cosine_part, sine_part = propagator(freq_whole, freq_own, distance)
    propagated = propagate(spectrum, cosine_part, sine_part)
    halfway = inverse_first(propagated).astype(jnp.bfloat16)
    restored = lax.all_to_all(
        jnp.swapaxes(halfway, 1, 2), "rows", split_axis=2, concat_axis=1, tiled=True
    )
    result_field = inverse_first(restored)
    intensities = [
        (result_field[0] * result_field[0] + result_field[1] * result_field[1]).astype(jnp.bfloat16)
    ]
    stacked = jnp.stack(intensities)
    padded = padded_2(stacked, (("depth", 0), ("rows", 2)), 1)
    centre_block = padded[1:-1, :, 1:-1]
    plane_ids = jnp.arange(PL_DEV, dtype=jnp.int32)[:, None, None]
    row_ids = jnp.arange(row_count, dtype=jnp.int32)[None, None, :]
    depth_count = lax.axis_size("depth")
    row_groups = lax.axis_size("rows")
    lower_plane = jnp.where(
        (depth_index == 0) & (plane_ids == 0), centre_block, padded[:-2, :, 1:-1]
    )
    upper_plane = jnp.where(
        (depth_index == depth_count - 1) & (plane_ids == PL_DEV - 1),
        centre_block,
        padded[2:, :, 1:-1],
    )
    north_row = jnp.where((row_index == 0) & (row_ids == 0), centre_block, padded[1:-1, :, :-2])
    south_row = jnp.where(
        (row_index == row_groups - 1) & (row_ids == row_count - 1),
        centre_block,
        padded[1:-1, :, 2:],
    )
    centre = centre_block.astype(jnp.float32)
    east_col = jnp.concatenate([centre[:, 1:], centre[:, -1:]], axis=1)
    west_col = jnp.concatenate([centre[:, :1], centre[:, :-1]], axis=1)
    depth_diff = upper_plane.astype(jnp.float32) - lower_plane.astype(jnp.float32)
    row_diff = south_row.astype(jnp.float32) - north_row.astype(jnp.float32)
    col_diff = east_col - west_col
    scores = (depth_diff * depth_diff + row_diff * row_diff + col_diff * col_diff) / 8.0
    sharpest = jnp.max(scores, axis=0)
    merged = lax.pmax(sharpest.astype(jnp.bfloat16), "depth").astype(sharpest.dtype)
    return merged.T


OUT = 16
INN = 256
CLS = 8
LANE = 128
MIB = 2**20
VMEM = 63 * MIB
SHARED = 36 * MIB


def slot_frequencies():
    table = np.arange(CLS)[:, None] + OUT * np.arange(INN)[None, :]
    half = np.arange(INN // 2)
    table[0] = np.concatenate([OUT * half, CLS + OUT * half])
    return table


def angles(products):
    return 2.0 * np.pi * (products % N) / N


def row_forward_tables():
    freq = slot_frequencies()
    theta = angles(np.arange(INN)[None, :, None] * freq[:, None, :])
    cos, sin = np.cos(theta) / 64.0, np.sin(theta) / 64.0
    top = np.stack([cos, -sin], axis=2)
    low = np.stack([sin, cos], axis=2)
    first = np.arange(INN) < INN // 2
    low[0] = np.where(first, 0.0, top[0])
    top[0] = np.where(first, top[0], 0.0)
    full = np.concatenate([top, low], axis=1)
    full = full.reshape(CLS, 2 * INN, 2, 2, LANE).transpose(0, 1, 3, 2, 4)
    return full.reshape(CLS, 2 * INN, 2 * INN).astype(jnp.bfloat16)


def row_forward_weights():
    a = np.arange(1, 5)
    rows = []
    for d in range(CLS // 2):
        even, odd = (2.0 * np.pi * c * a / OUT for c in (2 * d, 2 * d + 1))
        parts = np.cos(even), -np.sin(even[:3]), [float(d == 0)], np.cos(odd[:3]), -np.sin(odd), [0.0]
        rows.append(np.concatenate(parts))
    return np.concatenate(rows).astype(np.float32)


def row_inverse_tables():
    half = np.arange(INN // 2)
    position = np.arange(INN)[None, :]
    full = np.zeros((2, 2, INN, 2, INN))
    for first, place in ((0, 0), (CLS, 1)):
        theta = angles((first + OUT * half)[:, None] * position)
        rows = slice(place * INN // 2, (place + 1) * INN // 2)
        full[0, 0, rows, place], full[0, 1, rows, place] = np.cos(theta), -np.sin(theta)
    full[0, 0, 0, 0] = 0.5
    full[0, 1, 0, 0] = 0.5 * (-1.0) ** np.arange(INN)
    theta = angles(OUT * np.arange(INN)[:, None] * position)
    full[1, 0, :, 0], full[1, 0, :, 1] = np.cos(theta), np.sin(theta)
    full[1, 1, :, 0], full[1, 1, :, 1] = -np.sin(theta), np.cos(theta)
    full = full.reshape(2, 2, 2, LANE, 2 * INN).transpose(0, 2, 1, 3, 4) / 32.0
    turn = angles(np.arange(CLS)[:, None] * position)
    turn = np.concatenate([np.cos(turn), np.sin(turn)]).astype(np.float32)
    return full.reshape(2, 2 * INN, 2 * INN).astype(jnp.bfloat16), turn


def column_tables():
    turn = 2.0 * np.pi * np.arange(OUT)[:, None] * np.arange(OUT)[None, :] / OUT
    eye = np.eye(16)
    outer_cos, outer_sin = np.kron(np.cos(turn), eye) / 4.0, np.kron(np.sin(turn), eye) / 4.0
    complex_form = lambda cos, sin: np.concatenate(
        [np.concatenate([cos, -sin], axis=-1), np.concatenate([sin, cos], axis=-1)], axis=-2
    )
    slabs = lambda table: table.reshape(-1, 8, 2, 16).swapaxes(1, 2).reshape(table.shape)
    outer = complex_form(slabs(outer_cos), slabs(-outer_sin))
    half_rows = outer_cos.shape[0] // 2
    cut = lambda table, begin, size: table[begin : begin + size]
    back = np.stack(
        [
            complex_form(cut(outer_cos, begin, half_rows), cut(outer_sin, begin, half_rows))
            for begin in (0, half_rows)
        ]
    )
    beyond = np.stack(
        [complex_form(cut(outer_cos, a * 16, 16), cut(outer_sin, a * 16, 16)) for a in (8, 7)]
    )
    theta = angles(OUT * np.arange(INN)[:, None] * np.arange(INN)[None, :])
    inner = complex_form(np.cos(theta), -np.sin(theta)) / 16.0
    inner_back = complex_form(np.cos(theta), np.sin(theta)) / 16.0
    turn = angles(np.arange(OUT)[:, None] * np.arange(INN)[None, :])
    by_chunk = turn.reshape(OUT, 16, 16).swapaxes(1, 2).reshape(INN, 16)
    twist = np.zeros((2, INN, LANE), np.float32)
    for i, table in enumerate((by_chunk, turn.T)):
        twist[i, :, :16], twist[i, :, 16:32] = np.cos(table), np.sin(table)
    cast = lambda table: table.astype(jnp.bfloat16)
    return cast(outer), cast(inner), cast(inner_back), cast(back), cast(beyond), twist


def dot(left, right):
    return jnp.dot(left, right, preferred_element_type=jnp.float32)


def split_complex(both, width):
    rows = both.shape[0] // 2
    top, low = both[:rows], both[rows:]
    return top[:, :width] - low[:, width:], top[:, width:] + low[:, :width]


def quarter_kernel(radial):
    gap = wave_number * wave_number - radial
    root = jnp.sqrt(jnp.abs(gap))
    inside = gap > 0.0
    half_pi = 0.5 * math.pi
    angle = half_pi * (jnp.where(inside, root, 0.0) - wave_number)
    decay = jnp.exp(jnp.where(inside, 0.0, -half_pi * root))
    square = angle * angle
    sine = 1.0 / 362880.0
    for c in (-1.0 / 5040.0, 1.0 / 120.0, -1.0 / 6.0, 1.0):
        sine = sine * square + c
    cosine = -1.0 / 3628800.0
    for c in (1.0 / 40320.0, -1.0 / 720.0, 1.0 / 24.0, -0.5, 1.0):
        cosine = cosine * square + c
    return decay * cosine, decay * (sine * angle)


def squared(re, im):
    return (re - im) * (re + im), 2.0 * re * im


def start_and_step(radial):
    value = quarter_kernel(radial)
    distance = 0.25
    step = None
    while distance < depth_start:
        value = squared(*value)
        distance *= 2.0
        if distance == depth_step:
            step = value
    return value, step


def signed_fraction(natural):
    return jnp.where(natural >= N // 2, natural - N, natural).astype(jnp.float32) * (1.0 / N)


CHUNK = 64
BATCHES = ((1, 2), (3, 4), (5, 6, 7), (0,))


def sixteen_sums(term, w):
    c0, c8 = term(0), term(8)
    plus, minus = c0 + c8, c0 - c8
    c4, c12 = term(4), term(12)
    e4, o4 = c4 + c12, c4 - c12
    total = plus + e4
    eighth = total
    re_even = plus + w(3) * e4
    im_even = None
    re_odd, im_odd = minus, w(14) * o4
    for a in (1, 2, 3):
        p, q, r, s = term(a), term(16 - a), term(8 - a), term(8 + a)
        e, o, f, h = p + q, p - q, r + s, r - s
        both = e + f
        total = total + both
        eighth = eighth - both if a % 2 else eighth + both
        re_even = re_even + w(a - 1) * both
        term_im = w(3 + a) * (o - h)
        im_even = term_im if im_even is None else im_even + term_im
        re_odd = re_odd + w(7 + a) * (e - f)
        im_odd = im_odd + w(10 + a) * (o + h)
    return re_even, im_even + w(7) * eighth, re_odd, im_odd, total


def row_forward_kernel(
    own, weights, holo, back, table, out, holo_buf, back_buf, table_buf, acc, result, held, sems
):
    rows = holo.shape[0]
    group = own[0]
    chunks = rows // CHUNK
    loads = []
    for i in range(chunks):
        here = pl.ds(i * CHUNK, CHUNK)
        loads.append(
            (
                pltpu.make_async_copy(holo.at[here], holo_buf.at[here], sems.at[0, i]),
                pltpu.make_async_copy(back.at[here], back_buf.at[here], sems.at[1, i]),
            )
        )
        for load in loads[-1]:
            load.start()
        if i == 0:
            tables = pltpu.make_async_copy(table.at[pl.ds(2 * group, 2)], table_buf, sems.at[4, 0])
            tables.start()
    lane = lax.broadcasted_iota(jnp.int32, (16, INN), 1)
    sign = jnp.where(lane % 2 == 0, 1.0, -1.0).astype(jnp.bfloat16)
    stores = []
    for chunk in range(chunks):
        for load in loads[chunk]:
            load.wait()

        def strip(i, carry):
            here = pl.ds(pl.multiple_of(chunk * CHUNK + i * 16, 16), 16)

            def term(a):
                there = pl.ds(a * INN, INN)
                below = back_buf[here, there].astype(jnp.float32)
                inverse = pl.reciprocal(below, approx=True)
                inverse = inverse * (2.0 - below * inverse)
                value = holo_buf[here, there].astype(jnp.float32) * inverse
                return value - 1.0

            sums = sixteen_sums(term, lambda n: weights[group * 16 + n])
            for q in range(4):
                acc[q // 2, here, pl.ds((q % 2) * INN, INN)] = sums[q].astype(jnp.bfloat16)
            acc[2, here, pl.ds(0, INN)] = sums[4].astype(jnp.bfloat16)
            return carry

        lax.fori_loop(0, CHUNK // 16, strip, 0)
        batch = rows // 2 // CHUNK
        if chunk % batch != batch - 1:
            continue
        if chunk < batch:
            tables.wait()
        begin, end = (chunk + 1 - batch) * CHUNK, (chunk + 1) * CHUNK
        for q in range(2):
            both = dot(acc[q, begin:end], table_buf[q]).astype(jnp.bfloat16)
            for low in range(2):
                part = both[:, low * 2 * LANE : (low + 1) * 2 * LANE]
                result[low, q, begin:end, :] = part
        held[chunk // batch] = lax.dot_general(
            sign,
            acc[2, begin:end, :INN],
            (((1,), (1,)), ((), ())),
            preferred_element_type=jnp.float32,
        )
        here = pl.ds(begin, end - begin)
        if chunk == chunks - 1:
            index = lax.broadcasted_iota(jnp.int32, (16, INN), 0)
            extra = jnp.where(index == 0, held[0], held[1]) * (1.0 / 64.0)
            for low in range(2):
                for q in range(2):
                    result[low, q, rows:, :] = extra.astype(jnp.bfloat16)
            here = pl.ds(begin, end - begin + 16)
        for high in range(2):
            source, target = result.at[:, :, here, :], out.at[high, :, :, here, :]
            stores.append(pltpu.make_async_copy(source, target, sems.at[2 + high, chunk]))
            stores[-1].start()
    for store in stores:
        store.wait()


def row_forward(own, hologram, background):
    rows = hologram.shape[0]
    table = jnp.asarray(row_forward_tables())
    weights = jnp.asarray(row_forward_weights())
    hbm = pl.BlockSpec(memory_space=pl.ANY)
    chunks = rows // CHUNK
    return pl.pallas_call(
        row_forward_kernel,
        grid_spec=pltpu.PrefetchScalarGridSpec(
            num_scalar_prefetch=2,
            grid=(1,),
            in_specs=[hbm] * 3,
            out_specs=hbm,
            scratch_shapes=[
                pltpu.VMEM((rows, N), jnp.bfloat16),
                pltpu.VMEM((rows, N), jnp.bfloat16),
                pltpu.VMEM((2, 2 * INN, 2 * INN), jnp.bfloat16),
                pltpu.VMEM((3, rows, 2 * INN), jnp.bfloat16),
                pltpu.VMEM((2, 2, rows + 16, 2 * LANE), jnp.bfloat16),
                pltpu.VMEM((2, 16, INN), jnp.float32),
                pltpu.SemaphoreType.DMA((5, chunks)),
            ],
        ),
        out_shape=jax.ShapeDtypeStruct((2, 2, 2, rows + 16, 2 * LANE), jnp.bfloat16),
        compiler_params=pltpu.CompilerParams(vmem_limit_bytes=VMEM),
        cost_estimate=pl.CostEstimate(flops=10**10, bytes_accessed=12 * MIB, transcendentals=0),
        name="row_forward",
    )(own, weights, hologram, background, table)


def propagator_kernel(planes, fx2, out):
    step = pl.program_id(0)
    strip = 32
    for i in range(INN // strip):
        rows = slice(i * strip, (i + 1) * strip)
        position = lax.broadcasted_iota(jnp.int32, (strip, LANE), 0) + i * strip
        fy = signed_fraction(step + OUT * position)
        (kr, ki), (sr, si) = start_and_step(fy * fy + fx2[...])
        for g in range(planes):
            out[g, 0, rows, :LANE] = kr.astype(jnp.bfloat16)
            out[g, 0, rows, LANE:] = ki.astype(jnp.bfloat16)
            if g + 1 < planes:
                kr, ki = kr * sr - ki * si, kr * si + ki * sr


def propagators(planes, fx2):
    return pl.pallas_call(
        functools.partial(propagator_kernel, planes),
        grid=(OUT,),
        in_specs=[pl.BlockSpec((1, LANE), lambda i: (0, 0))],
        out_specs=pl.BlockSpec((planes, 1, INN, 2 * LANE), lambda i: (0, i, 0, 0)),
        out_shape=jax.ShapeDtypeStruct((planes, OUT, INN, 2 * LANE), jnp.bfloat16),
        compiler_params=pltpu.CompilerParams(vmem_limit_bytes=VMEM),
        cost_estimate=pl.CostEstimate(flops=10**9, bytes_accessed=16 * MIB, transcendentals=10**6),
        name="propagators",
    )(fx2)


PAIRS = OUT // 2


def mix_and_open(pair, both, kernels, inner_back, twist, mixed, second):
    wide = 2 * LANE
    for k in range(2):
        yr, yi = (both[p * INN : (p + 1) * INN, k * LANE : (k + 1) * LANE] for p in range(2))
        for part in range(2):
            factor = kernels[k, :, part * LANE : (part + 1) * LANE].astype(jnp.float32)
            lanes = slice(k * wide + part * LANE, k * wide + (part + 1) * LANE)
            mixed[:INN, lanes] = (yr * factor).astype(jnp.bfloat16)
            mixed[INN:, lanes] = (yi * factor).astype(jnp.bfloat16)
    opened = dot(inner_back[...], mixed[...])
    for k in range(2):
        at = pair * 2 + k
        re, im = (opened[p * INN : (p + 1) * INN, k * wide : (k + 1) * wide] for p in range(2))
        cos, sin = twist[1, :, at : at + 1], twist[1, :, 16 + at : 17 + at]
        second[0, at] = (re * cos - im * sin).astype(jnp.bfloat16)
        second[1, at] = (re * sin + im * cos).astype(jnp.bfloat16)


def outer_block(second, here):
    return second[:, :, here, :].reshape(2 * OUT * 16, 2 * LANE)


def spread(both):
    rows = both.shape[0] // 2
    re, im = both[:rows], both[rows:]
    return [re[:, :LANE], im[:, :LANE], re[:, LANE:], im[:, LANE:]]


def open_outside(half, beyond, second, outside):
    here = pl.ds(pl.multiple_of(half[0] * (INN - 16), 16), 16)
    both = dot(beyond, outer_block(second, here)).astype(jnp.bfloat16)
    for i, value in enumerate(spread(both)):
        outside[:, i * LANE : (i + 1) * LANE] = value


def close_chunk(here, back, second, store):
    both = dot(back, outer_block(second, here)).astype(jnp.bfloat16)
    for i, value in enumerate(spread(both)):
        value = value.reshape(2, 2, 2, 16, LANE)
        for low in range(2):
            for core in range(2):
                for high in range(2):
                    store(high, low, core, slice(i * LANE, (i + 1) * LANE), value[low, core, high])


def first_columns_kernel(
    half, data, kernels, outer_in, inner_in, inner_back_in, back_in, beyond_in, twist_in,
    out, spectrum, outside,
    data_buf, kernel_buf, outer, inner, inner_back, back, beyond, twist,
    out_buf, spectrum_buf, first, mixed, second, sems,
):
    rows = data_buf.shape[1]
    early = [
        pltpu.make_async_copy(source, target, sems.at[3, i])
        for i, (source, target) in enumerate(
            (
                (data.at[:, pl.ds(0, rows), :], data_buf),
                (outer_in, outer),
                (twist_in, twist),
                (inner_in, inner),
                (inner_back_in, inner_back),
                (back_in.at[half[0]], back),
                (beyond_in.at[half[0]], beyond),
            )
        )
    ]
    for load in early:
        load.start()
    loads = []
    for pair in range(PAIRS):
        here = pl.ds(2 * pair, 2)
        loads.append(
            pltpu.make_async_copy(kernels.at[0, here], kernel_buf.at[here], sems.at[1, pair])
        )
        loads[-1].start()
    for load in early[:3]:
        load.wait()
    for i in range(0, INN // 16, 2):
        pieces = []
        for part in range(2):
            lanes = slice(part * LANE, (part + 1) * LANE)
            for parity in range(2):
                at = parity * INN + i * 16
                block = data_buf[:, at : at + 32, lanes]
                block = jnp.concatenate([block[:, :16], block[:, 16:]], axis=2)
                pieces.append(block.reshape(OUT // 2 * 16, 2 * LANE))
        both = dot(outer[...], jnp.concatenate(pieces, axis=0))
        for c in range(2):
            re, im = (both[p * INN : (p + 1) * INN, c * LANE : (c + 1) * LANE] for p in range(2))
            cos, sin = (twist[0, :, t + i + c : t + i + c + 1] for t in (0, 16))
            here = slice((i + c) * 16, (i + c + 1) * 16)
            for part, value in enumerate((re * cos + im * sin, im * cos - re * sin)):
                value = value.astype(jnp.bfloat16).reshape(PAIRS, 2, 16, LANE)
                first[:, part, here, :LANE] = value[:, 0]
                first[:, part, here, LANE:] = value[:, 1]
    stores = []

    def transform(pair):
        block = jnp.concatenate(
            [first[pair + i].reshape(2 * INN, 2 * LANE) for i in range(2)], axis=1
        )
        both = dot(inner[...], block)
        result = []
        for i in range(2):
            result.append(both[:, i * 2 * LANE : (i + 1) * 2 * LANE])
            spectrum_buf[pair + i] = result[i].astype(jnp.bfloat16)
        here = pl.ds(pair, 2)
        copy = pltpu.make_async_copy(spectrum_buf.at[here], spectrum.at[here], sems.at[2, pair])
        stores.append(copy)
        copy.start()
        return result

    early[3].wait()
    both = transform(0)
    early[4].wait()
    for pair in range(PAIRS):
        if pair % 2 == 0:
            now_both = both
            both = transform(pair + 2) if pair + 2 < PAIRS else None
        loads[pair].wait()
        now = kernel_buf.at[pl.ds(2 * pair, 2)]
        mix_and_open(pair, now_both[pair % 2], now, inner_back, twist, mixed.at[pair % 2], second)
    for load in early[5:]:
        load.wait()
    open_outside(half, beyond[...], second, outside.at[0])
    for chunk in range(INN // 16):
        side, rows = chunk // 8, slice(chunk % 8 * 16, chunk % 8 * 16 + 16)

        def store(high, low, core, lanes, value):
            out_buf[side, high, low, core, rows, lanes] = value

        close_chunk(slice(chunk * 16, chunk * 16 + 16), back[...], second, store)
        if chunk % 4 == 3:
            here = pl.ds((chunk % 8 - 3) * 16, 64)
            source = out_buf.at[side, :, :, :, here, :]
            target = out.at[:, side, :, :, here, :]
            stores.append(pltpu.make_async_copy(source, target, sems.at[0, chunk // 4]))
            stores[-1].start()
    for copy in stores:
        copy.wait()


def next_columns_kernel(
    half, spectrum, kernels, inner_back, back, beyond, twist, out, outside, mixed, second
):
    step = pl.program_id(1)
    for s in range(2):

        @pl.when(step == s)
        def _():
            for i in range(PAIRS // 2):
                pair = s * (PAIRS // 2) + i
                both = spectrum[i].astype(jnp.float32)
                now = kernels.at[0, pl.ds(2 * i, 2)]
                mix_and_open(pair, both, now, inner_back, twist, mixed.at[i % 2], second)
            if s == 1:
                open_outside(half, beyond[0], second, outside.at[0])

    @pl.when(step >= 2)
    def _():
        for c in range(8):
            rows = slice(c * 16, (c + 1) * 16)

            def store(high, low, core, lanes, value):
                out[high, 0, low, core, rows, lanes] = value

            start = pl.multiple_of(((step - 2) * 8 + c) * 16, 16)
            close_chunk(pl.ds(start, 16), back[0], second, store)


def first_columns(half, data, kernels):
    tables = [jnp.asarray(t) for t in column_tables()]
    rows = data.shape[1] - 16
    bf16, f32 = jnp.bfloat16, jnp.float32
    hbm = pl.BlockSpec(memory_space=pl.ANY)
    return pl.pallas_call(
        first_columns_kernel,
        grid_spec=pltpu.PrefetchScalarGridSpec(
            num_scalar_prefetch=1,
            grid=(1,),
            in_specs=[hbm] * 8,
            out_specs=[hbm, hbm, pl.BlockSpec((1, 16, 4 * LANE), lambda i, o: (0, 0, 0))],
            scratch_shapes=[
                pltpu.VMEM((8, rows, 2 * LANE), bf16),
                pltpu.VMEM((OUT, INN, 2 * LANE), bf16),
                pltpu.VMEM((2 * INN, 2 * INN), bf16),
                pltpu.VMEM((2 * INN, 2 * INN), bf16),
                pltpu.VMEM((2 * INN, 2 * INN), bf16),
                pltpu.VMEM((INN, 2 * INN), bf16),
                pltpu.VMEM((32, 2 * INN), bf16),
                pltpu.VMEM((2, INN, LANE), f32),
                pltpu.VMEM((2, 2, 2, 2, LANE, 4 * LANE), bf16),
                pltpu.VMEM((PAIRS, 2 * INN, 2 * LANE), bf16),
                pltpu.VMEM((PAIRS, 2, INN, 2 * LANE), bf16),
                pltpu.VMEM((2, 2 * INN, 4 * LANE), bf16),
                pltpu.VMEM((2, OUT, INN, 2 * LANE), bf16),
                pltpu.SemaphoreType.DMA((4, PAIRS)),
            ],
        ),
        out_shape=[
            jax.ShapeDtypeStruct((2, 2, 2, 2, LANE, 4 * LANE), bf16),
            jax.ShapeDtypeStruct((PAIRS, 2 * INN, 2 * LANE), bf16),
            jax.ShapeDtypeStruct((1, 16, 4 * LANE), bf16),
        ],
        compiler_params=pltpu.CompilerParams(vmem_limit_bytes=VMEM),
        cost_estimate=pl.CostEstimate(flops=10**10, bytes_accessed=16 * MIB, transcendentals=0),
        name="first_columns",
    )(half, data, kernels, *tables)


def next_columns(half, plane, count, spectrum, kernels):
    tables = [jnp.asarray(t) for t in column_tables()[2:]]
    opening = lambda i: jnp.minimum(i, 1)
    closing = lambda i: jnp.maximum(i - 2, 0)
    own = lambda g, i, o: (o[0], 0, 0)
    return pl.pallas_call(
        next_columns_kernel,
        grid_spec=pltpu.PrefetchScalarGridSpec(
            num_scalar_prefetch=1,
            grid=(count, 4),
            in_specs=[
                pl.BlockSpec((PAIRS // 2, 2 * INN, 2 * LANE), lambda g, i, o: (opening(i), 0, 0)),
                pl.BlockSpec(
                    (1, OUT // 2, INN, 2 * LANE), lambda g, i, o: (plane + g, opening(i), 0, 0)
                ),
                pl.BlockSpec((2 * INN, 2 * INN), lambda g, i, o: (0, 0)),
                pl.BlockSpec((1, INN, 2 * INN), own),
                pl.BlockSpec((1, 32, 2 * INN), own),
                pl.BlockSpec((2, INN, LANE), lambda g, i, o: (0, 0, 0)),
            ],
            out_specs=[
                pl.BlockSpec(
                    (2, 1, 2, 2, LANE, 4 * LANE), lambda g, i, o: (0, closing(i), 0, 0, 0, g)
                ),
                pl.BlockSpec((1, 16, 4 * LANE), lambda g, i, o: (g, 0, 0)),
            ],
            scratch_shapes=[
                pltpu.VMEM((2, 2 * INN, 4 * LANE), jnp.bfloat16),
                pltpu.VMEM((2, OUT, INN, 2 * LANE), jnp.bfloat16),
            ],
        ),
        out_shape=[
            jax.ShapeDtypeStruct((2, 2, 2, 2, LANE, count * 4 * LANE), jnp.bfloat16),
            jax.ShapeDtypeStruct((count, 16, 4 * LANE), jnp.bfloat16),
        ],
        compiler_params=pltpu.CompilerParams(vmem_limit_bytes=VMEM),
        cost_estimate=pl.CostEstimate(
            flops=count * 7 * 10**9, bytes_accessed=count * 16 * MIB, transcendentals=0
        ),
        name="next_columns",
    )(half, spectrum, kernels, *tables)


def sixteen_points(re, im):
    c = math.sqrt(0.5)
    c1, c3 = math.cos(math.pi / 8), math.cos(3 * math.pi / 8)
    r0, r1, r2, r3, r4, r5, r6, r7 = re
    r8, i1, i2, i3, i4, i5, i6, i7 = im
    sum08, dif08, sum26, dif26 = r0 + r8, r0 - r8, r2 + r6, c * (r2 - r6)
    base = sum08 + r4
    even = [base + sum26, dif08 + dif26, sum08 - r4, dif08 - dif26, base - sum26]
    sum17, dif17, sum35, dif35 = r1 + r7, r1 - r7, r3 + r5, r3 - r5
    odd = [sum17 + sum35, c1 * dif17 + c3 * dif35, c * (sum17 - sum35), c3 * dif17 - c1 * dif35]
    cosines = [even[a] + odd[a] for a in range(4)] + [even[4]]
    cosines += [even[8 - a] - odd[8 - a] for a in range(5, 9)]
    s17, d17, s35, d35 = i1 + i7, i1 - i7, i3 + i5, i3 - i5
    sines_odd = [None, c3 * s17 + c1 * s35, c * (d17 + d35), c1 * s17 - c3 * s35, d17 - d35]
    s26 = c * (i2 + i6)
    sines_even = [None, s26 + i4, i2 - i6, s26 - i4]
    sines = [None] + [sines_odd[a] + sines_even[a] for a in (1, 2, 3)] + [sines_odd[4]]
    sines += [sines_odd[8 - a] - sines_even[8 - a] for a in (5, 6, 7)]
    result = [cosines[0]] + [cosines[a] - sines[a] for a in range(1, 8)] + [cosines[8]]
    return result + [cosines[16 - a] + sines[16 - a] for a in range(9, 16)]


def open_rows(group, both, turn):
    if group == 0:
        return both
    re, im = both[:, :INN], both[:, INN:]
    cos, sin = turn[group : group + 1, :], turn[CLS + group : CLS + group + 1, :]
    return jnp.concatenate([re * cos - im * sin, re * sin + im * cos], axis=1)


def open_classes(groups, halves, columns, table, turn, opened):
    blocks = []
    for group, (low, high) in zip(groups, halves):
        for part in range(2):
            lanes = slice(part * 2 * LANE, (part + 1) * 2 * LANE)
            first, rest = low[:, lanes], high[:, lanes]
            if group == 0:
                lane = lax.broadcasted_iota(jnp.int32, (first.shape[0], LANE), 1)
                im = jnp.where(lane == 0, columns[part], first[:, LANE:])
                first = jnp.concatenate([first[:, :LANE], im], axis=1)
            blocks.append(jnp.concatenate([first, rest], axis=1))
    rows = blocks[0].shape[0]
    both = dot(jnp.concatenate(blocks, axis=0), table[min(groups[0], 1)])
    for i, group in enumerate(groups):
        for part in range(2):
            at = (2 * i + part) * rows
            opened[part, group] = open_rows(group, both[at : at + rows], turn)


def strip_intensity(opened, here, tile):
    total = None
    for part in range(2):
        re = [opened[part, g, here, tile * LANE : (tile + 1) * LANE] for g in range(CLS)]
        im = [opened[part, g, here, INN + tile * LANE : INN + (tile + 1) * LANE] for g in range(CLS)]
        values = sixteen_points(re, im)
        if total is None:
            total = [v * v for v in values]
        else:
            total = [t + v * v for t, v in zip(total, values)]
    return total


def row_inverse_kernel(plane, parts, nyquist, table, turn, out, edges, opened):
    current = plane + pl.program_id(0)
    rows = parts.shape[3]
    lane = lax.broadcasted_iota(jnp.int32, (rows, LANE), 1)
    columns = []
    for part in range(2):
        mine = jnp.where(lane == current * 2 + part, nyquist[...], 0.0)
        columns.append(jnp.sum(mine, axis=1, keepdims=True).astype(jnp.bfloat16))
    for groups in BATCHES:
        halves = [[parts[g // 2, i, g % 2] for i in range(2)] for g in groups]
        open_classes(groups, halves, columns, table, turn, opened)

    def strip(i, carry):
        here = pl.ds(pl.multiple_of(i * 16, 16), 16)
        for tile in range(INN // LANE):
            total = strip_intensity(opened, here, tile)
            for a in range(OUT):
                lanes = slice(a * INN + tile * LANE, a * INN + (tile + 1) * LANE)
                out[0, here, lanes] = total[a].astype(jnp.bfloat16)
        return carry

    lax.fori_loop(0, rows // 16, strip, 0)
    edges[0, 0:8, :] = out[0, 0:16, :].astype(jnp.float32)[0:8]
    edges[0, 8:16, :] = out[0, rows - 16 :, :].astype(jnp.float32)[8:16]


def row_inverse(plane, count, parts, nyquist):
    rows = parts.shape[3]
    table, turn = (jnp.asarray(t) for t in row_inverse_tables())
    return pl.pallas_call(
        functools.partial(row_inverse_kernel, plane),
        grid=(count,),
        in_specs=[
            pl.BlockSpec((4, 2, 2, rows, 4 * LANE), lambda g: (0, 0, 0, 0, g)),
            pl.BlockSpec((rows, LANE), lambda g: (0, 0)),
            pl.BlockSpec((2, 2 * INN, 2 * INN), lambda g: (0, 0, 0)),
            pl.BlockSpec((2 * CLS, INN), lambda g: (0, 0)),
        ],
        out_specs=[
            pl.BlockSpec((1, rows, N), lambda g: (g, 0, 0)),
            pl.BlockSpec((1, 16, N), lambda g: (g, 0, 0)),
        ],
        out_shape=[
            jax.ShapeDtypeStruct((count, rows, N), jnp.bfloat16),
            jax.ShapeDtypeStruct((count, 16, N), jnp.float32),
        ],
        scratch_shapes=[pltpu.VMEM((2, CLS, rows, 2 * INN), jnp.float32)],
        compiler_params=pltpu.CompilerParams(vmem_limit_bytes=VMEM),
        cost_estimate=pl.CostEstimate(
            flops=count * 3 * 10**9, bytes_accessed=count * 8 * MIB, transcendentals=0
        ),
        name="row_inverse",
    )(parts, nyquist, table, turn)


def nyquist_kernel(planes, own, data, out):
    wide = lambda axis: lax.broadcasted_iota(jnp.int32, (INN, INN), axis)
    tall = lambda axis: lax.broadcasted_iota(jnp.int32, (OUT, INN), axis)
    small = lambda axis: lax.broadcasted_iota(jnp.int32, (OUT, OUT), axis)

    def wave(products, period):
        turn = (products % period).astype(jnp.float32) * (2.0 * math.pi / period)
        return jnp.cos(turn), jnp.sin(turn)

    def exact(left, right):
        return jnp.dot(left, right, preferred_element_type=jnp.float32, precision=lax.Precision.HIGHEST)

    def product(xr, xi, yr, yi):
        return exact(xr, yr) - exact(xi, yi), exact(xr, yi) + exact(xi, yr)

    def rotated(xr, xi, yr, yi):
        return xr * yr - xi * yi, xr * yi + xi * yr

    column = jnp.concatenate([data[i, 0:2, :].astype(jnp.float32) for i in range(8)], axis=0)
    wr, wi = wave(small(0) * small(1), OUT)
    inner_r, inner_i = wave(wide(0) * wide(1), INN)
    vr, vi = wave(tall(0) * tall(1), N)
    ar, ai = rotated(exact(wr, column), exact(-wi, column), vr, -vi)
    yr, yi = product(ar, ai, inner_r, -inner_i)
    fy = signed_fraction(tall(0) + OUT * tall(1))
    (kr, ki), (sr, si) = start_and_step(fy * fy + 0.25)
    block, blocks = own[0], own[1]
    k = lax.broadcasted_iota(jnp.int32, (8, OUT), 1)
    section = block // 2 + lax.broadcasted_iota(jnp.int32, (8, OUT), 0) + (OUT - 1)
    hr, hi = wave(k * (section % OUT), OUT)
    even = block % 2 == 0
    lane = lax.broadcasted_iota(jnp.int32, (1, LANE), 1)
    result, beside = [], []
    for g in range(planes):
        pr, pi = rotated(yr, yi, kr, ki)
        br, bi = rotated(*product(pr, pi, inner_r, inner_i), vr, vi)
        for value in product(hr, hi, br, bi):
            value = value * (1.0 / N)
            result.append(jnp.where(even, value[1:2, :LANE], value[1:2, LANE:]))
            above = jnp.where(even, value[0:1, INN - 1 :], value[1:2, LANE - 1 : LANE])
            above = jnp.where(block == 0, value[1:2, 0:1], above)
            below = jnp.where(even, value[1:2, LANE : LANE + 1], value[2:3, 0:1])
            below = jnp.where(block == blocks - 1, value[1:2, INN - 1 :], below)
            beside.append(jnp.where(lane == 0, above, jnp.where(lane == 1, below, 0.0)))
        kr, ki = rotated(kr, ki, sr, si)
    rest = [jnp.zeros((LANE - 2 * planes, LANE), jnp.float32)]
    out[:LANE, :] = jnp.concatenate(result + rest, axis=0).T
    out[LANE:, :] = jnp.concatenate(beside + rest, axis=0).T


def nyquist_column(own, planes, data):
    rows = data.shape[1] - 16
    return pl.pallas_call(
        functools.partial(nyquist_kernel, planes),
        grid_spec=pltpu.PrefetchScalarGridSpec(
            num_scalar_prefetch=1,
            grid=(1,),
            in_specs=[pl.BlockSpec((8, 16, 2 * LANE), lambda i, o: (0, rows // 16, 0))],
            out_specs=pl.BlockSpec((2 * LANE, LANE), lambda i, o: (0, 0)),
        ),
        out_shape=jax.ShapeDtypeStruct((2 * LANE, LANE), jnp.float32),
        compiler_params=pltpu.CompilerParams(vmem_limit_bytes=VMEM),
        cost_estimate=pl.CostEstimate(flops=10**9, bytes_accessed=2**18, transcendentals=0),
        name="nyquist",
    )(own, data)


TILE = 512


def across(centre, tile, west, east):
    lane = lax.broadcasted_iota(jnp.int32, centre.shape, 1)
    right = jnp.where(lane == TILE - 1, east, pltpu.roll(centre, TILE - 1, 1))
    left = jnp.where(lane == 0, west, pltpu.roll(centre, 1, 1))
    return (right - left) * (right - left)


def spatial_term(held, r, t):
    lanes = slice(t * TILE, (t + 1) * TILE)
    around = held[pl.ds(pl.multiple_of(r - 8, 8), 32), lanes]
    centre, down = around[8:24], around[9:25] - around[7:23]
    first, last = max(t * TILE - 1, 0), min((t + 1) * TILE, N - 1)
    here = pl.ds(r, 16)
    west, east = held[here, first : first + 1], held[here, last : last + 1]
    return centre, down * down + across(centre, TILE, west, east)


def hold(held, block, rows):
    held[8 : 8 + rows, :] = block.astype(jnp.float32)
    held[7:8, :] = held[8:9, :]
    held[8 + rows : 9 + rows, :] = held[7 + rows : 8 + rows, :]


def early_focus_kernel(first, others, best, spatial, held):
    rows = first.shape[1]
    for g in range(3):
        hold(held.at[g], first[0] if g == 0 else others[g - 1], rows)

    def strip(i, carry):
        r = pl.multiple_of(8 + i * 16, 8)
        here = pl.ds(pl.multiple_of(i * 16, 16), 16)
        for t in range(N // TILE):
            lanes = slice(t * TILE, (t + 1) * TILE)
            (c0, s0), (c1, s1), (c2, s2) = (spatial_term(held.at[g], r, t) for g in range(3))
            d0, d1 = c1 - c0, c2 - c0
            score = jnp.maximum(d0 * d0 + s0, d1 * d1 + s1)
            best[here, lanes] = (score * 0.125).astype(jnp.bfloat16)
            spatial[here, lanes] = s2.astype(jnp.bfloat16)
        return carry

    lax.fori_loop(0, rows // 16, strip, 0)


def early_focus(first, others):
    rows = first.shape[1]
    return pl.pallas_call(
        early_focus_kernel,
        out_shape=[
            jax.ShapeDtypeStruct((rows, N), jnp.bfloat16),
            jax.ShapeDtypeStruct((rows, N), jnp.bfloat16),
        ],
        scratch_shapes=[pltpu.VMEM((3, rows + 16, N), jnp.float32)],
        compiler_params=pltpu.CompilerParams(vmem_limit_bytes=VMEM),
        cost_estimate=pl.CostEstimate(flops=10**9, bytes_accessed=12 * MIB, transcendentals=0),
        name="early_focus",
    )(first, others)


def edge_rows(edges, halo):
    lane = lax.broadcasted_iota(jnp.int32, (2, N), 1)
    pair = lambda a, b: jnp.concatenate([a, b], axis=0)
    centre = [pair(e[0:1, :], e[15:16, :]) for e in edges]
    best = None
    for g, e in enumerate(edges):
        depth = centre[min(g + 1, 3)] - centre[max(g - 1, 0)]
        above, below = halo[2 * g : 2 * g + 1, :], halo[2 * g + 1 : 2 * g + 2, :]
        down = pair(e[1:2, :], below) - pair(above, e[14:15, :])
        c = centre[g]
        right = jnp.where(lane == N - 1, c, jnp.concatenate([c[:, 1:], c[:, :1]], axis=1))
        left = jnp.where(lane == 0, c, jnp.concatenate([c[:, -1:], c[:, :-1]], axis=1))
        score = depth * depth + down * down + (right - left) * (right - left)
        best = score if best is None else jnp.maximum(best, score)
    return best * 0.125


def last_rows_kernel(
    parts, best, spatial, others, nyquist_in, table_in, turn_in, edge0_in, edge12_in,
    upper_out, lower_out,
    both, nyquist, table, turn, edge0, edge12, part_buf, best_buf, spatial_buf, others_buf, opened, held, halo, edge, sems,
):
    rows = both.shape[0]
    loads = []
    for group in range(CLS):
        source = parts.at[group // 2, :, group % 2]
        loads.append(pltpu.make_async_copy(source, part_buf.at[group], sems.at[0, group]))
    late = (best, best_buf), (spatial, spatial_buf), (others, others_buf)
    late += (edge0_in, edge0), (edge12_in, edge12)
    for i, (source, target) in enumerate(late):
        loads.append(pltpu.make_async_copy(source, target, sems.at[1, i]))
    early = (turn_in, turn), (table_in.at[1], table.at[1])
    early += (table_in.at[0], table.at[0]), (nyquist_in, nyquist)
    early = [pltpu.make_async_copy(a, b, sems.at[2, i]) for i, (a, b) in enumerate(early)]
    for load in early[:2] + loads[1:CLS] + early[2:] + loads[:1] + loads[CLS:]:
        load.start()
    for load in early[:2]:
        load.wait()
    lane = lax.broadcasted_iota(jnp.int32, (rows, LANE), 1)
    few_lane = lax.broadcasted_iota(jnp.int32, (16, LANE), 1)
    few_row = lax.broadcasted_iota(jnp.int32, (16, LANE), 0)
    columns = []
    for groups in BATCHES:
        for group in groups:
            loads[group].wait()
        if groups[0] == 0:
            for load in early[2:]:
                load.wait()
            beside = jnp.where(few_row % 2 == 0, nyquist[rows : rows + 1, :], nyquist[rows + 1 : rows + 2, :])
            for part in range(2):
                mine = jnp.where(lane == 6 + part, nyquist[:rows, :], 0.0)
                few = jnp.where(few_lane == (few_row // 2) * 2 + part, beside, 0.0)
                column = jnp.sum(jnp.concatenate([mine, few], axis=0), axis=1, keepdims=True)
                columns.append(column.astype(jnp.bfloat16))
        halves = [[part_buf[g, i] for i in range(2)] for g in groups]
        open_classes(groups, halves, columns, table, turn, opened)

    def strip(i, carry):
        base = pl.multiple_of(i * 8, 8)
        for tile in range(INN // LANE):
            for a, value in enumerate(strip_intensity(opened, pl.ds(base, 8), tile)):
                lanes = slice(a * INN + tile * LANE, a * INN + (tile + 1) * LANE)
                value = value.astype(jnp.bfloat16).astype(jnp.float32)
                held[pl.ds(pl.multiple_of(base + 8, 8), 8), lanes] = value
        return carry

    lax.fori_loop(0, rows // 8 + 1, strip, 0)
    halo[...] = held[8 + rows : 16 + rows, :]
    held[7:8, :] = held[8:9, :]
    held[8 + rows : 9 + rows, :] = held[7 + rows : 8 + rows, :]
    edge[0:8, :] = held[8:16, :]
    edge[8:16, :] = held[rows : rows + 8, :]
    for load in loads[CLS:]:
        load.wait()
    ends = edge_rows([edge0.at[0], edge12.at[0], edge12.at[1], edge], halo)

    def measure(i, carry):
        r = pl.multiple_of(8 + i * 16, 8)
        here = pl.ds(pl.multiple_of(i * 16, 16), 16)
        for t in range(N // TILE):
            lanes = slice(t * TILE, (t + 1) * TILE)
            centre, term = spatial_term(held, r, t)
            d2 = centre - others_buf[0, here, lanes].astype(jnp.float32)
            d3 = centre - others_buf[1, here, lanes].astype(jnp.float32)
            score = jnp.maximum(d2 * d2 + spatial_buf[here, lanes].astype(jnp.float32), d3 * d3 + term)
            score = jnp.maximum(score * 0.125, best_buf[here, lanes].astype(jnp.float32))
            both[here, lanes] = score.astype(jnp.bfloat16)
        return carry

    half = rows // 2
    stores = []
    for side, out in enumerate((upper_out, lower_out)):
        lax.fori_loop(side * (half // 16), (side + 1) * (half // 16), measure, 0)
        here = slice(0, 16) if side == 0 else slice(rows - 16, rows)
        index = lax.broadcasted_iota(jnp.int32, (16, N), 0)
        value = jnp.where(index == 15 * side, ends[side : side + 1], both[here].astype(jnp.float32))
        both[here] = value.astype(jnp.bfloat16)
        source = both.at[pl.ds(side * half, half)]
        stores.append(pltpu.make_async_copy(source, out, sems.at[2, 4 + side]))
        stores[-1].start()
    for store in stores:
        store.wait()


def last_rows(parts, nyquist, best, spatial, others, edge0, edge12):
    rows = best.shape[0]
    table, turn = (jnp.asarray(t) for t in row_inverse_tables())
    hbm = pl.BlockSpec(memory_space=pl.ANY)
    bf16, f32 = jnp.bfloat16, jnp.float32
    return pl.pallas_call(
        last_rows_kernel,
        in_specs=[hbm] * 9,
        out_specs=[hbm] * 2,
        out_shape=[jax.ShapeDtypeStruct((rows // 2, N), bf16)] * 2,
        scratch_shapes=[
            pltpu.VMEM((rows, N), bf16),
            pltpu.VMEM((2 * LANE, LANE), f32),
            pltpu.VMEM((2, 2 * INN, 2 * INN), bf16),
            pltpu.VMEM((2 * CLS, INN), f32),
            pltpu.VMEM((1, 16, N), f32),
            pltpu.VMEM((2, 16, N), f32),
            pltpu.VMEM((CLS, 2, rows + 16, 4 * LANE), bf16),
            pltpu.VMEM((rows, N), bf16),
            pltpu.VMEM((rows, N), bf16),
            pltpu.VMEM((2, rows, N), bf16),
            pltpu.VMEM((2, CLS, rows + 16, 2 * INN), f32),
            pltpu.VMEM((rows + 16, N), f32),
            pltpu.VMEM((8, N), f32),
            pltpu.VMEM((16, N), f32),
            pltpu.SemaphoreType.DMA((3, CLS)),
        ],
        compiler_params=pltpu.CompilerParams(vmem_limit_bytes=VMEM),
        cost_estimate=pl.CostEstimate(flops=3 * 10**9, bytes_accessed=16 * MIB, transcendentals=0),
        name="last_rows",
    )(parts, best, spatial, others, nyquist, table, turn, edge0, edge12)


def assemble_kernel(own, *refs):
    slot, out = pl.program_id(0), refs[-1]
    half = refs[0].shape[0]
    for s in range(3):

        @pl.when(slot == s)
        def _():
            out[:half] = refs[s][...].astype(jnp.float32)
            out[half:] = refs[3 + s][...].astype(jnp.float32)


def assemble(depth_index, upper, lower):
    half = upper[0].shape[0]
    whole = pl.BlockSpec((half, N), lambda s, o: (0, 0))
    return pl.pallas_call(
        assemble_kernel,
        grid_spec=pltpu.PrefetchScalarGridSpec(
            num_scalar_prefetch=1,
            grid=(3,),
            in_specs=[whole] * 6,
            out_specs=pl.BlockSpec((2 * half, N), lambda s, o: (jnp.bitwise_xor(s, o[0]), 0)),
        ),
        out_shape=jax.ShapeDtypeStruct((8 * half, N), jnp.float32),
        compiler_params=pltpu.CompilerParams(vmem_limit_bytes=20 * MIB),
        cost_estimate=pl.CostEstimate(flops=10**6, bytes_accessed=10 * MIB, transcendentals=0),
        name="assemble",
    )(depth_index, *upper, *lower)


def complete_kernel(own, upper, lower, whole, out):
    step = pl.program_id(0)
    for s, ref in enumerate((upper, lower)):

        @pl.when(step == s)
        def _():
            out[...] = ref[...].astype(jnp.float32)


def complete(depth_index, upper, lower, whole):
    half = upper.shape[0]
    both = pl.BlockSpec((half, N), lambda i, o: (0, 0))
    place = lambda i, o: (jnp.bitwise_xor(3, o[0]) * 2 + i, 0)
    return pl.pallas_call(
        complete_kernel,
        grid_spec=pltpu.PrefetchScalarGridSpec(
            num_scalar_prefetch=1,
            grid=(2,),
            in_specs=[both, both, pl.BlockSpec(memory_space=pl.ANY)],
            out_specs=pl.BlockSpec((half, N), place),
        ),
        out_shape=jax.ShapeDtypeStruct(whole.shape, jnp.float32),
        input_output_aliases={3: 0},
        compiler_params=pltpu.CompilerParams(vmem_limit_bytes=20 * MIB),
        cost_estimate=pl.CostEstimate(flops=10**6, bytes_accessed=3 * MIB, transcendentals=0),
        name="complete",
    )(depth_index, upper, lower, whole)


OVER_X = [(i, i ^ 1) for i in range(4)]
OVER_Y = [(i, i ^ 2) for i in range(4)]


def exchange_depth(a, b):
    ax, by = lax.ppermute(a, "depth", OVER_X), lax.ppermute(b, "depth", OVER_Y)
    ay, axy = lax.ppermute(a, "depth", OVER_Y), lax.ppermute(ax, "depth", OVER_Y)
    bx, byx = lax.ppermute(b, "depth", OVER_X), lax.ppermute(by, "depth", OVER_X)
    return (a, ax, ay, axy), (b, bx, by, byx)


def border_rows(halfway, outside, high):
    lanes = 4 * LANE
    count = halfway.shape[-1] // lanes
    natural = lambda rows: rows.reshape(4, 2, 2, count, lanes).transpose(1, 2, 0, 3, 4).reshape(16, count, lanes)
    first, last = natural(halfway[..., 0, :]), natural(halfway[..., -1, :])
    above = jnp.where(high == 0, first[:1], outside[None, :, 15])
    below = jnp.where(high == 0, outside[None, :, 0], last[-1:])
    above = jnp.concatenate([above, last[:-1]])
    below = jnp.concatenate([first[1:], below])
    both = jnp.stack([above, below], axis=2).reshape(2, 2, 4, 2 * count, lanes)
    return both.transpose(2, 0, 1, 3, 4).reshape(16, 2 * count, lanes)


def half_spectrum_shards(hologram, background):
    rows = hologram.shape[0]
    planes = lax.axis_size("depth") * PL_DEV
    depth, high = lax.axis_index("depth"), lax.axis_index("high")
    low, core = lax.axis_index("low"), lax.axis_index("core")
    as_scalar = lambda value: jnp.reshape(value, (1,)).astype(jnp.int32)
    own = rows // 4
    block = ((high * 2 + low) * 2 + core) * 4 + depth
    place = jnp.stack([block, jnp.int32(N // own)]).astype(jnp.int32)

    sections = row_forward(as_scalar(depth), hologram, background)
    data = lax.all_to_all(
        sections.reshape(8, rows + 16, 2 * LANE),
        ("high", "low", "core"),
        split_axis=0,
        concat_axis=0,
        tiled=True,
    )

    group = depth * 2 + core
    slot = low * LANE + jnp.arange(LANE, dtype=jnp.int32)
    special = jnp.where(low == 0, 0, CLS) + OUT * jnp.arange(LANE, dtype=jnp.int32)
    fx = signed_fraction(jnp.where(group == 0, special, group + OUT * slot))
    kernels = propagators(planes, (fx * fx)[None])

    def to_rows(halfway):
        parts = lax.all_to_all(
            halfway.reshape(16, -1, halfway.shape[-1]),
            ("depth", "low", "core"),
            split_axis=0,
            concat_axis=0,
            tiled=True,
        )
        return parts.reshape(4, 2, 2, -1, halfway.shape[-1])

    halfway, spectrum, outside = first_columns(as_scalar(high), data, kernels)
    parts, borders = [to_rows(halfway)], [border_rows(halfway, outside, high)]
    for plane, count in ((1, 2), (3, 1)):
        halfway, outside = next_columns(as_scalar(high), plane, count, spectrum, kernels)
        borders.append(border_rows(halfway, outside, high))
        halfway = halfway.reshape(16, own, -1)
        if plane == 3:
            below = jnp.concatenate(borders, axis=1)
            below = jnp.pad(below, ((0, 0), (0, 16 - 2 * planes), (0, 0)))
            halfway = jnp.concatenate([halfway, below], axis=1)
        ready = parts[-1]
        if plane == 3:
            first, first_edge = row_inverse(0, 1, parts[0], middle)
            ready = ready, first, first_edge
        elif plane == 1:
            middle = nyquist_column(place, planes, data)
            ready = ready, middle
        halfway, ready = lax.optimization_barrier((halfway, ready))
        if plane == 3:
            parts[-1], first, first_edge = ready
        else:
            parts[-1], middle = ready
        parts.append(to_rows(halfway))
    others, others_edge = row_inverse(1, 2, parts[1], middle)
    best, spatial = early_focus(first, others)
    upper, lower = last_rows(parts[2], middle, best, spatial, others, first_edge, others_edge)
    upper, lower = exchange_depth(upper, lower)
    whole = assemble(as_scalar(depth), upper[:3], lower[:3])
    return complete(as_scalar(depth), upper[3], lower[3], whole)


def solution(mesh):
    spec = P("rows", None)
    if mesh.shape["depth"] == 4 and mesh.shape["rows"] == 8:
        split = Mesh(mesh.devices.reshape(4, 2, 2, 2), ("depth", "high", "low", "core"))
        spec = P(("high", "low", "core"), None)
        body = half_spectrum_shards
    else:
        split, body = mesh, shards
    return jax.shard_map(body, mesh=split, in_specs=(spec, spec), out_specs=spec, check_vma=False)
```
